32 devices in a mesh: box: 16 (over z, x, core), face: 2 (over y).
Axes of the slice: x: 2, y: 2, z: 4, core: 2. Of those that a mesh axis runs over, the one named last changes fastest.
Arguments:
- leaf_maps: bfloat16 [2, 1, 16, 3, 512, 1536], P(None, None, 'box', None, 'face'), may hold values from -6 to 6
- w_first: bfloat16 [2, 1, 4096, 512], P(None, None, 'box'), may hold values from -0.01171875 to 0.01171875
- w_second: bfloat16 [2, 1, 2048, 512], P(None, None, 'box'), may hold values from -0.01171875 to 0.01171875
- skel_first: int32 [1, 8, 512], replicated, may hold values from 0 to 1023, as said below
- skel_second: int32 [1, 4, 512], replicated, may hold values from 0 to 1023, as said below
Outputs:
- grand_maps: bfloat16 [2, 1, 8192, 1536], P(None, None, ('box', 'face'))
The draws below stay inside these ranges and needn't reach their ends.
Inputs may be any that keep to these rules, and one draw needn't show every extreme that they name: `skel_first`: each row holds 512 distinct indices, 0 and 1023 among them. `skel_second`: each row holds 512 distinct indices, 0 and 1023 among them.
All inputs are finite; a program needn't handle non-finite values.
Results may differ from the reference program's by a relative error of at most 0.0075.
Values may be sent and summed in bfloat16 or wider, within the bound.
No kernel may reach another device: no remote copies, remote signals or barrier semaphores. Data moves between devices by JAX's collectives and lax.ppermute only.
A program may use at most 64 MiB of HBM per device.

```python
import jax
import jax.numpy as jnp
from jax import lax

K = 512
TREES = 1
PARENTS = 8
GRANDS = 4
N_BOX = 16
N_FACE = 2


def skeleton_draw(base_key, count):
    block_len = K // N_FACE
    block_total = 2 * N_FACE
    whole_count = max(1, N_FACE // 2)
    rest_count = K - whole_count * block_len
    all_keys = jax.random.split(base_key, count)

    def one_row(row_key):
        src_key, dst_key, noise_key, inner_key, rest_key = jax.random.split(row_key, 5)
        src_order = jax.random.permutation(src_key, jnp.arange(block_total, dtype=jnp.int32))
        dst_order = jax.random.permutation(dst_key, jnp.arange(N_FACE, dtype=jnp.int32))
        whole_src = src_order[:whole_count]
        index_all = jnp.arange(2 * K, dtype=jnp.int32)
        in_whole = jnp.any((index_all // block_len)[:, None] == whole_src[None, :], axis=1)
        is_end = (index_all == 0) | (index_all == 2 * K - 1)
        noise = jax.random.permutation(noise_key, jnp.arange(2 * K, dtype=jnp.int32))
        score = noise + 2 * K * is_end.astype(jnp.int32) + 4 * K * in_whole.astype(jnp.int32)
        top_scores, chosen = lax.top_k(score, K)
        chosen = chosen.astype(jnp.int32)
        inner = jax.random.permutation(inner_key, jnp.arange(block_len, dtype=jnp.int32))
        whole_rows = whole_src[:, None] * block_len + inner[None, :]
        rest_rows = jax.random.permutation(rest_key, chosen[whole_count * block_len:])
        layout = jnp.zeros((N_FACE, block_len), jnp.int32)
        layout = layout.at[dst_order[:whole_count]].set(whole_rows)
        if rest_count > 0:
            layout = layout.at[dst_order[whole_count:]].set(rest_rows.reshape(N_FACE - whole_count, block_len))
        return layout.reshape(K)
    return jax.vmap(one_row)(all_keys)


def draw_skel_first(key, part):
    return skeleton_draw(jax.random.fold_in(key, 11), TREES * PARENTS).reshape(TREES, PARENTS, K)


def draw_skel_second(key, part):
    return skeleton_draw(jax.random.fold_in(key, 23), TREES * GRANDS).reshape(TREES, GRANDS, K)


def level_of(rng, shape, cuts, smallest, top_value):
    level, own = 1.0, jax.random.fold_in(rng, 6)
    for dim, shards_of in cuts:
        draws = jnp.exp(jax.random.uniform(jax.random.fold_in(own, dim), (shards_of,), jnp.float32, smallest / len(cuts), top_value / len(cuts)))
        level = level * jnp.repeat(draws, shape[dim] // shards_of).reshape([-1 if axis == dim else 1 for axis in range(len(shape))])
    return level


def scatter_about(own_key, shape, deviation, limit, pieces=(), kind=jnp.bfloat16):
    entries = jax.random.normal(own_key, shape, jnp.float32) * deviation
    if len(pieces) > 0:
        entries = level_of(own_key, shape, pieces, -0.22, 0.18) * entries
    return jnp.clip(entries, min=-limit, max=limit).astype(kind)


def setup_inputs(seed: int = 0) -> dict:
    splits = jax.random.split(jax.random.key(seed), 6)
    leaf_maps = scatter_about(splits[0], (2, TREES, N_BOX, 3, K, 3 * K), 1.0, 6.0, ((2, 16), (4, 2)))
    w_first = scatter_about(splits[1], (2, TREES, PARENTS * K, K), (K * K) ** -0.5, 0.01171875, ((2, 16),))
    w_second = scatter_about(splits[2], (2, TREES, GRANDS * K, K), (K * K) ** -0.5, 0.01171875, ((2, 16),))
    skel_first = draw_skel_first(jax.random.fold_in(splits[5], 71), 0)
    skel_second = draw_skel_second(jax.random.fold_in(splits[5], 71), 0)
    return {"leaf_maps": leaf_maps, "w_first": w_first, "w_second": w_second, "skel_first": skel_first, "skel_second": skel_second}


def complex_dot(left_op, right_op):
    left_op = left_op.astype(jnp.float32)
    right_op = right_op.astype(jnp.float32)

    def real_dot(first_op, second_op):
        return jnp.matmul(first_op, second_op, precision=lax.Precision.HIGHEST)

    real_part = real_dot(left_op[0], right_op[0]) - real_dot(left_op[1], right_op[1])
    imag_part = real_dot(left_op[0], right_op[1]) + real_dot(left_op[1], right_op[0])
    return jnp.stack([real_part, imag_part])


def merge_pair(left_map, right_map, weight_inv, skeleton, keep_rows):
    ext_left = jnp.concatenate([jnp.arange(K), jnp.arange(2 * K, 3 * K)]).astype(jnp.int32)
    int_left = jnp.arange(K, 2 * K).astype(jnp.int32)
    ext_right = jnp.concatenate([jnp.arange(2 * K, 3 * K), jnp.arange(K, 2 * K)]).astype(jnp.int32)
    int_right = jnp.arange(0, K).astype(jnp.int32)
    left_ext = jnp.take(left_map, ext_left, axis=1)
    right_ext = jnp.take(right_map, ext_right, axis=1)
    couple_rows = jnp.concatenate([jnp.take(left_ext, int_left, axis=2), jnp.take(right_ext, int_right, axis=2)], axis=1)
    iface_cols = jnp.concatenate([jnp.take(jnp.take(left_map, int_left, axis=1), ext_left, axis=2),
                                  jnp.take(jnp.take(right_map, int_right, axis=1), ext_right, axis=2)], axis=2)
    zero_block = jnp.zeros((2, 2 * K, 2 * K), left_map.dtype)
    block_diag = jnp.concatenate([
        jnp.concatenate([jnp.take(left_ext, ext_left, axis=2), zero_block], axis=2),
        jnp.concatenate([zero_block, jnp.take(right_ext, ext_right, axis=2)], axis=2)], axis=1)
    selected = jnp.concatenate([jnp.arange(K).astype(jnp.int32), jnp.arange(3 * K, 4 * K).astype(jnp.int32),
                                K + skeleton.astype(jnp.int32)])
    if keep_rows:
        couple_rows = jnp.take(couple_rows, selected, axis=1)
        block_diag = jnp.take(block_diag, selected, axis=1)
    hidden = complex_dot(couple_rows, weight_inv).astype(jnp.bfloat16)
    merged = jnp.take(block_diag, selected, axis=2).astype(jnp.float32) - complex_dot(hidden, jnp.take(iface_cols, selected, axis=2))
    return merged.astype(jnp.bfloat16)


def reference(leaf_maps, w_first, w_second, skel_first, skel_second):
    outputs = []
    for tree_index in range(TREES):
        leaves = leaf_maps[:, tree_index].reshape(2, PARENTS, 2, 3 * K, 3 * K)
        w_one = w_first[:, tree_index].reshape(2, PARENTS, K, K)
        w_two = w_second[:, tree_index].reshape(2, GRANDS, K, K)

        def level_one(parent):
            return merge_pair(leaves[:, parent, 0], leaves[:, parent, 1], w_one[:, parent],
                              skel_first[tree_index, parent], True)

        parents = lax.map(level_one, jnp.arange(PARENTS).astype(jnp.int32))
        paired = parents.reshape(GRANDS, 2, 2, 3 * K, 3 * K)

        def level_two(grand_index):
            return merge_pair(paired[grand_index, 0], paired[grand_index, 1], w_two[:, grand_index],
                              skel_second[tree_index, grand_index], False)

        grands = lax.map(level_two, jnp.arange(GRANDS).astype(jnp.int32))
        outputs.append(jnp.transpose(grands, (1, 0, 2, 3)).reshape(2, GRANDS * 4 * K, 3 * K))
    return jnp.stack(outputs, axis=1)
```

```python
import jax
import jax.numpy as jnp
from jax import lax
from jax.experimental import pallas as pl
from jax.experimental.pallas import tpu as pltpu
from jax.sharding import PartitionSpec as P

BF16 = jnp.bfloat16
F32 = jnp.float32
VMEM_BYTES = 48 * 1024 * 1024


def dot(first, second):
    return jnp.dot(first, second, preferred_element_type=F32)


def complex_dot(left, right):
    real = dot(left[0], right[0]) - dot(left[1], right[1])
    imag = dot(left[0], right[1]) + dot(left[1], right[0])
    return real, imag


def column_picker(skeleton, offset, count):
    rows = lax.broadcasted_iota(jnp.int32, (count, skeleton.shape[1]), 0) + offset
    return jnp.where(rows == skeleton, 1.0, 0.0).astype(BF16)


def row_picker(skeleton, offset, count):
    cols = lax.broadcasted_iota(jnp.int32, (skeleton.shape[0], count), 1) + offset
    return jnp.where(cols == skeleton, 1.0, 0.0).astype(BF16)


def call(kernel, scalars, inputs, in_specs, out_shapes, scratch=(), flops=0):
    whole = [
        pl.BlockSpec(s.shape, lambda i, sc, n=len(s.shape): (0,) * n) for s in out_shapes
    ]
    specs = [
        pl.BlockSpec(a.shape, lambda i, sc, n=a.ndim: (0,) * n) if s is None else s
        for a, s in zip(inputs, in_specs)
    ]
    moved = sum(s.size * s.dtype.itemsize for s in out_shapes)
    return pl.pallas_call(
        kernel,
        grid_spec=pltpu.PrefetchScalarGridSpec(
            num_scalar_prefetch=1, grid=(1,), in_specs=specs, out_specs=whole,
            scratch_shapes=list(scratch),
        ),
        out_shape=out_shapes,
        compiler_params=pltpu.CompilerParams(vmem_limit_bytes=VMEM_BYTES),
        cost_estimate=pl.CostEstimate(flops=flops, bytes_accessed=2 * moved, transcendentals=0),
    )(scalars, *inputs)


def on_device(leaf_maps, w_first, w_second, skel_first, skel_second):
    box = lax.axis_index("box")
    face = lax.axis_index("face")
    n_box, n_face = lax.axis_size("box"), lax.axis_size("face")
    fr = leaf_maps.shape[4]
    k = leaf_maps.shape[5] // 3
    half = k // 2
    leaf = leaf_maps[:, 0, 0]
    par = box % 2
    par2 = box // 2 % 2
    quarter = box % 4
    scalars = jnp.stack([par, par2, face, quarter]).astype(jnp.int32)

    def box_permute(array, mask, senders=None):
        pairs = [(b, b ^ mask) for b in range(n_box) if senders is None or senders(b)]
        return lax.ppermute(array, "box", pairs)

    def keeper(b):
        return (b & 1) != (b >> 1 & 1)

    def giver(b):
        return not keeper(b)

    def face_permute(array, step, senders=None):
        pairs = [
            (b * n_face + f, b * n_face + (f + n_face - step) % n_face)
            for b in range(n_box) if senders is None or senders(b)
            for f in range(n_face)
        ]
        return lax.ppermute(array, ("box", "face"), pairs)

    skel_one = lax.dynamic_index_in_dim(skel_first[0], box // 2, 0, keepdims=True)
    skel_two = lax.dynamic_index_in_dim(skel_second[0], box // 4, 0, keepdims=True)
    sds = jax.ShapeDtypeStruct

    end_own = lax.dynamic_slice(
        leaf, (0, 1 - par, 0, par * k), (2, 1, fr, k)
    ).reshape(2, fr, k)
    end_far = [face_permute(end_own, s) for s in range(1, n_face)]
    end_sib = box_permute(end_own, 1)

    def side_kernel(sc, rows_ref, skel_ref, out_ref):
        picker = column_picker(skel_ref[...], sc[0] * k, k)
        for t in range(2):
            out_ref[t] = dot(rows_ref[t], picker).astype(BF16)

    (side_own,) = call(
        side_kernel, scalars, [leaf, skel_one],
        [pl.BlockSpec((2, None, fr, k), lambda i, sc: (0, 1 - sc[0], 0, 2)), None],
        [sds((2, fr, k), BF16)], flops=4 * fr * k * k,
    )
    side = side_own + box_permute(side_own, 1)
    side_half = lax.dynamic_slice(side, (0, 0, par * half), (2, fr, half))
    side_far = [face_permute(side_half, s) for s in range(1, n_face)]

    w_one = jnp.roll(w_first[:, 0], -face * fr, axis=2)
    w_one_sib = box_permute(w_one, 1)
    w_two = jnp.roll(w_second[:, 0], -face * fr, axis=2)
    w_two_x = box_permute(w_two, 2)
    w_two_pair = jnp.stack([w_two, w_two_x])
    w_two_sib = box_permute(w_two_pair, 1)

    s_rows = leaf[:, 2]
    s_sib = box_permute(s_rows, 1, giver)
    skel_rows = skel_one.reshape(k, 1)

    def rows_kernel(sc, own_ref, sib_ref, end_ref, skel_ref, skel_col_ref, *outs):
        p, q, f = sc[0], sc[1], sc[2]

        def columns(ref, t, side, block):
            start = pl.multiple_of((side ^ block) * k, k) if block < 2 else 2 * k
            return ref[t, :, pl.ds(start, k)]

        @pl.when(p == q)
        def _():
            picker = column_picker(skel_ref[...], p * k, k)
            for t in range(2):
                outs[0][t, :, :k] = columns(end_ref, t, p, 1)
                outs[0][t, :, k : 2 * k] = columns(end_ref, t, p, 0)
                outs[0][t, :, 2 * k :] = dot(columns(end_ref, t, p, 2), picker).astype(BF16)

        @pl.when(p != q)
        def _():
            pick_own = column_picker(skel_ref[...], p * k, k)
            pick_sib = column_picker(skel_ref[...], (1 - p) * k, k)
            for t in range(2):
                own = [columns(own_ref, t, p, 1), columns(own_ref, t, p, 0),
                       dot(columns(own_ref, t, p, 2), pick_own).astype(BF16)]
                sib = [columns(sib_ref, t, 1 - p, 1), columns(sib_ref, t, 1 - p, 0),
                       dot(columns(sib_ref, t, 1 - p, 2), pick_sib).astype(BF16)]
                for s in range(n_face):
                    start = pl.multiple_of((f + n_face - s) % n_face * fr, fr)
                    slots = skel_col_ref[pl.ds(start, fr), :]
                    take_own = row_picker(slots, p * k + f * fr, fr)
                    take_sib = row_picker(slots, (1 - p) * k + f * fr, fr)
                    for c in range(3):
                        outs[s][t, :, c * k : (c + 1) * k] = (
                            dot(take_own, own[c]) + dot(take_sib, sib[c])
                        ).astype(BF16)

    face_block = (2, None, fr, 3 * k)
    kept = call(
        rows_kernel, scalars, [leaf, s_sib, leaf, skel_one, skel_rows],
        [pl.BlockSpec(face_block, lambda i, sc: (0, 2, 0, 0)), None,
         pl.BlockSpec(face_block, lambda i, sc: (0, sc[0], 0, 0)), None, None],
        [sds((2, fr, 3 * k), BF16)] * n_face, flops=16 * fr * fr * n_face * 3 * k,
    )
    kept_far = [face_permute(kept[s], s, keeper) for s in range(1, n_face)]

    end_sib_far = [box_permute(a, 1) for a in end_far]
    side_sib_far = [box_permute(a, 1) for a in side_far]
    ends_own = [end_own] + end_far
    ends_sib = [end_sib] + end_sib_far

    def side_product(sc, hidden, side_ref, far_refs, sib_refs, acc):
        p = sc[0]
        first = complex_dot([h[:, :fr] for h in hidden], [side_ref[0], side_ref[1]])
        for t in range(2):
            acc[t] -= first[t]
        for s in range(1, n_face):
            part = [h[:, s * fr : (s + 1) * fr] for h in hidden]
            for ref, which in ((far_refs[s - 1], p), (sib_refs[s - 1], 1 - p)):
                term = complex_dot(part, [ref[0], ref[1]])
                cols = pl.ds(pl.multiple_of(which * half, half), half)
                for t in range(2):
                    acc[t, :, cols] -= term[t]

    def block_product(hidden, refs):
        total = None
        for s, ref in enumerate(refs):
            term = complex_dot([h[:, s * fr : (s + 1) * fr] for h in hidden], [ref[0], ref[1]])
            total = term if total is None else [a + b for a, b in zip(total, term)]
        return total

    def weigh(couple_ref, p, own_ref, sib_ref):
        lo = pl.ds(pl.multiple_of(p * half, half), half)
        hi = pl.ds(pl.multiple_of((1 - p) * half, half), half)
        first = complex_dot([couple_ref[0, :, lo], couple_ref[1, :, lo]], [own_ref[0], own_ref[1]])
        second = complex_dot([couple_ref[0, :, hi], couple_ref[1, :, hi]], [sib_ref[0], sib_ref[1]])
        return [(a + b).astype(BF16) for a, b in zip(first, second)]

    nf = n_face - 1

    def iface_kernel(sc, couple_ref, sidecol_ref, w_ref, wsib_ref, skel_ref, skel2_ref, *rest):
        ends = rest[:n_face]
        side_ref = rest[n_face]
        far = rest[n_face + 1 : n_face + 1 + nf]
        sib = rest[n_face + 1 + nf : n_face + 1 + 2 * nf]
        end_out, side_out, acc = rest[n_face + 1 + 2 * nf :]
        p, q = sc[0], sc[1]

        @pl.when(p == q)
        def _():
            end_out[...] = jnp.zeros_like(end_out)
            side_out[...] = jnp.zeros_like(side_out)

        @pl.when(p != q)
        def _():
            hidden = weigh(couple_ref, p, w_ref, wsib_ref)
            ended = block_product(hidden, ends)
            picker = column_picker(skel_ref[...], p * k, k)
            for t in range(2):
                end_out[t] = (-ended[t]).astype(BF16)
                acc[t] = dot(sidecol_ref[t], picker)
            side_product(sc, hidden, side_ref, far, sib, acc)
            picker2 = column_picker(skel2_ref[...], q * k, k)
            for t in range(2):
                side_out[t] = dot(acc[t].astype(BF16), picker2).astype(BF16)

    end_rows = lambda block: pl.BlockSpec((2, None, fr, k), lambda i, sc: (0, sc[0], 0, block(sc)))
    two_end, two_side = call(
        iface_kernel, scalars,
        [leaf, leaf, w_one, w_one_sib, skel_one, skel_two, *ends_sib, side, *side_far, *side_sib_far],
        [end_rows(lambda sc: 1 - sc[0]), end_rows(lambda sc: 2)] + [None] * (5 + n_face + 2 * nf),
        [sds((2, fr, k), BF16)] * 2, [pltpu.VMEM((2, fr, k), F32)],
        flops=8 * fr * k * 3 * k,
    )

    side_x = box_permute(two_side, 3, keeper)
    end_x = box_permute(two_end, 3, keeper)
    two_sides = two_side + side_x
    two_half = lax.dynamic_slice(two_sides, (0, 0, par2 * half), (2, fr, half))
    end_y = [face_permute(two_end, s, keeper) for s in range(1, n_face)]
    half_y = [face_permute(two_half, s, keeper) for s in range(1, n_face)]
    end_xy = [box_permute(a, 3, keeper) for a in end_y]
    half_xy = [box_permute(a, 3, keeper) for a in half_y]
    gathered = [two_end, end_x, two_sides]
    for s in range(nf):
        gathered += [end_y[s], end_xy[s], half_y[s], half_xy[s]]
    forwarded = [box_permute(a, 1, keeper) for a in gathered]

    def level_one_kernel(sc, *rest):
        zs = rest[:n_face]
        skel_col_ref, w_ref, wsib_ref, w2_ref, w2sib_ref, skel2_ref = rest[n_face : n_face + 6]
        rest = rest[n_face + 6 :]
        own_ends, sib_ends = rest[:n_face], rest[n_face : 2 * n_face]
        rest = rest[2 * n_face :]
        side_ref, far, sib = rest[0], rest[1 : 1 + nf], rest[1 + nf : 1 + 2 * nf]
        hid_out, end_out, side_out, couple, acc, w2 = rest[1 + 2 * nf :]
        p, q, f, r = sc[0], sc[1], sc[2], sc[3]
        is_end = p == q

        def rows(t, c):
            total = zs[0][t, :, c * k : (c + 1) * k]
            for z in zs[1:]:
                total = total + z[t, :, c * k : (c + 1) * k]
            return total

        slots = skel_col_ref[pl.ds(pl.multiple_of(f * fr, fr), fr), :]
        right = jnp.where(slots >= k, 1, 0)
        right = jnp.where(is_end, p, right)
        own_side = right == p
        for t in range(2):
            couple[t] = rows(t, 0)
        hidden = weigh(couple, p, w_ref, wsib_ref)
        own = block_product(hidden, own_ends)
        other = block_product(hidden, sib_ends)
        for t in range(2):
            acc[t] = rows(t, 2).astype(F32)
        side_product(sc, hidden, side_ref, far, sib, acc)
        picker2 = column_picker(skel2_ref[...], q * k, k)
        for t in range(2):
            ends = rows(t, 1).astype(F32)
            nothing = jnp.zeros_like(ends)
            own_rows = (jnp.where(own_side, ends, nothing) - own[t]).astype(BF16)
            sib_rows = (jnp.where(own_side, nothing, ends) - other[t]).astype(BF16)
            end_out[t] = jnp.where(is_end, own_rows, sib_rows)
            couple[t] = jnp.where(is_end, sib_rows, own_rows)
            side_out[t] = dot(acc[t].astype(BF16), picker2).astype(BF16)
        blk = k // 4
        for i, (ref, part) in enumerate(((w2_ref, 0), (w2_ref, 1), (w2sib_ref, 0), (w2sib_ref, 1))):
            place = r ^ (part * 2) ^ (i // 2)
            for t in range(2):
                w2[t, pl.ds(pl.multiple_of(place * blk, blk), blk), :] = ref[part, t]
        second = complex_dot([couple[0], couple[1]], [w2[0], w2[1]])
        for t in range(2):
            hid_out[t] = second[t].astype(BF16)

    hid_two, diag_end, diag_side = call(
        level_one_kernel, scalars,
        [kept[0], *kept_far, skel_rows, w_one, w_one_sib, w_two_pair, w_two_sib, skel_two,
         *ends_own, *ends_sib, side, *side_far, *side_sib_far],
        [None] * (n_face + 6 + 2 * n_face + 1 + 2 * nf),
        [sds((2, fr, k), BF16)] * 3,
        [pltpu.VMEM((2, fr, k), BF16), pltpu.VMEM((2, fr, k), F32), pltpu.VMEM((2, k, k), BF16)],
        flops=8 * fr * k * 5 * k,
    )

    def final_kernel(sc, hid_ref, end_ref, side_ref, *rest):
        n = 3 + 4 * nf
        have, sent = rest[:n], rest[n : 2 * n]
        out_ref, acc = rest[2 * n :]
        q = sc[1]
        own_cols = pl.ds(pl.multiple_of(q * k, k), k)
        sib_cols = pl.ds(pl.multiple_of((1 - q) * k, k), k)
        hidden = [hid_ref[0], hid_ref[1]]

        def term(s, i):
            part = [h[:, s * fr : (s + 1) * fr] for h in hidden]
            return complex_dot(part, [have[i][t] + sent[i][t] for t in range(2)])

        own, other, sides = term(0, 0), term(0, 1), term(0, 2)
        for t in range(2):
            acc[t] = side_ref[t].astype(F32) - sides[t]
        for s in range(1, n_face):
            base = 3 + 4 * (s - 1)
            own = [a + b for a, b in zip(own, term(s, base))]
            other = [a + b for a, b in zip(other, term(s, base + 1))]
            for i, which in ((base + 2, q), (base + 3, 1 - q)):
                add = term(s, i)
                cols = pl.ds(pl.multiple_of(which * half, half), half)
                for t in range(2):
                    acc[t, :, cols] -= add[t]
        for t in range(2):
            out_ref[t, 0, :, own_cols] = (end_ref[t].astype(F32) - own[t]).astype(BF16)
            out_ref[t, 0, :, sib_cols] = (-other[t]).astype(BF16)
            out_ref[t, 0, :, 2 * k :] = acc[t].astype(BF16)

    (out,) = call(
        final_kernel, scalars, [hid_two, diag_end, diag_side, *gathered, *forwarded],
        [None] * (3 + 2 * (3 + 4 * nf)),
        [sds((2, 1, fr, 3 * k), BF16)], [pltpu.VMEM((2, fr, k), F32)],
        flops=8 * fr * k * 3 * k,
    )
    return out


def solution(mesh):
    return jax.shard_map(
        on_device,
        mesh=mesh,
        in_specs=(
            P(None, None, "box", None, "face", None),
            P(None, None, "box", None),
            P(None, None, "box", None),
            P(),
            P(),
        ),
        out_specs=P(None, None, ("box", "face"), None),
        check_vma=False,
    )
```

```python
import jax
import jax.numpy as jnp
from jax import lax
from jax.experimental import pallas as pl
from jax.experimental.pallas import tpu as pltpu
from jax.sharding import PartitionSpec as P

BF16 = jnp.bfloat16
F32 = jnp.float32
VMEM_BYTES = 28 * 1024 * 1024
ROW_CHUNKS = 2


def dot(first, second):
    return jnp.dot(first, second, preferred_element_type=F32)


def stacked(real, imag):
    return jnp.concatenate(
        [jnp.concatenate([real, -imag], axis=1), jnp.concatenate([imag, real], axis=1)], axis=0
    )


def flat(array):
    return array.reshape(array.shape[0] * array.shape[1], array.shape[2])


def column_picker(index, offset, count):
    rows = lax.broadcasted_iota(jnp.int32, (count, index.shape[1]), 0) + offset
    return jnp.where(rows == index, 1.0, 0.0).astype(BF16)


def row_picker(index, offset, count):
    cols = lax.broadcasted_iota(jnp.int32, (index.shape[0], count), 1) + offset
    return jnp.where(cols == index, 1.0, 0.0).astype(BF16)


def call(kernel, scalars, inputs, out_shapes, specs=None, out_specs=None, scratch=(), flops=0, aliases=None):
    specs = specs or [None] * len(inputs)
    out_specs = out_specs or [None] * len(out_shapes)

    def whole(array, spec):
        if spec is not None:
            return spec
        rank = len(array.shape)
        return pl.BlockSpec(array.shape, lambda i, sc: (0,) * rank)

    moved = sum(s.size * s.dtype.itemsize for s in out_shapes)
    return pl.pallas_call(
        kernel,
        grid_spec=pltpu.PrefetchScalarGridSpec(
            num_scalar_prefetch=1, grid=(1,),
            in_specs=[whole(a, s) for a, s in zip(inputs, specs)],
            out_specs=[whole(a, s) for a, s in zip(out_shapes, out_specs)],
            scratch_shapes=list(scratch),
        ),
        out_shape=out_shapes,
        input_output_aliases=aliases or {},
        compiler_params=pltpu.CompilerParams(vmem_limit_bytes=VMEM_BYTES),
        cost_estimate=pl.CostEstimate(flops=flops, bytes_accessed=2 * moved, transcendentals=0),
    )(scalars, *inputs)


def after(array, *others):
    return lax.optimization_barrier((array, *others))[0]


def on_device(leaf_maps, w_first, w_second, skel_first, skel_second):
    box = lax.axis_index("box")
    face = lax.axis_index("face")
    n_box, n_face = lax.axis_size("box"), lax.axis_size("face")
    nf = n_face - 1
    fr = leaf_maps.shape[4]
    hr = fr // 2
    k = leaf_maps.shape[5] // 3
    half = k // 2
    leaf = leaf_maps[:, 0, 0]
    par = box % 2
    par2 = box // 2 % 2
    scalars = jnp.stack([par, par2, face, box % 4]).astype(jnp.int32)
    sds = jax.ShapeDtypeStruct

    def box_permute(array, mask):
        return lax.ppermute(array, "box", [(b, b ^ mask) for b in range(n_box)])

    def keeper(b):
        return (b & 1) != (b >> 1 & 1)

    def giver(b):
        return not keeper(b)

    def face_permute(array, step, senders=None):
        pairs = [
            (b * n_face + f, b * n_face + (f + n_face - step) % n_face)
            for b in range(n_box) if senders is None or senders(b)
            for f in range(n_face)
        ]
        return lax.ppermute(array, ("box", "face"), pairs)

    def over_face(array, senders=None):
        return [face_permute(array, s, senders) for s in range(1, n_face)]

    skel_one = lax.dynamic_index_in_dim(skel_first[0], box // 2, 0, keepdims=True)
    skel_two = lax.dynamic_index_in_dim(skel_second[0], box // 4, 0, keepdims=True)

    def iface_cols(start):
        return lax.dynamic_slice(leaf, (0, 1 - par, 0, start), (2, 1, fr, k)).reshape(2, fr, k)

    end_own = iface_cols(par * k)
    end_far = over_face(end_own, giver)
    sides_raw = iface_cols(2 * k)
    sides_sib = box_permute(sides_raw, 1)
    end_sib = box_permute(end_own, 1)

    def slots_kernel(sc, own_ref, sib_ref, end_ref, skel_ref, skel2_ref,
                     comp_out, col_out, side_out, keep_out, send_out):
        p, q = sc[0], sc[1]
        rows = lax.broadcasted_iota(jnp.int32, (k, k), 0)
        cols = lax.broadcasted_iota(jnp.int32, (k, k), 1)
        skel = jnp.broadcast_to(skel_ref[...].astype(F32), (k, k))
        column = jnp.sum(jnp.where(rows == cols, skel, 0.0), axis=1, keepdims=True)
        col_out[...] = column.astype(jnp.int32)
        place = skel2_ref[...] - q * k
        taken = jnp.where(rows == place, jnp.broadcast_to(column, (k, k)), 0.0)
        comp = jnp.sum(taken, axis=0, keepdims=True).astype(jnp.int32)
        mine = jnp.logical_and(place >= 0, place < k)
        comp = jnp.where(mine, comp, -1)
        comp_out[...] = comp
        pick_own = column_picker(comp, p * k, k)
        pick_sib = column_picker(comp, (1 - p) * k, k)
        side = dot(flat(own_ref[...]), pick_own) + dot(flat(sib_ref[...]), pick_sib)
        side_out[...] = side.astype(BF16).reshape(2, fr, k)
        couple = pl.ds(pl.multiple_of((1 - p) * k, k), k)
        for ref, h in ((keep_out, p), (send_out, 1 - p)):
            take = pl.ds(pl.multiple_of(h * hr, hr), hr)
            for t in range(2):
                ref[t, :, :k] = end_ref[t, take, couple]
                ref[t, :, k:] = dot(end_ref[t, take, 2 * k :], pick_own).astype(BF16)

    comp, skel_col, side, v_keep, v_send = call(
        slots_kernel, scalars, [leaf, sides_sib, leaf, skel_one, skel_two],
        [sds((1, k), jnp.int32), sds((k, 1), jnp.int32), sds((2, fr, k), BF16),
         sds((2, hr, 2 * k), BF16), sds((2, hr, 2 * k), BF16)],
        specs=[pl.BlockSpec((2, None, fr, k), lambda i, sc: (0, 1 - sc[0], 0, 2)), None,
               pl.BlockSpec((2, None, fr, 3 * k), lambda i, sc: (0, sc[0], 0, 0)), None, None],
        flops=12 * fr * k * k,
    )
    side_far = over_face(side, keeper)
    v_recv = box_permute(v_send, 1)

    w_one = jnp.roll(w_first[:, 0], -face * fr, axis=2)
    w_one_sib = box_permute(w_one, 1)
    w_two = jnp.roll(w_second[:, 0], -face * fr, axis=2)
    w_two_pair = jnp.stack([w_two, box_permute(w_two, 2)])
    w_two_sib = box_permute(w_two_pair, 1)

    s_sib = box_permute(leaf[:, 2], 1)
    cr = fr // ROW_CHUNKS

    def rows_kernel(sc, own_ref, sib_ref, end_ref, comp_ref, col_ref, *outs):
        p, q, f = sc[0], sc[1], sc[2]

        @pl.when(p == q)
        def _():
            picker = column_picker(comp_ref[...], p * k, k)
            for t in range(2):
                outs[0][t, :, : 2 * k] = end_ref[t, :, : 2 * k]
                outs[0][t, :, 2 * k :] = dot(end_ref[t, :, 2 * k :], picker).astype(BF16)

        @pl.when(p != q)
        def _():
            pick_own = column_picker(comp_ref[...], p * k, k)
            pick_sib = column_picker(comp_ref[...], (1 - p) * k, k)
            takes = []
            for s in range(n_face):
                start = pl.multiple_of((f + n_face - s) % n_face * fr, fr)
                slots = col_ref[pl.ds(start, fr), :]
                takes.append([row_picker(slots, p * k + f * fr, fr),
                              row_picker(slots, (1 - p) * k + f * fr, fr)])
            take_own = jnp.concatenate([t[0] for t in takes], axis=0)
            take_sib = jnp.concatenate([t[1] for t in takes], axis=0)
            for t in range(2):
                sides = [dot(ref[t, :, 2 * k :], pick).astype(BF16)
                         for ref, pick in ((own_ref, pick_own), (sib_ref, pick_sib))]
                for c in range(3):
                    cols = slice(c * k, (c + 1) * k)
                    own, sib = sides if c == 2 else (own_ref[t, :, cols], sib_ref[t, :, cols])
                    picked = (dot(take_own, own) + dot(take_sib, sib)).astype(BF16)
                    outs[0][t, :, cols] = picked[:fr]
                    for s in range(1, n_face):
                        for i in range(ROW_CHUNKS):
                            lo = s * fr + i * cr
                            outs[1 + (s - 1) * ROW_CHUNKS + i][t, :, cols] = picked[lo : lo + cr]

    def face_block(which):
        return pl.BlockSpec((2, None, fr, 3 * k), lambda i, sc: (0, which(sc), 0, 0))

    kept, *kept_out = call(
        rows_kernel, scalars, [leaf, s_sib, leaf, comp, skel_col],
        [sds((2, fr, 3 * k), BF16)] + [sds((2, cr, 3 * k), BF16)] * (nf * ROW_CHUNKS),
        specs=[face_block(lambda sc: 2), None, face_block(lambda sc: sc[0]), None, None],
        flops=16 * fr * fr * n_face * 3 * k,
    )

    end_fwd = [box_permute(a, 1) for a in end_far]
    side_fwd = [box_permute(a, 1) for a in side_far]
    rest_far = over_face(after(end_own, *side_far), keeper)
    rest_fwd = [box_permute(a, 1) for a in rest_far]

    def hidden_rows(couple, p, own_ref, sib_ref, m):
        lo = pl.ds(pl.multiple_of(p * half, half), half)
        hi = pl.ds(pl.multiple_of((1 - p) * half, half), half)
        both = dot(stacked(couple(0, lo), couple(1, lo)), flat(own_ref[...]))
        both = both + dot(stacked(couple(0, hi), couple(1, hi)), flat(sib_ref[...]))
        both = both.astype(BF16)
        return both[:m], both[m:]

    def piece(hidden, start, count):
        return stacked(hidden[0][:, start : start + count], hidden[1][:, start : start + count])

    def iface_kernel(sc, keep_ref, recv_ref, own_ref, sib_ref, end_ref, endsib_ref, side_ref,
                     acc_out, hid_out, rows):
        p, q = sc[0], sc[1]

        @pl.when(p == q)
        def _():
            rows[...] = recv_ref[...]

        @pl.when(p != q)
        def _():
            rows[...] = keep_ref[...]

        hidden = hidden_rows(lambda t, c: rows[t, :, c], p, own_ref, sib_ref, hr)
        hid_out[0] = hidden[0]
        hid_out[1] = hidden[1]
        left = piece(hidden, 0, fr)
        is_end = p == q
        ends = jnp.where(is_end, end_ref[...], endsib_ref[...])
        acc_out[:, :, :k] = -dot(left, flat(ends)).reshape(2, hr, k)
        acc_out[:, :, k:] = rows[:, :, k:].astype(F32) - dot(left, flat(side_ref[...])).reshape(2, hr, k)

    v_acc, v_hid = call(
        iface_kernel, scalars, [v_keep, v_recv, w_one, w_one_sib, end_own, end_sib, side],
        [sds((2, hr, 2 * k), F32), sds((2, hr, k), BF16)],
        scratch=[pltpu.VMEM((2, hr, 2 * k), BF16)], flops=8 * hr * k * 2 * k,
    )

    def iface_far_kernel(sc, acc_ref, hid_ref, *rest):
        far, fwd, side_f, side_w = (rest[i * nf : (i + 1) * nf] for i in range(4))
        end_out, side_out = rest[4 * nf :]
        hidden = [hid_ref[0], hid_ref[1]]
        end = acc_ref[:, :, :k]
        side = acc_ref[:, :, k:]
        for s in range(nf):
            left = piece(hidden, (s + 1) * fr, fr)
            end = end - dot(left, flat(far[s][...] + fwd[s][...])).reshape(2, hr, k)
            side = side - dot(left, flat(side_f[s][...] + side_w[s][...])).reshape(2, hr, k)
        end_out[...] = end.astype(BF16)
        side_out[...] = side.astype(BF16)

    two_end, two_side = call(
        iface_far_kernel, scalars, [v_acc, v_hid, *end_far, *end_fwd, *side_far, *side_fwd],
        [sds((2, hr, k), BF16)] * 2, flops=8 * hr * k * k,
    )

    side_x = box_permute(two_side, 2)
    end_y = over_face(two_end)
    end_x = box_permute(two_end, 2)

    def half_slots(array):
        return lax.dynamic_slice(array, (0, 0, par2 * half), (2, hr, half))

    half_y = over_face(half_slots(two_side) + half_slots(side_x))
    end_xy = [box_permute(a, 2) for a in end_y]
    half_xy = [box_permute(a, 2) for a in half_y]

    def join_kernel(sc, end_ref, endx_ref, side_ref, sidex_ref, out_ref):
        q = sc[1]
        out_ref[:, :, pl.ds(pl.multiple_of(q * k, k), k)] = end_ref[...]
        out_ref[:, :, pl.ds(pl.multiple_of((1 - q) * k, k), k)] = endx_ref[...]
        out_ref[:, :, 2 * k :] = side_ref[...] + sidex_ref[...]

    def join_far_kernel(sc, end_ref, endx_ref, side_ref, sidex_ref, out_ref):
        q = sc[1]
        out_ref[:, :, pl.ds(pl.multiple_of(q * k, k), k)] = end_ref[...]
        out_ref[:, :, pl.ds(pl.multiple_of((1 - q) * k, k), k)] = endx_ref[...]
        out_ref[:, :, pl.ds(pl.multiple_of(2 * k + q * half, half), half)] = side_ref[...]
        out_ref[:, :, pl.ds(pl.multiple_of(2 * k + (1 - q) * half, half), half)] = sidex_ref[...]

    two_shape = [sds((2, hr, 3 * k), BF16)]
    two_rows = call(join_kernel, scalars, [two_end, end_x, two_side, side_x], two_shape)
    for s in range(nf):
        two_rows += call(join_far_kernel, scalars, [end_y[s], end_xy[s], half_y[s], half_xy[s]], two_shape)
    two_sib = [box_permute(a, 1) for a in two_rows]

    def gather_kernel(sc, own_ref, sib_ref, side_ref, *rest):
        far, fwd, rfar, rfwd, sfar, sfwd = (rest[i * nf : (i + 1) * nf] for i in range(6))
        out_ref = rest[6 * nf]
        p, q = sc[0], sc[1]

        def block(which):
            return pl.ds(pl.multiple_of(which * k, k), k)

        out_ref[0, :, :, block(p)] = own_ref[...]
        out_ref[0, :, :, block(1 - p)] = sib_ref[...]
        out_ref[0, :, :, 2 * k :] = side_ref[...]
        for s in range(nf):
            out_ref[s + 1, :, :, block(q)] = far[s][...] + fwd[s][...]
            out_ref[s + 1, :, :, block(1 - q)] = rfar[s][...] + rfwd[s][...]
            out_ref[s + 1, :, :, 2 * k :] = sfar[s][...] + sfwd[s][...]

    (iface,) = call(
        gather_kernel, scalars,
        [end_own, end_sib, side, *end_far, *end_fwd, *rest_far, *rest_fwd, *side_far, *side_fwd],
        [sds((n_face, 2, fr, 3 * k), BF16)],
    )

    def keep_kernel(chunk, sc, *refs):
        kept_ref, refs = refs[0], refs[1:]
        far, refs = refs[:nf], refs[nf:]
        col_ref, own_ref, sib_ref, w2_ref, w2sib_ref, iface_ref = refs[:6]
        mine, sibs = refs[6 : 6 + n_face], refs[6 + n_face : 6 + 2 * n_face]
        out_ref, hid, w2 = refs[-3:]
        p, q, f, r = sc[0], sc[1], sc[2], sc[3]
        is_end = p == q

        def rows(t, c):
            total = kept_ref[t, :, c * k : (c + 1) * k]
            for z in far:
                total = total + z[t, :, c * k : (c + 1) * k]
            return total

        slots = col_ref[pl.ds(pl.multiple_of(f * fr + chunk * cr, cr), cr), :]
        right = jnp.where(slots >= k, 1, 0)
        right = jnp.where(is_end, p, right) > 0
        lefts = [rows(t, 0) for t in range(2)]
        rights = [rows(t, 1) for t in range(2)]
        couple = [jnp.where(right, a, b) for a, b in zip(lefts, rights)]

        def columns(t, which):
            return jnp.where(which == 0, couple[t][:, :half], couple[t][:, half:])

        own = stacked(columns(0, p), columns(1, p))
        sib = stacked(columns(0, 1 - p), columns(1, 1 - p))
        both = (dot(own, flat(own_ref[...])) + dot(sib, flat(sib_ref[...]))).astype(BF16)
        hidden = both[:cr], both[cr:]
        nothing = jnp.zeros((cr, k), BF16)
        start = [
            jnp.concatenate([jnp.where(right, nothing, a) for a in lefts], axis=0),
            jnp.concatenate([jnp.where(right, a, nothing) for a in rights], axis=0),
            jnp.concatenate([rows(t, 2) for t in range(2)], axis=0),
        ]
        merged = []
        for c in range(3):
            total = start[c].astype(F32)
            for s in range(n_face):
                total = total - dot(piece(hidden, s * fr, fr), flat(iface_ref[s, :, :, c * k : (c + 1) * k]))
            merged.append(total.astype(BF16))
        is_left = q == 0
        blk = k // 4
        for i, (ref, part) in enumerate(((w2_ref, 0), (w2_ref, 1), (w2sib_ref, 0), (w2sib_ref, 1))):
            place = r ^ (part * 2) ^ (i // 2)
            for t in range(2):
                w2[t, pl.ds(pl.multiple_of(place * blk, blk), blk), :] = ref[part, t]
        couple2 = jnp.where(is_left, merged[1], merged[0])
        second = dot(stacked(couple2[:cr], couple2[cr:]), flat(w2[...])).astype(BF16)
        for s in range(n_face):
            for h in range(2):
                hid[s * 2 + h] = piece((second[:cr], second[cr:]), s * fr + h * hr, hr)
        none = jnp.zeros_like(merged[0])
        first = [jnp.where(is_left, merged[0], none), jnp.where(is_left, none, merged[1]), merged[2]]
        for c in range(3):
            cols = slice(c * k, (c + 1) * k)
            total = first[c].astype(F32)
            for s in range(n_face):
                total = total - dot(hid[s * 2 + p], flat(mine[s][:, :, cols]))
                total = total - dot(hid[s * 2 + 1 - p], flat(sibs[s][:, :, cols]))
            total = total.astype(BF16)
            out_ref[0, 0, :, cols] = total[:cr]
            out_ref[1, 0, :, cols] = total[cr:]

    out = None
    sent = rest_far
    chunks = []
    for i in range(ROW_CHUNKS):
        outgoing = [kept_out[(s - 1) * ROW_CHUNKS + i] for s in range(1, n_face)]
        outgoing = [after(a, *sent) for a in outgoing]
        sent = [face_permute(a, s + 1, keeper) for s, a in enumerate(outgoing)]
        chunks.append(sent)
    for i in range(ROW_CHUNKS):
        inputs = [kept, *chunks[i], skel_col, w_one, w_one_sib, w_two_pair, w_two_sib, iface, *two_rows, *two_sib]
        specs = [pl.BlockSpec((2, cr, 3 * k), lambda g, sc, i=i: (0, i, 0))]
        specs += [None] * (len(inputs) - 1)
        aliases = None
        if out is not None:
            inputs.append(out)
            specs.append(pl.BlockSpec(memory_space=pl.ANY))
            aliases = {len(inputs): 0}
        (out,) = call(
            lambda sc, *refs, i=i: keep_kernel(i, sc, *refs), scalars, inputs,
            [sds((2, 1, fr, 3 * k), BF16)], specs=specs,
            out_specs=[pl.BlockSpec((2, 1, cr, 3 * k), lambda g, sc, i=i: (0, 0, i, 0))],
            scratch=[pltpu.VMEM((2 * n_face, 2 * cr, 2 * hr), BF16), pltpu.VMEM((2, k, k), BF16)],
            flops=8 * cr * k * 8 * k, aliases=aliases,
        )
    return out


def solution(mesh):
    return jax.shard_map(
        on_device,
        mesh=mesh,
        in_specs=(
            P(None, None, "box", None, "face", None),
            P(None, None, "box", None),
            P(None, None, "box", None),
            P(),
            P(),
        ),
        out_specs=P(None, None, ("box", "face"), None),
        check_vma=False,
    )
```

```python
import jax
import jax.numpy as jnp
from jax import lax
from jax.experimental import pallas as pl
from jax.experimental.pallas import tpu as pltpu
from jax.sharding import PartitionSpec as P

BF16 = jnp.bfloat16
F32 = jnp.float32
VMEM_BYTES = 28 * 1024 * 1024
ROW_CHUNKS = 2


def dot(first, second):
    return jnp.dot(first, second, preferred_element_type=F32)


def stacked(real, imag):
    return jnp.concatenate(
        [jnp.concatenate([real, -imag], axis=1), jnp.concatenate([imag, real], axis=1)], axis=0
    )


def flat(array):
    return array.reshape(array.shape[0] * array.shape[1], array.shape[2])


def column_picker(index, offset, count):
    rows = lax.broadcasted_iota(jnp.int32, (count, index.shape[1]), 0) + offset
    return jnp.where(rows == index, 1.0, 0.0).astype(BF16)


def row_picker(index, offset, count):
    cols = lax.broadcasted_iota(jnp.int32, (index.shape[0], count), 1) + offset
    return jnp.where(cols == index, 1.0, 0.0).astype(BF16)


def call(kernel, scalars, inputs, out_shapes, specs=None, out_specs=None, scratch=(), aliases=None):
    in_vmem = pl.BlockSpec(memory_space=pltpu.VMEM)
    specs = specs or [in_vmem] * len(inputs)
    out_specs = out_specs or [in_vmem] * len(out_shapes)
    return pl.pallas_call(
        kernel,
        in_specs=[pl.BlockSpec(memory_space=pltpu.SMEM)] + specs,
        out_specs=out_specs,
        out_shape=out_shapes,
        scratch_shapes=list(scratch),
        input_output_aliases=aliases or {},
        compiler_params=pltpu.CompilerParams(vmem_limit_bytes=VMEM_BYTES),
        cost_estimate=pl.CostEstimate(flops=0, bytes_accessed=0, transcendentals=0),
    )(scalars, *inputs)


def after(array, *others):
    return lax.optimization_barrier((array, *others))[0]


def on_device(leaf_maps, w_first, w_second, skel_first, skel_second):
    box = lax.axis_index("box")
    face = lax.axis_index("face")
    n_box, n_face = lax.axis_size("box"), lax.axis_size("face")
    nf = n_face - 1
    fr = leaf_maps.shape[4]
    hr = fr // 2
    k = leaf_maps.shape[5] // 3
    half = k // 2
    leaf = leaf_maps[:, 0, 0]
    par = box % 2
    par2 = box // 2 % 2
    scalars = jnp.stack([par, par2, face, box % 4]).astype(jnp.int32)
    sds = jax.ShapeDtypeStruct

    def box_permute(array, mask):
        return lax.ppermute(array, "box", [(b, b ^ mask) for b in range(n_box)])

    def keeper(b):
        return (b & 1) != (b >> 1 & 1)

    def giver(b):
        return not keeper(b)

    def face_permute(array, step, senders=None):
        pairs = [
            (b * n_face + f, b * n_face + (f + n_face - step) % n_face)
            for b in range(n_box) if senders is None or senders(b)
            for f in range(n_face)
        ]
        return lax.ppermute(array, ("box", "face"), pairs)

    def over_face(array, senders=None):
        return [face_permute(array, s, senders) for s in range(1, n_face)]

    skel_one = lax.dynamic_index_in_dim(skel_first[0], box // 2, 0, keepdims=True)
    skel_two = lax.dynamic_index_in_dim(skel_second[0], box // 4, 0, keepdims=True)

    in_hbm = pl.BlockSpec(memory_space=pl.ANY)

    def copy_kernel(parts, sc, leaf_ref, *rest):
        outs, sems = rest[:-1], rest[-1]
        copies = [
            pltpu.make_async_copy(part(sc, leaf_ref), out, sems.at[i])
            for i, (part, out) in enumerate(zip(parts, outs))
        ]
        for copy in copies:
            copy.start()
        for copy in copies:
            copy.wait()

    def copy_parts(parts, width):
        return call(
            lambda *refs: copy_kernel(parts, *refs), scalars, [leaf],
            [sds((2, fr, width), BF16)] * len(parts), specs=[in_hbm],
            scratch=[pltpu.SemaphoreType.DMA((len(parts),))],
        )

    end_own, sides_raw = copy_parts([
        lambda sc, ref: ref.at[:, 1 - sc[0], :, pl.ds(pl.multiple_of(sc[0] * k, k), k)],
        lambda sc, ref: ref.at[:, 1 - sc[0], :, pl.ds(2 * k, k)],
    ], k)
    end_far = over_face(end_own, giver)
    sides_sib = box_permute(sides_raw, 1)
    end_sib = box_permute(end_own, 1)
    s_rows, end_rows = copy_parts([
        lambda sc, ref: ref.at[:, 2], lambda sc, ref: ref.at[:, sc[0]],
    ], 3 * k)
    s_sib = box_permute(s_rows, 1)

    def slots_kernel(sc, own_ref, sib_ref, end_ref, skel_ref, skel2_ref,
                     comp_out, col_out, side_out, keep_out, send_out):
        p, q = sc[0], sc[1]
        rows = lax.broadcasted_iota(jnp.int32, (k, k), 0)
        cols = lax.broadcasted_iota(jnp.int32, (k, k), 1)
        skel = jnp.broadcast_to(skel_ref[...].astype(F32), (k, k))
        column = jnp.sum(jnp.where(rows == cols, skel, 0.0), axis=1, keepdims=True)
        col_out[...] = column.astype(jnp.int32)
        place = skel2_ref[...] - q * k
        taken = jnp.where(rows == place, jnp.broadcast_to(column, (k, k)), 0.0)
        comp = jnp.sum(taken, axis=0, keepdims=True).astype(jnp.int32)
        mine = jnp.logical_and(place >= 0, place < k)
        comp = jnp.where(mine, comp, -1)
        comp_out[...] = comp
        pick_own = column_picker(comp, p * k, k)
        pick_sib = column_picker(comp, (1 - p) * k, k)
        side = dot(flat(own_ref[...]), pick_own) + dot(flat(sib_ref[...]), pick_sib)
        side_out[...] = side.astype(BF16).reshape(2, fr, k)
        couple = pl.ds(pl.multiple_of((1 - p) * k, k), k)
        for ref, h in ((keep_out, p), (send_out, 1 - p)):
            take = pl.ds(pl.multiple_of(h * hr, hr), hr)
            for t in range(2):
                ref[t, :, :k] = end_ref[t, take, couple]
                ref[t, :, k:] = dot(end_ref[t, take, 2 * k :], pick_own).astype(BF16)

    comp, skel_col, side, v_keep, v_send = call(
        slots_kernel, scalars, [sides_raw, sides_sib, end_rows, skel_one, skel_two],
        [sds((1, k), jnp.int32), sds((k, 1), jnp.int32), sds((2, fr, k), BF16),
         sds((2, hr, 2 * k), BF16), sds((2, hr, 2 * k), BF16)],
    )
    side_far = over_face(side, keeper)
    v_recv = box_permute(v_send, 1)

    w_one = jnp.roll(w_first[:, 0], -face * fr, axis=2)
    w_one_sib = box_permute(w_one, 1)
    w_two = jnp.roll(w_second[:, 0], -face * fr, axis=2)
    w_two_pair = jnp.stack([w_two, box_permute(w_two, 2)])
    w_two_sib = box_permute(w_two_pair, 1)

    cr = fr // ROW_CHUNKS

    def rows_kernel(sc, own_ref, sib_ref, end_ref, comp_ref, col_ref, *outs):
        p, q, f = sc[0], sc[1], sc[2]

        @pl.when(p == q)
        def _():
            picker = column_picker(comp_ref[...], p * k, k)
            for t in range(2):
                outs[0][t, :, : 2 * k] = end_ref[t, :, : 2 * k]
                outs[0][t, :, 2 * k :] = dot(end_ref[t, :, 2 * k :], picker).astype(BF16)

        @pl.when(p != q)
        def _():
            pick_own = column_picker(comp_ref[...], p * k, k)
            pick_sib = column_picker(comp_ref[...], (1 - p) * k, k)
            takes = []
            for s in range(n_face):
                start = pl.multiple_of((f + n_face - s) % n_face * fr, fr)
                slots = col_ref[pl.ds(start, fr), :]
                takes.append([row_picker(slots, p * k + f * fr, fr),
                              row_picker(slots, (1 - p) * k + f * fr, fr)])
            take_own = jnp.concatenate([t[0] for t in takes], axis=0)
            take_sib = jnp.concatenate([t[1] for t in takes], axis=0)
            for t in range(2):
                sides = [dot(ref[t, :, 2 * k :], pick).astype(BF16)
                         for ref, pick in ((own_ref, pick_own), (sib_ref, pick_sib))]
                for c in range(3):
                    cols = slice(c * k, (c + 1) * k)
                    own, sib = sides if c == 2 else (own_ref[t, :, cols], sib_ref[t, :, cols])
                    picked = (dot(take_own, own) + dot(take_sib, sib)).astype(BF16)
                    outs[0][t, :, cols] = picked[:fr]
                    for s in range(1, n_face):
                        for i in range(ROW_CHUNKS):
                            lo = s * fr + i * cr
                            outs[1 + (s - 1) * ROW_CHUNKS + i][t, :, cols] = picked[lo : lo + cr]

    kept, *kept_out = call(
        rows_kernel, scalars, [s_rows, s_sib, end_rows, comp, skel_col],
        [sds((2, fr, 3 * k), BF16)] + [sds((2, cr, 3 * k), BF16)] * (nf * ROW_CHUNKS),
    )

    end_fwd = [box_permute(a, 1) for a in end_far]
    side_fwd = [box_permute(a, 1) for a in side_far]
    rest_far = over_face(after(end_own, *side_far), keeper)
    rest_fwd = [box_permute(a, 1) for a in rest_far]

    def hidden_rows(couple, p, own_ref, sib_ref, m):
        lo = pl.ds(pl.multiple_of(p * half, half), half)
        hi = pl.ds(pl.multiple_of((1 - p) * half, half), half)
        both = dot(stacked(couple(0, lo), couple(1, lo)), flat(own_ref[...]))
        both = both + dot(stacked(couple(0, hi), couple(1, hi)), flat(sib_ref[...]))
        both = both.astype(BF16)
        return both[:m], both[m:]

    def piece(hidden, start, count):
        return stacked(hidden[0][:, start : start + count], hidden[1][:, start : start + count])

    def iface_kernel(sc, keep_ref, recv_ref, own_ref, sib_ref, end_ref, endsib_ref, side_ref,
                     acc_out, hid_out, rows):
        p, q = sc[0], sc[1]

        @pl.when(p == q)
        def _():
            rows[...] = recv_ref[...]

        @pl.when(p != q)
        def _():
            rows[...] = keep_ref[...]

        hidden = hidden_rows(lambda t, c: rows[t, :, c], p, own_ref, sib_ref, hr)
        hid_out[0] = hidden[0]
        hid_out[1] = hidden[1]
        left = piece(hidden, 0, fr)
        is_end = p == q
        ends = jnp.where(is_end, end_ref[...], endsib_ref[...])
        acc_out[:, :, :k] = -dot(left, flat(ends)).reshape(2, hr, k)
        acc_out[:, :, k:] = rows[:, :, k:].astype(F32) - dot(left, flat(side_ref[...])).reshape(2, hr, k)

    v_acc, v_hid = call(
        iface_kernel, scalars, [after(v_keep, kept, w_two_sib), v_recv, w_one, w_one_sib, end_own, end_sib, side],
        [sds((2, hr, 2 * k), F32), sds((2, hr, k), BF16)],
        scratch=[pltpu.VMEM((2, hr, 2 * k), BF16)],
    )

    def iface_far_kernel(sc, acc_ref, hid_ref, *rest):
        far, fwd, side_f, side_w = (rest[i * nf : (i + 1) * nf] for i in range(4))
        end_out, side_out = rest[4 * nf :]
        hidden = [hid_ref[0], hid_ref[1]]
        end = acc_ref[:, :, :k]
        side = acc_ref[:, :, k:]
        for s in range(nf):
            left = piece(hidden, (s + 1) * fr, fr)
            end = end - dot(left, flat(far[s][...] + fwd[s][...])).reshape(2, hr, k)
            side = side - dot(left, flat(side_f[s][...] + side_w[s][...])).reshape(2, hr, k)
        end_out[...] = end.astype(BF16)
        side_out[...] = side.astype(BF16)

    two_end, two_side = call(
        iface_far_kernel, scalars, [v_acc, v_hid, *end_far, *end_fwd, *side_far, *side_fwd],
        [sds((2, hr, k), BF16)] * 2,
    )

    side_x = box_permute(two_side, 2)
    end_y = over_face(two_end)
    end_x = box_permute(two_end, 2)

    def half_kernel(sc, own_ref, x_ref, out_ref):
        cols = pl.ds(pl.multiple_of(sc[1] * half, half), half)
        out_ref[...] = own_ref[:, :, cols] + x_ref[:, :, cols]

    (two_half,) = call(half_kernel, scalars, [two_side, side_x], [sds((2, hr, half), BF16)])
    half_y = over_face(two_half)
    end_xy = [box_permute(a, 2) for a in end_y]
    half_xy = [box_permute(a, 2) for a in half_y]

    def join_kernel(sc, end_ref, endx_ref, side_ref, sidex_ref, out_ref):
        q = sc[1]
        out_ref[:, :, pl.ds(pl.multiple_of(q * k, k), k)] = end_ref[...]
        out_ref[:, :, pl.ds(pl.multiple_of((1 - q) * k, k), k)] = endx_ref[...]
        out_ref[:, :, 2 * k :] = side_ref[...] + sidex_ref[...]

    def join_far_kernel(sc, end_ref, endx_ref, side_ref, sidex_ref, out_ref):
        q = sc[1]
        out_ref[:, :, pl.ds(pl.multiple_of(q * k, k), k)] = end_ref[...]
        out_ref[:, :, pl.ds(pl.multiple_of((1 - q) * k, k), k)] = endx_ref[...]
        out_ref[:, :, pl.ds(pl.multiple_of(2 * k + q * half, half), half)] = side_ref[...]
        out_ref[:, :, pl.ds(pl.multiple_of(2 * k + (1 - q) * half, half), half)] = sidex_ref[...]

    two_shape = [sds((2, hr, 3 * k), BF16)]
    two_rows = call(join_kernel, scalars, [two_end, end_x, two_side, side_x], two_shape)
    for s in range(nf):
        two_rows += call(join_far_kernel, scalars, [end_y[s], end_xy[s], half_y[s], half_xy[s]], two_shape)
    two_sib = [box_permute(a, 1) for a in two_rows]

    def gather_kernel(sc, own_ref, sib_ref, side_ref, *rest):
        far, fwd, rfar, rfwd, sfar, sfwd = (rest[i * nf : (i + 1) * nf] for i in range(6))
        out_ref = rest[6 * nf]
        p, q = sc[0], sc[1]

        def block(which):
            return pl.ds(pl.multiple_of(which * k, k), k)

        out_ref[0, :, :, block(p)] = own_ref[...]
        out_ref[0, :, :, block(1 - p)] = sib_ref[...]
        out_ref[0, :, :, 2 * k :] = side_ref[...]
        for s in range(nf):
            out_ref[s + 1, :, :, block(q)] = far[s][...] + fwd[s][...]
            out_ref[s + 1, :, :, block(1 - q)] = rfar[s][...] + rfwd[s][...]
            out_ref[s + 1, :, :, 2 * k :] = sfar[s][...] + sfwd[s][...]

    (iface,) = call(
        gather_kernel, scalars,
        [end_own, end_sib, side, *end_far, *end_fwd, *rest_far, *rest_fwd, *side_far, *side_fwd],
        [sds((n_face, 2, fr, 3 * k), BF16)],
    )

    def keep_kernel(chunk, sc, *refs):
        kept_ref, refs = refs[0], refs[1:]
        far, refs = refs[:nf], refs[nf:]
        col_ref, own_ref, sib_ref, w2_ref, w2sib_ref, iface_ref = refs[:6]
        mine, sibs = refs[6 : 6 + n_face], refs[6 + n_face : 6 + 2 * n_face]
        out_ref, hid, w2, stage, sems = refs[-5:]
        p, q, f, r = sc[0], sc[1], sc[2], sc[3]
        is_end = p == q

        def rows(t, c):
            total = kept_ref[t, chunk * cr : (chunk + 1) * cr, c * k : (c + 1) * k]
            for z in far:
                total = total + z[t, :, c * k : (c + 1) * k]
            return total

        slots = col_ref[pl.ds(pl.multiple_of(f * fr + chunk * cr, cr), cr), :]
        right = jnp.where(slots >= k, 1, 0)
        right = jnp.where(is_end, p, right) > 0
        lefts = [rows(t, 0) for t in range(2)]
        rights = [rows(t, 1) for t in range(2)]
        couple = [jnp.where(right, a, b) for a, b in zip(lefts, rights)]

        def columns(t, which):
            return jnp.where(which == 0, couple[t][:, :half], couple[t][:, half:])

        own = stacked(columns(0, p), columns(1, p))
        sib = stacked(columns(0, 1 - p), columns(1, 1 - p))
        both = (dot(own, flat(own_ref[...])) + dot(sib, flat(sib_ref[...]))).astype(BF16)
        hidden = both[:cr], both[cr:]
        nothing = jnp.zeros((cr, k), BF16)
        start = [
            jnp.concatenate([jnp.where(right, nothing, a) for a in lefts], axis=0),
            jnp.concatenate([jnp.where(right, a, nothing) for a in rights], axis=0),
            jnp.concatenate([rows(t, 2) for t in range(2)], axis=0),
        ]
        merged = []
        for c in range(3):
            total = start[c].astype(F32)
            for s in range(n_face):
                total = total - dot(piece(hidden, s * fr, fr), flat(iface_ref[s, :, :, c * k : (c + 1) * k]))
            merged.append(total.astype(BF16))
        is_left = q == 0
        blk = k // 4
        for i, (ref, part) in enumerate(((w2_ref, 0), (w2_ref, 1), (w2sib_ref, 0), (w2sib_ref, 1))):
            place = r ^ (part * 2) ^ (i // 2)
            for t in range(2):
                w2[t, pl.ds(pl.multiple_of(place * blk, blk), blk), :] = ref[part, t]
        couple2 = jnp.where(is_left, merged[1], merged[0])
        second = dot(stacked(couple2[:cr], couple2[cr:]), flat(w2[...])).astype(BF16)
        for s in range(n_face):
            for h in range(2):
                hid[s * 2 + h] = piece((second[:cr], second[cr:]), s * fr + h * hr, hr)
        none = jnp.zeros_like(merged[0])
        copies = []
        first = [jnp.where(is_left, merged[0], none), jnp.where(is_left, none, merged[1]), merged[2]]
        for c in range(3):
            cols = slice(c * k, (c + 1) * k)
            total = first[c].astype(F32)
            for s in range(n_face):
                total = total - dot(hid[s * 2 + p], flat(mine[s][:, :, cols]))
                total = total - dot(hid[s * 2 + 1 - p], flat(sibs[s][:, :, cols]))
            stage[:, :, cols] = total.astype(BF16).reshape(2, cr, k)
            copies.append(pltpu.make_async_copy(
                stage.at[:, :, pl.ds(c * k, k)],
                out_ref.at[:, 0, pl.ds(chunk * cr, cr), pl.ds(c * k, k)],
                sems.at[c],
            ))
            copies[-1].start()
        for copy in copies:
            copy.wait()

    out = None
    chunks = []
    for i, waits in enumerate((end_y, half_y)):
        outgoing = [after(kept_out[(s - 1) * ROW_CHUNKS + i], *waits) for s in range(1, n_face)]
        chunks.append([face_permute(a, s + 1, keeper) for s, a in enumerate(outgoing)])
    for i in range(ROW_CHUNKS):
        inputs = [kept, *chunks[i], skel_col, w_one, w_one_sib, w_two_pair, w_two_sib, iface, *two_rows, *two_sib]
        specs = [pl.BlockSpec(memory_space=pltpu.VMEM)] * len(inputs)
        aliases = None
        if out is not None:
            inputs.append(out)
            specs.append(in_hbm)
            aliases = {len(inputs): 0}
        (out,) = call(
            lambda sc, *refs, i=i: keep_kernel(i, sc, *refs), scalars, inputs,
            [sds((2, 1, fr, 3 * k), BF16)], specs=specs, out_specs=[in_hbm],
            scratch=[pltpu.VMEM((2 * n_face, 2 * cr, 2 * hr), BF16), pltpu.VMEM((2, k, k), BF16),
                     pltpu.VMEM((2, cr, 3 * k), BF16), pltpu.SemaphoreType.DMA((3,))],
            aliases=aliases,
        )
    return out


def solution(mesh):
    return jax.shard_map(
        on_device,
        mesh=mesh,
        in_specs=(
            P(None, None, "box", None, "face", None),
            P(None, None, "box", None),
            P(None, None, "box", None),
            P(),
            P(),
        ),
        out_specs=P(None, None, ("box", "face"), None),
        check_vma=False,
    )
```

```python
import jax
import jax.numpy as jnp
from jax import lax
from jax.experimental import pallas as pl
from jax.experimental.pallas import tpu as pltpu
from jax.sharding import PartitionSpec as P

BF16 = jnp.bfloat16
F32 = jnp.float32
VMEM_BYTES = 28 * 1024 * 1024
LEAF_VMEM_BYTES = 60 * 1024 * 1024
ROW_CHUNKS = 2


def dot(first, second):
    return jnp.dot(first, second, preferred_element_type=F32)


def stacked(real, imag):
    return jnp.concatenate(
        [jnp.concatenate([real, -imag], axis=1), jnp.concatenate([imag, real], axis=1)], axis=0
    )


def flat(array):
    return array.reshape(array.shape[0] * array.shape[1], array.shape[2])


def column_picker(index, offset, count):
    rows = lax.broadcasted_iota(jnp.int32, (count, index.shape[1]), 0) + offset
    return jnp.where(rows == index, 1.0, 0.0).astype(BF16)


def row_picker(index, offset, count):
    cols = lax.broadcasted_iota(jnp.int32, (index.shape[0], count), 1) + offset
    return jnp.where(cols == index, 1.0, 0.0).astype(BF16)


def call(kernel, scalars, inputs, out_shapes, specs=None, out_specs=None, scratch=(), aliases=None, vmem=VMEM_BYTES):
    in_vmem = pl.BlockSpec(memory_space=pltpu.VMEM)
    specs = specs or [in_vmem] * len(inputs)
    out_specs = out_specs or [in_vmem] * len(out_shapes)
    return pl.pallas_call(
        kernel,
        in_specs=[pl.BlockSpec(memory_space=pltpu.SMEM)] + specs,
        out_specs=out_specs,
        out_shape=out_shapes,
        scratch_shapes=list(scratch),
        input_output_aliases=aliases or {},
        compiler_params=pltpu.CompilerParams(vmem_limit_bytes=vmem),
        cost_estimate=pl.CostEstimate(flops=0, bytes_accessed=0, transcendentals=0),
    )(scalars, *inputs)


def after(array, *others):
    return lax.optimization_barrier((array, *others))[0]


def on_device(leaf_maps, w_first, w_second, skel_first, skel_second):
    box = lax.axis_index("box")
    face = lax.axis_index("face")
    n_box, n_face = lax.axis_size("box"), lax.axis_size("face")
    nf = n_face - 1
    fr = leaf_maps.shape[4]
    hr = fr // 2
    k = leaf_maps.shape[5] // 3
    half = k // 2
    leaf = leaf_maps[:, 0, 0]
    par = box % 2
    par2 = box // 2 % 2
    scalars = jnp.stack([par, par2, face, box % 4]).astype(jnp.int32)
    sds = jax.ShapeDtypeStruct

    def box_permute(array, mask):
        return lax.ppermute(array, "box", [(b, b ^ mask) for b in range(n_box)])

    def keeper(b):
        return (b & 1) != (b >> 1 & 1)

    def giver(b):
        return not keeper(b)

    def face_permute(array, step, senders=None):
        pairs = [
            (b * n_face + f, b * n_face + (f + n_face - step) % n_face)
            for b in range(n_box) if senders is None or senders(b)
            for f in range(n_face)
        ]
        return lax.ppermute(array, ("box", "face"), pairs)

    def over_face(array, senders=None):
        return [face_permute(array, s, senders) for s in range(1, n_face)]

    skel_one = lax.dynamic_index_in_dim(skel_first[0], box // 2, 0, keepdims=True)
    skel_two = lax.dynamic_index_in_dim(skel_second[0], box // 4, 0, keepdims=True)

    in_hbm = pl.BlockSpec(memory_space=pltpu.HBM)

    def copy_kernel(parts, sc, leaf_ref, *rest):
        outs, sems = rest[:-1], rest[-1]
        copies = [
            pltpu.make_async_copy(part(sc, leaf_ref), out, sems.at[i])
            for i, (part, out) in enumerate(zip(parts, outs))
        ]
        for copy in copies:
            copy.start()
        for copy in copies:
            copy.wait()

    def copy_parts(where, parts, width):
        return call(
            lambda *refs: copy_kernel(parts, *refs), where, [leaf],
            [sds((2, fr, width), BF16)] * len(parts), specs=[in_hbm],
            scratch=[pltpu.SemaphoreType.DMA((len(parts),))], vmem=LEAF_VMEM_BYTES,
        )

    end_own, sides_raw = copy_parts(scalars, [
        lambda sc, ref: ref.at[:, 1 - sc[0], :, pl.ds(pl.multiple_of(sc[0] * k, k), k)],
        lambda sc, ref: ref.at[:, 1 - sc[0], :, pl.ds(2 * k, k)],
    ], k)
    end_far = over_face(end_own, giver)
    sides_sib = box_permute(sides_raw, 1)
    s_rows, end_rows = copy_parts(
        after(scalars, sides_sib), [lambda sc, ref: ref.at[:, 2], lambda sc, ref: ref.at[:, sc[0]]], 3 * k
    )
    s_sib = box_permute(s_rows, 1)
    end_sib = box_permute(end_own, 1)

    def slots_kernel(sc, end_ref, own_ref, sib_ref, skel_ref, skel2_ref,
                     comp_out, col_out, side_out, keep_out, send_out):
        p, q = sc[0], sc[1]
        rows = lax.broadcasted_iota(jnp.int32, (k, k), 0)
        cols = lax.broadcasted_iota(jnp.int32, (k, k), 1)
        skel = jnp.broadcast_to(skel_ref[...].astype(F32), (k, k))
        column = jnp.sum(jnp.where(rows == cols, skel, 0.0), axis=1, keepdims=True)
        col_out[...] = column.astype(jnp.int32)
        place = skel2_ref[...] - q * k
        taken = jnp.where(rows == place, jnp.broadcast_to(column, (k, k)), 0.0)
        comp = jnp.sum(taken, axis=0, keepdims=True).astype(jnp.int32)
        mine = jnp.logical_and(place >= 0, place < k)
        comp = jnp.where(mine, comp, -1)
        comp_out[...] = comp
        pick_own = column_picker(comp, p * k, k)
        pick_sib = column_picker(comp, (1 - p) * k, k)
        side = dot(flat(own_ref[...]), pick_own) + dot(flat(sib_ref[...]), pick_sib)
        side_out[...] = side.astype(BF16).reshape(2, fr, k)
        couple = pl.ds(pl.multiple_of((1 - p) * k, k), k)
        for ref, h in ((keep_out, p), (send_out, 1 - p)):
            take = pl.ds(pl.multiple_of(h * hr, hr), hr)
            for t in range(2):
                ref[t, :, :k] = end_ref[t, take, couple]
                ref[t, :, k:] = dot(end_ref[t, take, 2 * k :], pick_own).astype(BF16)

    comp, skel_col, side, v_keep, v_send = call(
        slots_kernel, scalars, [end_rows, sides_raw, sides_sib, skel_one, skel_two],
        [sds((1, k), jnp.int32), sds((k, 1), jnp.int32), sds((2, fr, k), BF16),
         sds((2, hr, 2 * k), BF16), sds((2, hr, 2 * k), BF16)],
    )
    side_far = over_face(after(side, *end_far), keeper)
    v_recv = box_permute(v_send, 1)

    w_one = jnp.roll(w_first[:, 0], -face * fr, axis=2)
    w_one_sib = box_permute(w_one, 1)
    w_two = jnp.roll(after(w_second, comp)[:, 0], -face * fr, axis=2)
    w_two_pair = jnp.stack([w_two, box_permute(w_two, 2)])
    w_two_sib = box_permute(w_two_pair, 1)

    def weights_kernel(sc, one_ref, onesib_ref, two_ref, twosib_ref, one_out, two_out):
        p, r = sc[0], sc[3]
        one_out[:, pl.ds(pl.multiple_of(p * half, half), half), :] = one_ref[...]
        one_out[:, pl.ds(pl.multiple_of((1 - p) * half, half), half), :] = onesib_ref[...]
        blk = k // 4
        for i, (ref, part) in enumerate(((two_ref, 0), (two_ref, 1), (twosib_ref, 0), (twosib_ref, 1))):
            place = r ^ (part * 2) ^ (i // 2)
            two_out[:, pl.ds(pl.multiple_of(place * blk, blk), blk), :] = ref[part]

    weight_one, weight_two = call(
        weights_kernel, scalars, [w_one, w_one_sib, w_two_pair, w_two_sib], [sds((2, k, k), BF16)] * 2,
    )

    cr = fr // ROW_CHUNKS

    def rows_kernel(sc, own_ref, sib_ref, end_ref, comp_ref, col_ref, *outs):
        p, q, f = sc[0], sc[1], sc[2]

        @pl.when(p == q)
        def _():
            picker = column_picker(comp_ref[...], p * k, k)
            for t in range(2):
                outs[0][t, :, : 2 * k] = end_ref[t, :, : 2 * k]
                outs[0][t, :, 2 * k :] = dot(end_ref[t, :, 2 * k :], picker).astype(BF16)

        @pl.when(p != q)
        def _():
            pick_own = column_picker(comp_ref[...], p * k, k)
            pick_sib = column_picker(comp_ref[...], (1 - p) * k, k)
            takes = []
            for s in range(n_face):
                start = pl.multiple_of((f + n_face - s) % n_face * fr, fr)
                slots = col_ref[pl.ds(start, fr), :]
                takes.append([row_picker(slots, p * k + f * fr, fr),
                              row_picker(slots, (1 - p) * k + f * fr, fr)])
            take_own = jnp.concatenate([t[0] for t in takes], axis=0)
            take_sib = jnp.concatenate([t[1] for t in takes], axis=0)
            for t in range(2):
                sides = [dot(ref[t, :, 2 * k :], pick).astype(BF16)
                         for ref, pick in ((own_ref, pick_own), (sib_ref, pick_sib))]
                for c in range(3):
                    cols = slice(c * k, (c + 1) * k)
                    own, sib = sides if c == 2 else (own_ref[t, :, cols], sib_ref[t, :, cols])
                    picked = (dot(take_own, own) + dot(take_sib, sib)).astype(BF16)
                    outs[0][t, :, cols] = picked[:fr]
                    for s in range(1, n_face):
                        for i in range(ROW_CHUNKS):
                            lo = s * fr + i * cr
                            outs[1 + (s - 1) * ROW_CHUNKS + i][t, :, cols] = picked[lo : lo + cr]

    kept, *kept_out = call(
        rows_kernel, scalars, [s_rows, s_sib, end_rows, comp, skel_col],
        [sds((2, fr, 3 * k), BF16)] + [sds((2, cr, 3 * k), BF16)] * (nf * ROW_CHUNKS),
    )

    end_fwd = [box_permute(a, 1) for a in end_far]
    rest_far = over_face(after(end_own, *side_far), keeper)

    def piece(hidden, start, count):
        return stacked(hidden[0][:, start : start + count], hidden[1][:, start : start + count])

    def iface_kernel(sc, keep_ref, recv_ref, w_ref, end_ref, endsib_ref, side_ref,
                     acc_out, hid_out, rows):
        p, q = sc[0], sc[1]

        @pl.when(p == q)
        def _():
            rows[...] = recv_ref[...]

        @pl.when(p != q)
        def _():
            rows[...] = keep_ref[...]

        both = dot(stacked(rows[0, :, :k], rows[1, :, :k]), flat(w_ref[...])).astype(BF16)
        hidden = both[:hr], both[hr:]
        hid_out[0] = hidden[0]
        hid_out[1] = hidden[1]
        left = piece(hidden, 0, fr)
        is_end = p == q
        ends = jnp.where(is_end, end_ref[...], endsib_ref[...])
        acc_out[:, :, :k] = -dot(left, flat(ends)).reshape(2, hr, k)
        acc_out[:, :, k:] = rows[:, :, k:].astype(F32) - dot(left, flat(side_ref[...])).reshape(2, hr, k)

    v_acc, v_hid = call(
        iface_kernel, scalars, [v_keep, v_recv, weight_one, end_own, end_sib, side],
        [sds((2, hr, 2 * k), F32), sds((2, hr, k), BF16)],
        scratch=[pltpu.VMEM((2, hr, 2 * k), BF16)],
    )
    side_fwd = [box_permute(after(a, kept, v_acc), 1) for a in side_far]
    rest_fwd = [box_permute(a, 1) for a in rest_far]

    def iface_far_kernel(sc, acc_ref, hid_ref, *rest):
        far, fwd, side_f, side_w = (rest[i * nf : (i + 1) * nf] for i in range(4))
        end_out, side_out = rest[4 * nf :]
        hidden = [hid_ref[0], hid_ref[1]]
        end = acc_ref[:, :, :k]
        side = acc_ref[:, :, k:]
        for s in range(nf):
            left = piece(hidden, (s + 1) * fr, fr)
            end = end - dot(left, flat(far[s][...] + fwd[s][...])).reshape(2, hr, k)
            side = side - dot(left, flat(side_f[s][...] + side_w[s][...])).reshape(2, hr, k)
        end_out[...] = end.astype(BF16)
        side_out[...] = side.astype(BF16)

    two_end, two_side = call(
        iface_far_kernel, scalars, [v_acc, v_hid, *end_far, *end_fwd, *side_far, *side_fwd],
        [sds((2, hr, k), BF16)] * 2,
    )

    side_x = box_permute(two_side, 2)
    end_y = over_face(after(two_end, *rest_far))
    end_x = box_permute(two_end, 2)

    def half_kernel(sc, own_ref, x_ref, out_ref):
        cols = pl.ds(pl.multiple_of(sc[1] * half, half), half)
        out_ref[...] = own_ref[:, :, cols] + x_ref[:, :, cols]

    (two_half,) = call(half_kernel, scalars, [two_side, side_x], [sds((2, hr, half), BF16)])
    half_y = over_face(two_half)
    end_xy = [box_permute(a, 2) for a in end_y]
    half_xy = [box_permute(a, 2) for a in half_y]

    def join_kernel(sc, end_ref, endx_ref, side_ref, sidex_ref, out_ref):
        q = sc[1]
        out_ref[:, :, pl.ds(pl.multiple_of(q * k, k), k)] = end_ref[...]
        out_ref[:, :, pl.ds(pl.multiple_of((1 - q) * k, k), k)] = endx_ref[...]
        out_ref[:, :, 2 * k :] = side_ref[...] + sidex_ref[...]

    def join_far_kernel(sc, end_ref, endx_ref, side_ref, sidex_ref, out_ref):
        q = sc[1]
        out_ref[:, :, pl.ds(pl.multiple_of(q * k, k), k)] = end_ref[...]
        out_ref[:, :, pl.ds(pl.multiple_of((1 - q) * k, k), k)] = endx_ref[...]
        out_ref[:, :, pl.ds(pl.multiple_of(2 * k + q * half, half), half)] = side_ref[...]
        out_ref[:, :, pl.ds(pl.multiple_of(2 * k + (1 - q) * half, half), half)] = sidex_ref[...]

    two_shape = [sds((2, hr, 3 * k), BF16)]
    two_rows = call(join_kernel, scalars, [two_end, end_x, two_side, side_x], two_shape)
    for s in range(nf):
        two_rows += call(join_far_kernel, scalars, [end_y[s], end_xy[s], half_y[s], half_xy[s]], two_shape)
    two_sib = [box_permute(a, 1) for a in two_rows]

    def level_two_kernel(sc, *refs):
        out_ref = refs[-1]
        p = sc[0]
        for s in range(n_face):
            out_ref[s, :, pl.ds(pl.multiple_of(p * hr, hr), hr), :] = refs[s][...]
            out_ref[s, :, pl.ds(pl.multiple_of((1 - p) * hr, hr), hr), :] = refs[n_face + s][...]

    (iface_two,) = call(
        level_two_kernel, scalars, [*two_rows, *two_sib], [sds((n_face, 2, fr, 3 * k), BF16)],
    )

    def gather_kernel(sc, own_ref, sib_ref, side_ref, *rest):
        far, fwd, rfar, rfwd, sfar, sfwd = (rest[i * nf : (i + 1) * nf] for i in range(6))
        out_ref = rest[6 * nf]
        p, q = sc[0], sc[1]

        def block(which):
            return pl.ds(pl.multiple_of(which * k, k), k)

        out_ref[0, :, :, block(p)] = own_ref[...]
        out_ref[0, :, :, block(1 - p)] = sib_ref[...]
        out_ref[0, :, :, 2 * k :] = side_ref[...]
        for s in range(nf):
            out_ref[s + 1, :, :, block(q)] = far[s][...] + fwd[s][...]
            out_ref[s + 1, :, :, block(1 - q)] = rfar[s][...] + rfwd[s][...]
            out_ref[s + 1, :, :, 2 * k :] = sfar[s][...] + sfwd[s][...]

    (iface,) = call(
        gather_kernel, scalars,
        [end_own, end_sib, side, *end_far, *end_fwd, *rest_far, *rest_fwd, *side_far, *side_fwd],
        [sds((n_face, 2, fr, 3 * k), BF16)],
    )

    def keep_kernel(chunk, sc, *refs):
        kept_ref, refs = refs[0], refs[1:]
        far, refs = refs[:nf], refs[nf:]
        col_ref, w_ref, w2_ref, iface_ref, iface2_ref = refs[:5]
        out_ref, stage, sems = refs[-3:]
        p, q, f = sc[0], sc[1], sc[2]
        is_end = p == q

        def wide(rows):
            parts = [piece((rows[:cr], rows[cr:]), s * fr, fr) for s in range(n_face)]
            return jnp.concatenate(parts, axis=1)

        def gathered(ref, c):
            return ref[:, :, :, c * k : (c + 1) * k].reshape(n_face * 2 * fr, k)

        def rows(t, c):
            total = kept_ref[t, chunk * cr : (chunk + 1) * cr, c * k : (c + 1) * k]
            for z in far:
                total = total + z[t, :, c * k : (c + 1) * k]
            return total

        slots = col_ref[pl.ds(pl.multiple_of(f * fr + chunk * cr, cr), cr), :]
        right = jnp.where(slots >= k, 1, 0)
        right = jnp.where(is_end, p, right) > 0
        lefts = [rows(t, 0) for t in range(2)]
        rights = [rows(t, 1) for t in range(2)]
        couple = [jnp.where(right, a, b) for a, b in zip(lefts, rights)]

        both = dot(stacked(couple[0], couple[1]), flat(w_ref[...])).astype(BF16)
        left = wide(both)
        nothing = jnp.zeros((cr, k), BF16)
        start = [
            jnp.concatenate([jnp.where(right, nothing, a) for a in lefts], axis=0),
            jnp.concatenate([jnp.where(right, a, nothing) for a in rights], axis=0),
            jnp.concatenate([rows(t, 2) for t in range(2)], axis=0),
        ]
        merged = []
        for c in range(3):
            merged.append((start[c].astype(F32) - dot(left, gathered(iface_ref, c))).astype(BF16))
        is_left = q == 0
        couple2 = jnp.where(is_left, merged[1], merged[0])
        second = dot(stacked(couple2[:cr], couple2[cr:]), flat(w2_ref[...])).astype(BF16)
        left = wide(second)
        none = jnp.zeros_like(merged[0])
        copies = []
        first = [jnp.where(is_left, merged[0], none), jnp.where(is_left, none, merged[1]), merged[2]]
        for c in range(3):
            cols = slice(c * k, (c + 1) * k)
            total = first[c].astype(F32) - dot(left, gathered(iface2_ref, c))
            stage[:, :, cols] = total.astype(BF16).reshape(2, cr, k)
            copies.append(pltpu.make_async_copy(
                stage.at[:, :, pl.ds(c * k, k)],
                out_ref.at[:, 0, pl.ds(chunk * cr, cr), pl.ds(c * k, k)],
                sems.at[c],
            ))
            copies[-1].start()
        for copy in copies:
            copy.wait()

    out = None
    chunks = []
    for i, waits in enumerate((rest_far, end_y)):
        outgoing = [after(kept_out[(s - 1) * ROW_CHUNKS + i], *waits) for s in range(1, n_face)]
        chunks.append([face_permute(a, s + 1, keeper) for s, a in enumerate(outgoing)])
    for i in range(ROW_CHUNKS):
        inputs = [kept, *chunks[i], skel_col, weight_one, weight_two, iface, iface_two]
        specs = [pl.BlockSpec(memory_space=pltpu.VMEM)] * len(inputs)
        aliases = None
        if out is not None:
            inputs.append(out)
            specs.append(in_hbm)
            aliases = {len(inputs): 0}
        (out,) = call(
            lambda sc, *refs, i=i: keep_kernel(i, sc, *refs), scalars, inputs,
            [sds((2, 1, fr, 3 * k), BF16)], specs=specs, out_specs=[in_hbm],
            scratch=[pltpu.VMEM((2, cr, 3 * k), BF16), pltpu.SemaphoreType.DMA((3,))],
            aliases=aliases,
        )
    return out


def solution(mesh):
    return jax.shard_map(
        on_device,
        mesh=mesh,
        in_specs=(
            P(None, None, "box", None, "face", None),
            P(None, None, "box", None),
            P(None, None, "box", None),
            P(),
            P(),
        ),
        out_specs=P(None, None, ("box", "face"), None),
        check_vma=False,
    )
```

```python
import jax
import jax.numpy as jnp
from jax import lax
from jax.experimental import pallas as pl
from jax.experimental.pallas import tpu as pltpu
from jax.sharding import PartitionSpec as P

BF16 = jnp.bfloat16
F32 = jnp.float32
VMEM_BYTES = 28 * 1024 * 1024
SLOTS_COST = 20_000_000_000
LEAF_VMEM_BYTES = 60 * 1024 * 1024


def dot(first, second):
    return jnp.dot(first, second, preferred_element_type=F32)


def stacked(real, imag):
    return jnp.concatenate(
        [jnp.concatenate([real, -imag], axis=1), jnp.concatenate([imag, real], axis=1)], axis=0
    )


def flat(array):
    return array.reshape(array.shape[0] * array.shape[1], array.shape[2])


def column_picker(index, offset, count):
    rows = lax.broadcasted_iota(jnp.int32, (count, index.shape[1]), 0) + offset
    return jnp.where(rows == index, 1.0, 0.0).astype(BF16)


def row_picker(index, offset, count):
    cols = lax.broadcasted_iota(jnp.int32, (index.shape[0], count), 1) + offset
    return jnp.where(cols == index, 1.0, 0.0).astype(BF16)


def call(kernel, scalars, inputs, out_shapes, specs=None, out_specs=None, scratch=(), cost=0, vmem=VMEM_BYTES):
    in_vmem = pl.BlockSpec(memory_space=pltpu.VMEM)
    specs = specs or [in_vmem] * len(inputs)
    out_specs = out_specs or [in_vmem] * len(out_shapes)
    return pl.pallas_call(
        kernel,
        in_specs=[pl.BlockSpec(memory_space=pltpu.SMEM)] + specs,
        out_specs=out_specs,
        out_shape=out_shapes,
        scratch_shapes=list(scratch),
        compiler_params=pltpu.CompilerParams(vmem_limit_bytes=vmem),
        cost_estimate=pl.CostEstimate(flops=cost, bytes_accessed=0, transcendentals=0),
    )(scalars, *inputs)


def after(array, *others):
    return lax.optimization_barrier((array, *others))[0]


def on_device(leaf_maps, w_first, w_second, skel_first, skel_second):
    box = lax.axis_index("box")
    face = lax.axis_index("face")
    n_box, n_face = lax.axis_size("box"), lax.axis_size("face")
    nf = n_face - 1
    fr = leaf_maps.shape[4]
    hr = fr // 2
    k = leaf_maps.shape[5] // 3
    half = k // 2
    leaf = leaf_maps[:, 0, 0]
    par = box % 2
    par2 = box // 2 % 2
    scalars = jnp.stack([par, par2, face, box % 4]).astype(jnp.int32)
    sds = jax.ShapeDtypeStruct

    def box_permute(array, mask):
        return lax.ppermute(array, "box", [(b, b ^ mask) for b in range(n_box)])

    def keeper(b):
        return (b & 1) != (b >> 1 & 1)

    def giver(b):
        return not keeper(b)

    def face_permute(array, step, senders=None):
        pairs = [
            (b * n_face + f, b * n_face + (f + n_face - step) % n_face)
            for b in range(n_box) if senders is None or senders(b)
            for f in range(n_face)
        ]
        return lax.ppermute(array, ("box", "face"), pairs)

    def over_face(array, senders=None):
        return [face_permute(array, s, senders) for s in range(1, n_face)]

    skel_one = lax.dynamic_index_in_dim(skel_first[0], box // 2, 0, keepdims=True)
    skel_two = lax.dynamic_index_in_dim(skel_second[0], box // 4, 0, keepdims=True)

    in_hbm = pl.BlockSpec(memory_space=pltpu.HBM)
    in_vmem = pl.BlockSpec(memory_space=pltpu.VMEM)
    splits = 4
    qr = fr // splits

    def copy_kernel(sc, leaf_ref, end_out, side_out, sems):
        p = sc[0]
        copies = []
        for t in range(2):
            for i in range(splits):
                rows = pl.ds(i * qr, qr)
                for j, (out, start) in enumerate(((end_out, p * k), (side_out, 2 * k))):
                    copies.append(pltpu.make_async_copy(
                        leaf_ref.at[t, 1 - p, rows, pl.ds(pl.multiple_of(start, k), k)],
                        out.at[t, rows], sems.at[t, i, j],
                    ))
        for copy in copies:
            copy.start()
        for copy in copies:
            copy.wait()

    end_own, sides_raw = call(
        copy_kernel, scalars, [leaf], [sds((2, fr, k), BF16)] * 2, specs=[in_hbm], out_specs=[in_hbm] * 2,
        scratch=[pltpu.SemaphoreType.DMA((2, splits, 2))], vmem=LEAF_VMEM_BYTES,
    )
    end_sib = box_permute(end_own, 1)
    sides_sib = box_permute(sides_raw, 1)

    def split_kernel(sc, own_ref, sib_ref, first_out, rest_out):
        p, q = sc[0], sc[1]
        rows = pl.ds(pl.multiple_of(p * hr, hr), hr)
        own, sib = own_ref[:, rows, :], sib_ref[:, rows, :]
        first_out[...] = jnp.where(p == q, own, sib)
        rest_out[...] = jnp.where(p == q, sib, own)

    first_send, rest_send = call(
        split_kernel, scalars, [end_own, end_sib], [sds((2, hr, k), BF16)] * 2,
    )
    first_far = over_face(first_send)
    first_fwd = [box_permute(a, 1) for a in first_far]

    def slots_kernel(sc, leaf_ref, own_ref, sib_ref, skel_ref, skel2_ref,
                     comp_out, col_out, side_out, half_out, keep_out, send_out, rows_out, end_out):
        p, q = sc[0], sc[1]
        rows = lax.broadcasted_iota(jnp.int32, (k, k), 0)
        cols = lax.broadcasted_iota(jnp.int32, (k, k), 1)
        skel = jnp.broadcast_to(skel_ref[...].astype(F32), (k, k))
        column = jnp.sum(jnp.where(rows == cols, skel, 0.0), axis=1, keepdims=True)
        col_out[...] = column.astype(jnp.int32)
        place = skel2_ref[...] - q * k
        taken = jnp.where(rows == place, jnp.broadcast_to(column, (k, k)), 0.0)
        comp = jnp.sum(taken, axis=0, keepdims=True).astype(jnp.int32)
        mine = jnp.logical_and(place >= 0, place < k)
        comp = jnp.where(mine, comp, -1)
        comp_out[...] = comp
        pick_own = column_picker(comp, p * k, k)
        pick_sib = column_picker(comp, (1 - p) * k, k)
        side = dot(flat(own_ref[...]), pick_own) + dot(flat(sib_ref[...]), pick_sib)
        side_out[...] = side.astype(BF16).reshape(2, fr, k)
        half_out[...] = side_out[:, pl.ds(pl.multiple_of(p * hr, hr), hr), :]
        rows_out[...] = leaf_ref[:, 2]
        for t in range(2):
            end_out[t, :, : 2 * k] = leaf_ref[t, p, :, : 2 * k]
            end_out[t, :, 2 * k :] = dot(leaf_ref[t, p, :, 2 * k :], pick_own).astype(BF16)
        couple = pl.ds(pl.multiple_of((1 - p) * k, k), k)
        for ref, h in ((keep_out, p), (send_out, 1 - p)):
            take = pl.ds(pl.multiple_of(h * hr, hr), hr)
            for t in range(2):
                ref[t, :, :k] = leaf_ref[t, p, take, couple]
                ref[t, :, k:] = end_out[t, take, 2 * k :]

    comp, skel_col, side, side_half, v_keep, v_send, s_rows, end_kept = call(
        slots_kernel, after(scalars, first_send), [leaf, sides_raw, sides_sib, skel_one, skel_two],
        [sds((1, k), jnp.int32), sds((k, 1), jnp.int32), sds((2, fr, k), BF16),
         sds((2, hr, k), BF16), sds((2, hr, 2 * k), BF16), sds((2, hr, 2 * k), BF16),
         sds((2, fr, 3 * k), BF16), sds((2, fr, 3 * k), BF16)], cost=SLOTS_COST,
    )
    s_sib = box_permute(after(s_rows, *first_far), 1)
    side_far = over_face(after(side_half, *first_far))
    v_recv = box_permute(after(v_send, *first_far), 1)

    w_one = jnp.roll(w_first[:, 0], -face * fr, axis=2)
    w_one_sib = box_permute(w_one, 1)
    w_two = jnp.roll(w_second[:, 0], -face * fr, axis=2)
    w_two_x = box_permute(after(w_two, first_send), 2)

    def weight_one_kernel(sc, own_ref, sib_ref, out_ref):
        p = sc[0]
        out_ref[:, pl.ds(pl.multiple_of(p * half, half), half), :] = own_ref[...]
        out_ref[:, pl.ds(pl.multiple_of((1 - p) * half, half), half), :] = sib_ref[...]

    (weight_one,) = call(weight_one_kernel, scalars, [w_one, w_one_sib], [sds((2, k, k), BF16)])


    def rows_kernel(sc, own_ref, sib_ref, comp_ref, col_ref, kept_out, *outs):
        p, q, f = sc[0], sc[1], sc[2]
        pick_own = column_picker(comp_ref[...], p * k, k)
        pick_sib = column_picker(comp_ref[...], (1 - p) * k, k)

        def pick(slots, write):
            take_own = row_picker(slots, p * k + f * fr, fr)
            take_sib = row_picker(slots, (1 - p) * k + f * fr, fr)
            for t in range(2):
                for c in range(3):
                    cols = slice(c * k, (c + 1) * k)
                    own, sib = own_ref[t, :, cols], sib_ref[t, :, cols]
                    if c == 2:
                        own, sib = [dot(a, b).astype(BF16) for a, b in ((own, pick_own), (sib, pick_sib))]
                    write(t, cols, (dot(take_own, own) + dot(take_sib, sib)).astype(BF16))

        def col_half(s):
            start = (f + n_face - s - 1) % n_face * fr + p * hr
            return col_ref[pl.ds(pl.multiple_of(start, hr), hr), :]

        @pl.when(p == q)
        def _():
            far = jnp.concatenate([col_half(s) for s in range(nf)], axis=0)

            def write(t, cols, picked):
                for s in range(nf):
                    outs[s][t, :, cols] = picked[s * hr : (s + 1) * hr]

            pick(far, write)

        @pl.when(p != q)
        def _():
            far = jnp.concatenate([col_half(s) for s in range(nf)], axis=0)
            slots = jnp.concatenate([col_ref[pl.ds(pl.multiple_of(f * fr, fr), fr), :], far], axis=0)

            def write(t, cols, picked):
                kept_out[t, :, cols] = picked[:fr]
                for s in range(nf):
                    outs[s][t, :, cols] = picked[fr + s * hr : fr + (s + 1) * hr]

            pick(slots, write)

    kept, *kept_out = call(
        rows_kernel, scalars, [s_rows, s_sib, comp, skel_col],
        [sds((2, fr, 3 * k), BF16)] + [sds((2, hr, 3 * k), BF16)] * nf,
    )

    def piece(hidden, start, count):
        return stacked(hidden[0][:, start : start + count], hidden[1][:, start : start + count])

    def iface_kernel(sc, keep_ref, recv_ref, w_ref, end_ref, endsib_ref, side_ref,
                     acc_out, hid_out, rows):
        p, q = sc[0], sc[1]

        @pl.when(p == q)
        def _():
            rows[...] = recv_ref[...]

        @pl.when(p != q)
        def _():
            rows[...] = keep_ref[...]

        both = dot(stacked(rows[0, :, :k], rows[1, :, :k]), flat(w_ref[...])).astype(BF16)
        hidden = both[:hr], both[hr:]
        hid_out[0] = hidden[0]
        hid_out[1] = hidden[1]
        left = piece(hidden, 0, fr)
        is_end = p == q
        ends = jnp.where(is_end, end_ref[...], endsib_ref[...])
        acc_out[:, :, :k] = -dot(left, flat(ends)).reshape(2, hr, k)
        acc_out[:, :, k:] = rows[:, :, k:].astype(F32) - dot(left, flat(side_ref[...])).reshape(2, hr, k)

    v_acc, v_hid = call(
        iface_kernel, scalars, [v_keep, v_recv, weight_one, end_own, end_sib, side],
        [sds((2, hr, 2 * k), F32), sds((2, hr, k), BF16)],
        scratch=[pltpu.VMEM((2, hr, 2 * k), BF16)],
    )
    w_two_pair = jnp.stack([w_two, w_two_x])
    w_two_sib = box_permute(w_two_pair, 1)

    def weight_two_kernel(sc, own_ref, sib_ref, out_ref):
        r = sc[3]
        blk = k // 4
        for i, (ref, part) in enumerate(((own_ref, 0), (own_ref, 1), (sib_ref, 0), (sib_ref, 1))):
            place = r ^ (part * 2) ^ (i // 2)
            out_ref[:, pl.ds(pl.multiple_of(place * blk, blk), blk), :] = ref[part]

    (weight_two,) = call(weight_two_kernel, scalars, [w_two_pair, w_two_sib], [sds((2, k, k), BF16)])

    side_fwd = [box_permute(after(a, kept, v_acc, w_two_x), 1) for a in side_far]
    rest_far = over_face(after(rest_send, kept, v_acc))

    def iface_far_kernel(sc, acc_ref, hid_ref, *rest):
        refs = [rest[i * nf : (i + 1) * nf] for i in range(4)]
        out_ref, rows = rest[4 * nf :]
        p = sc[0]
        mine = pl.ds(pl.multiple_of(p * hr, hr), hr)
        other = pl.ds(pl.multiple_of((1 - p) * hr, hr), hr)
        hidden = [hid_ref[0], hid_ref[1]]
        total = acc_ref[...]
        for s in range(nf):
            rows[:, mine, :k] = refs[0][s][...]
            rows[:, other, :k] = refs[1][s][...]
            rows[:, mine, k:] = refs[2][s][...]
            rows[:, other, k:] = refs[3][s][...]
            left = piece(hidden, (s + 1) * fr, fr)
            total = total - dot(left, flat(rows[...])).reshape(2, hr, 2 * k)
        out_ref[...] = total.astype(BF16)

    (two_own,) = call(
        iface_far_kernel, scalars, [v_acc, v_hid, *first_far, *first_fwd, *side_far, *side_fwd],
        [sds((2, hr, 2 * k), BF16)], scratch=[pltpu.VMEM((2, fr, 2 * k), BF16)],
    )
    rest_fwd = [box_permute(after(a, two_own), 1) for a in rest_far]

    def gather_kernel(sc, own_ref, sib_ref, side_ref, *rest):
        refs = [rest[i * nf : (i + 1) * nf] for i in range(6)]
        out_ref = rest[6 * nf]
        p, q = sc[0], sc[1]

        def block(which):
            return pl.ds(pl.multiple_of(which * k, k), k)

        out_ref[0, :, :, block(p)] = own_ref[...]
        out_ref[0, :, :, block(1 - p)] = sib_ref[...]
        out_ref[0, :, :, 2 * k :] = side_ref[...]
        for i, which in enumerate((q, 1 - q, 2)):
            for h in range(2):
                rows = pl.ds(pl.multiple_of((p ^ h) * hr, hr), hr)
                for s in range(nf):
                    out_ref[s + 1, :, rows, block(which)] = refs[2 * i + h][s][...]

    (iface,) = call(
        gather_kernel, scalars,
        [end_own, end_sib, side, *first_far, *first_fwd, *rest_far, *rest_fwd, *side_far, *side_fwd],
        [sds((n_face, 2, fr, 3 * k), BF16)],
    )

    two_x = box_permute(two_own, 2)
    two_y = over_face(after(two_own, *rest_far))
    two_xy = [box_permute(after(a, two_x), 2) for a in two_y]

    def join_kernel(sc, own_ref, x_ref, out_ref):
        q = sc[1]
        out_ref[:, :, pl.ds(pl.multiple_of(q * k, k), k)] = own_ref[:, :, :k]
        out_ref[:, :, pl.ds(pl.multiple_of((1 - q) * k, k), k)] = x_ref[:, :, :k]
        out_ref[:, :, 2 * k :] = own_ref[:, :, k:] + x_ref[:, :, k:]

    two_rows = []
    ready = after(scalars, weight_two, iface)
    for own, other in zip([two_own, *two_y], [two_x, *two_xy]):
        two_rows += call(join_kernel, ready, [own, other], [sds((2, hr, 3 * k), BF16)])
    two_sib = [box_permute(a, 1) for a in two_rows]

    def level_two_kernel(sc, *refs):
        out_ref = refs[-1]
        p = sc[0]
        for s in range(n_face):
            out_ref[s, :, pl.ds(pl.multiple_of(p * hr, hr), hr), :] = refs[s][...]
            out_ref[s, :, pl.ds(pl.multiple_of((1 - p) * hr, hr), hr), :] = refs[n_face + s][...]

    (iface_two,) = call(
        level_two_kernel, scalars, [*two_rows, *two_sib], [sds((n_face, 2, fr, 3 * k), BF16)],
    )

    kept_far = [face_permute(after(a, two_own), i + 1) for i, a in enumerate(kept_out)]
    kept_fwd = [box_permute(a, 1) for a in kept_far]

    cr = fr

    def keep_kernel(sc, *refs):
        end_ref, kept_ref, *refs = refs
        far, fwd, refs = refs[:nf], refs[nf : 2 * nf], refs[2 * nf :]
        col_ref, w_ref, w2_ref, iface_ref, iface2_ref, out_ref, zs, stage, sems = refs
        p, q, f = sc[0], sc[1], sc[2]
        is_end = p == q

        @pl.when(is_end)
        def _():
            zs[...] = end_ref[...]

        @pl.when(p != q)
        def _():
            for h, parts in enumerate((far, fwd)):
                take = pl.ds(pl.multiple_of((p ^ h) * hr, hr), hr)
                total = kept_ref[:, take, :]
                for part in parts:
                    total = total + part[...]
                zs[:, take, :] = total

        def wide(rows):
            parts = [piece((rows[:cr], rows[cr:]), s * fr, fr) for s in range(n_face)]
            return jnp.concatenate(parts, axis=1)

        def gathered(ref, c):
            return ref[:, :, :, c * k : (c + 1) * k].reshape(n_face * 2 * fr, k)

        def rows(t, c):
            return zs[t, :, c * k : (c + 1) * k]

        slots = col_ref[pl.ds(pl.multiple_of(f * fr, fr), fr), :]
        right = jnp.where(slots >= k, 1, 0)
        right = jnp.where(is_end, p, right) > 0
        lefts = [rows(t, 0) for t in range(2)]
        rights = [rows(t, 1) for t in range(2)]
        couple = [jnp.where(right, a, b) for a, b in zip(lefts, rights)]

        both = dot(stacked(couple[0], couple[1]), flat(w_ref[...])).astype(BF16)
        left = wide(both)
        nothing = jnp.zeros((cr, k), BF16)
        start = [
            jnp.concatenate([jnp.where(right, nothing, a) for a in lefts], axis=0),
            jnp.concatenate([jnp.where(right, a, nothing) for a in rights], axis=0),
            jnp.concatenate([rows(t, 2) for t in range(2)], axis=0),
        ]
        merged = []
        for c in range(3):
            merged.append((start[c].astype(F32) - dot(left, gathered(iface_ref, c))).astype(BF16))
        is_left = q == 0
        couple2 = jnp.where(is_left, merged[1], merged[0])
        second = dot(stacked(couple2[:cr], couple2[cr:]), flat(w2_ref[...])).astype(BF16)
        left = wide(second)
        none = jnp.zeros_like(merged[0])
        copies = []
        first = [jnp.where(is_left, merged[0], none), jnp.where(is_left, none, merged[1]), merged[2]]
        for c in range(3):
            cols = slice(c * k, (c + 1) * k)
            total = first[c].astype(F32) - dot(left, gathered(iface2_ref, c))
            stage[:, :, cols] = total.astype(BF16).reshape(2, cr, k)
            copies.append(pltpu.make_async_copy(
                stage.at[:, :, pl.ds(c * k, k)],
                out_ref.at[:, 0, :, pl.ds(c * k, k)],
                sems.at[c],
            ))
            copies[-1].start()
        for copy in copies:
            copy.wait()

    (out,) = call(
        keep_kernel, scalars,
        [end_kept, kept, *kept_far, *kept_fwd, skel_col, weight_one, weight_two, iface, iface_two],
        [sds((2, 1, fr, 3 * k), BF16)], out_specs=[in_hbm],
        scratch=[pltpu.VMEM((2, fr, 3 * k), BF16), pltpu.VMEM((2, fr, 3 * k), BF16),
                 pltpu.SemaphoreType.DMA((3,))],
    )
    return out


def solution(mesh):
    return jax.shard_map(
        on_device,
        mesh=mesh,
        in_specs=(
            P(None, None, "box", None, "face", None),
            P(None, None, "box", None),
            P(None, None, "box", None),
            P(),
            P(),
        ),
        out_specs=P(None, None, ("box", "face"), None),
        check_vma=False,
    )
```

```python
import jax
import jax.numpy as jnp
from jax import lax
from jax.experimental import pallas as pl
from jax.experimental.pallas import tpu as pltpu
from jax.sharding import PartitionSpec as P

BF16 = jnp.bfloat16
F32 = jnp.float32
VMEM_BYTES = 28 * 1024 * 1024
SLOTS_COST = 20_000_000_000


def dot(first, second):
    return jnp.dot(first, second, preferred_element_type=F32)


def stacked(real, imag):
    return jnp.concatenate(
        [jnp.concatenate([real, -imag], axis=1), jnp.concatenate([imag, real], axis=1)], axis=0
    )


def flat(array):
    return array.reshape(array.shape[0] * array.shape[1], array.shape[2])


def column_picker(index, offset, count):
    rows = lax.broadcasted_iota(jnp.int32, (count, index.shape[1]), 0) + offset
    return jnp.where(rows == index, 1.0, 0.0).astype(BF16)


def row_picker(index, offset, count):
    cols = lax.broadcasted_iota(jnp.int32, (index.shape[0], count), 1) + offset
    return jnp.where(cols == index, 1.0, 0.0).astype(BF16)


def call(kernel, scalars, inputs, out_shapes, specs=None, out_specs=None, scratch=(), cost=0, vmem=VMEM_BYTES):
    in_vmem = pl.BlockSpec(memory_space=pltpu.VMEM)
    specs = specs or [in_vmem] * len(inputs)
    out_specs = out_specs or [in_vmem] * len(out_shapes)
    return pl.pallas_call(
        kernel,
        in_specs=[pl.BlockSpec(memory_space=pltpu.SMEM)] + specs,
        out_specs=out_specs,
        out_shape=out_shapes,
        scratch_shapes=list(scratch),
        compiler_params=pltpu.CompilerParams(vmem_limit_bytes=vmem),
        cost_estimate=pl.CostEstimate(flops=cost, bytes_accessed=0, transcendentals=0),
    )(scalars, *inputs)


def after(array, *others):
    return lax.optimization_barrier((array, *others))[0]


def on_device(leaf_maps, w_first, w_second, skel_first, skel_second):
    box = lax.axis_index("box")
    face = lax.axis_index("face")
    n_box, n_face = lax.axis_size("box"), lax.axis_size("face")
    nf = n_face - 1
    fr = leaf_maps.shape[4]
    hr = fr // 2
    k = leaf_maps.shape[5] // 3
    half = k // 2
    leaf = leaf_maps[:, 0, 0]
    par = box % 2
    par2 = box // 2 % 2
    scalars = jnp.stack([par, par2, face, box % 4]).astype(jnp.int32)
    sds = jax.ShapeDtypeStruct

    def box_permute(array, mask):
        return lax.ppermute(array, "box", [(b, b ^ mask) for b in range(n_box)])

    def keeper(b):
        return (b & 1) != (b >> 1 & 1)

    def giver(b):
        return not keeper(b)

    def face_permute(array, step, senders=None):
        pairs = [
            (b * n_face + f, b * n_face + (f + n_face - step) % n_face)
            for b in range(n_box) if senders is None or senders(b)
            for f in range(n_face)
        ]
        return lax.ppermute(array, ("box", "face"), pairs)

    def over_face(array, senders=None):
        return [face_permute(array, s, senders) for s in range(1, n_face)]

    skel_one = lax.dynamic_index_in_dim(skel_first[0], box // 2, 0, keepdims=True)
    skel_two = lax.dynamic_index_in_dim(skel_second[0], box // 4, 0, keepdims=True)

    in_hbm = pl.BlockSpec(memory_space=pltpu.HBM)

    def parts_kernel(sc, leaf_ref, end_out, side_out, rows_out):
        p = sc[0]
        end_out[...] = leaf_ref[:, 1 - p, :, pl.ds(pl.multiple_of(p * k, k), k)]
        side_out[...] = leaf_ref[:, 1 - p, :, 2 * k :]
        rows_out[...] = leaf_ref[:, 2]

    end_own, sides_raw, s_rows = call(
        parts_kernel, scalars, [leaf], [sds((2, fr, k), BF16)] * 2 + [sds((2, fr, 3 * k), BF16)]
    )
    end_far = over_face(end_own)
    sides_sib = box_permute(sides_raw, 1)
    end_sib = box_permute(end_own, 1)
    s_sib = box_permute(s_rows, 1)

    def slots_kernel(sc, leaf_ref, own_ref, sib_ref, skel_ref, skel2_ref,
                     comp_out, col_out, side_out, half_out, keep_out, send_out, end_out):
        p, q = sc[0], sc[1]
        rows = lax.broadcasted_iota(jnp.int32, (k, k), 0)
        cols = lax.broadcasted_iota(jnp.int32, (k, k), 1)
        skel = jnp.broadcast_to(skel_ref[...].astype(F32), (k, k))
        column = jnp.sum(jnp.where(rows == cols, skel, 0.0), axis=1, keepdims=True)
        col_out[...] = column.astype(jnp.int32)
        place = skel2_ref[...] - q * k
        taken = jnp.where(rows == place, jnp.broadcast_to(column, (k, k)), 0.0)
        comp = jnp.sum(taken, axis=0, keepdims=True).astype(jnp.int32)
        mine = jnp.logical_and(place >= 0, place < k)
        comp = jnp.where(mine, comp, -1)
        comp_out[...] = comp
        pick_own = column_picker(comp, p * k, k)
        pick_sib = column_picker(comp, (1 - p) * k, k)
        side = dot(flat(own_ref[...]), pick_own) + dot(flat(sib_ref[...]), pick_sib)
        side_out[...] = side.astype(BF16).reshape(2, fr, k)
        half_out[...] = side_out[:, pl.ds(pl.multiple_of(p * hr, hr), hr), :]
        for t in range(2):
            end_out[t, :, : 2 * k] = leaf_ref[t, p, :, : 2 * k]
            end_out[t, :, 2 * k :] = dot(leaf_ref[t, p, :, 2 * k :], pick_own).astype(BF16)
        couple = pl.ds(pl.multiple_of((1 - p) * k, k), k)
        for ref, h in ((keep_out, p), (send_out, 1 - p)):
            take = pl.ds(pl.multiple_of(h * hr, hr), hr)
            for t in range(2):
                ref[t, :, :k] = leaf_ref[t, p, take, couple]
                ref[t, :, k:] = end_out[t, take, 2 * k :]

    comp, skel_col, side, side_half, v_keep, v_send, end_kept = call(
        slots_kernel, scalars, [leaf, sides_raw, sides_sib, skel_one, skel_two],
        [sds((1, k), jnp.int32), sds((k, 1), jnp.int32), sds((2, fr, k), BF16),
         sds((2, hr, k), BF16), sds((2, hr, 2 * k), BF16), sds((2, hr, 2 * k), BF16),
         sds((2, fr, 3 * k), BF16)], cost=SLOTS_COST,
    )
    side_far = over_face(side_half)
    v_recv = box_permute(v_send, 1)

    w_one = jnp.roll(w_first[:, 0], -face * fr, axis=2)
    w_one_sib = box_permute(w_one, 1)
    w_two = jnp.roll(w_second[:, 0], -face * fr, axis=2)
    w_two_x = box_permute(after(w_two, side_half), 2)

    def weight_one_kernel(sc, own_ref, sib_ref, out_ref):
        p = sc[0]
        out_ref[:, pl.ds(pl.multiple_of(p * half, half), half), :] = own_ref[...]
        out_ref[:, pl.ds(pl.multiple_of((1 - p) * half, half), half), :] = sib_ref[...]

    (weight_one,) = call(weight_one_kernel, scalars, [w_one, w_one_sib], [sds((2, k, k), BF16)])


    def rows_kernel(sc, own_ref, sib_ref, comp_ref, col_ref, kept_out, *outs):
        p, q, f = sc[0], sc[1], sc[2]
        pick_own = column_picker(comp_ref[...], p * k, k)
        pick_sib = column_picker(comp_ref[...], (1 - p) * k, k)

        def pick(slots, write):
            take_own = row_picker(slots, p * k + f * fr, fr)
            take_sib = row_picker(slots, (1 - p) * k + f * fr, fr)
            for t in range(2):
                for c in range(3):
                    cols = slice(c * k, (c + 1) * k)
                    own, sib = own_ref[t, :, cols], sib_ref[t, :, cols]
                    if c == 2:
                        own, sib = [dot(a, b).astype(BF16) for a, b in ((own, pick_own), (sib, pick_sib))]
                    write(t, cols, (dot(take_own, own) + dot(take_sib, sib)).astype(BF16))

        def col_half(s):
            start = (f + n_face - s - 1) % n_face * fr + p * hr
            return col_ref[pl.ds(pl.multiple_of(start, hr), hr), :]

        @pl.when(p == q)
        def _():
            far = jnp.concatenate([col_half(s) for s in range(nf)], axis=0)

            def write(t, cols, picked):
                for s in range(nf):
                    outs[s][t, :, cols] = picked[s * hr : (s + 1) * hr]

            pick(far, write)

        @pl.when(p != q)
        def _():
            far = jnp.concatenate([col_half(s) for s in range(nf)], axis=0)
            slots = jnp.concatenate([col_ref[pl.ds(pl.multiple_of(f * fr, fr), fr), :], far], axis=0)

            def write(t, cols, picked):
                kept_out[t, :, cols] = picked[:fr]
                for s in range(nf):
                    outs[s][t, :, cols] = picked[fr + s * hr : fr + (s + 1) * hr]

            pick(slots, write)

    kept, *kept_out = call(
        rows_kernel, after(scalars, *end_far), [s_rows, s_sib, comp, skel_col],
        [sds((2, fr, 3 * k), BF16)] + [sds((2, hr, 3 * k), BF16)] * nf,
    )

    def piece(hidden, start, count):
        return stacked(hidden[0][:, start : start + count], hidden[1][:, start : start + count])

    def iface_kernel(sc, keep_ref, recv_ref, w_ref, end_ref, endsib_ref, side_ref,
                     acc_out, hid_out, rows):
        p, q = sc[0], sc[1]

        @pl.when(p == q)
        def _():
            rows[...] = recv_ref[...]

        @pl.when(p != q)
        def _():
            rows[...] = keep_ref[...]

        both = dot(stacked(rows[0, :, :k], rows[1, :, :k]), flat(w_ref[...])).astype(BF16)
        hidden = both[:hr], both[hr:]
        hid_out[0] = hidden[0]
        hid_out[1] = hidden[1]
        left = piece(hidden, 0, fr)
        is_end = p == q
        ends = jnp.where(is_end, end_ref[...], endsib_ref[...])
        acc_out[:, :, :k] = -dot(left, flat(ends)).reshape(2, hr, k)
        acc_out[:, :, k:] = rows[:, :, k:].astype(F32) - dot(left, flat(side_ref[...])).reshape(2, hr, k)

    v_acc, v_hid = call(
        iface_kernel, after(scalars, *end_far), [v_keep, v_recv, weight_one, end_own, end_sib, side],
        [sds((2, hr, 2 * k), F32), sds((2, hr, k), BF16)],
        scratch=[pltpu.VMEM((2, hr, 2 * k), BF16)],
    )
    w_two_pair = jnp.stack([w_two, w_two_x])
    w_two_sib = box_permute(w_two_pair, 1)

    def weight_two_kernel(sc, own_ref, sib_ref, out_ref):
        r = sc[3]
        blk = k // 4
        for i, (ref, part) in enumerate(((own_ref, 0), (own_ref, 1), (sib_ref, 0), (sib_ref, 1))):
            place = r ^ (part * 2) ^ (i // 2)
            out_ref[:, pl.ds(pl.multiple_of(place * blk, blk), blk), :] = ref[part]

    (weight_two,) = call(weight_two_kernel, scalars, [w_two_pair, w_two_sib], [sds((2, k, k), BF16)])

    side_fwd = [box_permute(after(a, kept, v_acc, w_two_x), 1) for a in side_far]
    end_fwd = [box_permute(a, 1) for a in end_far]

    def iface_far_kernel(sc, acc_ref, hid_ref, *rest):
        refs = [rest[i * nf : (i + 1) * nf] for i in range(4)]
        out_ref, rows = rest[4 * nf :]
        p, q = sc[0], sc[1]
        mine = pl.ds(pl.multiple_of(p * hr, hr), hr)
        other = pl.ds(pl.multiple_of((1 - p) * hr, hr), hr)
        hidden = [hid_ref[0], hid_ref[1]]
        total = acc_ref[...]
        for s in range(nf):
            rows[:, :, :k] = jnp.where(p == q, refs[0][s][...], refs[1][s][...])
            rows[:, mine, k:] = refs[2][s][...]
            rows[:, other, k:] = refs[3][s][...]
            left = piece(hidden, (s + 1) * fr, fr)
            total = total - dot(left, flat(rows[...])).reshape(2, hr, 2 * k)
        out_ref[...] = total.astype(BF16)

    (two_own,) = call(
        iface_far_kernel, scalars, [v_acc, v_hid, *end_far, *end_fwd, *side_far, *side_fwd],
        [sds((2, hr, 2 * k), BF16)], scratch=[pltpu.VMEM((2, fr, 2 * k), BF16)],
    )
    def weighted(w_ref, rows, out_ref):
        left = jnp.concatenate([piece((w_ref[0], w_ref[1]), s * fr, fr) for s in range(n_face)], axis=1)
        for c in range(3):
            cols = slice(c * k, (c + 1) * k)
            right = rows[:, :, :, cols].reshape(n_face * 2 * fr, k)
            out_ref[:, :, cols] = dot(left, right).astype(BF16).reshape(2, k, k)

    def weighted_one_kernel(sc, w_ref, own_ref, sib_ref, side_ref, *rest):
        far, fwd, sfar, sfwd = (rest[i * nf : (i + 1) * nf] for i in range(4))
        out_ref, rows = rest[4 * nf :]
        p = sc[0]
        own_cols = pl.ds(pl.multiple_of(p * k, k), k)
        sib_cols = pl.ds(pl.multiple_of((1 - p) * k, k), k)
        mine = pl.ds(pl.multiple_of(p * hr, hr), hr)
        other = pl.ds(pl.multiple_of((1 - p) * hr, hr), hr)
        rows[0, :, :, own_cols] = own_ref[...]
        rows[0, :, :, sib_cols] = sib_ref[...]
        rows[0, :, :, 2 * k :] = side_ref[...]
        for s in range(nf):
            rows[s + 1, :, :, own_cols] = far[s][...]
            rows[s + 1, :, :, sib_cols] = fwd[s][...]
            rows[s + 1, :, mine, 2 * k :] = sfar[s][...]
            rows[s + 1, :, other, 2 * k :] = sfwd[s][...]
        weighted(w_ref, rows, out_ref)

    (solved_one,) = call(
        weighted_one_kernel, after(scalars, two_own),
        [weight_one, end_own, end_sib, side, *end_far, *end_fwd, *side_far, *side_fwd],
        [sds((2, k, 3 * k), BF16)], scratch=[pltpu.VMEM((n_face, 2, fr, 3 * k), BF16)],
    )

    two_x = box_permute(two_own, 2)
    two_y = over_face(two_own)
    two_xy = [box_permute(after(a, two_x), 2) for a in two_y]

    def join_kernel(sc, own_ref, x_ref, out_ref):
        q = sc[1]
        out_ref[:, :, pl.ds(pl.multiple_of(q * k, k), k)] = own_ref[:, :, :k]
        out_ref[:, :, pl.ds(pl.multiple_of((1 - q) * k, k), k)] = x_ref[:, :, :k]
        out_ref[:, :, 2 * k :] = own_ref[:, :, k:] + x_ref[:, :, k:]

    two_rows = []
    ready = after(scalars, weight_two, solved_one)
    for own, other in zip([two_own, *two_y], [two_x, *two_xy]):
        two_rows += call(join_kernel, ready, [own, other], [sds((2, hr, 3 * k), BF16)])
    two_sib = [box_permute(a, 1) for a in two_rows]

    def weighted_two_kernel(sc, w_ref, *refs):
        out_ref, rows = refs[2 * n_face :]
        p = sc[0]
        for s in range(n_face):
            rows[s, :, pl.ds(pl.multiple_of(p * hr, hr), hr), :] = refs[s][...]
            rows[s, :, pl.ds(pl.multiple_of((1 - p) * hr, hr), hr), :] = refs[n_face + s][...]
        weighted(w_ref, rows, out_ref)

    (solved_two,) = call(
        weighted_two_kernel, scalars, [weight_two, *two_rows, *two_sib],
        [sds((2, k, 3 * k), BF16)], scratch=[pltpu.VMEM((n_face, 2, fr, 3 * k), BF16)],
    )

    kept_far = [face_permute(after(a, two_own), i + 1) for i, a in enumerate(kept_out)]
    kept_fwd = [box_permute(a, 1) for a in kept_far]

    cr = fr

    def keep_kernel(sc, *refs):
        end_ref, kept_ref, *refs = refs
        far, fwd, refs = refs[:nf], refs[nf : 2 * nf], refs[2 * nf :]
        col_ref, one_ref, two_ref, out_ref, zs, stage, sems = refs
        p, q, f = sc[0], sc[1], sc[2]
        is_end = p == q

        @pl.when(is_end)
        def _():
            zs[...] = end_ref[...]

        @pl.when(p != q)
        def _():
            for h, parts in enumerate((far, fwd)):
                take = pl.ds(pl.multiple_of((p ^ h) * hr, hr), hr)
                total = kept_ref[:, take, :]
                for part in parts:
                    total = total + part[...]
                zs[:, take, :] = total

        def solved(ref, c):
            return flat(ref[:, :, c * k : (c + 1) * k])

        def rows(t, c):
            return zs[t, :, c * k : (c + 1) * k]

        slots = col_ref[pl.ds(pl.multiple_of(f * fr, fr), fr), :]
        right = jnp.where(slots >= k, 1, 0)
        right = jnp.where(is_end, p, right) > 0
        lefts = [rows(t, 0) for t in range(2)]
        rights = [rows(t, 1) for t in range(2)]
        couple = [jnp.where(right, a, b) for a, b in zip(lefts, rights)]

        left = stacked(couple[0], couple[1])
        nothing = jnp.zeros((cr, k), BF16)
        start = [
            jnp.concatenate([jnp.where(right, nothing, a) for a in lefts], axis=0),
            jnp.concatenate([jnp.where(right, a, nothing) for a in rights], axis=0),
            jnp.concatenate([rows(t, 2) for t in range(2)], axis=0),
        ]
        merged = []
        for c in range(3):
            merged.append((start[c].astype(F32) - dot(left, solved(one_ref, c))).astype(BF16))
        is_left = q == 0
        couple2 = jnp.where(is_left, merged[1], merged[0])
        left = stacked(couple2[:cr], couple2[cr:])
        none = jnp.zeros_like(merged[0])
        copies = []
        first = [jnp.where(is_left, merged[0], none), jnp.where(is_left, none, merged[1]), merged[2]]
        for c in range(3):
            cols = slice(c * k, (c + 1) * k)
            total = first[c].astype(F32) - dot(left, solved(two_ref, c))
            stage[:, :, cols] = total.astype(BF16).reshape(2, cr, k)
            copies.append(pltpu.make_async_copy(
                stage.at[:, :, pl.ds(c * k, k)],
                out_ref.at[:, 0, :, pl.ds(c * k, k)],
                sems.at[c],
            ))
            copies[-1].start()
        for copy in copies:
            copy.wait()

    (out,) = call(
        keep_kernel, scalars,
        [end_kept, kept, *kept_far, *kept_fwd, skel_col, solved_one, solved_two],
        [sds((2, 1, fr, 3 * k), BF16)], out_specs=[in_hbm],
        scratch=[pltpu.VMEM((2, fr, 3 * k), BF16), pltpu.VMEM((2, fr, 3 * k), BF16),
                 pltpu.SemaphoreType.DMA((3,))],
    )
    return out


def solution(mesh):
    return jax.shard_map(
        on_device,
        mesh=mesh,
        in_specs=(
            P(None, None, "box", None, "face", None),
            P(None, None, "box", None),
            P(None, None, "box", None),
            P(),
            P(),
        ),
        out_specs=P(None, None, ("box", "face"), None),
        check_vma=False,
    )
```

```python
import jax
import jax.numpy as jnp
from jax import lax
from jax.experimental import pallas as pl
from jax.experimental.pallas import tpu as pltpu
from jax.sharding import PartitionSpec as P

BF16 = jnp.bfloat16
F32 = jnp.float32
VMEM_BYTES = 16 * 1024 * 1024
SLOTS_COST = 20_000_000_000
JOIN_COST = 300_000_000


def dot(first, second):
    return jnp.dot(first, second, preferred_element_type=F32)


def stacked(real, imag):
    return jnp.concatenate(
        [jnp.concatenate([real, -imag], axis=1), jnp.concatenate([imag, real], axis=1)], axis=0
    )


def flat(array):
    return array.reshape(array.shape[0] * array.shape[1], array.shape[2])


def column_picker(index, offset, count):
    rows = lax.broadcasted_iota(jnp.int32, (count, index.shape[1]), 0) + offset
    return jnp.where(rows == index, 1.0, 0.0).astype(BF16)


def row_picker(index, offset, count):
    cols = lax.broadcasted_iota(jnp.int32, (index.shape[0], count), 1) + offset
    return jnp.where(cols == index, 1.0, 0.0).astype(BF16)


def call(kernel, scalars, inputs, out_shapes, specs=None, out_specs=None, scratch=(), cost=0, vmem=VMEM_BYTES):
    in_vmem = pl.BlockSpec(memory_space=pltpu.VMEM)
    specs = specs or [in_vmem] * len(inputs)
    out_specs = out_specs or [in_vmem] * len(out_shapes)
    return pl.pallas_call(
        kernel,
        in_specs=[pl.BlockSpec(memory_space=pltpu.SMEM)] + specs,
        out_specs=out_specs,
        out_shape=out_shapes,
        scratch_shapes=list(scratch),
        compiler_params=pltpu.CompilerParams(vmem_limit_bytes=vmem),
        cost_estimate=pl.CostEstimate(flops=cost, bytes_accessed=0, transcendentals=0),
    )(scalars, *inputs)


def after(array, *others):
    return lax.optimization_barrier((array, *others))[0]


def on_device(leaf_maps, w_first, w_second, skel_first, skel_second):
    box = lax.axis_index("box")
    face = lax.axis_index("face")
    n_box, n_face = lax.axis_size("box"), lax.axis_size("face")
    nf = n_face - 1
    fr = leaf_maps.shape[4]
    hr = fr // 2
    k = leaf_maps.shape[5] // 3
    half = k // 2
    leaf = leaf_maps[:, 0, 0]
    par = box % 2
    par2 = box // 2 % 2
    scalars = jnp.stack([par, par2, face, box % 4]).astype(jnp.int32)
    sds = jax.ShapeDtypeStruct

    def box_permute(array, mask):
        return lax.ppermute(array, "box", [(b, b ^ mask) for b in range(n_box)])

    def keeper(b):
        return (b & 1) != (b >> 1 & 1)

    def giver(b):
        return not keeper(b)

    def face_permute(array, step, senders=None):
        pairs = [
            (b * n_face + f, b * n_face + (f + n_face - step) % n_face)
            for b in range(n_box) if senders is None or senders(b)
            for f in range(n_face)
        ]
        return lax.ppermute(array, ("box", "face"), pairs)

    def over_face(array, senders=None):
        return [face_permute(array, s, senders) for s in range(1, n_face)]

    skel_one = lax.dynamic_index_in_dim(skel_first[0], box // 2, 0, keepdims=True)
    skel_two = lax.dynamic_index_in_dim(skel_second[0], box // 4, 0, keepdims=True)

    in_hbm = pl.BlockSpec(memory_space=pltpu.HBM)

    def parts_kernel(sc, leaf_ref, end_out, side_out, rows_out, ends_out):
        p = sc[0]
        end_out[...] = leaf_ref[:, 1 - p, :, pl.ds(pl.multiple_of(p * k, k), k)]
        side_out[...] = leaf_ref[:, 1 - p, :, 2 * k :]
        rows_out[...] = leaf_ref[:, 2]
        ends_out[...] = leaf_ref[:, p]

    end_own, sides_raw, s_rows, end_rows = call(
        parts_kernel, scalars, [leaf], [sds((2, fr, k), BF16)] * 2 + [sds((2, fr, 3 * k), BF16)] * 2
    )
    end_sib = box_permute(end_own, 1)
    sides_sib = box_permute(sides_raw, 1)
    s_sib = box_permute(s_rows, 1)

    def split_kernel(sc, own_ref, sib_ref, first_out, rest_out):
        p, q = sc[0], sc[1]
        rows = pl.ds(pl.multiple_of(p * hr, hr), hr)
        own, sib = own_ref[:, rows, :], sib_ref[:, rows, :]
        first_out[...] = jnp.where(p == q, own, sib)
        rest_out[...] = jnp.where(p == q, sib, own)

    first_send, rest_send = call(split_kernel, scalars, [end_own, end_sib], [sds((2, hr, k), BF16)] * 2)
    first_far = over_face(first_send)
    first_fwd = [box_permute(a, 1) for a in first_far]

    def slots_kernel(sc, end_ref, own_ref, sib_ref, skel_ref, skel2_ref,
                     comp_out, col_out, side_out, half_out, keep_out, send_out, end_out):
        p, q = sc[0], sc[1]
        rows = lax.broadcasted_iota(jnp.int32, (k, k), 0)
        cols = lax.broadcasted_iota(jnp.int32, (k, k), 1)
        skel = jnp.broadcast_to(skel_ref[...].astype(F32), (k, k))
        column = jnp.sum(jnp.where(rows == cols, skel, 0.0), axis=1, keepdims=True)
        col_out[...] = column.astype(jnp.int32)
        place = skel2_ref[...] - q * k
        taken = jnp.where(rows == place, jnp.broadcast_to(column, (k, k)), 0.0)
        comp = jnp.sum(taken, axis=0, keepdims=True).astype(jnp.int32)
        mine = jnp.logical_and(place >= 0, place < k)
        comp = jnp.where(mine, comp, -1)
        comp_out[...] = comp
        pick_own = column_picker(comp, p * k, k)
        pick_sib = column_picker(comp, (1 - p) * k, k)
        side = dot(flat(own_ref[...]), pick_own) + dot(flat(sib_ref[...]), pick_sib)
        side_out[...] = side.astype(BF16).reshape(2, fr, k)
        half_out[...] = side_out[:, pl.ds(pl.multiple_of(p * hr, hr), hr), :]
        for t in range(2):
            end_out[t, :, : 2 * k] = end_ref[t, :, : 2 * k]
            end_out[t, :, 2 * k :] = dot(end_ref[t, :, 2 * k :], pick_own).astype(BF16)
        couple = pl.ds(pl.multiple_of((1 - p) * k, k), k)
        for ref, h in ((keep_out, p), (send_out, 1 - p)):
            take = pl.ds(pl.multiple_of(h * hr, hr), hr)
            for t in range(2):
                ref[t, :, :k] = end_ref[t, take, couple]
                ref[t, :, k:] = end_out[t, take, 2 * k :]

    comp, skel_col, side, side_half, v_keep, v_send, end_kept = call(
        slots_kernel, after(scalars, first_send), [end_rows, sides_raw, sides_sib, skel_one, skel_two],
        [sds((1, k), jnp.int32), sds((k, 1), jnp.int32), sds((2, fr, k), BF16),
         sds((2, hr, k), BF16), sds((2, hr, 2 * k), BF16), sds((2, hr, 2 * k), BF16),
         sds((2, fr, 3 * k), BF16)], cost=SLOTS_COST,
    )
    side_far = over_face(side_half)
    v_recv = box_permute(v_send, 1)

    w_one = jnp.roll(w_first[:, 0], -face * fr, axis=2)
    w_one_sib = box_permute(w_one, 1)
    w_two = jnp.roll(w_second[:, 0], -face * fr, axis=2)
    w_two_x = box_permute(after(w_two, side_half), 2)

    def weight_one_kernel(sc, own_ref, sib_ref, out_ref):
        p = sc[0]
        out_ref[:, pl.ds(pl.multiple_of(p * half, half), half), :] = own_ref[...]
        out_ref[:, pl.ds(pl.multiple_of((1 - p) * half, half), half), :] = sib_ref[...]

    (weight_one,) = call(weight_one_kernel, scalars, [w_one, w_one_sib], [sds((2, k, k), BF16)])


    def rows_kernel(sc, own_ref, sib_ref, comp_ref, col_ref, rest_ref, kept_out, *outs):
        p, q, f = sc[0], sc[1], sc[2]
        pick_own = column_picker(comp_ref[...], p * k, k)
        pick_sib = column_picker(comp_ref[...], (1 - p) * k, k)

        def pick(slots, write):
            take_own = row_picker(slots, p * k + f * fr, fr)
            take_sib = row_picker(slots, (1 - p) * k + f * fr, fr)
            for t in range(2):
                for c in range(3):
                    cols = slice(c * k, (c + 1) * k)
                    own, sib = own_ref[t, :, cols], sib_ref[t, :, cols]
                    if c == 2:
                        own, sib = [dot(a, b).astype(BF16) for a, b in ((own, pick_own), (sib, pick_sib))]
                    write(t, c, (dot(take_own, own) + dot(take_sib, sib)).astype(BF16))

        for s in range(nf):
            outs[s][:, :, :k] = rest_ref[...]

        def write_far(s, t, c, picked):
            if c == 0:
                outs[s][t, :, k:] = picked
            else:
                outs[nf + s][t, :, (c - 1) * k : c * k] = picked

        def col_half(s):
            start = (f + n_face - s - 1) % n_face * fr + p * hr
            return col_ref[pl.ds(pl.multiple_of(start, hr), hr), :]

        @pl.when(p == q)
        def _():
            far = jnp.concatenate([col_half(s) for s in range(nf)], axis=0)

            def write(t, c, picked):
                for s in range(nf):
                    write_far(s, t, c, picked[s * hr : (s + 1) * hr])

            pick(far, write)

        @pl.when(p != q)
        def _():
            far = jnp.concatenate([col_half(s) for s in range(nf)], axis=0)
            slots = jnp.concatenate([col_ref[pl.ds(pl.multiple_of(f * fr, fr), fr), :], far], axis=0)

            def write(t, c, picked):
                kept_out[t, :, c * k : (c + 1) * k] = picked[:fr]
                for s in range(nf):
                    write_far(s, t, c, picked[fr + s * hr : fr + (s + 1) * hr])

            pick(slots, write)

    kept, *kept_out = call(
        rows_kernel, after(scalars, *first_far), [s_rows, s_sib, comp, skel_col, rest_send],
        [sds((2, fr, 3 * k), BF16)] + [sds((2, hr, 2 * k), BF16)] * (2 * nf),
    )

    def piece(hidden, start, count):
        return stacked(hidden[0][:, start : start + count], hidden[1][:, start : start + count])

    def iface_kernel(sc, keep_ref, recv_ref, w_ref, end_ref, endsib_ref, side_ref,
                     acc_out, hid_out, rows):
        p, q = sc[0], sc[1]

        @pl.when(p == q)
        def _():
            rows[...] = recv_ref[...]

        @pl.when(p != q)
        def _():
            rows[...] = keep_ref[...]

        both = dot(stacked(rows[0, :, :k], rows[1, :, :k]), flat(w_ref[...])).astype(BF16)
        hidden = both[:hr], both[hr:]
        hid_out[0] = hidden[0]
        hid_out[1] = hidden[1]
        left = piece(hidden, 0, fr)
        is_end = p == q
        ends = jnp.where(is_end, end_ref[...], endsib_ref[...])
        acc_out[:, :, :k] = -dot(left, flat(ends)).reshape(2, hr, k)
        acc_out[:, :, k:] = rows[:, :, k:].astype(F32) - dot(left, flat(side_ref[...])).reshape(2, hr, k)

    v_acc, v_hid = call(
        iface_kernel, after(scalars, *first_far), [v_keep, v_recv, weight_one, end_own, end_sib, side],
        [sds((2, hr, 2 * k), F32), sds((2, hr, k), BF16)],
        scratch=[pltpu.VMEM((2, hr, 2 * k), BF16)],
    )
    w_two_pair = jnp.stack([w_two, w_two_x])
    w_two_sib = box_permute(w_two_pair, 1)

    def weight_two_kernel(sc, own_ref, sib_ref, out_ref):
        r = sc[3]
        blk = k // 4
        for i, (ref, part) in enumerate(((own_ref, 0), (own_ref, 1), (sib_ref, 0), (sib_ref, 1))):
            place = r ^ (part * 2) ^ (i // 2)
            out_ref[:, pl.ds(pl.multiple_of(place * blk, blk), blk), :] = ref[part]

    (weight_two,) = call(weight_two_kernel, scalars, [w_two_pair, w_two_sib], [sds((2, k, k), BF16)])

    side_fwd = [box_permute(after(a, kept, v_acc, w_two_x), 1) for a in side_far]
    mixed_far = [face_permute(after(a, v_acc), i + 1) for i, a in enumerate(kept_out[:nf])]

    def iface_far_kernel(sc, acc_ref, hid_ref, *rest):
        refs = [rest[i * nf : (i + 1) * nf] for i in range(4)]
        end_out, keep_out, send_out, rows = rest[4 * nf :]
        p, q = sc[0], sc[1]
        mine = pl.ds(pl.multiple_of(p * hr, hr), hr)
        other = pl.ds(pl.multiple_of((1 - p) * hr, hr), hr)
        hidden = [hid_ref[0], hid_ref[1]]
        total = acc_ref[...]
        for s in range(nf):
            rows[:, mine, :k] = refs[0][s][...]
            rows[:, other, :k] = refs[1][s][...]
            rows[:, mine, k:] = refs[2][s][...]
            rows[:, other, k:] = refs[3][s][...]
            left = piece(hidden, (s + 1) * fr, fr)
            total = total - dot(left, flat(rows[...])).reshape(2, hr, 2 * k)
        total = total.astype(BF16)
        end_out[...] = total[:, :, :k]
        low, high = total[:, :, k : k + half], total[:, :, k + half :]
        keep_out[...] = jnp.where(q == 0, low, high)
        send_out[...] = jnp.where(q == 0, high, low)

    two_end, side_keep, side_send = call(
        iface_far_kernel, scalars, [v_acc, v_hid, *first_far, *first_fwd, *side_far, *side_fwd],
        [sds((2, hr, k), BF16)] + [sds((2, hr, half), BF16)] * 2, scratch=[pltpu.VMEM((2, fr, 2 * k), BF16)],
    )

    side_x = box_permute(side_send, 2)

    def pack_kernel(sc, end_ref, keep_ref, x_ref, out_ref):
        out_ref[:, :, :k] = end_ref[...]
        out_ref[:, :, k:] = keep_ref[...] + x_ref[...]

    (two_own,) = call(
        pack_kernel, scalars, [two_end, side_keep, side_x], [sds((2, hr, k + half), BF16)]
    )
    two_x = box_permute(two_own, 2)
    two_y = over_face(after(two_own, *mixed_far))
    mixed_fwd = [box_permute(after(a, two_own), 1) for a in mixed_far]

    def weighted(w_ref, rows, out_ref):
        left = jnp.concatenate([piece((w_ref[0], w_ref[1]), s * fr, fr) for s in range(n_face)], axis=1)
        for c in range(3):
            cols = slice(c * k, (c + 1) * k)
            right = rows[:, :, :, cols].reshape(n_face * 2 * fr, k)
            out_ref[:, :, cols] = dot(left, right).astype(BF16).reshape(2, k, k)

    def weighted_one_kernel(sc, w_ref, own_ref, sib_ref, side_ref, *rest):
        refs = [rest[i * nf : (i + 1) * nf] for i in range(6)]
        out_ref, rows = rest[6 * nf :]
        p, q = sc[0], sc[1]
        first_cols = pl.ds(pl.multiple_of(q * k, k), k)
        rest_cols = pl.ds(pl.multiple_of((1 - q) * k, k), k)
        own_cols = pl.ds(pl.multiple_of(p * k, k), k)
        sib_cols = pl.ds(pl.multiple_of((1 - p) * k, k), k)
        mine = pl.ds(pl.multiple_of(p * hr, hr), hr)
        other = pl.ds(pl.multiple_of((1 - p) * hr, hr), hr)
        rows[0, :, :, own_cols] = own_ref[...]
        rows[0, :, :, sib_cols] = sib_ref[...]
        rows[0, :, :, 2 * k :] = side_ref[...]
        for s in range(nf):
            for h, take in enumerate((mine, other)):
                rows[s + 1, :, take, first_cols] = refs[h][s][...]
                rows[s + 1, :, take, rest_cols] = refs[2 + h][s][:, :, :k]
                rows[s + 1, :, take, 2 * k :] = refs[4 + h][s][...]
        weighted(w_ref, rows, out_ref)

    (solved_one,) = call(
        weighted_one_kernel, scalars,
        [weight_one, end_own, end_sib, side, *first_far, *first_fwd, *mixed_far, *mixed_fwd, *side_far, *side_fwd],
        [sds((2, k, 3 * k), BF16)], scratch=[pltpu.VMEM((n_face, 2, fr, 3 * k), BF16)],
    )

    def join_kernel(sc, own_ref, x_ref, out_ref):
        q = sc[1]
        for ref, which in ((own_ref, q), (x_ref, 1 - q)):
            out_ref[:, :, pl.ds(pl.multiple_of(which * k, k), k)] = ref[:, :, :k]
            out_ref[:, :, pl.ds(pl.multiple_of(2 * k + which * half, half), half)] = ref[:, :, k:]

    two_shape = [sds((2, hr, 3 * k), BF16)]
    two_rows = call(join_kernel, scalars, [two_own, two_x], two_shape, cost=JOIN_COST)
    two_xy = [box_permute(after(a, *two_rows), 2) for a in two_y]
    for own, other in zip(two_y, two_xy):
        two_rows += call(join_kernel, after(scalars, weight_two, solved_one), [own, other], two_shape)
    two_sib = [box_permute(a, 1) for a in two_rows]

    def level_two_kernel(sc, *refs):
        out_ref = refs[-1]
        p = sc[0]
        for s in range(n_face):
            out_ref[s, :, pl.ds(pl.multiple_of(p * hr, hr), hr), :] = refs[s][...]
            out_ref[s, :, pl.ds(pl.multiple_of((1 - p) * hr, hr), hr), :] = refs[n_face + s][...]

    (iface_two,) = call(
        level_two_kernel, scalars, [*two_rows, *two_sib], [sds((n_face, 2, fr, 3 * k), BF16)]
    )

    kept_far = [face_permute(after(a, two_own), i + 1) for i, a in enumerate(kept_out[nf:])]
    kept_fwd = [box_permute(a, 1) for a in kept_far]

    cr = fr

    def keep_kernel(sc, *refs):
        end_ref, kept_ref, *refs = refs
        parts = [refs[i * nf : (i + 1) * nf] for i in range(4)]
        col_ref, one_ref, w_ref, two_ref, out_ref, zs, stage, sems = refs[4 * nf :]
        p, q, f = sc[0], sc[1], sc[2]
        is_end = p == q

        @pl.when(is_end)
        def _():
            zs[...] = end_ref[...]

        @pl.when(p != q)
        def _():
            for h in range(2):
                take = pl.ds(pl.multiple_of((p ^ h) * hr, hr), hr)
                for refs, cols, source in (
                    (parts[h], slice(0, k), slice(k, 2 * k)), (parts[2 + h], slice(k, 3 * k), slice(0, 2 * k)),
                ):
                    total = kept_ref[:, take, cols]
                    for ref in refs:
                        total = total + ref[:, :, source]
                    zs[:, take, cols] = total

        def wide(rows):
            parts = [piece((rows[:cr], rows[cr:]), s * fr, fr) for s in range(n_face)]
            return jnp.concatenate(parts, axis=1)

        def solved(ref, c):
            return flat(ref[:, :, c * k : (c + 1) * k])

        def gathered(ref, c):
            return ref[:, :, :, c * k : (c + 1) * k].reshape(n_face * 2 * fr, k)

        def rows(t, c):
            return zs[t, :, c * k : (c + 1) * k]

        slots = col_ref[pl.ds(pl.multiple_of(f * fr, fr), fr), :]
        right = jnp.where(slots >= k, 1, 0)
        right = jnp.where(is_end, p, right) > 0
        lefts = [rows(t, 0) for t in range(2)]
        rights = [rows(t, 1) for t in range(2)]
        couple = [jnp.where(right, a, b) for a, b in zip(lefts, rights)]

        left = stacked(couple[0], couple[1])
        nothing = jnp.zeros((cr, k), BF16)
        start = [
            jnp.concatenate([jnp.where(right, nothing, a) for a in lefts], axis=0),
            jnp.concatenate([jnp.where(right, a, nothing) for a in rights], axis=0),
            jnp.concatenate([rows(t, 2) for t in range(2)], axis=0),
        ]
        merged = []
        for c in range(3):
            merged.append((start[c].astype(F32) - dot(left, solved(one_ref, c))).astype(BF16))
        is_left = q == 0
        couple2 = jnp.where(is_left, merged[1], merged[0])
        second = dot(stacked(couple2[:cr], couple2[cr:]), flat(w_ref[...])).astype(BF16)
        left = wide(second)
        none = jnp.zeros_like(merged[0])
        copies = []
        first = [jnp.where(is_left, merged[0], none), jnp.where(is_left, none, merged[1]), merged[2]]
        for c in range(3):
            cols = slice(c * k, (c + 1) * k)
            total = first[c].astype(F32) - dot(left, gathered(two_ref, c))
            stage[:, :, cols] = total.astype(BF16).reshape(2, cr, k)
            copies.append(pltpu.make_async_copy(
                stage.at[:, :, pl.ds(c * k, k)],
                out_ref.at[:, 0, :, pl.ds(c * k, k)],
                sems.at[c],
            ))
            copies[-1].start()
        for copy in copies:
            copy.wait()

    (out,) = call(
        keep_kernel, scalars,
        [end_kept, kept, *mixed_far, *mixed_fwd, *kept_far, *kept_fwd, skel_col, solved_one, weight_two, iface_two],
        [sds((2, 1, fr, 3 * k), BF16)], out_specs=[in_hbm],
        scratch=[pltpu.VMEM((2, fr, 3 * k), BF16), pltpu.VMEM((2, fr, 3 * k), BF16),
                 pltpu.SemaphoreType.DMA((3,))],
    )
    return out


def solution(mesh):
    return jax.shard_map(
        on_device,
        mesh=mesh,
        in_specs=(
            P(None, None, "box", None, "face", None),
            P(None, None, "box", None),
            P(None, None, "box", None),
            P(),
            P(),
        ),
        out_specs=P(None, None, ("box", "face"), None),
        check_vma=False,
    )
```

```python
import jax
import jax.numpy as jnp
from jax import lax
from jax.experimental import pallas as pl
from jax.experimental.pallas import tpu as pltpu
from jax.sharding import PartitionSpec as P

BF16 = jnp.bfloat16
F32 = jnp.float32
VMEM_BYTES = 16 * 1024 * 1024
SLOTS_COST = 20_000_000_000
JOIN_COST = 300_000_000
MERGE_COST = 2_000_000_000
KEEP_COST = 6_000_000_000
SLOT_ROWS_COST = 2_000_000_000


def dot(first, second):
    return jnp.dot(first, second, preferred_element_type=F32)


def stacked(real, imag):
    return jnp.concatenate(
        [jnp.concatenate([real, -imag], axis=1), jnp.concatenate([imag, real], axis=1)], axis=0
    )


def flat(array):
    return array.reshape(array.shape[0] * array.shape[1], array.shape[2])


def column_picker(index, offset, count):
    rows = lax.broadcasted_iota(jnp.int32, (count, index.shape[1]), 0) + offset
    return jnp.where(rows == index, 1.0, 0.0).astype(BF16)


def row_picker(index, offset, count):
    cols = lax.broadcasted_iota(jnp.int32, (index.shape[0], count), 1) + offset
    return jnp.where(cols == index, 1.0, 0.0).astype(BF16)


def call(kernel, scalars, inputs, out_shapes, specs=None, out_specs=None, scratch=(), cost=0, aliases=None):
    in_vmem = pl.BlockSpec(memory_space=pltpu.VMEM)
    specs = specs or [in_vmem] * len(inputs)
    out_specs = out_specs or [in_vmem] * len(out_shapes)
    return pl.pallas_call(
        kernel,
        in_specs=[pl.BlockSpec(memory_space=pltpu.SMEM)] + specs,
        out_specs=out_specs,
        out_shape=out_shapes,
        scratch_shapes=list(scratch),
        input_output_aliases=aliases or {},
        compiler_params=pltpu.CompilerParams(vmem_limit_bytes=VMEM_BYTES),
        cost_estimate=pl.CostEstimate(flops=cost, bytes_accessed=0, transcendentals=0),
    )(scalars, *inputs)


def after(array, *others):
    return lax.optimization_barrier((array, *others))[0]


def on_device(leaf_maps, w_first, w_second, skel_first, skel_second):
    box = lax.axis_index("box")
    face = lax.axis_index("face")
    n_box, n_face = lax.axis_size("box"), lax.axis_size("face")
    nf = n_face - 1
    fr = leaf_maps.shape[4]
    hr = fr // 2
    k = leaf_maps.shape[5] // 3
    half = k // 2
    leaf = leaf_maps[:, 0, 0]
    par = box % 2
    par2 = box // 2 % 2
    scalars = jnp.stack([par, par2, face, box % 4]).astype(jnp.int32)
    sds = jax.ShapeDtypeStruct

    def box_permute(array, mask):
        return lax.ppermute(array, "box", [(b, b ^ mask) for b in range(n_box)])

    def keeper(b):
        return (b & 1) != (b >> 1 & 1)

    def giver(b):
        return not keeper(b)

    def face_permute(array, step, senders=None):
        pairs = [
            (b * n_face + f, b * n_face + (f + n_face - step) % n_face)
            for b in range(n_box) if senders is None or senders(b)
            for f in range(n_face)
        ]
        return lax.ppermute(array, ("box", "face"), pairs)

    def over_face(array, senders=None):
        return [face_permute(array, s, senders) for s in range(1, n_face)]

    skel_one = lax.dynamic_index_in_dim(skel_first[0], box // 2, 0, keepdims=True)
    skel_two = lax.dynamic_index_in_dim(skel_second[0], box // 4, 0, keepdims=True)

    in_hbm = pl.BlockSpec(memory_space=pltpu.HBM)

    def parts_kernel(sc, leaf_ref, end_out, side_out):
        p = sc[0]
        end_out[...] = leaf_ref[:, 1 - p, :, pl.ds(pl.multiple_of(p * k, k), k)]
        side_out[...] = leaf_ref[:, 1 - p, :, 2 * k :]

    end_own, sides_raw = call(parts_kernel, scalars, [leaf], [sds((2, fr, k), BF16)] * 2)
    end_sib = box_permute(end_own, 1)
    sides_sib = box_permute(sides_raw, 1)

    def slots_kernel(sc, leaf_ref, skel_ref, skel2_ref, comp_out, col_out, keep_out, send_out, end_out, rows_out):
        p, q = sc[0], sc[1]
        rows = lax.broadcasted_iota(jnp.int32, (k, k), 0)
        cols = lax.broadcasted_iota(jnp.int32, (k, k), 1)
        skel = jnp.broadcast_to(skel_ref[...].astype(F32), (k, k))
        column = jnp.sum(jnp.where(rows == cols, skel, 0.0), axis=1, keepdims=True)
        col_out[...] = column.astype(jnp.int32)
        place = skel2_ref[...] - q * k
        taken = jnp.where(rows == place, jnp.broadcast_to(column, (k, k)), 0.0)
        comp = jnp.sum(taken, axis=0, keepdims=True).astype(jnp.int32)
        mine = jnp.logical_and(place >= 0, place < k)
        comp = jnp.where(mine, comp, -1)
        comp_out[...] = comp
        rows_out[...] = leaf_ref[:, 2]
        pick_own = column_picker(comp, p * k, k)
        for t in range(2):
            end_out[t, :, : 2 * k] = leaf_ref[t, p, :, : 2 * k]
            end_out[t, :, 2 * k :] = dot(leaf_ref[t, p, :, 2 * k :], pick_own).astype(BF16)
        couple = pl.ds(pl.multiple_of((1 - p) * k, k), k)
        for ref, h in ((keep_out, p), (send_out, 1 - p)):
            take = pl.ds(pl.multiple_of(h * hr, hr), hr)
            ref[:, :, :k] = end_out[:, take, couple]
            ref[:, :, k:] = end_out[:, take, 2 * k :]

    comp, skel_col, v_keep, v_send, end_kept, s_rows = call(
        slots_kernel, scalars, [leaf, skel_one, skel_two],
        [sds((1, k), jnp.int32), sds((k, 1), jnp.int32), sds((2, hr, 2 * k), BF16), sds((2, hr, 2 * k), BF16),
         sds((2, fr, 3 * k), BF16), sds((2, fr, 3 * k), BF16)],
    )
    s_sib = box_permute(s_rows, 1)
    v_recv = box_permute(v_send, 1)

    def split_kernel(sc, own_ref, sib_ref, first_out, rest_out):
        p, q = sc[0], sc[1]
        rows = pl.ds(pl.multiple_of(p * hr, hr), hr)
        own, sib = own_ref[:, rows, :], sib_ref[:, rows, :]
        first_out[...] = jnp.where(p == q, own, sib)
        rest_out[...] = jnp.where(p == q, sib, own)

    first_send, rest_send = call(split_kernel, after(scalars, comp), [end_own, end_sib], [sds((2, hr, k), BF16)] * 2)
    first_far = over_face(first_send)
    first_fwd = [box_permute(a, 1) for a in first_far]

    def merge_kernel(sc, *refs):
        p = sc[0]
        mine = pl.ds(pl.multiple_of(p * hr, hr), hr)
        other = pl.ds(pl.multiple_of((1 - p) * hr, hr), hr)
        for s in range(nf):
            refs[2 * nf + s][:, mine, :] = refs[s][...]
            refs[2 * nf + s][:, other, :] = refs[nf + s][...]

    first_rows = call(
        merge_kernel, scalars, [*first_far, *first_fwd], [sds((2, fr, k), BF16)] * nf, cost=MERGE_COST
    )

    def side_kernel(sc, own_ref, sib_ref, comp_ref, side_out, half_out):
        p = sc[0]
        pick_own = column_picker(comp_ref[...], p * k, k)
        pick_sib = column_picker(comp_ref[...], (1 - p) * k, k)
        side = dot(flat(own_ref[...]), pick_own) + dot(flat(sib_ref[...]), pick_sib)
        side_out[...] = side.astype(BF16).reshape(2, fr, k)
        half_out[...] = side_out[:, pl.ds(pl.multiple_of(p * hr, hr), hr), :]

    side, side_half = call(
        side_kernel, after(scalars, first_send), [sides_raw, sides_sib, comp],
        [sds((2, fr, k), BF16), sds((2, hr, k), BF16)], cost=SLOTS_COST,
    )
    side_far = over_face(side_half)

    w_one = jnp.roll(w_first[:, 0], -face * fr, axis=2)
    w_one_sib = box_permute(w_one, 1)
    w_two = jnp.roll(w_second[:, 0], -face * fr, axis=2)
    w_two_x = box_permute(after(w_two, first_send), 2)

    def weight_one_kernel(sc, own_ref, sib_ref, out_ref):
        p = sc[0]
        out_ref[:, pl.ds(pl.multiple_of(p * half, half), half), :] = own_ref[...]
        out_ref[:, pl.ds(pl.multiple_of((1 - p) * half, half), half), :] = sib_ref[...]

    (weight_one,) = call(weight_one_kernel, scalars, [w_one, w_one_sib], [sds((2, k, k), BF16)])


    def rows_kernel(sc, own_ref, sib_ref, comp_ref, col_ref, rest_ref, kept_out, *outs):
        p, q, f = sc[0], sc[1], sc[2]
        pick_own = column_picker(comp_ref[...], p * k, k)
        pick_sib = column_picker(comp_ref[...], (1 - p) * k, k)

        def pick(slots, write):
            take_own = row_picker(slots, p * k + f * fr, fr)
            take_sib = row_picker(slots, (1 - p) * k + f * fr, fr)
            for t in range(2):
                for c in range(3):
                    cols = slice(c * k, (c + 1) * k)
                    own, sib = own_ref[t, :, cols], sib_ref[t, :, cols]
                    if c == 2:
                        own, sib = [dot(a, b).astype(BF16) for a, b in ((own, pick_own), (sib, pick_sib))]
                    write(t, c, (dot(take_own, own) + dot(take_sib, sib)).astype(BF16))

        for s in range(nf):
            outs[s][:, :, :k] = rest_ref[...]

        def write_far(s, t, c, picked):
            if c == 0:
                outs[s][t, :, k:] = picked
            else:
                outs[c * nf + s][t] = picked

        def col_half(s):
            start = (f + n_face - s - 1) % n_face * fr + p * hr
            return col_ref[pl.ds(pl.multiple_of(start, hr), hr), :]

        @pl.when(p == q)
        def _():
            far = jnp.concatenate([col_half(s) for s in range(nf)], axis=0)

            def write(t, c, picked):
                for s in range(nf):
                    write_far(s, t, c, picked[s * hr : (s + 1) * hr])

            pick(far, write)

        @pl.when(p != q)
        def _():
            far = jnp.concatenate([col_half(s) for s in range(nf)], axis=0)
            slots = jnp.concatenate([col_ref[pl.ds(pl.multiple_of(f * fr, fr), fr), :], far], axis=0)

            def write(t, c, picked):
                kept_out[t, :, c * k : (c + 1) * k] = picked[:fr]
                for s in range(nf):
                    write_far(s, t, c, picked[fr + s * hr : fr + (s + 1) * hr])

            pick(slots, write)

    kept, *kept_out = call(
        rows_kernel, scalars, [s_rows, s_sib, comp, skel_col, rest_send],
        [sds((2, fr, 3 * k), BF16)] + [sds((2, hr, 2 * k), BF16)] * nf + [sds((2, hr, k), BF16)] * (2 * nf),
    )

    def piece(hidden, start, count):
        return stacked(hidden[0][:, start : start + count], hidden[1][:, start : start + count])

    def iface_kernel(sc, keep_ref, recv_ref, w_ref, end_ref, endsib_ref, side_ref,
                     acc_out, hid_out, rows):
        p, q = sc[0], sc[1]

        @pl.when(p == q)
        def _():
            rows[...] = recv_ref[...]

        @pl.when(p != q)
        def _():
            rows[...] = keep_ref[...]

        both = dot(stacked(rows[0, :, :k], rows[1, :, :k]), flat(w_ref[...])).astype(BF16)
        hidden = both[:hr], both[hr:]
        hid_out[0] = hidden[0]
        hid_out[1] = hidden[1]
        left = piece(hidden, 0, fr)
        is_end = p == q
        ends = jnp.where(is_end, end_ref[...], endsib_ref[...])
        acc_out[:, :, :k] = -dot(left, flat(ends)).reshape(2, hr, k)
        acc_out[:, :, k:] = rows[:, :, k:].astype(F32) - dot(left, flat(side_ref[...])).reshape(2, hr, k)

    v_acc, v_hid = call(
        iface_kernel, scalars, [v_keep, v_recv, weight_one, end_own, end_sib, side],
        [sds((2, hr, 2 * k), F32), sds((2, hr, k), BF16)],
        scratch=[pltpu.VMEM((2, hr, 2 * k), BF16)],
    )
    w_two_pair = jnp.stack([w_two, w_two_x])
    w_two_sib = box_permute(w_two_pair, 1)

    def weight_two_kernel(sc, own_ref, sib_ref, out_ref):
        r = sc[3]
        blk = k // 4
        for i, (ref, part) in enumerate(((own_ref, 0), (own_ref, 1), (sib_ref, 0), (sib_ref, 1))):
            place = r ^ (part * 2) ^ (i // 2)
            out_ref[:, pl.ds(pl.multiple_of(place * blk, blk), blk), :] = ref[part]

    (weight_two,) = call(weight_two_kernel, scalars, [w_two_pair, w_two_sib], [sds((2, k, k), BF16)])

    side_fwd = [box_permute(after(a, kept, w_two_x, weight_one), 1) for a in side_far]
    mixed_far = [face_permute(a, i + 1) for i, a in enumerate(kept_out[:nf])]

    def iface_far_kernel(sc, acc_ref, hid_ref, *rest):
        refs = [rest[i * nf : (i + 1) * nf] for i in range(3)]
        end_out, keep_out, send_out, rows = rest[3 * nf :]
        p, q = sc[0], sc[1]
        mine = pl.ds(pl.multiple_of(p * hr, hr), hr)
        other = pl.ds(pl.multiple_of((1 - p) * hr, hr), hr)
        hidden = [hid_ref[0], hid_ref[1]]
        total = acc_ref[...]
        for s in range(nf):
            rows[:, mine, :] = refs[1][s][...]
            rows[:, other, :] = refs[2][s][...]
            left = piece(hidden, (s + 1) * fr, fr)
            far = jnp.concatenate([dot(left, flat(refs[0][s][...])), dot(left, flat(rows[...]))], axis=1)
            total = total - far.reshape(2, hr, 2 * k)
        total = total.astype(BF16)
        end_out[...] = total[:, :, :k]
        low, high = total[:, :, k : k + half], total[:, :, k + half :]
        keep_out[...] = jnp.where(q == 0, low, high)
        send_out[...] = jnp.where(q == 0, high, low)

    two_end, side_keep, side_send = call(
        iface_far_kernel, scalars, [v_acc, v_hid, *first_rows, *side_far, *side_fwd],
        [sds((2, hr, k), BF16)] + [sds((2, hr, half), BF16)] * 2, scratch=[pltpu.VMEM((2, fr, k), BF16)],
    )

    side_x = box_permute(side_send, 2)

    def pack_kernel(sc, end_ref, keep_ref, x_ref, out_ref):
        out_ref[:, :, :k] = end_ref[...]
        out_ref[:, :, k:] = keep_ref[...] + x_ref[...]

    (two_own,) = call(
        pack_kernel, scalars, [two_end, side_keep, side_x], [sds((2, hr, k + half), BF16)]
    )
    two_x = box_permute(two_own, 2)
    two_y = over_face(after(two_own, *mixed_far))
    mixed_fwd = [box_permute(after(a, two_own), 1) for a in mixed_far]

    def weighted(w_ref, rows, out_ref):
        left = jnp.concatenate([piece((w_ref[0], w_ref[1]), s * fr, fr) for s in range(n_face)], axis=1)
        for c in range(3):
            cols = slice(c * k, (c + 1) * k)
            right = rows[:, :, :, cols].reshape(n_face * 2 * fr, k)
            out_ref[:, :, cols] = dot(left, right).astype(BF16).reshape(2, k, k)

    def weighted_one_kernel(sc, w_ref, own_ref, sib_ref, side_ref, *rest):
        refs = [rest[i * nf : (i + 1) * nf] for i in range(5)]
        out_ref, rows = rest[5 * nf :]
        p, q = sc[0], sc[1]
        first_cols = pl.ds(pl.multiple_of(q * k, k), k)
        rest_cols = pl.ds(pl.multiple_of((1 - q) * k, k), k)
        own_cols = pl.ds(pl.multiple_of(p * k, k), k)
        sib_cols = pl.ds(pl.multiple_of((1 - p) * k, k), k)
        mine = pl.ds(pl.multiple_of(p * hr, hr), hr)
        other = pl.ds(pl.multiple_of((1 - p) * hr, hr), hr)
        rows[0, :, :, own_cols] = own_ref[...]
        rows[0, :, :, sib_cols] = sib_ref[...]
        rows[0, :, :, 2 * k :] = side_ref[...]
        for s in range(nf):
            rows[s + 1, :, :, first_cols] = refs[0][s][...]
            for h, take in enumerate((mine, other)):
                rows[s + 1, :, take, rest_cols] = refs[1 + h][s][:, :, :k]
                rows[s + 1, :, take, 2 * k :] = refs[3 + h][s][...]
        weighted(w_ref, rows, out_ref)

    (solved_one,) = call(
        weighted_one_kernel, scalars,
        [weight_one, end_own, end_sib, side, *first_rows, *mixed_far, *mixed_fwd, *side_far, *side_fwd],
        [sds((2, k, 3 * k), BF16)], scratch=[pltpu.VMEM((n_face, 2, fr, 3 * k), BF16)],
    )

    def join_kernel(sc, own_ref, x_ref, out_ref):
        q = sc[1]
        for ref, which in ((own_ref, q), (x_ref, 1 - q)):
            out_ref[:, :, pl.ds(pl.multiple_of(which * k, k), k)] = ref[:, :, :k]
            out_ref[:, :, pl.ds(pl.multiple_of(2 * k + which * half, half), half)] = ref[:, :, k:]

    two_shape = [sds((2, hr, 3 * k), BF16)]
    two_rows = call(join_kernel, after(scalars, solved_one), [two_own, two_x], two_shape, cost=JOIN_COST)
    two_xy = [box_permute(after(a, *two_rows), 2) for a in two_y]
    for own, other in zip(two_y, two_xy):
        two_rows += call(join_kernel, after(scalars, weight_two), [own, other], two_shape)
    two_sib = [box_permute(a, 1) for a in two_rows]

    ends_far = [face_permute(after(a, two_own), i + 1) for i, a in enumerate(kept_out[nf : 2 * nf])]
    ends_fwd = [box_permute(a, 1) for a in ends_far]
    slots_far = [face_permute(after(a, two_own), i + 1) for i, a in enumerate(kept_out[2 * nf :])]

    def whole_rows(sc, out_ref, cols, end_ref, kept_ref, far, fwd, source, place=slice(None)):
        p, q = sc[0], sc[1]

        @pl.when(p == q)
        def _():
            out_ref[:, :, place] = end_ref[:, :, cols]

        @pl.when(p != q)
        def _():
            for h, parts in enumerate((far, fwd)):
                take = pl.ds(pl.multiple_of((p ^ h) * hr, hr), hr)
                total = kept_ref[:, take, cols]
                for part in parts:
                    total = total + part[:, :, source]
                out_ref[:, take, place] = total

    def level_one_kernel(sc, end_ref, kept_ref, *refs):
        parts = [refs[i * nf : (i + 1) * nf] for i in range(4)]
        col_ref, one_ref, w_ref, hid_out, first_out, sub_out, zs = refs[4 * nf :]
        p, q, f = sc[0], sc[1], sc[2]
        whole_rows(sc, zs, slice(0, k), end_ref, kept_ref, parts[0], parts[1], slice(k, 2 * k), slice(0, k))
        whole_rows(sc, zs, slice(k, 2 * k), end_ref, kept_ref, parts[2], parts[3], slice(0, k), slice(k, 2 * k))
        slots = col_ref[pl.ds(pl.multiple_of(f * fr, fr), fr), :]
        right = jnp.where(slots >= k, 1, 0)
        right = jnp.where(p == q, p, right) > 0
        lefts = [zs[t, :, :k] for t in range(2)]
        rights = [zs[t, :, k:] for t in range(2)]
        left = stacked(*[jnp.where(right, a, b) for a, b in zip(lefts, rights)])
        nothing = jnp.zeros((fr, k), BF16)
        start = [
            jnp.concatenate([jnp.where(right, nothing, a) for a in lefts], axis=0),
            jnp.concatenate([jnp.where(right, a, nothing) for a in rights], axis=0),
        ]
        merged = [
            (start[c].astype(F32) - dot(left, flat(one_ref[:, :, c * k : (c + 1) * k]))).astype(BF16)
            for c in range(2)
        ]
        sub_out[...] = dot(left, flat(one_ref[:, :, 2 * k :]))
        is_left = q == 0
        first_out[...] = jnp.where(is_left, merged[0], merged[1])
        couple = jnp.where(is_left, merged[1], merged[0])
        second = dot(stacked(couple[:fr], couple[fr:]), flat(w_ref[...])).astype(BF16)
        for s in range(n_face):
            hid_out[s] = piece((second[:fr], second[fr:]), s * fr, fr)

    hid_two, first_two, sub_one = call(
        level_one_kernel, scalars,
        [end_kept, kept, *mixed_far, *mixed_fwd, *ends_far, *ends_fwd, skel_col, solved_one, weight_two],
        [sds((n_face, 2 * fr, 2 * fr), BF16), sds((2 * fr, k), BF16), sds((2 * fr, k), F32)],
        scratch=[pltpu.VMEM((2, fr, 2 * k), BF16)], cost=KEEP_COST,
    )

    slots_fwd = [box_permute(after(a, hid_two), 1) for a in slots_far]

    def level_two_kernel(sc, hid_ref, first_ref, *refs):
        out_ref, sub_out, rows, stage, sems = refs[2 * n_face :]
        p, q = sc[0], sc[1]
        left = jnp.concatenate([hid_ref[s] for s in range(n_face)], axis=1)
        for s in range(n_face):
            rows[s, :, pl.ds(pl.multiple_of(p * hr, hr), hr), :] = refs[s][...]
            rows[s, :, pl.ds(pl.multiple_of((1 - p) * hr, hr), hr), :] = refs[n_face + s][...]
        copies = []
        for c in range(2):
            first = jnp.where(q == c, first_ref[...], jnp.zeros((2 * fr, k), BF16)).astype(F32)
            right = rows[:, :, :, c * k : (c + 1) * k].reshape(n_face * 2 * fr, k)
            stage[c] = (first - dot(left, right)).astype(BF16).reshape(2, fr, k)
            copies.append(pltpu.make_async_copy(
                stage.at[c], out_ref.at[:, 0, :, pl.ds(c * k, k)], sems.at[c]
            ))
            copies[-1].start()
        sub_out[...] = dot(left, rows[:, :, :, 2 * k :].reshape(n_face * 2 * fr, k))
        for copy in copies:
            copy.wait()

    out, sub_two = call(
        level_two_kernel, scalars, [hid_two, first_two, *two_rows, *two_sib],
        [sds((2, 1, fr, 3 * k), BF16), sds((2 * fr, k), F32)],
        out_specs=[in_hbm, pl.BlockSpec(memory_space=pltpu.VMEM)],
        scratch=[pltpu.VMEM((n_face, 2, fr, 3 * k), BF16), pltpu.VMEM((2, 2, fr, k), BF16),
                 pltpu.SemaphoreType.DMA((2,))],
    )

    def slot_rows_kernel(sc, end_ref, kept_ref, *refs):
        whole_rows(sc, refs[2 * nf], slice(2 * k, 3 * k), end_ref, kept_ref, refs[:nf], refs[nf : 2 * nf], slice(0, k))

    (slot_rows,) = call(
        slot_rows_kernel, scalars, [end_kept, kept, *slots_far, *slots_fwd], [sds((2, fr, k), BF16)], cost=SLOT_ROWS_COST
    )

    def finish_kernel(sc, rows_ref, one_ref, two_ref, _, out_ref, stage, sem):
        merged = (flat(rows_ref[...]).astype(F32) - one_ref[...]).astype(BF16)
        stage[...] = (merged.astype(F32) - two_ref[...]).astype(BF16).reshape(2, fr, k)
        copy = pltpu.make_async_copy(stage, out_ref.at[:, 0, :, pl.ds(2 * k, k)], sem.at[0])
        copy.start()
        copy.wait()

    (out,) = call(
        finish_kernel, scalars, [slot_rows, sub_one, sub_two, out], [sds((2, 1, fr, 3 * k), BF16)],
        specs=[pl.BlockSpec(memory_space=pltpu.VMEM)] * 3 + [in_hbm], out_specs=[in_hbm],
        scratch=[pltpu.VMEM((2, fr, k), BF16), pltpu.SemaphoreType.DMA((1,))], aliases={4: 0},
    )
    return out


def solution(mesh):
    return jax.shard_map(
        on_device,
        mesh=mesh,
        in_specs=(
            P(None, None, "box", None, "face", None),
            P(None, None, "box", None),
            P(None, None, "box", None),
            P(),
            P(),
        ),
        out_specs=P(None, None, ("box", "face"), None),
        check_vma=False,
    )
```

```python
import functools

import jax
import jax.numpy as jnp
from jax import lax
from jax.experimental import pallas as pl
from jax.experimental.pallas import tpu as pltpu
from jax.sharding import PartitionSpec as P

BF16 = jnp.bfloat16
F32 = jnp.float32
VMEM_BYTES = 16 * 1024 * 1024
JOIN_COST = 300_000_000
ROWS_COST = 0
OWN_COST = 1_000_000_000
KEEP_COST = 6_000_000_000
SLOT_ROWS_COST = 2_000_000_000


def dot(first, second):
    return jnp.dot(first, second, preferred_element_type=F32)


def stacked(real, imag):
    return jnp.concatenate(
        [jnp.concatenate([real, -imag], axis=1), jnp.concatenate([imag, real], axis=1)], axis=0
    )


def flat(array):
    return array.reshape(array.shape[0] * array.shape[1], array.shape[2])


def column_picker(index, offset, count):
    rows = lax.broadcasted_iota(jnp.int32, (count, index.shape[1]), 0) + offset
    return jnp.where(rows == index, 1.0, 0.0).astype(BF16)


def row_picker(index, offset, count):
    cols = lax.broadcasted_iota(jnp.int32, (index.shape[0], count), 1) + offset
    return jnp.where(cols == index, 1.0, 0.0).astype(BF16)


def call(kernel, scalars, inputs, out_shapes, specs=None, out_specs=None, scratch=(), cost=0, aliases=None):
    in_vmem = pl.BlockSpec(memory_space=pltpu.VMEM)
    specs = specs or [in_vmem] * len(inputs)
    out_specs = out_specs or [in_vmem] * len(out_shapes)
    return pl.pallas_call(
        kernel,
        in_specs=[pl.BlockSpec(memory_space=pltpu.SMEM)] + specs,
        out_specs=out_specs,
        out_shape=out_shapes,
        scratch_shapes=list(scratch),
        input_output_aliases=aliases or {},
        compiler_params=pltpu.CompilerParams(vmem_limit_bytes=VMEM_BYTES),
        cost_estimate=pl.CostEstimate(flops=cost, bytes_accessed=0, transcendentals=0),
    )(scalars, *inputs)


def after(array, *others):
    return lax.optimization_barrier((array, *others))[0]


def on_device(leaf_maps, w_first, w_second, skel_first, skel_second):
    box = lax.axis_index("box")
    face = lax.axis_index("face")
    n_box, n_face = lax.axis_size("box"), lax.axis_size("face")
    nf = n_face - 1
    fr = leaf_maps.shape[4]
    hr = fr // 2
    k = leaf_maps.shape[5] // 3
    half = k // 2
    leaf = leaf_maps[:, 0, 0]
    scalars = jnp.stack([box % 2, box // 2 % 2, face, box % 4, box // 2, box // 4]).astype(jnp.int32)
    sds = jax.ShapeDtypeStruct
    in_hbm = pl.BlockSpec(memory_space=pltpu.HBM)

    def box_permute(array, mask):
        return lax.ppermute(array, "box", [(b, b ^ mask) for b in range(n_box)])

    def face_permute(array, step):
        pairs = [
            (b * n_face + f, b * n_face + (f + n_face - step) % n_face)
            for b in range(n_box) for f in range(n_face)
        ]
        return lax.ppermute(array, ("box", "face"), pairs)

    def over_face(array):
        return [face_permute(array, s) for s in range(1, n_face)]

    def halves(p):
        mine = pl.ds(pl.multiple_of(p * hr, hr), hr)
        other = pl.ds(pl.multiple_of((1 - p) * hr, hr), hr)
        return mine, other

    def slots_kernel(sc, skel_ref, skel2_ref, comp_out, col_out):
        q = sc[1]
        rows = lax.broadcasted_iota(jnp.int32, (k, k), 0)
        cols = lax.broadcasted_iota(jnp.int32, (k, k), 1)
        skel = jnp.broadcast_to(skel_ref[pl.ds(sc[4], 1), :].astype(F32), (k, k))
        column = jnp.sum(jnp.where(rows == cols, skel, 0.0), axis=1, keepdims=True)
        col_out[...] = column.astype(jnp.int32)
        place = skel2_ref[pl.ds(sc[5], 1), :] - q * k
        taken = jnp.where(rows == place, jnp.broadcast_to(column, (k, k)), 0.0)
        found = jnp.sum(taken, axis=0, keepdims=True).astype(jnp.int32)
        comp_out[...] = jnp.where(jnp.logical_and(place >= 0, place < k), found, -1)

    comp, skel_col = call(
        slots_kernel, scalars, [skel_first[0], skel_second[0]], [sds((1, k), jnp.int32), sds((k, 1), jnp.int32)]
    )

    def parts_kernel(sc, leaf_ref, end_out, side_out, *rows_outs):
        p = sc[0]
        end_out[...] = leaf_ref[:, 1 - p, :, pl.ds(pl.multiple_of(p * k, k), k)]
        side_out[...] = leaf_ref[:, 1 - p, :, 2 * k :]
        for i, rows_out in enumerate(rows_outs):
            rows_out[...] = leaf_ref[:, 2, i % 2 * hr : (i % 2 + 1) * hr, i // 2 * k : (i // 2 + 1) * k]

    end_own, sides_raw, *s_rows = call(
        parts_kernel, scalars, [leaf], [sds((2, fr, k), BF16)] * 2 + [sds((2, hr, k), BF16)] * 6
    )
    sides_sib = box_permute(sides_raw, 1)
    end_sib = box_permute(end_own, 1)
    s_sib = [box_permute(a, 1) for a in s_rows]

    def side_kernel(sc, own_ref, sib_ref, comp_ref, end_ref, side_out, send_out):
        p, q = sc[0], sc[1]
        pick_own = column_picker(comp_ref[...], p * k, k)
        pick_sib = column_picker(comp_ref[...], (1 - p) * k, k)
        side = dot(flat(own_ref[...]), pick_own) + dot(flat(sib_ref[...]), pick_sib)
        side_out[...] = side.astype(BF16).reshape(2, fr, k)
        send_out[...] = jnp.where(p == q, end_ref[...], side_out[...])

    side, first_send = call(
        side_kernel, scalars, [sides_raw, sides_sib, comp, end_own], [sds((2, fr, k), BF16)] * 2
    )
    first_far = over_face(first_send)

    def ends_kernel(sc, leaf_ref, comp_ref, keep_out, send_out, end_out):
        p = sc[0]
        pick_own = column_picker(comp_ref[...], p * k, k)
        for t in range(2):
            end_out[t, :, : 2 * k] = leaf_ref[t, p, :, : 2 * k]
            end_out[t, :, 2 * k :] = dot(leaf_ref[t, p, :, 2 * k :], pick_own).astype(BF16)
        couple = pl.ds(pl.multiple_of((1 - p) * k, k), k)
        for ref, take in zip((keep_out, send_out), halves(p)):
            ref[:, :, :k] = end_out[:, take, couple]
            ref[:, :, k:] = end_out[:, take, 2 * k :]

    v_keep, v_send, end_kept = call(
        ends_kernel, after(scalars, side), [leaf, comp],
        [sds((2, hr, 2 * k), BF16)] * 2 + [sds((2, fr, 3 * k), BF16)],
    )
    v_recv = box_permute(v_send, 1)

    w_one, w_two = w_first[:, 0], w_second[:, 0]
    w_one_sib = box_permute(after(w_one, side), 1)
    w_two_x = box_permute(after(w_two, side), 2)
    w_two_sib = box_permute(after(w_two, side), 1)
    w_two_x_sib = box_permute(w_two_x, 1)

    def weight_kernel(place, sc, *refs):
        out_ref = refs[-1]
        count = refs[0].shape[1]
        for i, ref in enumerate(refs[:-1]):
            take = pl.ds(pl.multiple_of(place(sc, i) * count, count), count)
            for f in range(n_face):
                @pl.when(sc[2] == f)
                def _(ref=ref, take=take, f=f):
                    out_ref[:, take, : k - f * fr] = ref[:, :, f * fr :]
                    if f > 0:
                        out_ref[:, take, k - f * fr :] = ref[:, :, : f * fr]

    (weight_one,) = call(
        functools.partial(weight_kernel, lambda sc, i: sc[0] ^ i), scalars, [w_one, w_one_sib],
        [sds((2, k, k), BF16)],
    )
    (weight_two,) = call(
        functools.partial(weight_kernel, lambda sc, i: sc[3] ^ (0, 2, 1, 3)[i]), scalars,
        [w_two, w_two_x, w_two_sib, w_two_x_sib], [sds((2, k, k), BF16)],
    )

    def rows_kernel(sc, *refs):
        owns, sibs, refs = refs[:6], refs[6:12], refs[12:]
        comp_ref, col_ref, end_ref, endsib_ref, rest_out, kept_out, *outs = refs
        p, q, f = sc[0], sc[1], sc[2]
        mine, _ = halves(p)
        rest_out[...] = jnp.where(p == q, endsib_ref[:, mine, :], end_ref[:, mine, :])
        pick_own = column_picker(comp_ref[...], p * k, k)
        pick_sib = column_picker(comp_ref[...], (1 - p) * k, k)

        def pick(slots, write):
            take_own = row_picker(slots, p * k + f * fr, fr)
            take_sib = row_picker(slots, (1 - p) * k + f * fr, fr)
            for t in range(2):
                for c in range(3):
                    own, sib = [
                        jnp.concatenate([a[2 * c][t], a[2 * c + 1][t]], axis=0) for a in (owns, sibs)
                    ]
                    if c == 2:
                        own, sib = [dot(a, b).astype(BF16) for a, b in ((own, pick_own), (sib, pick_sib))]
                    write(t, c, (dot(take_own, own) + dot(take_sib, sib)).astype(BF16))

        def write_far(s, t, c, picked):
            if c < 2:
                outs[s][t, :, c * k : (c + 1) * k] = picked
            else:
                outs[nf + s][t] = picked

        def col_half(s):
            start = (f + n_face - s - 1) % n_face * fr + p * hr
            return col_ref[pl.ds(pl.multiple_of(start, hr), hr), :]

        far = jnp.concatenate([col_half(s) for s in range(nf)], axis=0)

        @pl.when(p == q)
        def _():
            def write(t, c, picked):
                for s in range(nf):
                    write_far(s, t, c, picked[s * hr : (s + 1) * hr])

            pick(far, write)

        @pl.when(p != q)
        def _():
            def write(t, c, picked):
                kept_out[t, :, c * k : (c + 1) * k] = picked[:fr]
                for s in range(nf):
                    write_far(s, t, c, picked[fr + s * hr : fr + (s + 1) * hr])

            pick(jnp.concatenate([col_ref[pl.ds(pl.multiple_of(f * fr, fr), fr), :], far], axis=0), write)

    rest_send, kept, *kept_out = call(
        rows_kernel, scalars, [*s_rows, *s_sib, comp, skel_col, end_own, end_sib],
        [sds((2, hr, k), BF16), sds((2, fr, 3 * k), BF16)] + [sds((2, hr, 2 * k), BF16)] * nf
        + [sds((2, hr, k), BF16)] * nf, cost=ROWS_COST,
    )
    rest_far = over_face(rest_send)

    def piece(hidden, start, count):
        return stacked(hidden[0][:, start : start + count], hidden[1][:, start : start + count])

    def iface_kernel(sc, keep_ref, recv_ref, w_ref, end_ref, endsib_ref, side_ref,
                     acc_out, hid_out, rows):
        p, q = sc[0], sc[1]

        @pl.when(p == q)
        def _():
            rows[...] = recv_ref[...]

        @pl.when(p != q)
        def _():
            rows[...] = keep_ref[...]

        both = dot(stacked(rows[0, :, :k], rows[1, :, :k]), flat(w_ref[...])).astype(BF16)
        hidden = both[:hr], both[hr:]
        hid_out[0] = hidden[0]
        hid_out[1] = hidden[1]
        left = piece(hidden, 0, fr)
        is_end = p == q
        ends = jnp.where(is_end, end_ref[...], endsib_ref[...])
        acc_out[:, :, :k] = -dot(left, flat(ends)).reshape(2, hr, k)
        acc_out[:, :, k:] = rows[:, :, k:].astype(F32) - dot(left, flat(side_ref[...])).reshape(2, hr, k)

    v_acc, v_hid = call(
        iface_kernel, scalars, [v_keep, v_recv, weight_one, end_own, end_sib, side],
        [sds((2, hr, 2 * k), F32), sds((2, hr, k), BF16)],
        scratch=[pltpu.VMEM((2, hr, 2 * k), BF16)], cost=OWN_COST,
    )
    first_fwd = [box_permute(after(a, kept, w_two_x), 1) for a in first_far]

    def iface_far_kernel(sc, acc_ref, hid_ref, *rest):
        far, fwd, out_ref = rest[:nf], rest[nf : 2 * nf], rest[2 * nf]
        is_end = sc[0] == sc[1]
        hidden = [hid_ref[0], hid_ref[1]]
        total = acc_ref[...]
        for s in range(nf):
            left = piece(hidden, (s + 1) * fr, fr)
            mine, other = dot(left, flat(far[s][...])), dot(left, flat(fwd[s][...]))
            both = [jnp.where(is_end, mine, other), jnp.where(is_end, other, mine)]
            total = total - jnp.concatenate(both, axis=1).reshape(2, hr, 2 * k)
        out_ref[...] = total.astype(BF16)

    (two_own,) = call(
        iface_far_kernel, scalars, [v_acc, v_hid, *first_far, *first_fwd], [sds((2, hr, 2 * k), BF16)],
    )

    two_x = box_permute(two_own, 2)
    two_y = over_face(after(two_own, *rest_far))
    rest_fwd = [box_permute(after(a, two_own), 1) for a in rest_far]

    def weighted(w_ref, rows, out_ref):
        left = jnp.concatenate([piece((w_ref[0], w_ref[1]), s * fr, fr) for s in range(n_face)], axis=1)
        for c in range(3):
            cols = slice(c * k, (c + 1) * k)
            right = rows[:, :, :, cols].reshape(n_face * 2 * fr, k)
            out_ref[:, :, cols] = dot(left, right).astype(BF16).reshape(2, k, k)

    def weighted_one_kernel(sc, w_ref, own_ref, sib_ref, side_ref, *rest):
        refs = [rest[i * nf : (i + 1) * nf] for i in range(4)]
        out_ref, rows = rest[4 * nf :]
        p, q = sc[0], sc[1]
        is_end = p == q
        first_cols = pl.ds(pl.multiple_of(q * k, k), k)
        rest_cols = pl.ds(pl.multiple_of((1 - q) * k, k), k)
        rows[0, :, :, pl.ds(pl.multiple_of(p * k, k), k)] = own_ref[...]
        rows[0, :, :, pl.ds(pl.multiple_of((1 - p) * k, k), k)] = sib_ref[...]
        rows[0, :, :, 2 * k :] = side_ref[...]
        for s in range(nf):
            mine, other = refs[0][s][...], refs[1][s][...]
            rows[s + 1, :, :, first_cols] = jnp.where(is_end, mine, other)
            rows[s + 1, :, :, 2 * k :] = jnp.where(is_end, other, mine)
            for take, parts in zip(halves(p), refs[2:]):
                rows[s + 1, :, take, rest_cols] = parts[s][...]
        weighted(w_ref, rows, out_ref)

    (solved_one,) = call(
        weighted_one_kernel, scalars,
        [weight_one, end_own, end_sib, side, *first_far, *first_fwd, *rest_far, *rest_fwd],
        [sds((2, k, 3 * k), BF16)], scratch=[pltpu.VMEM((n_face, 2, fr, 3 * k), BF16)],
    )

    def join_kernel(sc, own_ref, x_ref, out_ref):
        q = sc[1]
        out_ref[:, :, pl.ds(pl.multiple_of(q * k, k), k)] = own_ref[:, :, :k]
        out_ref[:, :, pl.ds(pl.multiple_of((1 - q) * k, k), k)] = x_ref[:, :, :k]
        out_ref[:, :, 2 * k :] = own_ref[:, :, k:] + x_ref[:, :, k:]

    two_shape = [sds((2, hr, 3 * k), BF16)]
    two_rows = call(join_kernel, after(scalars, solved_one), [two_own, two_x], two_shape, cost=JOIN_COST)
    two_xy = [box_permute(after(a, *two_rows), 2) for a in two_y]
    for own, other in zip(two_y, two_xy):
        two_rows += call(join_kernel, after(scalars, weight_two), [own, other], two_shape)
    two_sib = [box_permute(a, 1) for a in two_rows]

    ends_far = [face_permute(after(a, two_own), i + 1) for i, a in enumerate(kept_out[:nf])]
    ends_fwd = [box_permute(a, 1) for a in ends_far]
    slots_far = [face_permute(after(a, two_own), i + 1) for i, a in enumerate(kept_out[nf:])]

    def whole_rows(sc, out_ref, cols, end_ref, kept_ref, far, fwd):
        p, q = sc[0], sc[1]

        @pl.when(p == q)
        def _():
            out_ref[...] = end_ref[:, :, cols]

        @pl.when(p != q)
        def _():
            for h, parts in enumerate((far, fwd)):
                take = pl.ds(pl.multiple_of((p ^ h) * hr, hr), hr)
                total = kept_ref[:, take, cols]
                for part in parts:
                    total = total + part[...]
                out_ref[:, take, :] = total

    def level_one_kernel(sc, end_ref, kept_ref, *refs):
        far, fwd = refs[:nf], refs[nf : 2 * nf]
        col_ref, one_ref, w_ref, hid_out, first_out, sub_out, zs = refs[2 * nf :]
        p, q, f = sc[0], sc[1], sc[2]
        whole_rows(sc, zs, slice(0, 2 * k), end_ref, kept_ref, far, fwd)
        slots = col_ref[pl.ds(pl.multiple_of(f * fr, fr), fr), :]
        right = jnp.where(slots >= k, 1, 0)
        right = jnp.where(p == q, p, right) > 0
        lefts = [zs[t, :, :k] for t in range(2)]
        rights = [zs[t, :, k:] for t in range(2)]
        left = stacked(*[jnp.where(right, a, b) for a, b in zip(lefts, rights)])
        nothing = jnp.zeros((fr, k), BF16)
        start = [
            jnp.concatenate([jnp.where(right, nothing, a) for a in lefts], axis=0),
            jnp.concatenate([jnp.where(right, a, nothing) for a in rights], axis=0),
        ]
        merged = [
            (start[c].astype(F32) - dot(left, flat(one_ref[:, :, c * k : (c + 1) * k]))).astype(BF16)
            for c in range(2)
        ]
        sub_out[...] = dot(left, flat(one_ref[:, :, 2 * k :]))
        is_left = q == 0
        first_out[...] = jnp.where(is_left, merged[0], merged[1])
        couple = jnp.where(is_left, merged[1], merged[0])
        second = dot(stacked(couple[:fr], couple[fr:]), flat(w_ref[...])).astype(BF16)
        for s in range(n_face):
            hid_out[s] = piece((second[:fr], second[fr:]), s * fr, fr)

    hid_two, first_two, sub_one = call(
        level_one_kernel, scalars,
        [end_kept, kept, *ends_far, *ends_fwd, skel_col, solved_one, weight_two],
        [sds((n_face, 2 * fr, 2 * fr), BF16), sds((2 * fr, k), BF16), sds((2 * fr, k), F32)],
        scratch=[pltpu.VMEM((2, fr, 2 * k), BF16)], cost=KEEP_COST,
    )

    slots_fwd = [box_permute(after(a, hid_two), 1) for a in slots_far]

    def level_two_kernel(sc, hid_ref, first_ref, *refs):
        out_ref, sub_out, rows, stage, sems = refs[2 * n_face :]
        p, q = sc[0], sc[1]
        left = jnp.concatenate([hid_ref[s] for s in range(n_face)], axis=1)
        for s in range(n_face):
            rows[s, :, pl.ds(pl.multiple_of(p * hr, hr), hr), :] = refs[s][...]
            rows[s, :, pl.ds(pl.multiple_of((1 - p) * hr, hr), hr), :] = refs[n_face + s][...]
        copies = []
        for c in range(2):
            first = jnp.where(q == c, first_ref[...], jnp.zeros((2 * fr, k), BF16)).astype(F32)
            right = rows[:, :, :, c * k : (c + 1) * k].reshape(n_face * 2 * fr, k)
            stage[c] = (first - dot(left, right)).astype(BF16).reshape(2, fr, k)
            copies.append(pltpu.make_async_copy(
                stage.at[c], out_ref.at[:, 0, :, pl.ds(c * k, k)], sems.at[c]
            ))
            copies[-1].start()
        sub_out[...] = dot(left, rows[:, :, :, 2 * k :].reshape(n_face * 2 * fr, k))
        for copy in copies:
            copy.wait()

    out, sub_two = call(
        level_two_kernel, scalars, [hid_two, first_two, *two_rows, *two_sib],
        [sds((2, 1, fr, 3 * k), BF16), sds((2 * fr, k), F32)],
        out_specs=[in_hbm, pl.BlockSpec(memory_space=pltpu.VMEM)],
        scratch=[pltpu.VMEM((n_face, 2, fr, 3 * k), BF16), pltpu.VMEM((2, 2, fr, k), BF16),
                 pltpu.SemaphoreType.DMA((2,))],
    )

    def slot_rows_kernel(sc, end_ref, kept_ref, *refs):
        whole_rows(sc, refs[2 * nf], slice(2 * k, 3 * k), end_ref, kept_ref, refs[:nf], refs[nf : 2 * nf])

    (slot_rows,) = call(
        slot_rows_kernel, scalars, [end_kept, kept, *slots_far, *slots_fwd], [sds((2, fr, k), BF16)], cost=SLOT_ROWS_COST
    )

    def finish_kernel(sc, rows_ref, one_ref, two_ref, _, out_ref, stage, sem):
        merged = (flat(rows_ref[...]).astype(F32) - one_ref[...]).astype(BF16)
        stage[...] = (merged.astype(F32) - two_ref[...]).astype(BF16).reshape(2, fr, k)
        copy = pltpu.make_async_copy(stage, out_ref.at[:, 0, :, pl.ds(2 * k, k)], sem.at[0])
        copy.start()
        copy.wait()

    (out,) = call(
        finish_kernel, scalars, [slot_rows, sub_one, sub_two, out], [sds((2, 1, fr, 3 * k), BF16)],
        specs=[pl.BlockSpec(memory_space=pltpu.VMEM)] * 3 + [in_hbm], out_specs=[in_hbm],
        scratch=[pltpu.VMEM((2, fr, k), BF16), pltpu.SemaphoreType.DMA((1,))], aliases={4: 0},
    )
    return out


def solution(mesh):
    return jax.shard_map(
        on_device,
        mesh=mesh,
        in_specs=(
            P(None, None, "box", None, "face", None),
            P(None, None, "box", None),
            P(None, None, "box", None),
            P(),
            P(),
        ),
        out_specs=P(None, None, ("box", "face"), None),
        check_vma=False,
    )
```

```python
import functools

import jax
import jax.numpy as jnp
from jax import lax
from jax.experimental import pallas as pl
from jax.experimental.pallas import tpu as pltpu
from jax.sharding import PartitionSpec as P

BF16 = jnp.bfloat16
F32 = jnp.float32
VMEM_BYTES = 16 * 1024 * 1024
JOIN_COST = 300000000
OWN_COST = 1_000_000_000
KEEP_COST = 2000000000


def dot(first, second):
    return jnp.dot(first, second, preferred_element_type=F32)


def stacked(real, imag):
    return jnp.concatenate(
        [jnp.concatenate([real, -imag], axis=1), jnp.concatenate([imag, real], axis=1)], axis=0
    )


def flat(array):
    return array.reshape(array.shape[0] * array.shape[1], array.shape[2])


def column_picker(index, offset, count):
    rows = lax.broadcasted_iota(jnp.int32, (count, index.shape[1]), 0) + offset
    return jnp.where(rows == index, 1.0, 0.0).astype(BF16)


def row_picker(index, offset, count):
    cols = lax.broadcasted_iota(jnp.int32, (index.shape[0], count), 1) + offset
    return jnp.where(cols == index, 1.0, 0.0).astype(BF16)


def call(kernel, scalars, inputs, out_shapes, specs=None, out_specs=None, scratch=(), cost=0, aliases=None):
    in_vmem = pl.BlockSpec(memory_space=pltpu.VMEM)
    specs = specs or [in_vmem] * len(inputs)
    out_specs = out_specs or [in_vmem] * len(out_shapes)
    return pl.pallas_call(
        kernel,
        in_specs=[pl.BlockSpec(memory_space=pltpu.SMEM)] + specs,
        out_specs=out_specs,
        out_shape=out_shapes,
        scratch_shapes=list(scratch),
        input_output_aliases=aliases or {},
        compiler_params=pltpu.CompilerParams(vmem_limit_bytes=VMEM_BYTES),
        cost_estimate=pl.CostEstimate(flops=cost, bytes_accessed=0, transcendentals=0),
    )(scalars, *inputs)


def after(array, *others):
    return lax.optimization_barrier((array, *others))[0]


def on_device(leaf_maps, w_first, w_second, skel_first, skel_second):
    box = lax.axis_index("box")
    face = lax.axis_index("face")
    n_box, n_face = lax.axis_size("box"), lax.axis_size("face")
    nf = n_face - 1
    fr = leaf_maps.shape[4]
    hr = fr // 2
    k = leaf_maps.shape[5] // 3
    half = k // 2
    leaf = leaf_maps[:, 0, 0]
    scalars = jnp.stack([box % 2, box // 2 % 2, face, box % 4, box // 2, box // 4]).astype(jnp.int32)
    sds = jax.ShapeDtypeStruct
    in_hbm = pl.BlockSpec(memory_space=pltpu.HBM)

    def box_permute(array, mask):
        return lax.ppermute(array, "box", [(b, b ^ mask) for b in range(n_box)])

    def face_permute(array, step):
        pairs = [
            (b * n_face + f, b * n_face + (f + n_face - step) % n_face)
            for b in range(n_box) for f in range(n_face)
        ]
        return lax.ppermute(array, ("box", "face"), pairs)

    def over_face(array):
        return [face_permute(array, s) for s in range(1, n_face)]

    def halves(p):
        mine = pl.ds(pl.multiple_of(p * hr, hr), hr)
        other = pl.ds(pl.multiple_of((1 - p) * hr, hr), hr)
        return mine, other

    def slots_kernel(sc, skel_ref, skel2_ref, comp_out, col_out):
        q = sc[1]
        rows = lax.broadcasted_iota(jnp.int32, (k, k), 0)
        cols = lax.broadcasted_iota(jnp.int32, (k, k), 1)
        skel = jnp.broadcast_to(skel_ref[pl.ds(sc[4], 1), :].astype(F32), (k, k))
        column = jnp.sum(jnp.where(rows == cols, skel, 0.0), axis=1, keepdims=True)
        col_out[...] = column.astype(jnp.int32)
        place = skel2_ref[pl.ds(sc[5], 1), :] - q * k
        taken = jnp.where(rows == place, jnp.broadcast_to(column, (k, k)), 0.0)
        found = jnp.sum(taken, axis=0, keepdims=True).astype(jnp.int32)
        comp_out[...] = jnp.where(jnp.logical_and(place >= 0, place < k), found, -1)

    comp, skel_col = call(
        slots_kernel, scalars, [skel_first[0], skel_second[0]], [sds((1, k), jnp.int32), sds((k, 1), jnp.int32)]
    )

    def parts_kernel(sc, leaf_ref, end_out, side_out, *rows_outs):
        p = sc[0]
        end_out[...] = leaf_ref[:, 1 - p, :, pl.ds(pl.multiple_of(p * k, k), k)]
        side_out[...] = leaf_ref[:, 1 - p, :, 2 * k :]
        for i, rows_out in enumerate(rows_outs):
            rows_out[...] = leaf_ref[:, 2, i % 2 * hr : (i % 2 + 1) * hr, i // 2 * k : (i // 2 + 1) * k]

    end_own, sides_raw, *s_rows = call(
        parts_kernel, scalars, [leaf], [sds((2, fr, k), BF16)] * 2 + [sds((2, hr, k), BF16)] * 6
    )
    sides_sib = box_permute(sides_raw, 1)
    end_sib = box_permute(end_own, 1)
    s_sib = [box_permute(a, 1) for a in s_rows]

    def side_kernel(sc, own_ref, sib_ref, comp_ref, end_ref, side_out, send_out):
        p, q = sc[0], sc[1]
        pick_own = column_picker(comp_ref[...], p * k, k)
        pick_sib = column_picker(comp_ref[...], (1 - p) * k, k)
        side = dot(flat(own_ref[...]), pick_own) + dot(flat(sib_ref[...]), pick_sib)
        side_out[...] = side.astype(BF16).reshape(2, fr, k)
        send_out[...] = jnp.where(p == q, end_ref[...], side_out[...])

    side, first_send = call(
        side_kernel, scalars, [sides_raw, sides_sib, comp, end_own], [sds((2, fr, k), BF16)] * 2
    )
    first_far = over_face(first_send)

    def ends_kernel(sc, leaf_ref, comp_ref, keep_out, send_out, end_out):
        p = sc[0]
        pick_own = column_picker(comp_ref[...], p * k, k)
        for t in range(2):
            end_out[t, :, : 2 * k] = leaf_ref[t, p, :, : 2 * k]
            end_out[t, :, 2 * k :] = dot(leaf_ref[t, p, :, 2 * k :], pick_own).astype(BF16)
        couple = pl.ds(pl.multiple_of((1 - p) * k, k), k)
        for ref, take in zip((keep_out, send_out), halves(p)):
            ref[:, :, :k] = end_out[:, take, couple]
            ref[:, :, k:] = end_out[:, take, 2 * k :]

    v_keep, v_send, end_kept = call(
        ends_kernel, after(scalars, side), [leaf, comp],
        [sds((2, hr, 2 * k), BF16)] * 2 + [sds((2, fr, 3 * k), BF16)],
    )
    v_recv = box_permute(v_send, 1)

    w_one, w_two = w_first[:, 0], w_second[:, 0]
    w_one_sib = box_permute(after(w_one, side), 1)
    w_two_x = box_permute(after(w_two, side), 2)
    w_two_sib = box_permute(after(w_two, side), 1)
    w_two_x_sib = box_permute(w_two_x, 1)

    def weight_kernel(place, sc, *refs):
        out_ref = refs[-1]
        count = refs[0].shape[1]
        for i, ref in enumerate(refs[:-1]):
            take = pl.ds(pl.multiple_of(place(sc, i) * count, count), count)
            for f in range(n_face):
                @pl.when(sc[2] == f)
                def _(ref=ref, take=take, f=f):
                    out_ref[:, take, : k - f * fr] = ref[:, :, f * fr :]
                    if f > 0:
                        out_ref[:, take, k - f * fr :] = ref[:, :, : f * fr]

    (weight_one,) = call(
        functools.partial(weight_kernel, lambda sc, i: sc[0] ^ i), scalars, [w_one, w_one_sib],
        [sds((2, k, k), BF16)],
    )
    (weight_two,) = call(
        functools.partial(weight_kernel, lambda sc, i: sc[3] ^ (0, 2, 1, 3)[i]), scalars,
        [w_two, w_two_x, w_two_sib, w_two_x_sib], [sds((2, k, k), BF16)],
    )

    def rows_kernel(sc, *refs):
        owns, sibs, refs = refs[:6], refs[6:12], refs[12:]
        comp_ref, col_ref, end_ref, endsib_ref, rest_out, kept_out, *outs = refs
        p, q, f = sc[0], sc[1], sc[2]
        mine, _ = halves(p)
        rest_out[...] = jnp.where(p == q, endsib_ref[:, mine, :], end_ref[:, mine, :])
        pick_own = column_picker(comp_ref[...], p * k, k)
        pick_sib = column_picker(comp_ref[...], (1 - p) * k, k)

        def pick(slots, write):
            take_own = row_picker(slots, p * k + f * fr, fr)
            take_sib = row_picker(slots, (1 - p) * k + f * fr, fr)
            for t in range(2):
                for c in range(3):
                    own, sib = [
                        jnp.concatenate([a[2 * c][t], a[2 * c + 1][t]], axis=0) for a in (owns, sibs)
                    ]
                    if c == 2:
                        own, sib = [dot(a, b).astype(BF16) for a, b in ((own, pick_own), (sib, pick_sib))]
                    write(t, c, (dot(take_own, own) + dot(take_sib, sib)).astype(BF16))

        def write_far(s, t, c, picked):
            if c < 2:
                outs[s][t, :, c * k : (c + 1) * k] = picked
            else:
                outs[nf + s][t] = picked

        def col_half(s):
            start = (f + n_face - s - 1) % n_face * fr + p * hr
            return col_ref[pl.ds(pl.multiple_of(start, hr), hr), :]

        far = jnp.concatenate([col_half(s) for s in range(nf)], axis=0)

        @pl.when(p == q)
        def _():
            def write(t, c, picked):
                for s in range(nf):
                    write_far(s, t, c, picked[s * hr : (s + 1) * hr])

            pick(far, write)

        @pl.when(p != q)
        def _():
            def write(t, c, picked):
                kept_out[t, :, c * k : (c + 1) * k] = picked[:fr]
                for s in range(nf):
                    write_far(s, t, c, picked[fr + s * hr : fr + (s + 1) * hr])

            pick(jnp.concatenate([col_ref[pl.ds(pl.multiple_of(f * fr, fr), fr), :], far], axis=0), write)

    rest_send, kept, *kept_out = call(
        rows_kernel, scalars, [*s_rows, *s_sib, comp, skel_col, end_own, end_sib],
        [sds((2, hr, k), BF16), sds((2, fr, 3 * k), BF16)] + [sds((2, hr, 2 * k), BF16)] * nf
        + [sds((2, hr, k), BF16)] * nf,
    )
    rest_far = over_face(rest_send)

    def piece(hidden, start, count):
        return stacked(hidden[0][:, start : start + count], hidden[1][:, start : start + count])

    def iface_kernel(sc, keep_ref, recv_ref, w_ref, end_ref, endsib_ref, side_ref,
                     acc_out, hid_out, rows):
        p, q = sc[0], sc[1]

        @pl.when(p == q)
        def _():
            rows[...] = recv_ref[...]

        @pl.when(p != q)
        def _():
            rows[...] = keep_ref[...]

        both = dot(stacked(rows[0, :, :k], rows[1, :, :k]), flat(w_ref[...])).astype(BF16)
        hidden = both[:hr], both[hr:]
        hid_out[0] = hidden[0]
        hid_out[1] = hidden[1]
        left = piece(hidden, 0, fr)
        is_end = p == q
        ends = jnp.where(is_end, end_ref[...], endsib_ref[...])
        acc_out[:, :, :k] = -dot(left, flat(ends)).reshape(2, hr, k)
        acc_out[:, :, k:] = rows[:, :, k:].astype(F32) - dot(left, flat(side_ref[...])).reshape(2, hr, k)

    v_acc, v_hid = call(
        iface_kernel, scalars, [v_keep, v_recv, weight_one, end_own, end_sib, side],
        [sds((2, hr, 2 * k), F32), sds((2, hr, k), BF16)],
        scratch=[pltpu.VMEM((2, hr, 2 * k), BF16)], cost=OWN_COST,
    )
    first_fwd = [box_permute(after(a, kept, w_two_x), 1) for a in first_far]

    def iface_far_kernel(sc, acc_ref, hid_ref, *rest):
        far, fwd, out_ref = rest[:nf], rest[nf : 2 * nf], rest[2 * nf]
        is_end = sc[0] == sc[1]
        hidden = [hid_ref[0], hid_ref[1]]
        total = acc_ref[...]
        for s in range(nf):
            left = piece(hidden, (s + 1) * fr, fr)
            mine, other = dot(left, flat(far[s][...])), dot(left, flat(fwd[s][...]))
            both = [jnp.where(is_end, mine, other), jnp.where(is_end, other, mine)]
            total = total - jnp.concatenate(both, axis=1).reshape(2, hr, 2 * k)
        out_ref[...] = total.astype(BF16)

    (two_own,) = call(
        iface_far_kernel, scalars, [v_acc, v_hid, *first_far, *first_fwd], [sds((2, hr, 2 * k), BF16)],
    )

    two_x = box_permute(two_own, 2)
    two_y = over_face(two_own)
    rest_fwd = [box_permute(after(a, two_own), 1) for a in rest_far]

    def weighted(w_ref, rows, out_ref):
        left = jnp.concatenate([piece((w_ref[0], w_ref[1]), s * fr, fr) for s in range(n_face)], axis=1)
        for c in range(3):
            cols = slice(c * k, (c + 1) * k)
            right = rows[:, :, :, cols].reshape(n_face * 2 * fr, k)
            out_ref[:, :, cols] = dot(left, right).astype(BF16).reshape(2, k, k)

    def weighted_one_kernel(sc, w_ref, own_ref, sib_ref, side_ref, *rest):
        refs = [rest[i * nf : (i + 1) * nf] for i in range(4)]
        out_ref, rows = rest[4 * nf :]
        p, q = sc[0], sc[1]
        is_end = p == q
        first_cols = pl.ds(pl.multiple_of(q * k, k), k)
        rest_cols = pl.ds(pl.multiple_of((1 - q) * k, k), k)
        rows[0, :, :, pl.ds(pl.multiple_of(p * k, k), k)] = own_ref[...]
        rows[0, :, :, pl.ds(pl.multiple_of((1 - p) * k, k), k)] = sib_ref[...]
        rows[0, :, :, 2 * k :] = side_ref[...]
        for s in range(nf):
            mine, other = refs[0][s][...], refs[1][s][...]
            rows[s + 1, :, :, first_cols] = jnp.where(is_end, mine, other)
            rows[s + 1, :, :, 2 * k :] = jnp.where(is_end, other, mine)
            for take, parts in zip(halves(p), refs[2:]):
                rows[s + 1, :, take, rest_cols] = parts[s][...]
        weighted(w_ref, rows, out_ref)

    (solved_one,) = call(
        weighted_one_kernel, scalars,
        [weight_one, end_own, end_sib, side, *first_far, *first_fwd, *rest_far, *rest_fwd],
        [sds((2, k, 3 * k), BF16)], scratch=[pltpu.VMEM((n_face, 2, fr, 3 * k), BF16)],
    )

    ends_far = [face_permute(after(a, two_own), i + 1) for i, a in enumerate(kept_out[:nf])]
    ends_fwd = [box_permute(a, 1) for a in ends_far]
    slots_far = [face_permute(after(a, two_own), i + 1) for i, a in enumerate(kept_out[nf:])]

    def join_kernel(sc, own_ref, x_ref, out_ref):
        q = sc[1]
        out_ref[:, :, pl.ds(pl.multiple_of(q * k, k), k)] = own_ref[:, :, :k]
        out_ref[:, :, pl.ds(pl.multiple_of((1 - q) * k, k), k)] = x_ref[:, :, :k]
        out_ref[:, :, 2 * k :] = own_ref[:, :, k:] + x_ref[:, :, k:]

    two_shape = [sds((2, hr, 3 * k), BF16)]
    two_rows = call(join_kernel, after(scalars, solved_one, weight_two), [two_own, two_x], two_shape, cost=JOIN_COST)
    two_xy = [box_permute(after(a, *two_rows), 2) for a in two_y]

    for own, other in zip(two_y, two_xy):
        two_rows += call(join_kernel, after(scalars, *slots_far), [own, other], two_shape)
    two_sib = [box_permute(a, 1) for a in two_rows]

    def whole_rows(sc, out_ref, cols, end_ref, kept_ref, far, fwd):
        p, q = sc[0], sc[1]

        @pl.when(p == q)
        def _():
            out_ref[...] = end_ref[:, :, cols]

        @pl.when(p != q)
        def _():
            for h, parts in enumerate((far, fwd)):
                take = pl.ds(pl.multiple_of((p ^ h) * hr, hr), hr)
                total = kept_ref[:, take, cols]
                for part in parts:
                    total = total + part[...]
                out_ref[:, take, :] = total

    def level_one_kernel(sc, end_ref, kept_ref, *refs):
        far, fwd = refs[:nf], refs[nf : 2 * nf]
        col_ref, one_ref, w_ref, hid_out, first_out, sub_out, zs = refs[2 * nf :]
        p, q, f = sc[0], sc[1], sc[2]
        whole_rows(sc, zs, slice(0, 2 * k), end_ref, kept_ref, far, fwd)
        slots = col_ref[pl.ds(pl.multiple_of(f * fr, fr), fr), :]
        right = jnp.where(slots >= k, 1, 0)
        right = jnp.where(p == q, p, right) > 0
        lefts = [zs[t, :, :k] for t in range(2)]
        rights = [zs[t, :, k:] for t in range(2)]
        left = stacked(*[jnp.where(right, a, b) for a, b in zip(lefts, rights)])
        nothing = jnp.zeros((fr, k), BF16)
        start = [
            jnp.concatenate([jnp.where(right, nothing, a) for a in lefts], axis=0),
            jnp.concatenate([jnp.where(right, a, nothing) for a in rights], axis=0),
        ]
        merged = [
            (start[c].astype(F32) - dot(left, flat(one_ref[:, :, c * k : (c + 1) * k]))).astype(BF16)
            for c in range(2)
        ]
        sub_out[...] = dot(left, flat(one_ref[:, :, 2 * k :]))
        is_left = q == 0
        first_out[...] = jnp.where(is_left, merged[0], merged[1])
        couple = jnp.where(is_left, merged[1], merged[0])
        second = dot(stacked(couple[:fr], couple[fr:]), flat(w_ref[...])).astype(BF16)
        for s in range(n_face):
            hid_out[s] = piece((second[:fr], second[fr:]), s * fr, fr)

    hid_two, first_two, sub_one = call(
        level_one_kernel, scalars,
        [end_kept, kept, *ends_far, *ends_fwd, skel_col, solved_one, weight_two],
        [sds((n_face, 2 * fr, 2 * fr), BF16), sds((2 * fr, k), BF16), sds((2 * fr, k), F32)],
        scratch=[pltpu.VMEM((2, fr, 2 * k), BF16)], cost=KEEP_COST,
    )

    slots_fwd = [box_permute(after(a, hid_two), 1) for a in slots_far]

    def level_two_kernel(sc, hid_ref, first_ref, *refs):
        out_ref, sub_out, rows, stage, sems = refs[2 * n_face :]
        p, q = sc[0], sc[1]
        left = jnp.concatenate([hid_ref[s] for s in range(n_face)], axis=1)
        for s in range(n_face):
            rows[s, :, pl.ds(pl.multiple_of(p * hr, hr), hr), :] = refs[s][...]
            rows[s, :, pl.ds(pl.multiple_of((1 - p) * hr, hr), hr), :] = refs[n_face + s][...]
        copies = []
        for c in range(2):
            first = jnp.where(q == c, first_ref[...], jnp.zeros((2 * fr, k), BF16)).astype(F32)
            right = rows[:, :, :, c * k : (c + 1) * k].reshape(n_face * 2 * fr, k)
            stage[c] = (first - dot(left, right)).astype(BF16).reshape(2, fr, k)
            copies.append(pltpu.make_async_copy(
                stage.at[c], out_ref.at[:, 0, :, pl.ds(c * k, k)], sems.at[c]
            ))
            copies[-1].start()
        sub_out[...] = dot(left, rows[:, :, :, 2 * k :].reshape(n_face * 2 * fr, k))
        for copy in copies:
            copy.wait()

    out, sub_two = call(
        level_two_kernel, scalars, [hid_two, first_two, *two_rows, *two_sib],
        [sds((2, 1, fr, 3 * k), BF16), sds((2 * fr, k), F32)],
        out_specs=[in_hbm, pl.BlockSpec(memory_space=pltpu.VMEM)],
        scratch=[pltpu.VMEM((n_face, 2, fr, 3 * k), BF16), pltpu.VMEM((2, 2, fr, k), BF16),
                 pltpu.SemaphoreType.DMA((2,))],
    )

    def finish_kernel(sc, end_ref, kept_ref, *refs):
        one_ref, two_ref, _, out_ref, rows, stage, sem = refs[2 * nf :]
        whole_rows(sc, rows, slice(2 * k, 3 * k), end_ref, kept_ref, refs[:nf], refs[nf : 2 * nf])
        merged = (flat(rows[...]).astype(F32) - one_ref[...]).astype(BF16)
        stage[...] = (merged.astype(F32) - two_ref[...]).astype(BF16).reshape(2, fr, k)
        copy = pltpu.make_async_copy(stage, out_ref.at[:, 0, :, pl.ds(2 * k, k)], sem.at[0])
        copy.start()
        copy.wait()

    inputs = [end_kept, kept, *slots_far, *slots_fwd, sub_one, sub_two, out]
    (out,) = call(
        finish_kernel, scalars, inputs, [sds((2, 1, fr, 3 * k), BF16)],
        specs=[pl.BlockSpec(memory_space=pltpu.VMEM)] * (len(inputs) - 1) + [in_hbm], out_specs=[in_hbm],
        scratch=[pltpu.VMEM((2, fr, k), BF16)] * 2 + [pltpu.SemaphoreType.DMA((1,))], aliases={len(inputs): 0},
    )
    return out


def solution(mesh):
    return jax.shard_map(
        on_device,
        mesh=mesh,
        in_specs=(
            P(None, None, "box", None, "face", None),
            P(None, None, "box", None),
            P(None, None, "box", None),
            P(),
            P(),
        ),
        out_specs=P(None, None, ("box", "face"), None),
        check_vma=False,
    )
```

```python
import functools

import jax
import jax.numpy as jnp
from jax import lax
from jax.experimental import pallas as pl
from jax.experimental.pallas import tpu as pltpu
from jax.sharding import PartitionSpec as P

BF16 = jnp.bfloat16
F32 = jnp.float32
VMEM_BYTES = 16 * 1024 * 1024
JOIN_COST = 300000000
OWN_COST = 1_000_000_000
KEEP_COST = 2_000_000_000


def dot(first, second):
    return jnp.dot(first, second, preferred_element_type=F32)


def stacked(real, imag):
    return jnp.concatenate(
        [jnp.concatenate([real, -imag], axis=1), jnp.concatenate([imag, real], axis=1)], axis=0
    )


def flat(array):
    return array.reshape(array.shape[0] * array.shape[1], array.shape[2])


def column_picker(index, offset, count):
    rows = lax.broadcasted_iota(jnp.int32, (count, index.shape[1]), 0) + offset
    return jnp.where(rows == index, 1.0, 0.0).astype(BF16)


def row_picker(index, offset, count):
    cols = lax.broadcasted_iota(jnp.int32, (index.shape[0], count), 1) + offset
    return jnp.where(cols == index, 1.0, 0.0).astype(BF16)


def call(kernel, scalars, inputs, out_shapes, specs=None, out_specs=None, scratch=(), cost=0):
    in_vmem = pl.BlockSpec(memory_space=pltpu.VMEM)
    specs = specs or [in_vmem] * len(inputs)
    out_specs = out_specs or [in_vmem] * len(out_shapes)
    return pl.pallas_call(
        kernel,
        in_specs=[pl.BlockSpec(memory_space=pltpu.SMEM)] + specs,
        out_specs=out_specs,
        out_shape=out_shapes,
        scratch_shapes=list(scratch),
        compiler_params=pltpu.CompilerParams(vmem_limit_bytes=VMEM_BYTES),
        cost_estimate=pl.CostEstimate(flops=cost, bytes_accessed=0, transcendentals=0),
    )(scalars, *inputs)


def after(array, *others):
    return lax.optimization_barrier((array, *others))[0]


def on_device(leaf_maps, w_first, w_second, skel_first, skel_second):
    box = lax.axis_index("box")
    face = lax.axis_index("face")
    n_box, n_face = lax.axis_size("box"), lax.axis_size("face")
    nf = n_face - 1
    fr = leaf_maps.shape[4]
    hr = fr // 2
    k = leaf_maps.shape[5] // 3
    half = k // 2
    leaf = leaf_maps[:, 0, 0]
    scalars = jnp.stack([box % 2, box // 2 % 2, face, box % 4, box // 2, box // 4]).astype(jnp.int32)
    sds = jax.ShapeDtypeStruct
    in_hbm = pl.BlockSpec(memory_space=pltpu.HBM)

    def box_permute(array, mask):
        return lax.ppermute(array, "box", [(b, b ^ mask) for b in range(n_box)])

    def face_permute(array, step):
        pairs = [
            (b * n_face + f, b * n_face + (f + n_face - step) % n_face)
            for b in range(n_box) for f in range(n_face)
        ]
        return lax.ppermute(array, ("box", "face"), pairs)

    def over_face(array):
        return [face_permute(array, s) for s in range(1, n_face)]

    def halves(p):
        mine = pl.ds(pl.multiple_of(p * hr, hr), hr)
        other = pl.ds(pl.multiple_of((1 - p) * hr, hr), hr)
        return mine, other

    def slots_kernel(sc, skel_ref, skel2_ref, comp_out, col_out):
        q = sc[1]
        rows = lax.broadcasted_iota(jnp.int32, (k, k), 0)
        cols = lax.broadcasted_iota(jnp.int32, (k, k), 1)
        skel = jnp.broadcast_to(skel_ref[pl.ds(sc[4], 1), :].astype(F32), (k, k))
        column = jnp.sum(jnp.where(rows == cols, skel, 0.0), axis=1, keepdims=True)
        col_out[...] = column.astype(jnp.int32)
        place = skel2_ref[pl.ds(sc[5], 1), :] - q * k
        taken = jnp.where(rows == place, jnp.broadcast_to(column, (k, k)), 0.0)
        found = jnp.sum(taken, axis=0, keepdims=True).astype(jnp.int32)
        comp_out[...] = jnp.where(jnp.logical_and(place >= 0, place < k), found, -1)

    comp, skel_col = call(
        slots_kernel, scalars, [skel_first[0], skel_second[0]], [sds((1, k), jnp.int32), sds((k, 1), jnp.int32)]
    )

    def parts_kernel(sc, leaf_ref, end_out, side_out, *rows_outs):
        p = sc[0]
        end_out[...] = leaf_ref[:, 1 - p, :, pl.ds(pl.multiple_of(p * k, k), k)]
        side_out[...] = leaf_ref[:, 1 - p, :, 2 * k :]
        for i, rows_out in enumerate(rows_outs):
            rows_out[...] = leaf_ref[:, 2, i % 2 * hr : (i % 2 + 1) * hr, i // 2 * k : (i // 2 + 1) * k]

    end_own, sides_raw, *s_rows = call(
        parts_kernel, scalars, [leaf], [sds((2, fr, k), BF16)] * 2 + [sds((2, hr, k), BF16)] * 6
    )
    sides_sib = box_permute(sides_raw, 1)
    end_sib = box_permute(end_own, 1)
    s_sib = [box_permute(a, 1) for a in s_rows]

    def side_kernel(sc, own_ref, sib_ref, comp_ref, end_ref, side_out, send_out):
        p, q = sc[0], sc[1]
        pick_own = column_picker(comp_ref[...], p * k, k)
        pick_sib = column_picker(comp_ref[...], (1 - p) * k, k)
        side = dot(flat(own_ref[...]), pick_own) + dot(flat(sib_ref[...]), pick_sib)
        side_out[...] = side.astype(BF16).reshape(2, fr, k)
        send_out[...] = jnp.where(p == q, end_ref[...], side_out[...])

    side, first_send = call(
        side_kernel, scalars, [sides_raw, sides_sib, comp, end_own], [sds((2, fr, k), BF16)] * 2
    )
    first_far = over_face(first_send)

    def ends_kernel(sc, leaf_ref, comp_ref, keep_out, send_out, end_out):
        p = sc[0]
        pick_own = column_picker(comp_ref[...], p * k, k)
        for t in range(2):
            end_out[t, :, : 2 * k] = leaf_ref[t, p, :, : 2 * k]
            end_out[t, :, 2 * k :] = dot(leaf_ref[t, p, :, 2 * k :], pick_own).astype(BF16)
        couple = pl.ds(pl.multiple_of((1 - p) * k, k), k)
        for ref, take in zip((keep_out, send_out), halves(p)):
            ref[:, :, :k] = end_out[:, take, couple]
            ref[:, :, k:] = end_out[:, take, 2 * k :]

    v_keep, v_send, end_kept = call(
        ends_kernel, after(scalars, side), [leaf, comp],
        [sds((2, hr, 2 * k), BF16)] * 2 + [sds((2, fr, 3 * k), BF16)],
    )
    v_recv = box_permute(v_send, 1)

    w_one, w_two = w_first[:, 0], w_second[:, 0]
    w_one_sib = box_permute(after(w_one, side), 1)
    w_two_x = box_permute(after(w_two, side), 2)
    w_two_sib = box_permute(after(w_two, side), 1)
    w_two_x_sib = box_permute(w_two_x, 1)

    def weight_kernel(place, sc, *refs):
        out_ref = refs[-1]
        count = refs[0].shape[1]
        for i, ref in enumerate(refs[:-1]):
            take = pl.ds(pl.multiple_of(place(sc, i) * count, count), count)
            for f in range(n_face):
                @pl.when(sc[2] == f)
                def _(ref=ref, take=take, f=f):
                    out_ref[:, take, : k - f * fr] = ref[:, :, f * fr :]
                    if f > 0:
                        out_ref[:, take, k - f * fr :] = ref[:, :, : f * fr]

    (weight_one,) = call(
        functools.partial(weight_kernel, lambda sc, i: sc[0] ^ i), scalars, [w_one, w_one_sib],
        [sds((2, k, k), BF16)],
    )
    (weight_two,) = call(
        functools.partial(weight_kernel, lambda sc, i: sc[3] ^ (0, 2, 1, 3)[i]), scalars,
        [w_two, w_two_x, w_two_sib, w_two_x_sib], [sds((2, k, k), BF16)],
    )

    def rows_kernel(sc, *refs):
        owns, sibs, refs = refs[:6], refs[6:12], refs[12:]
        comp_ref, col_ref, end_ref, endsib_ref, kept_out, *outs = refs
        p, q, f = sc[0], sc[1], sc[2]
        mine, _ = halves(p)
        rest = jnp.where(p == q, endsib_ref[:, mine, :], end_ref[:, mine, :])
        for s in range(nf):
            outs[nf + s][:, :, :k] = rest
        pick_own = column_picker(comp_ref[...], p * k, k)
        pick_sib = column_picker(comp_ref[...], (1 - p) * k, k)

        def pick(slots, write):
            take_own = row_picker(slots, p * k + f * fr, fr)
            take_sib = row_picker(slots, (1 - p) * k + f * fr, fr)
            for t in range(2):
                for c in range(3):
                    own, sib = [
                        jnp.concatenate([a[2 * c][t], a[2 * c + 1][t]], axis=0) for a in (owns, sibs)
                    ]
                    if c == 2:
                        own, sib = [dot(a, b).astype(BF16) for a, b in ((own, pick_own), (sib, pick_sib))]
                    write(t, c, (dot(take_own, own) + dot(take_sib, sib)).astype(BF16))

        def write_far(s, t, c, picked):
            if c < 2:
                outs[s][t, :, c * k : (c + 1) * k] = picked
            else:
                outs[nf + s][t, :, k:] = picked

        def col_half(s):
            start = (f + n_face - s - 1) % n_face * fr + p * hr
            return col_ref[pl.ds(pl.multiple_of(start, hr), hr), :]

        far = jnp.concatenate([col_half(s) for s in range(nf)], axis=0)

        @pl.when(p == q)
        def _():
            def write(t, c, picked):
                for s in range(nf):
                    write_far(s, t, c, picked[s * hr : (s + 1) * hr])

            pick(far, write)

        @pl.when(p != q)
        def _():
            def write(t, c, picked):
                kept_out[t, :, c * k : (c + 1) * k] = picked[:fr]
                for s in range(nf):
                    write_far(s, t, c, picked[fr + s * hr : fr + (s + 1) * hr])

            pick(jnp.concatenate([col_ref[pl.ds(pl.multiple_of(f * fr, fr), fr), :], far], axis=0), write)

    kept, *kept_out = call(
        rows_kernel, scalars, [*s_rows, *s_sib, comp, skel_col, end_own, end_sib],
        [sds((2, fr, 3 * k), BF16)] + [sds((2, hr, 2 * k), BF16)] * (2 * nf),
    )
    mixed_far = [face_permute(a, i + 1) for i, a in enumerate(kept_out[nf:])]

    def piece(hidden, start, count):
        return stacked(hidden[0][:, start : start + count], hidden[1][:, start : start + count])

    def iface_kernel(sc, keep_ref, recv_ref, w_ref, end_ref, endsib_ref, side_ref,
                     acc_out, hid_out, rows):
        p, q = sc[0], sc[1]

        @pl.when(p == q)
        def _():
            rows[...] = recv_ref[...]

        @pl.when(p != q)
        def _():
            rows[...] = keep_ref[...]

        both = dot(stacked(rows[0, :, :k], rows[1, :, :k]), flat(w_ref[...])).astype(BF16)
        hidden = both[:hr], both[hr:]
        hid_out[0] = hidden[0]
        hid_out[1] = hidden[1]
        left = piece(hidden, 0, fr)
        is_end = p == q
        ends = jnp.where(is_end, end_ref[...], endsib_ref[...])
        acc_out[:, :, :k] = -dot(left, flat(ends)).reshape(2, hr, k)
        acc_out[:, :, k:] = rows[:, :, k:].astype(F32) - dot(left, flat(side_ref[...])).reshape(2, hr, k)

    v_acc, v_hid = call(
        iface_kernel, scalars, [v_keep, v_recv, weight_one, end_own, end_sib, side],
        [sds((2, hr, 2 * k), F32), sds((2, hr, k), BF16)],
        scratch=[pltpu.VMEM((2, hr, 2 * k), BF16)], cost=OWN_COST,
    )
    first_fwd = [box_permute(after(a, kept, w_two_x), 1) for a in first_far]

    def iface_far_kernel(sc, acc_ref, hid_ref, *rest):
        far, fwd = rest[:nf], rest[nf : 2 * nf]
        end_out, keep_out, send_out = rest[2 * nf :]
        q = sc[1]
        is_end = sc[0] == q
        hidden = [hid_ref[0], hid_ref[1]]
        total = acc_ref[...]
        for s in range(nf):
            left = piece(hidden, (s + 1) * fr, fr)
            mine, other = dot(left, flat(far[s][...])), dot(left, flat(fwd[s][...]))
            both = [jnp.where(is_end, mine, other), jnp.where(is_end, other, mine)]
            total = total - jnp.concatenate(both, axis=1).reshape(2, hr, 2 * k)
        total = total.astype(BF16)
        end_out[...] = total[:, :, :k]
        low, high = total[:, :, k : k + half], total[:, :, k + half :]
        keep_out[...] = jnp.where(q == 0, low, high)
        send_out[...] = jnp.where(q == 0, high, low)

    two_end, side_keep, side_send = call(
        iface_far_kernel, scalars, [v_acc, v_hid, *first_far, *first_fwd],
        [sds((2, hr, k), BF16)] + [sds((2, hr, half), BF16)] * 2,
    )

    side_x = box_permute(side_send, 2)

    def pack_kernel(sc, end_ref, keep_ref, x_ref, out_ref):
        out_ref[:, :, :k] = end_ref[...]
        out_ref[:, :, k:] = keep_ref[...] + x_ref[...]

    (two_own,) = call(
        pack_kernel, scalars, [two_end, side_keep, side_x], [sds((2, hr, k + half), BF16)]
    )
    two_x = box_permute(two_own, 2)
    two_y = over_face(two_own)
    mixed_fwd = [box_permute(after(a, two_own), 1) for a in mixed_far]

    def weighted(w_ref, rows, out_ref):
        left = jnp.concatenate([piece((w_ref[0], w_ref[1]), s * fr, fr) for s in range(n_face)], axis=1)
        for c in range(3):
            cols = slice(c * k, (c + 1) * k)
            right = rows[:, :, :, cols].reshape(n_face * 2 * fr, k)
            out_ref[:, :, cols] = dot(left, right).astype(BF16).reshape(2, k, k)

    def weighted_one_kernel(sc, w_ref, own_ref, sib_ref, side_ref, *rest):
        refs = [rest[i * nf : (i + 1) * nf] for i in range(4)]
        out_ref, rows = rest[4 * nf :]
        p, q = sc[0], sc[1]
        is_end = p == q
        first_cols = pl.ds(pl.multiple_of(q * k, k), k)
        rest_cols = pl.ds(pl.multiple_of((1 - q) * k, k), k)
        rows[0, :, :, pl.ds(pl.multiple_of(p * k, k), k)] = own_ref[...]
        rows[0, :, :, pl.ds(pl.multiple_of((1 - p) * k, k), k)] = sib_ref[...]
        rows[0, :, :, 2 * k :] = side_ref[...]
        for s in range(nf):
            mine, other = refs[0][s][...], refs[1][s][...]
            rows[s + 1, :, :, first_cols] = jnp.where(is_end, mine, other)
            rows[s + 1, :, :, 2 * k :] = jnp.where(is_end, other, mine)
            for take, parts in zip(halves(p), refs[2:]):
                rows[s + 1, :, take, rest_cols] = parts[s][:, :, :k]
        weighted(w_ref, rows, out_ref)

    (solved_one,) = call(
        weighted_one_kernel, scalars,
        [weight_one, end_own, end_sib, side, *first_far, *first_fwd, *mixed_far, *mixed_fwd],
        [sds((2, k, 3 * k), BF16)], scratch=[pltpu.VMEM((n_face, 2, fr, 3 * k), BF16)],
    )

    def join_kernel(sc, own_ref, x_ref, out_ref):
        q = sc[1]
        for ref, which in ((own_ref, q), (x_ref, 1 - q)):
            out_ref[:, :, pl.ds(pl.multiple_of(which * k, k), k)] = ref[:, :, :k]
            out_ref[:, :, pl.ds(pl.multiple_of(2 * k + which * half, half), half)] = ref[:, :, k:]

    two_shape = [sds((2, hr, 3 * k), BF16)]
    two_rows = call(join_kernel, after(scalars, weight_two), [two_own, two_x], two_shape, cost=JOIN_COST)
    two_xy = [box_permute(after(a, *two_rows), 2) for a in two_y]
    for own, other in zip(two_y, two_xy):
        two_rows += call(join_kernel, after(scalars, solved_one), [own, other], two_shape)
    two_sib = [box_permute(a, 1) for a in two_rows]

    ends_far = [face_permute(after(a, two_own), i + 1) for i, a in enumerate(kept_out[:nf])]
    ends_fwd = [box_permute(a, 1) for a in ends_far]

    def level_one_kernel(sc, end_ref, kept_ref, *refs):
        parts = [refs[i * nf : (i + 1) * nf] for i in range(4)]
        col_ref, one_ref, w_ref, hid_out, first_out, slots_out, zs = refs[4 * nf :]
        p, q, f = sc[0], sc[1], sc[2]

        @pl.when(p == q)
        def _():
            zs[...] = end_ref[...]

        @pl.when(p != q)
        def _():
            for h, take in enumerate(halves(p)):
                for part, cols, source in (
                    (parts[h], slice(2 * k, 3 * k), slice(k, 2 * k)), (parts[2 + h], slice(0, 2 * k), slice(0, 2 * k)),
                ):
                    total = kept_ref[:, take, cols]
                    for ref in part:
                        total = total + ref[:, :, source]
                    zs[:, take, cols] = total

        slots = col_ref[pl.ds(pl.multiple_of(f * fr, fr), fr), :]
        right = jnp.where(slots >= k, 1, 0)
        right = jnp.where(p == q, p, right) > 0
        lefts = [zs[t, :, :k] for t in range(2)]
        rights = [zs[t, :, k : 2 * k] for t in range(2)]
        left = stacked(*[jnp.where(right, a, b) for a, b in zip(lefts, rights)])
        nothing = jnp.zeros((fr, k), BF16)
        start = [
            jnp.concatenate([jnp.where(right, nothing, a) for a in lefts], axis=0),
            jnp.concatenate([jnp.where(right, a, nothing) for a in rights], axis=0),
            flat(zs[:, :, 2 * k :]),
        ]
        merged = [
            (start[c].astype(F32) - dot(left, flat(one_ref[:, :, c * k : (c + 1) * k]))).astype(BF16)
            for c in range(3)
        ]
        is_left = q == 0
        first_out[...] = jnp.where(is_left, merged[0], merged[1])
        slots_out[...] = merged[2]
        couple = jnp.where(is_left, merged[1], merged[0])
        second = dot(stacked(couple[:fr], couple[fr:]), flat(w_ref[...])).astype(BF16)
        for s in range(n_face):
            hid_out[s] = piece((second[:fr], second[fr:]), s * fr, fr)

    hid_two, first_two, slots_two = call(
        level_one_kernel, scalars,
        [end_kept, kept, *mixed_far, *mixed_fwd, *ends_far, *ends_fwd, skel_col, solved_one, weight_two],
        [sds((n_face, 2 * fr, 2 * fr), BF16), sds((2 * fr, k), BF16), sds((2 * fr, k), BF16)],
        scratch=[pltpu.VMEM((2, fr, 3 * k), BF16)], cost=KEEP_COST,
    )

    def level_two_kernel(sc, hid_ref, first_ref, slots_ref, *refs):
        out_ref, rows, stage, sems = refs[2 * n_face :]
        q = sc[1]
        left = jnp.concatenate([hid_ref[s] for s in range(n_face)], axis=1)
        for h, take in enumerate(halves(sc[0])):
            for s in range(n_face):
                rows[s, :, take, :] = refs[h * n_face + s][...]
        copies = []
        for c in range(3):
            first = slots_ref[...]
            if c < 2:
                first = jnp.where(q == c, first_ref[...], jnp.zeros((2 * fr, k), BF16))
            right = rows[:, :, :, c * k : (c + 1) * k].reshape(n_face * 2 * fr, k)
            stage[c] = (first.astype(F32) - dot(left, right)).astype(BF16).reshape(2, fr, k)
            copies.append(pltpu.make_async_copy(
                stage.at[c], out_ref.at[:, 0, :, pl.ds(c * k, k)], sems.at[c]
            ))
            copies[-1].start()
        for copy in copies:
            copy.wait()

    (out,) = call(
        level_two_kernel, scalars, [hid_two, first_two, slots_two, *two_rows, *two_sib],
        [sds((2, 1, fr, 3 * k), BF16)], out_specs=[in_hbm],
        scratch=[pltpu.VMEM((n_face, 2, fr, 3 * k), BF16), pltpu.VMEM((3, 2, fr, k), BF16),
                 pltpu.SemaphoreType.DMA((3,))],
    )
    return out


def solution(mesh):
    return jax.shard_map(
        on_device,
        mesh=mesh,
        in_specs=(
            P(None, None, "box", None, "face", None),
            P(None, None, "box", None),
            P(None, None, "box", None),
            P(),
            P(),
        ),
        out_specs=P(None, None, ("box", "face"), None),
        check_vma=False,
    )
```

```python
import functools

import jax
import jax.numpy as jnp
from jax import lax
from jax.experimental import pallas as pl
from jax.experimental.pallas import tpu as pltpu
from jax.sharding import PartitionSpec as P

BF16 = jnp.bfloat16
F32 = jnp.float32
VMEM_BYTES = 16 * 1024 * 1024
JOIN_COST = 300000000
SLOTS_COST = 0
OWN_COST = 700000000
SOLVED_COST = 2200000000
KEEP_COST = 2_000_000_000


def dot(first, second):
    return jnp.dot(first, second, preferred_element_type=F32)


def stacked(real, imag):
    return jnp.concatenate(
        [jnp.concatenate([real, -imag], axis=1), jnp.concatenate([imag, real], axis=1)], axis=0
    )


def flat(array):
    return array.reshape(array.shape[0] * array.shape[1], array.shape[2])


def column_picker(index, offset, count):
    rows = lax.broadcasted_iota(jnp.int32, (count, index.shape[1]), 0) + offset
    return jnp.where(rows == index, 1.0, 0.0).astype(BF16)


def row_picker(index, offset, count):
    cols = lax.broadcasted_iota(jnp.int32, (index.shape[0], count), 1) + offset
    return jnp.where(cols == index, 1.0, 0.0).astype(BF16)


def call(kernel, scalars, inputs, out_shapes, specs=None, out_specs=None, scratch=(), cost=0):
    in_vmem = pl.BlockSpec(memory_space=pltpu.VMEM)
    specs = specs or [in_vmem] * len(inputs)
    out_specs = out_specs or [in_vmem] * len(out_shapes)
    return pl.pallas_call(
        kernel,
        in_specs=[pl.BlockSpec(memory_space=pltpu.SMEM)] + specs,
        out_specs=out_specs,
        out_shape=out_shapes,
        scratch_shapes=list(scratch),
        compiler_params=pltpu.CompilerParams(vmem_limit_bytes=VMEM_BYTES),
        cost_estimate=pl.CostEstimate(flops=cost, bytes_accessed=0, transcendentals=0),
    )(scalars, *inputs)


def after(array, *others):
    return lax.optimization_barrier((array, *others))[0]


def on_device(leaf_maps, w_first, w_second, skel_first, skel_second):
    box = lax.axis_index("box")
    face = lax.axis_index("face")
    n_box, n_face = lax.axis_size("box"), lax.axis_size("face")
    nf = n_face - 1
    fr = leaf_maps.shape[4]
    hr = fr // 2
    k = leaf_maps.shape[5] // 3
    half = k // 2
    leaf = leaf_maps[:, 0, 0]
    scalars = jnp.stack([box % 2, box // 2 % 2, face, box % 4, box // 2, box // 4]).astype(jnp.int32)
    sds = jax.ShapeDtypeStruct
    in_hbm = pl.BlockSpec(memory_space=pltpu.HBM)

    def box_permute(array, mask):
        return lax.ppermute(array, "box", [(b, b ^ mask) for b in range(n_box)])

    def face_permute(array, step):
        pairs = [
            (b * n_face + f, b * n_face + (f + n_face - step) % n_face)
            for b in range(n_box) for f in range(n_face)
        ]
        return lax.ppermute(array, ("box", "face"), pairs)

    def over_face(array):
        return [face_permute(array, s) for s in range(1, n_face)]

    def halves(p):
        mine = pl.ds(pl.multiple_of(p * hr, hr), hr)
        other = pl.ds(pl.multiple_of((1 - p) * hr, hr), hr)
        return mine, other

    def slots_kernel(sc, skel_ref, skel2_ref, comp_out, col_out):
        q = sc[1]
        rows = lax.broadcasted_iota(jnp.int32, (k, k), 0)
        cols = lax.broadcasted_iota(jnp.int32, (k, k), 1)
        skel = jnp.broadcast_to(skel_ref[pl.ds(sc[4], 1), :].astype(F32), (k, k))
        column = jnp.sum(jnp.where(rows == cols, skel, 0.0), axis=1, keepdims=True)
        col_out[...] = column.astype(jnp.int32)
        place = skel2_ref[pl.ds(sc[5], 1), :] - q * k
        taken = jnp.where(rows == place, jnp.broadcast_to(column, (k, k)), 0.0)
        found = jnp.sum(taken, axis=0, keepdims=True).astype(jnp.int32)
        comp_out[...] = jnp.where(jnp.logical_and(place >= 0, place < k), found, -1)

    comp, skel_col = call(
        slots_kernel, scalars, [skel_first[0], skel_second[0]], [sds((1, k), jnp.int32), sds((k, 1), jnp.int32)],
        cost=SLOTS_COST,
    )

    def parts_kernel(sc, leaf_ref, end_out, side_out, *rows_outs):
        p = sc[0]
        end_out[...] = leaf_ref[:, 1 - p, :, pl.ds(pl.multiple_of(p * k, k), k)]
        side_out[...] = leaf_ref[:, 1 - p, :, 2 * k :]
        for i, rows_out in enumerate(rows_outs):
            rows_out[...] = leaf_ref[:, 2, i % 2 * hr : (i % 2 + 1) * hr, i // 2 * k : (i // 2 + 1) * k]

    end_own, sides_raw, *s_rows = call(
        parts_kernel, scalars, [leaf], [sds((2, fr, k), BF16)] * 2 + [sds((2, hr, k), BF16)] * 6
    )
    sides_sib = box_permute(sides_raw, 1)
    end_sib = box_permute(end_own, 1)
    s_sib = [box_permute(after(a, comp), 1) for a in s_rows]

    def side_kernel(sc, own_ref, sib_ref, comp_ref, end_ref, side_out, *send_outs):
        p, q = sc[0], sc[1]
        pick_own = column_picker(comp_ref[...], p * k, k)
        pick_sib = column_picker(comp_ref[...], (1 - p) * k, k)
        side = dot(flat(own_ref[...]), pick_own) + dot(flat(sib_ref[...]), pick_sib)
        side_out[...] = side.astype(BF16).reshape(2, fr, k)
        for h, send_out in enumerate(send_outs):
            take = slice(h * hr, (h + 1) * hr)
            send_out[...] = jnp.where(p == q, end_ref[:, take, :], side_out[:, take, :])

    side, *first_send = call(
        side_kernel, scalars, [sides_raw, sides_sib, comp, end_own],
        [sds((2, fr, k), BF16)] + [sds((2, hr, k), BF16)] * 2,
    )
    first_far = [face_permute(a, s) for s in range(1, n_face) for a in first_send]

    def ends_kernel(sc, leaf_ref, comp_ref, keep_out, couple_out, slots_out, end_out):
        p = sc[0]
        pick_own = column_picker(comp_ref[...], p * k, k)
        for t in range(2):
            end_out[t, :, : 2 * k] = leaf_ref[t, p, :, : 2 * k]
            end_out[t, :, 2 * k :] = dot(leaf_ref[t, p, :, 2 * k :], pick_own).astype(BF16)
        couple = pl.ds(pl.multiple_of((1 - p) * k, k), k)
        mine, other = halves(p)
        keep_out[:, :, :k] = end_out[:, mine, couple]
        keep_out[:, :, k:] = end_out[:, mine, 2 * k :]
        couple_out[...] = end_out[:, other, couple]
        slots_out[...] = end_out[:, other, 2 * k :]

    v_keep, *v_send, end_kept = call(
        ends_kernel, after(scalars, side), [leaf, comp],
        [sds((2, hr, 2 * k), BF16)] + [sds((2, hr, k), BF16)] * 2 + [sds((2, fr, 3 * k), BF16)],
    )
    v_recv = [box_permute(a, 1) for a in v_send]

    w_one, w_two = w_first[:, 0], w_second[:, 0]
    w_one_sib = box_permute(after(w_one, side), 1)
    w_two_x = box_permute(after(w_two, side), 2)
    w_two_sib = box_permute(after(w_two, side), 1)
    w_two_x_sib = box_permute(w_two_x, 1)

    def weight_kernel(place, sc, *refs):
        out_ref = refs[-1]
        count = refs[0].shape[1]
        for i, ref in enumerate(refs[:-1]):
            take = pl.ds(pl.multiple_of(place(sc, i) * count, count), count)
            for f in range(n_face):
                @pl.when(sc[2] == f)
                def _(ref=ref, take=take, f=f):
                    out_ref[:, take, : k - f * fr] = ref[:, :, f * fr :]
                    if f > 0:
                        out_ref[:, take, k - f * fr :] = ref[:, :, : f * fr]

    (weight_one,) = call(
        functools.partial(weight_kernel, lambda sc, i: sc[0] ^ i), scalars, [w_one, w_one_sib],
        [sds((2, k, k), BF16)],
    )
    (weight_two,) = call(
        functools.partial(weight_kernel, lambda sc, i: sc[3] ^ (0, 2, 1, 3)[i]), scalars,
        [w_two, w_two_x, w_two_sib, w_two_x_sib], [sds((2, k, k), BF16)],
    )

    def rows_kernel(sc, *refs):
        owns, sibs, refs = refs[:6], refs[6:12], refs[12:]
        comp_ref, col_ref, end_ref, endsib_ref, kept_out, *outs = refs
        p, q, f = sc[0], sc[1], sc[2]
        mine, _ = halves(p)
        rest = jnp.where(p == q, endsib_ref[:, mine, :], end_ref[:, mine, :])
        for s in range(nf):
            outs[nf + s][:, :, :k] = rest
        pick_own = column_picker(comp_ref[...], p * k, k)
        pick_sib = column_picker(comp_ref[...], (1 - p) * k, k)

        def pick(slots, write):
            take_own = row_picker(slots, p * k + f * fr, fr)
            take_sib = row_picker(slots, (1 - p) * k + f * fr, fr)
            for t in range(2):
                for c in range(3):
                    own, sib = [
                        jnp.concatenate([a[2 * c][t], a[2 * c + 1][t]], axis=0) for a in (owns, sibs)
                    ]
                    if c == 2:
                        own, sib = [dot(a, b).astype(BF16) for a, b in ((own, pick_own), (sib, pick_sib))]
                    write(t, c, (dot(take_own, own) + dot(take_sib, sib)).astype(BF16))

        def write_far(s, t, c, picked):
            if c < 2:
                outs[s][t, :, c * k : (c + 1) * k] = picked
            else:
                outs[nf + s][t, :, k:] = picked

        def col_half(s):
            start = (f + n_face - s - 1) % n_face * fr + p * hr
            return col_ref[pl.ds(pl.multiple_of(start, hr), hr), :]

        far = jnp.concatenate([col_half(s) for s in range(nf)], axis=0)

        @pl.when(p == q)
        def _():
            def write(t, c, picked):
                for s in range(nf):
                    write_far(s, t, c, picked[s * hr : (s + 1) * hr])

            pick(far, write)

        @pl.when(p != q)
        def _():
            def write(t, c, picked):
                kept_out[t, :, c * k : (c + 1) * k] = picked[:fr]
                for s in range(nf):
                    write_far(s, t, c, picked[fr + s * hr : fr + (s + 1) * hr])

            pick(jnp.concatenate([col_ref[pl.ds(pl.multiple_of(f * fr, fr), fr), :], far], axis=0), write)

    kept, *kept_out = call(
        rows_kernel, scalars, [*s_rows, *s_sib, comp, skel_col, end_own, end_sib],
        [sds((2, fr, 3 * k), BF16)] + [sds((2, hr, 2 * k), BF16)] * (2 * nf),
    )
    mixed_far = [face_permute(a, i + 1) for i, a in enumerate(kept_out[nf:])]

    def piece(hidden, start, count):
        return stacked(hidden[0][:, start : start + count], hidden[1][:, start : start + count])

    def iface_kernel(sc, keep_ref, couple_ref, slots_ref, w_ref, end_ref, endsib_ref, side_ref,
                     acc_out, hid_out, rows):
        p, q = sc[0], sc[1]

        @pl.when(p == q)
        def _():
            rows[:, :, :k] = couple_ref[...]
            rows[:, :, k:] = slots_ref[...]

        @pl.when(p != q)
        def _():
            rows[...] = keep_ref[...]

        both = dot(stacked(rows[0, :, :k], rows[1, :, :k]), flat(w_ref[...])).astype(BF16)
        hidden = both[:hr], both[hr:]
        hid_out[0] = hidden[0]
        hid_out[1] = hidden[1]
        left = piece(hidden, 0, fr)
        is_end = p == q
        ends = jnp.where(is_end, end_ref[...], endsib_ref[...])
        acc_out[:, :, :k] = -dot(left, flat(ends)).reshape(2, hr, k)
        acc_out[:, :, k:] = rows[:, :, k:].astype(F32) - dot(left, flat(side_ref[...])).reshape(2, hr, k)

    v_acc, v_hid = call(
        iface_kernel, scalars, [v_keep, *v_recv, weight_one, end_own, end_sib, side],
        [sds((2, hr, 2 * k), F32), sds((2, hr, k), BF16)],
        scratch=[pltpu.VMEM((2, hr, 2 * k), BF16)], cost=OWN_COST,
    )
    first_fwd = [box_permute(after(a, kept, w_two_x), 1) for a in first_far]

    def iface_far_kernel(sc, acc_ref, hid_ref, *rest):
        far, fwd = rest[: 2 * nf], rest[2 * nf : 4 * nf]
        end_out, keep_out, send_out = rest[4 * nf :]
        q = sc[1]
        is_end = sc[0] == q
        hidden = [hid_ref[0], hid_ref[1]]
        total = acc_ref[...]
        for i in range(2 * nf):
            left = piece(hidden, fr + i * hr, hr)
            mine, other = dot(left, flat(far[i][...])), dot(left, flat(fwd[i][...]))
            both = [jnp.where(is_end, mine, other), jnp.where(is_end, other, mine)]
            total = total - jnp.concatenate(both, axis=1).reshape(2, hr, 2 * k)
        total = total.astype(BF16)
        end_out[...] = total[:, :, :k]
        low, high = total[:, :, k : k + half], total[:, :, k + half :]
        keep_out[...] = jnp.where(q == 0, low, high)
        send_out[...] = jnp.where(q == 0, high, low)

    two_end, side_keep, side_send = call(
        iface_far_kernel, scalars, [v_acc, v_hid, *first_far, *first_fwd],
        [sds((2, hr, k), BF16)] + [sds((2, hr, half), BF16)] * 2,
    )

    side_x = box_permute(side_send, 2)

    def pack_kernel(sc, end_ref, keep_ref, x_ref, out_ref):
        out_ref[:, :, :k] = end_ref[...]
        out_ref[:, :, k:] = keep_ref[...] + x_ref[...]

    (two_own,) = call(
        pack_kernel, scalars, [two_end, side_keep, side_x], [sds((2, hr, k + half), BF16)]
    )
    two_x = box_permute(two_own, 2)
    two_y = over_face(two_own)
    mixed_fwd = [box_permute(after(a, two_own), 1) for a in mixed_far]

    def weighted(w_ref, rows, out_ref):
        left = jnp.concatenate([piece((w_ref[0], w_ref[1]), s * fr, fr) for s in range(n_face)], axis=1)
        for c in range(3):
            cols = slice(c * k, (c + 1) * k)
            right = rows[:, :, :, cols].reshape(n_face * 2 * fr, k)
            out_ref[:, :, cols] = dot(left, right).astype(BF16).reshape(2, k, k)

    def weighted_one_kernel(sc, w_ref, own_ref, sib_ref, side_ref, *rest):
        refs = [rest[i * nf : (i + 1) * nf] for i in range(6)]
        far, fwd = rest[: 2 * nf], rest[2 * nf : 4 * nf]
        out_ref, rows = rest[6 * nf :]
        p, q = sc[0], sc[1]
        is_end = p == q
        first_cols = pl.ds(pl.multiple_of(q * k, k), k)
        rest_cols = pl.ds(pl.multiple_of((1 - q) * k, k), k)
        rows[0, :, :, pl.ds(pl.multiple_of(p * k, k), k)] = own_ref[...]
        rows[0, :, :, pl.ds(pl.multiple_of((1 - p) * k, k), k)] = sib_ref[...]
        rows[0, :, :, 2 * k :] = side_ref[...]
        for s in range(nf):
            for h in range(2):
                take = slice(h * hr, (h + 1) * hr)
                mine, other = far[2 * s + h][...], fwd[2 * s + h][...]
                rows[s + 1, :, take, first_cols] = jnp.where(is_end, mine, other)
                rows[s + 1, :, take, 2 * k :] = jnp.where(is_end, other, mine)
            for take, parts in zip(halves(p), refs[4:]):
                rows[s + 1, :, take, rest_cols] = parts[s][:, :, :k]
        weighted(w_ref, rows, out_ref)

    (solved_one,) = call(
        weighted_one_kernel, scalars,
        [weight_one, end_own, end_sib, side, *first_far, *first_fwd, *mixed_far, *mixed_fwd],
        [sds((2, k, 3 * k), BF16)], scratch=[pltpu.VMEM((n_face, 2, fr, 3 * k), BF16)], cost=SOLVED_COST,
    )

    def join_kernel(sc, own_ref, x_ref, out_ref):
        q = sc[1]
        for ref, which in ((own_ref, q), (x_ref, 1 - q)):
            out_ref[:, :, pl.ds(pl.multiple_of(which * k, k), k)] = ref[:, :, :k]
            out_ref[:, :, pl.ds(pl.multiple_of(2 * k + which * half, half), half)] = ref[:, :, k:]

    two_shape = [sds((2, hr, 3 * k), BF16)]
    two_rows = call(join_kernel, after(scalars, weight_two), [two_own, two_x], two_shape, cost=JOIN_COST)
    two_xy = [box_permute(after(a, *two_rows), 2) for a in two_y]
    for own, other in zip(two_y, two_xy):
        two_rows += call(join_kernel, after(scalars, solved_one), [own, other], two_shape)
    two_sib = [box_permute(a, 1) for a in two_rows]

    ends_far = [face_permute(after(a, two_own), i + 1) for i, a in enumerate(kept_out[:nf])]
    ends_fwd = [box_permute(a, 1) for a in ends_far]

    def level_one_kernel(sc, end_ref, kept_ref, *refs):
        parts = [refs[i * nf : (i + 1) * nf] for i in range(4)]
        col_ref, one_ref, w_ref, hid_out, first_out, slots_out, zs = refs[4 * nf :]
        p, q, f = sc[0], sc[1], sc[2]

        @pl.when(p == q)
        def _():
            zs[...] = end_ref[...]

        @pl.when(p != q)
        def _():
            for h, take in enumerate(halves(p)):
                for part, cols, source in (
                    (parts[h], slice(2 * k, 3 * k), slice(k, 2 * k)), (parts[2 + h], slice(0, 2 * k), slice(0, 2 * k)),
                ):
                    total = kept_ref[:, take, cols]
                    for ref in part:
                        total = total + ref[:, :, source]
                    zs[:, take, cols] = total

        slots = col_ref[pl.ds(pl.multiple_of(f * fr, fr), fr), :]
        right = jnp.where(slots >= k, 1, 0)
        right = jnp.where(p == q, p, right) > 0
        lefts = [zs[t, :, :k] for t in range(2)]
        rights = [zs[t, :, k : 2 * k] for t in range(2)]
        left = stacked(*[jnp.where(right, a, b) for a, b in zip(lefts, rights)])
        nothing = jnp.zeros((fr, k), BF16)
        start = [
            jnp.concatenate([jnp.where(right, nothing, a) for a in lefts], axis=0),
            jnp.concatenate([jnp.where(right, a, nothing) for a in rights], axis=0),
            flat(zs[:, :, 2 * k :]),
        ]
        merged = [
            (start[c].astype(F32) - dot(left, flat(one_ref[:, :, c * k : (c + 1) * k]))).astype(BF16)
            for c in range(3)
        ]
        is_left = q == 0
        first_out[...] = jnp.where(is_left, merged[0], merged[1])
        slots_out[...] = merged[2]
        couple = jnp.where(is_left, merged[1], merged[0])
        second = dot(stacked(couple[:fr], couple[fr:]), flat(w_ref[...])).astype(BF16)
        for s in range(n_face):
            hid_out[s] = piece((second[:fr], second[fr:]), s * fr, fr)

    hid_two, first_two, slots_two = call(
        level_one_kernel, scalars,
        [end_kept, kept, *mixed_far, *mixed_fwd, *ends_far, *ends_fwd, skel_col, solved_one, weight_two],
        [sds((n_face, 2 * fr, 2 * fr), BF16), sds((2 * fr, k), BF16), sds((2 * fr, k), BF16)],
        scratch=[pltpu.VMEM((2, fr, 3 * k), BF16)], cost=KEEP_COST,
    )

    def level_two_kernel(sc, hid_ref, first_ref, slots_ref, *refs):
        out_ref, rows, stage, sems = refs[2 * n_face :]
        q = sc[1]
        left = jnp.concatenate([hid_ref[s] for s in range(n_face)], axis=1)
        for h, take in enumerate(halves(sc[0])):
            for s in range(n_face):
                rows[s, :, take, :] = refs[h * n_face + s][...]
        copies = []
        for c in range(3):
            first = slots_ref[...]
            if c < 2:
                first = jnp.where(q == c, first_ref[...], jnp.zeros((2 * fr, k), BF16))
            right = rows[:, :, :, c * k : (c + 1) * k].reshape(n_face * 2 * fr, k)
            stage[c] = (first.astype(F32) - dot(left, right)).astype(BF16).reshape(2, fr, k)
            copies.append(pltpu.make_async_copy(
                stage.at[c], out_ref.at[:, 0, :, pl.ds(c * k, k)], sems.at[c]
            ))
            copies[-1].start()
        for copy in copies:
            copy.wait()

    (out,) = call(
        level_two_kernel, scalars, [hid_two, first_two, slots_two, *two_rows, *two_sib],
        [sds((2, 1, fr, 3 * k), BF16)], out_specs=[in_hbm],
        scratch=[pltpu.VMEM((n_face, 2, fr, 3 * k), BF16), pltpu.VMEM((3, 2, fr, k), BF16),
                 pltpu.SemaphoreType.DMA((3,))],
    )
    return out


def solution(mesh):
    return jax.shard_map(
        on_device,
        mesh=mesh,
        in_specs=(
            P(None, None, "box", None, "face", None),
            P(None, None, "box", None),
            P(None, None, "box", None),
            P(),
            P(),
        ),
        out_specs=P(None, None, ("box", "face"), None),
        check_vma=False,
    )
```

```python
import functools

import jax
import jax.numpy as jnp
from jax import lax
from jax.experimental import pallas as pl
from jax.experimental.pallas import tpu as pltpu
from jax.sharding import PartitionSpec as P

BF16 = jnp.bfloat16
F32 = jnp.float32
VMEM_BYTES = 16 * 1024 * 1024
JOIN_COST = 300000000
SLOTS_COST = 0
OWN_COST = 700000000
SOLVED_COST = 2200000000
KEEP_COST = 2_000_000_000


def dot(first, second):
    return jnp.dot(first, second, preferred_element_type=F32)


def stacked(real, imag):
    return jnp.concatenate(
        [jnp.concatenate([real, -imag], axis=1), jnp.concatenate([imag, real], axis=1)], axis=0
    )


def flat(array):
    return array.reshape(array.shape[0] * array.shape[1], array.shape[2])


def column_picker(index, offset, count):
    rows = lax.broadcasted_iota(jnp.int32, (count, index.shape[1]), 0) + offset
    return jnp.where(rows == index, 1.0, 0.0).astype(BF16)


def row_picker(index, offset, count):
    cols = lax.broadcasted_iota(jnp.int32, (index.shape[0], count), 1) + offset
    return jnp.where(cols == index, 1.0, 0.0).astype(BF16)


def call(kernel, scalars, inputs, out_shapes, specs=None, out_specs=None, scratch=(), cost=0):
    in_vmem = pl.BlockSpec(memory_space=pltpu.VMEM)
    specs = specs or [in_vmem] * len(inputs)
    out_specs = out_specs or [in_vmem] * len(out_shapes)
    return pl.pallas_call(
        kernel,
        in_specs=[pl.BlockSpec(memory_space=pltpu.SMEM)] + specs,
        out_specs=out_specs,
        out_shape=out_shapes,
        scratch_shapes=list(scratch),
        compiler_params=pltpu.CompilerParams(vmem_limit_bytes=VMEM_BYTES),
        cost_estimate=pl.CostEstimate(flops=cost, bytes_accessed=0, transcendentals=0),
    )(scalars, *inputs)


def after(array, *others):
    return lax.optimization_barrier((array, *others))[0]


def on_device(leaf_maps, w_first, w_second, skel_first, skel_second):
    box = lax.axis_index("box")
    face = lax.axis_index("face")
    n_box, n_face = lax.axis_size("box"), lax.axis_size("face")
    nf = n_face - 1
    fr = leaf_maps.shape[4]
    hr = fr // 2
    k = leaf_maps.shape[5] // 3
    half = k // 2
    leaf = leaf_maps[:, 0, 0]
    scalars = jnp.stack([box % 2, box // 2 % 2, face, box % 4, box // 2, box // 4]).astype(jnp.int32)
    sds = jax.ShapeDtypeStruct
    in_hbm = pl.BlockSpec(memory_space=pltpu.HBM)

    def box_permute(array, mask):
        return lax.ppermute(array, "box", [(b, b ^ mask) for b in range(n_box)])

    def face_permute(array, step):
        pairs = [
            (b * n_face + f, b * n_face + (f + n_face - step) % n_face)
            for b in range(n_box) for f in range(n_face)
        ]
        return lax.ppermute(array, ("box", "face"), pairs)

    def over_face(array):
        return [face_permute(array, s) for s in range(1, n_face)]

    def halves(p):
        mine = pl.ds(pl.multiple_of(p * hr, hr), hr)
        other = pl.ds(pl.multiple_of((1 - p) * hr, hr), hr)
        return mine, other

    def slots_kernel(sc, skel_ref, skel2_ref, comp_out, col_out):
        q = sc[1]
        rows = lax.broadcasted_iota(jnp.int32, (k, k), 0)
        cols = lax.broadcasted_iota(jnp.int32, (k, k), 1)
        skel = jnp.broadcast_to(skel_ref[pl.ds(sc[4], 1), :].astype(F32), (k, k))
        column = jnp.sum(jnp.where(rows == cols, skel, 0.0), axis=1, keepdims=True)
        col_out[...] = column.astype(jnp.int32)
        place = skel2_ref[pl.ds(sc[5], 1), :] - q * k
        taken = jnp.where(rows == place, jnp.broadcast_to(column, (k, k)), 0.0)
        found = jnp.sum(taken, axis=0, keepdims=True).astype(jnp.int32)
        comp_out[...] = jnp.where(jnp.logical_and(place >= 0, place < k), found, -1)

    comp, skel_col = call(
        slots_kernel, scalars, [skel_first[0], skel_second[0]], [sds((1, k), jnp.int32), sds((k, 1), jnp.int32)],
        cost=SLOTS_COST,
    )

    def parts_kernel(sc, leaf_ref, end_out, side_out, *rows_outs):
        p = sc[0]
        end_out[...] = leaf_ref[:, 1 - p, :, pl.ds(pl.multiple_of(p * k, k), k)]
        side_out[...] = leaf_ref[:, 1 - p, :, 2 * k :]
        for i, rows_out in enumerate(rows_outs):
            rows_out[...] = leaf_ref[:, 2, :, i * k : (i + 1) * k]

    end_own, sides_raw, *s_rows = call(
        parts_kernel, scalars, [leaf], [sds((2, fr, k), BF16)] * 5
    )
    sides_sib = box_permute(sides_raw, 1)
    end_sib = box_permute(end_own, 1)
    s_sib = [box_permute(a, 1) for a in s_rows]

    def side_kernel(sc, own_ref, sib_ref, comp_ref, end_ref, side_out, *send_outs):
        p, q = sc[0], sc[1]
        pick_own = column_picker(comp_ref[...], p * k, k)
        pick_sib = column_picker(comp_ref[...], (1 - p) * k, k)
        side = dot(flat(own_ref[...]), pick_own) + dot(flat(sib_ref[...]), pick_sib)
        side_out[...] = side.astype(BF16).reshape(2, fr, k)
        for h, send_out in enumerate(send_outs):
            take = slice(h * hr, (h + 1) * hr)
            send_out[...] = jnp.where(p == q, end_ref[:, take, :], side_out[:, take, :])

    side, *first_send = call(
        side_kernel, scalars, [sides_raw, sides_sib, comp, end_own],
        [sds((2, fr, k), BF16)] + [sds((2, hr, k), BF16)] * 2,
    )
    first_far = [face_permute(a, s) for s in range(1, n_face) for a in first_send]

    def ends_kernel(sc, leaf_ref, comp_ref, keep_out, couple_out, slots_out, end_out):
        p = sc[0]
        pick_own = column_picker(comp_ref[...], p * k, k)
        for t in range(2):
            end_out[t, :, : 2 * k] = leaf_ref[t, p, :, : 2 * k]
            end_out[t, :, 2 * k :] = dot(leaf_ref[t, p, :, 2 * k :], pick_own).astype(BF16)
        couple = pl.ds(pl.multiple_of((1 - p) * k, k), k)
        mine, other = halves(p)
        keep_out[:, :, :k] = end_out[:, mine, couple]
        keep_out[:, :, k:] = end_out[:, mine, 2 * k :]
        couple_out[...] = end_out[:, other, couple]
        slots_out[...] = end_out[:, other, 2 * k :]

    v_keep, *v_send, end_kept = call(
        ends_kernel, after(scalars, side), [leaf, comp],
        [sds((2, hr, 2 * k), BF16)] + [sds((2, hr, k), BF16)] * 2 + [sds((2, fr, 3 * k), BF16)],
    )
    v_recv = [box_permute(a, 1) for a in v_send]

    w_one, w_two = w_first[:, 0], w_second[:, 0]
    w_one_sib = box_permute(after(w_one, side), 1)
    w_two_x = box_permute(after(w_two, side), 2)
    w_two_sib = box_permute(after(w_two, side), 1)
    w_two_x_sib = box_permute(w_two_x, 1)

    def weight_kernel(place, sc, *refs):
        out_ref = refs[-1]
        count = refs[0].shape[1]
        for i, ref in enumerate(refs[:-1]):
            take = pl.ds(pl.multiple_of(place(sc, i) * count, count), count)
            for f in range(n_face):
                @pl.when(sc[2] == f)
                def _(ref=ref, take=take, f=f):
                    out_ref[:, take, : k - f * fr] = ref[:, :, f * fr :]
                    if f > 0:
                        out_ref[:, take, k - f * fr :] = ref[:, :, : f * fr]

    (weight_one,) = call(
        functools.partial(weight_kernel, lambda sc, i: sc[0] ^ i), scalars, [w_one, w_one_sib],
        [sds((2, k, k), BF16)],
    )
    (weight_two,) = call(
        functools.partial(weight_kernel, lambda sc, i: sc[3] ^ (0, 2, 1, 3)[i]), scalars,
        [w_two, w_two_x, w_two_sib, w_two_x_sib], [sds((2, k, k), BF16)],
    )

    def rows_kernel(sc, *refs):
        owns, sibs, refs = refs[:3], refs[3:6], refs[6:]
        comp_ref, col_ref, end_ref, endsib_ref, kept_out, *outs = refs
        p, q, f = sc[0], sc[1], sc[2]
        mine, _ = halves(p)
        rest = jnp.where(p == q, endsib_ref[:, mine, :], end_ref[:, mine, :])
        for s in range(nf):
            outs[nf + s][:, :, :k] = rest
        pick_own = column_picker(comp_ref[...], p * k, k)
        pick_sib = column_picker(comp_ref[...], (1 - p) * k, k)

        def pick(slots, write):
            take_own = row_picker(slots, p * k + f * fr, fr)
            take_sib = row_picker(slots, (1 - p) * k + f * fr, fr)
            for t in range(2):
                for c in range(3):
                    own, sib = owns[c][t], sibs[c][t]
                    if c == 2:
                        own, sib = [dot(a, b).astype(BF16) for a, b in ((own, pick_own), (sib, pick_sib))]
                    write(t, c, (dot(take_own, own) + dot(take_sib, sib)).astype(BF16))

        def write_far(s, t, c, picked):
            if c < 2:
                outs[s][t, :, c * k : (c + 1) * k] = picked
            else:
                outs[nf + s][t, :, k:] = picked

        def col_half(s):
            start = (f + n_face - s - 1) % n_face * fr + p * hr
            return col_ref[pl.ds(pl.multiple_of(start, hr), hr), :]

        far = jnp.concatenate([col_half(s) for s in range(nf)], axis=0)

        @pl.when(p == q)
        def _():
            def write(t, c, picked):
                for s in range(nf):
                    write_far(s, t, c, picked[s * hr : (s + 1) * hr])

            pick(far, write)

        @pl.when(p != q)
        def _():
            def write(t, c, picked):
                kept_out[t, :, c * k : (c + 1) * k] = picked[:fr]
                for s in range(nf):
                    write_far(s, t, c, picked[fr + s * hr : fr + (s + 1) * hr])

            pick(jnp.concatenate([col_ref[pl.ds(pl.multiple_of(f * fr, fr), fr), :], far], axis=0), write)

    kept, *kept_out = call(
        rows_kernel, scalars, [*s_rows, *s_sib, comp, skel_col, end_own, end_sib],
        [sds((2, fr, 3 * k), BF16)] + [sds((2, hr, 2 * k), BF16)] * (2 * nf),
    )
    mixed_far = [face_permute(a, i + 1) for i, a in enumerate(kept_out[nf:])]

    def piece(hidden, start, count):
        return stacked(hidden[0][:, start : start + count], hidden[1][:, start : start + count])

    def iface_kernel(sc, keep_ref, couple_ref, slots_ref, w_ref, end_ref, endsib_ref, side_ref,
                     acc_out, hid_out, rows):
        p, q = sc[0], sc[1]

        @pl.when(p == q)
        def _():
            rows[:, :, :k] = couple_ref[...]
            rows[:, :, k:] = slots_ref[...]

        @pl.when(p != q)
        def _():
            rows[...] = keep_ref[...]

        both = dot(stacked(rows[0, :, :k], rows[1, :, :k]), flat(w_ref[...])).astype(BF16)
        hidden = both[:hr], both[hr:]
        hid_out[0] = hidden[0]
        hid_out[1] = hidden[1]
        left = piece(hidden, 0, fr)
        is_end = p == q
        ends = jnp.where(is_end, end_ref[...], endsib_ref[...])
        acc_out[:, :, :k] = -dot(left, flat(ends)).reshape(2, hr, k)
        acc_out[:, :, k:] = rows[:, :, k:].astype(F32) - dot(left, flat(side_ref[...])).reshape(2, hr, k)

    v_acc, v_hid = call(
        iface_kernel, scalars, [v_keep, *v_recv, weight_one, end_own, end_sib, side],
        [sds((2, hr, 2 * k), F32), sds((2, hr, k), BF16)],
        scratch=[pltpu.VMEM((2, hr, 2 * k), BF16)], cost=OWN_COST,
    )
    first_fwd = [box_permute(after(a, kept, w_two_x), 1) for a in first_far]

    def iface_far_kernel(sc, acc_ref, hid_ref, *rest):
        far, fwd = rest[: 2 * nf], rest[2 * nf : 4 * nf]
        end_out, keep_out, send_out = rest[4 * nf :]
        q = sc[1]
        is_end = sc[0] == q
        hidden = [hid_ref[0], hid_ref[1]]
        total = acc_ref[...]
        for i in range(2 * nf):
            left = piece(hidden, fr + i * hr, hr)
            mine, other = dot(left, flat(far[i][...])), dot(left, flat(fwd[i][...]))
            both = [jnp.where(is_end, mine, other), jnp.where(is_end, other, mine)]
            total = total - jnp.concatenate(both, axis=1).reshape(2, hr, 2 * k)
        total = total.astype(BF16)
        end_out[...] = total[:, :, :k]
        low, high = total[:, :, k : k + half], total[:, :, k + half :]
        keep_out[...] = jnp.where(q == 0, low, high)
        send_out[...] = jnp.where(q == 0, high, low)

    two_end, side_keep, side_send = call(
        iface_far_kernel, scalars, [v_acc, v_hid, *first_far, *first_fwd],
        [sds((2, hr, k), BF16)] + [sds((2, hr, half), BF16)] * 2,
    )

    side_x = box_permute(side_send, 2)

    def pack_kernel(sc, end_ref, keep_ref, x_ref, out_ref):
        out_ref[:, :, :k] = end_ref[...]
        out_ref[:, :, k:] = keep_ref[...] + x_ref[...]

    (two_own,) = call(
        pack_kernel, scalars, [two_end, side_keep, side_x], [sds((2, hr, k + half), BF16)]
    )
    two_x = box_permute(two_own, 2)
    two_y = over_face(two_own)
    mixed_fwd = [box_permute(after(a, two_own), 1) for a in mixed_far]

    def weighted(w_ref, rows, out_ref):
        left = jnp.concatenate([piece((w_ref[0], w_ref[1]), s * fr, fr) for s in range(n_face)], axis=1)
        for c in range(3):
            cols = slice(c * k, (c + 1) * k)
            right = rows[:, :, :, cols].reshape(n_face * 2 * fr, k)
            out_ref[:, :, cols] = dot(left, right).astype(BF16).reshape(2, k, k)

    def weighted_one_kernel(sc, w_ref, own_ref, sib_ref, side_ref, *rest):
        refs = [rest[i * nf : (i + 1) * nf] for i in range(6)]
        far, fwd = rest[: 2 * nf], rest[2 * nf : 4 * nf]
        out_ref, rows = rest[6 * nf :]
        p, q = sc[0], sc[1]
        is_end = p == q
        first_cols = pl.ds(pl.multiple_of(q * k, k), k)
        rest_cols = pl.ds(pl.multiple_of((1 - q) * k, k), k)
        rows[0, :, :, pl.ds(pl.multiple_of(p * k, k), k)] = own_ref[...]
        rows[0, :, :, pl.ds(pl.multiple_of((1 - p) * k, k), k)] = sib_ref[...]
        rows[0, :, :, 2 * k :] = side_ref[...]
        for s in range(nf):
            for h in range(2):
                take = slice(h * hr, (h + 1) * hr)
                mine, other = far[2 * s + h][...], fwd[2 * s + h][...]
                rows[s + 1, :, take, first_cols] = jnp.where(is_end, mine, other)
                rows[s + 1, :, take, 2 * k :] = jnp.where(is_end, other, mine)
            for take, parts in zip(halves(p), refs[4:]):
                rows[s + 1, :, take, rest_cols] = parts[s][:, :, :k]
        weighted(w_ref, rows, out_ref)

    (solved_one,) = call(
        weighted_one_kernel, scalars,
        [weight_one, end_own, end_sib, side, *first_far, *first_fwd, *mixed_far, *mixed_fwd],
        [sds((2, k, 3 * k), BF16)], scratch=[pltpu.VMEM((n_face, 2, fr, 3 * k), BF16)], cost=SOLVED_COST,
    )

    def join_kernel(sc, own_ref, x_ref, out_ref):
        q = sc[1]
        for ref, which in ((own_ref, q), (x_ref, 1 - q)):
            out_ref[:, :, pl.ds(pl.multiple_of(which * k, k), k)] = ref[:, :, :k]
            out_ref[:, :, pl.ds(pl.multiple_of(2 * k + which * half, half), half)] = ref[:, :, k:]

    two_shape = [sds((2, hr, 3 * k), BF16)]
    two_rows = call(join_kernel, after(scalars, weight_two), [two_own, two_x], two_shape, cost=JOIN_COST)
    two_xy = [box_permute(after(a, *two_rows), 2) for a in two_y]
    for own, other in zip(two_y, two_xy):
        two_rows += call(join_kernel, after(scalars, solved_one), [own, other], two_shape)
    two_sib = [box_permute(a, 1) for a in two_rows]

    ends_far = [face_permute(after(a, two_own), i + 1) for i, a in enumerate(kept_out[:nf])]
    ends_fwd = [box_permute(a, 1) for a in ends_far]

    def level_one_kernel(sc, end_ref, kept_ref, *refs):
        parts = [refs[i * nf : (i + 1) * nf] for i in range(4)]
        col_ref, one_ref, w_ref, hid_out, first_out, slots_out, zs = refs[4 * nf :]
        p, q, f = sc[0], sc[1], sc[2]

        @pl.when(p == q)
        def _():
            zs[...] = end_ref[...]

        @pl.when(p != q)
        def _():
            for h, take in enumerate(halves(p)):
                for part, cols, source in (
                    (parts[h], slice(2 * k, 3 * k), slice(k, 2 * k)), (parts[2 + h], slice(0, 2 * k), slice(0, 2 * k)),
                ):
                    total = kept_ref[:, take, cols]
                    for ref in part:
                        total = total + ref[:, :, source]
                    zs[:, take, cols] = total

        slots = col_ref[pl.ds(pl.multiple_of(f * fr, fr), fr), :]
        right = jnp.where(slots >= k, 1, 0)
        right = jnp.where(p == q, p, right) > 0
        lefts = [zs[t, :, :k] for t in range(2)]
        rights = [zs[t, :, k : 2 * k] for t in range(2)]
        left = stacked(*[jnp.where(right, a, b) for a, b in zip(lefts, rights)])
        nothing = jnp.zeros((fr, k), BF16)
        start = [
            jnp.concatenate([jnp.where(right, nothing, a) for a in lefts], axis=0),
            jnp.concatenate([jnp.where(right, a, nothing) for a in rights], axis=0),
            flat(zs[:, :, 2 * k :]),
        ]
        merged = [
            (start[c].astype(F32) - dot(left, flat(one_ref[:, :, c * k : (c + 1) * k]))).astype(BF16)
            for c in range(3)
        ]
        is_left = q == 0
        first_out[...] = jnp.where(is_left, merged[0], merged[1])
        slots_out[...] = merged[2]
        couple = jnp.where(is_left, merged[1], merged[0])
        second = dot(stacked(couple[:fr], couple[fr:]), flat(w_ref[...])).astype(BF16)
        for s in range(n_face):
            hid_out[s] = piece((second[:fr], second[fr:]), s * fr, fr)

    hid_two, first_two, slots_two = call(
        level_one_kernel, scalars,
        [end_kept, kept, *mixed_far, *mixed_fwd, *ends_far, *ends_fwd, skel_col, solved_one, weight_two],
        [sds((n_face, 2 * fr, 2 * fr), BF16), sds((2 * fr, k), BF16), sds((2 * fr, k), BF16)],
        scratch=[pltpu.VMEM((2, fr, 3 * k), BF16)], cost=KEEP_COST,
    )

    def level_two_kernel(sc, hid_ref, first_ref, slots_ref, *refs):
        out_ref, rows, stage, sems = refs[2 * n_face :]
        q = sc[1]
        left = jnp.concatenate([hid_ref[s] for s in range(n_face)], axis=1)
        for h, take in enumerate(halves(sc[0])):
            for s in range(n_face):
                rows[s, :, take, :] = refs[h * n_face + s][...]
        copies = []
        for c in range(3):
            first = slots_ref[...]
            if c < 2:
                first = jnp.where(q == c, first_ref[...], jnp.zeros((2 * fr, k), BF16))
            right = rows[:, :, :, c * k : (c + 1) * k].reshape(n_face * 2 * fr, k)
            stage[c] = (first.astype(F32) - dot(left, right)).astype(BF16).reshape(2, fr, k)
            copies.append(pltpu.make_async_copy(
                stage.at[c], out_ref.at[:, 0, :, pl.ds(c * k, k)], sems.at[c]
            ))
            copies[-1].start()
        for copy in copies:
            copy.wait()

    (out,) = call(
        level_two_kernel, scalars, [hid_two, first_two, slots_two, *two_rows, *two_sib],
        [sds((2, 1, fr, 3 * k), BF16)], out_specs=[in_hbm],
        scratch=[pltpu.VMEM((n_face, 2, fr, 3 * k), BF16), pltpu.VMEM((3, 2, fr, k), BF16),
                 pltpu.SemaphoreType.DMA((3,))],
    )
    return out


def solution(mesh):
    return jax.shard_map(
        on_device,
        mesh=mesh,
        in_specs=(
            P(None, None, "box", None, "face", None),
            P(None, None, "box", None),
            P(None, None, "box", None),
            P(),
            P(),
        ),
        out_specs=P(None, None, ("box", "face"), None),
        check_vma=False,
    )
```

```python
import functools

import jax
import jax.numpy as jnp
from jax import lax
from jax.experimental import pallas as pl
from jax.experimental.pallas import tpu as pltpu
from jax.sharding import PartitionSpec as P

BF16 = jnp.bfloat16
F32 = jnp.float32
VMEM_BYTES = 16 * 1024 * 1024
JOIN_COST = 300000000
SLOTS_COST = 0
OWN_COST = 700_000_000
SOLVED_COST = 800_000_000
KEEP_COST = 300_000_000


def dot(first, second):
    return jnp.dot(first, second, preferred_element_type=F32)


def stacked(real, imag):
    return jnp.concatenate(
        [jnp.concatenate([real, -imag], axis=1), jnp.concatenate([imag, real], axis=1)], axis=0
    )


def flat(array):
    return array.reshape(array.shape[0] * array.shape[1], array.shape[2])


def column_picker(index, offset, count):
    rows = lax.broadcasted_iota(jnp.int32, (count, index.shape[1]), 0) + offset
    return jnp.where(rows == index, 1.0, 0.0).astype(BF16)


def row_picker(index, offset, count):
    cols = lax.broadcasted_iota(jnp.int32, (index.shape[0], count), 1) + offset
    return jnp.where(cols == index, 1.0, 0.0).astype(BF16)


def call(kernel, scalars, inputs, out_shapes, specs=None, out_specs=None, scratch=(), cost=0):
    in_vmem = pl.BlockSpec(memory_space=pltpu.VMEM)
    specs = specs or [in_vmem] * len(inputs)
    out_specs = out_specs or [in_vmem] * len(out_shapes)
    return pl.pallas_call(
        kernel,
        in_specs=[pl.BlockSpec(memory_space=pltpu.SMEM)] + specs,
        out_specs=out_specs,
        out_shape=out_shapes,
        scratch_shapes=list(scratch),
        compiler_params=pltpu.CompilerParams(vmem_limit_bytes=VMEM_BYTES),
        cost_estimate=pl.CostEstimate(flops=cost, bytes_accessed=0, transcendentals=0),
    )(scalars, *inputs)


def after(array, *others):
    return lax.optimization_barrier((array, *others))[0]


def on_device(leaf_maps, w_first, w_second, skel_first, skel_second):
    box = lax.axis_index("box")
    face = lax.axis_index("face")
    n_box, n_face = lax.axis_size("box"), lax.axis_size("face")
    nf = n_face - 1
    fr = leaf_maps.shape[4]
    hr = fr // 2
    k = leaf_maps.shape[5] // 3
    half = k // 2
    leaf = leaf_maps[:, 0, 0]
    scalars = jnp.stack([box % 2, box // 2 % 2, face, box % 4, box // 2, box // 4]).astype(jnp.int32)
    sds = jax.ShapeDtypeStruct
    in_hbm = pl.BlockSpec(memory_space=pltpu.HBM)

    def box_permute(array, mask):
        return lax.ppermute(array, "box", [(b, b ^ mask) for b in range(n_box)])

    def face_permute(array, step):
        pairs = [
            (b * n_face + f, b * n_face + (f + n_face - step) % n_face)
            for b in range(n_box) for f in range(n_face)
        ]
        return lax.ppermute(array, ("box", "face"), pairs)

    def over_face(array):
        return [face_permute(array, s) for s in range(1, n_face)]

    def halves(p):
        mine = pl.ds(pl.multiple_of(p * hr, hr), hr)
        other = pl.ds(pl.multiple_of((1 - p) * hr, hr), hr)
        return mine, other

    def slots_kernel(sc, skel_ref, skel2_ref, comp_out, col_out):
        q = sc[1]
        rows = lax.broadcasted_iota(jnp.int32, (k, k), 0)
        cols = lax.broadcasted_iota(jnp.int32, (k, k), 1)
        skel = jnp.broadcast_to(skel_ref[pl.ds(sc[4], 1), :].astype(F32), (k, k))
        column = jnp.sum(jnp.where(rows == cols, skel, 0.0), axis=1, keepdims=True)
        col_out[...] = column.astype(jnp.int32)
        place = skel2_ref[pl.ds(sc[5], 1), :] - q * k
        taken = jnp.where(rows == place, jnp.broadcast_to(column, (k, k)), 0.0)
        found = jnp.sum(taken, axis=0, keepdims=True).astype(jnp.int32)
        comp_out[...] = jnp.where(jnp.logical_and(place >= 0, place < k), found, -1)

    comp, skel_col = call(
        slots_kernel, scalars, [skel_first[0], skel_second[0]], [sds((1, k), jnp.int32), sds((k, 1), jnp.int32)],
        cost=SLOTS_COST,
    )

    def parts_kernel(sc, leaf_ref, end_out, side_out, *rows_outs):
        p = sc[0]
        end_out[...] = leaf_ref[:, 1 - p, :, pl.ds(pl.multiple_of(p * k, k), k)]
        side_out[...] = leaf_ref[:, 1 - p, :, 2 * k :]
        for i, rows_out in enumerate(rows_outs):
            rows_out[...] = leaf_ref[:, 2, :, i * k : (i + 1) * k]

    end_own, sides_raw, *s_rows = call(
        parts_kernel, scalars, [leaf], [sds((2, fr, k), BF16)] * 5
    )
    sides_sib = box_permute(sides_raw, 1)
    end_sib = box_permute(end_own, 1)
    s_sib = [box_permute(a, 1) for a in s_rows]

    def side_kernel(sc, own_ref, sib_ref, comp_ref, end_ref, side_out, *send_outs):
        p, q = sc[0], sc[1]
        pick_own = column_picker(comp_ref[...], p * k, k)
        pick_sib = column_picker(comp_ref[...], (1 - p) * k, k)
        side = dot(flat(own_ref[...]), pick_own) + dot(flat(sib_ref[...]), pick_sib)
        side_out[...] = side.astype(BF16).reshape(2, fr, k)
        for h, send_out in enumerate(send_outs):
            take = slice(h * hr, (h + 1) * hr)
            send_out[...] = jnp.where(p == q, end_ref[:, take, :], side_out[:, take, :])

    side, *first_send = call(
        side_kernel, scalars, [sides_raw, sides_sib, comp, end_own],
        [sds((2, fr, k), BF16)] + [sds((2, hr, k), BF16)] * 2,
    )
    first_far = [face_permute(a, s) for s in range(1, n_face) for a in first_send]

    def ends_kernel(sc, leaf_ref, comp_ref, keep_out, couple_out, slots_out, end_out):
        p = sc[0]
        pick_own = column_picker(comp_ref[...], p * k, k)
        for t in range(2):
            end_out[t, :, : 2 * k] = leaf_ref[t, p, :, : 2 * k]
            end_out[t, :, 2 * k :] = dot(leaf_ref[t, p, :, 2 * k :], pick_own).astype(BF16)
        couple = pl.ds(pl.multiple_of((1 - p) * k, k), k)
        mine, other = halves(p)
        keep_out[:, :, :k] = end_out[:, mine, couple]
        keep_out[:, :, k:] = end_out[:, mine, 2 * k :]
        couple_out[...] = end_out[:, other, couple]
        slots_out[...] = end_out[:, other, 2 * k :]

    v_keep, *v_send, end_kept = call(
        ends_kernel, after(scalars, side), [leaf, comp],
        [sds((2, hr, 2 * k), BF16)] + [sds((2, hr, k), BF16)] * 2 + [sds((2, fr, 3 * k), BF16)],
    )
    v_recv = [box_permute(a, 1) for a in v_send]

    w_one, w_two = w_first[:, 0], w_second[:, 0]
    w_one_sib = box_permute(after(w_one, side), 1)
    w_two_x = box_permute(after(w_two, side), 2)
    w_two_sib = box_permute(after(w_two, side), 1)
    w_two_x_sib = box_permute(w_two_x, 1)

    def weight_kernel(place, sc, *refs):
        out_ref = refs[-1]
        count = refs[0].shape[1]
        for i, ref in enumerate(refs[:-1]):
            take = pl.ds(pl.multiple_of(place(sc, i) * count, count), count)
            for f in range(n_face):
                @pl.when(sc[2] == f)
                def _(ref=ref, take=take, f=f):
                    out_ref[:, take, : k - f * fr] = ref[:, :, f * fr :]
                    if f > 0:
                        out_ref[:, take, k - f * fr :] = ref[:, :, : f * fr]

    (weight_one,) = call(
        functools.partial(weight_kernel, lambda sc, i: sc[0] ^ i), scalars, [w_one, w_one_sib],
        [sds((2, k, k), BF16)],
    )
    (weight_two,) = call(
        functools.partial(weight_kernel, lambda sc, i: sc[3] ^ (0, 2, 1, 3)[i]), scalars,
        [w_two, w_two_x, w_two_sib, w_two_x_sib], [sds((2, k, k), BF16)],
    )

    def rows_kernel(sc, *refs):
        owns, sibs, refs = refs[:3], refs[3:6], refs[6:]
        comp_ref, col_ref, end_ref, endsib_ref, kept_out, *outs = refs
        p, q, f = sc[0], sc[1], sc[2]
        mine, _ = halves(p)
        rest = jnp.where(p == q, endsib_ref[:, mine, :], end_ref[:, mine, :])
        for s in range(nf):
            outs[nf + s][:, :, :k] = rest
        pick_own = column_picker(comp_ref[...], p * k, k)
        pick_sib = column_picker(comp_ref[...], (1 - p) * k, k)

        def pick(slots, write):
            take_own = row_picker(slots, p * k + f * fr, fr)
            take_sib = row_picker(slots, (1 - p) * k + f * fr, fr)
            for t in range(2):
                for c in range(3):
                    own, sib = owns[c][t], sibs[c][t]
                    if c == 2:
                        own, sib = [dot(a, b).astype(BF16) for a, b in ((own, pick_own), (sib, pick_sib))]
                    write(t, c, (dot(take_own, own) + dot(take_sib, sib)).astype(BF16))

        def write_far(s, t, c, picked):
            if c < 2:
                outs[s][t, :, c * k : (c + 1) * k] = picked
            else:
                outs[nf + s][t, :, k:] = picked

        def col_half(s):
            start = (f + n_face - s - 1) % n_face * fr + p * hr
            return col_ref[pl.ds(pl.multiple_of(start, hr), hr), :]

        far = jnp.concatenate([col_half(s) for s in range(nf)], axis=0)

        @pl.when(p == q)
        def _():
            def write(t, c, picked):
                for s in range(nf):
                    write_far(s, t, c, picked[s * hr : (s + 1) * hr])

            pick(far, write)

        @pl.when(p != q)
        def _():
            def write(t, c, picked):
                kept_out[t, :, c * k : (c + 1) * k] = picked[:fr]
                for s in range(nf):
                    write_far(s, t, c, picked[fr + s * hr : fr + (s + 1) * hr])

            pick(jnp.concatenate([col_ref[pl.ds(pl.multiple_of(f * fr, fr), fr), :], far], axis=0), write)

    kept, *kept_out = call(
        rows_kernel, scalars, [*s_rows, *s_sib, comp, skel_col, end_own, end_sib],
        [sds((2, fr, 3 * k), BF16)] + [sds((2, hr, 2 * k), BF16)] * (2 * nf),
    )
    mixed_far = [face_permute(a, i + 1) for i, a in enumerate(kept_out[nf:])]

    def piece(hidden, start, count):
        return stacked(hidden[0][:, start : start + count], hidden[1][:, start : start + count])

    def iface_kernel(sc, keep_ref, couple_ref, slots_ref, w_ref, end_ref, endsib_ref, side_ref,
                     acc_out, hid_out, rows):
        p, q = sc[0], sc[1]

        @pl.when(p == q)
        def _():
            rows[:, :, :k] = couple_ref[...]
            rows[:, :, k:] = slots_ref[...]

        @pl.when(p != q)
        def _():
            rows[...] = keep_ref[...]

        both = dot(stacked(rows[0, :, :k], rows[1, :, :k]), flat(w_ref[...])).astype(BF16)
        hidden = both[:hr], both[hr:]
        hid_out[0] = hidden[0]
        hid_out[1] = hidden[1]
        left = piece(hidden, 0, fr)
        is_end = p == q
        ends = jnp.where(is_end, end_ref[...], endsib_ref[...])
        acc_out[:, :, :k] = -dot(left, flat(ends)).reshape(2, hr, k)
        acc_out[:, :, k:] = rows[:, :, k:].astype(F32) - dot(left, flat(side_ref[...])).reshape(2, hr, k)

    v_acc, v_hid = call(
        iface_kernel, scalars, [v_keep, *v_recv, weight_one, end_own, end_sib, side],
        [sds((2, hr, 2 * k), F32), sds((2, hr, k), BF16)],
        scratch=[pltpu.VMEM((2, hr, 2 * k), BF16)], cost=OWN_COST,
    )
    first_fwd = [box_permute(after(a, kept, w_two_x), 1) for a in first_far]

    def iface_far_kernel(sc, acc_ref, hid_ref, *rest):
        far, fwd = rest[: 2 * nf], rest[2 * nf : 4 * nf]
        end_out, keep_out, send_out = rest[4 * nf :]
        q = sc[1]
        is_end = sc[0] == q
        hidden = [hid_ref[0], hid_ref[1]]
        total = acc_ref[...]
        for i in range(2 * nf):
            left = piece(hidden, fr + i * hr, hr)
            mine, other = dot(left, flat(far[i][...])), dot(left, flat(fwd[i][...]))
            both = [jnp.where(is_end, mine, other), jnp.where(is_end, other, mine)]
            total = total - jnp.concatenate(both, axis=1).reshape(2, hr, 2 * k)
        total = total.astype(BF16)
        end_out[...] = total[:, :, :k]
        low, high = total[:, :, k : k + half], total[:, :, k + half :]
        keep_out[...] = jnp.where(q == 0, low, high)
        send_out[...] = jnp.where(q == 0, high, low)

    two_end, side_keep, side_send = call(
        iface_far_kernel, scalars, [v_acc, v_hid, *first_far, *first_fwd],
        [sds((2, hr, k), BF16)] + [sds((2, hr, half), BF16)] * 2,
    )

    side_x = box_permute(side_send, 2)

    def pack_kernel(sc, end_ref, keep_ref, x_ref, out_ref):
        out_ref[:, :, :k] = end_ref[...]
        out_ref[:, :, k:] = keep_ref[...] + x_ref[...]

    (two_own,) = call(
        pack_kernel, scalars, [two_end, side_keep, side_x], [sds((2, hr, k + half), BF16)]
    )
    two_x = box_permute(two_own, 2)
    two_y = over_face(two_own)
    mixed_fwd = [box_permute(after(a, two_own), 1) for a in mixed_far]

    def weighted(w_ref, rows, out_ref):
        left = jnp.concatenate([piece((w_ref[0], w_ref[1]), s * fr, fr) for s in range(n_face)], axis=1)
        for c in range(3):
            cols = slice(c * k, (c + 1) * k)
            right = rows[:, :, :, cols].reshape(n_face * 2 * fr, k)
            out_ref[:, :, cols] = dot(left, right).astype(BF16).reshape(2, k, k)

    def weighted_one_kernel(sc, w_ref, own_ref, sib_ref, side_ref, *rest):
        refs = [rest[i * nf : (i + 1) * nf] for i in range(6)]
        far, fwd = rest[: 2 * nf], rest[2 * nf : 4 * nf]
        out_ref, rows = rest[6 * nf :]
        p, q = sc[0], sc[1]
        is_end = p == q
        first_cols = pl.ds(pl.multiple_of(q * k, k), k)
        rest_cols = pl.ds(pl.multiple_of((1 - q) * k, k), k)
        rows[0, :, :, pl.ds(pl.multiple_of(p * k, k), k)] = own_ref[...]
        rows[0, :, :, pl.ds(pl.multiple_of((1 - p) * k, k), k)] = sib_ref[...]
        rows[0, :, :, 2 * k :] = side_ref[...]
        for s in range(nf):
            for h in range(2):
                take = slice(h * hr, (h + 1) * hr)
                mine, other = far[2 * s + h][...], fwd[2 * s + h][...]
                rows[s + 1, :, take, first_cols] = jnp.where(is_end, mine, other)
                rows[s + 1, :, take, 2 * k :] = jnp.where(is_end, other, mine)
            for take, parts in zip(halves(p), refs[4:]):
                rows[s + 1, :, take, rest_cols] = parts[s][:, :, :k]
        weighted(w_ref, rows, out_ref)

    (solved_one,) = call(
        weighted_one_kernel, scalars,
        [weight_one, end_own, end_sib, side, *first_far, *first_fwd, *mixed_far, *mixed_fwd],
        [sds((2, k, 3 * k), BF16)], scratch=[pltpu.VMEM((n_face, 2, fr, 3 * k), BF16)], cost=SOLVED_COST,
    )

    def join_kernel(sc, own_ref, x_ref, out_ref):
        q = sc[1]
        for ref, which in ((own_ref, q), (x_ref, 1 - q)):
            out_ref[:, :, pl.ds(pl.multiple_of(which * k, k), k)] = ref[:, :, :k]
            out_ref[:, :, pl.ds(pl.multiple_of(2 * k + which * half, half), half)] = ref[:, :, k:]

    two_shape = [sds((2, hr, 3 * k), BF16)]
    two_rows = call(join_kernel, after(scalars, weight_two), [two_own, two_x], two_shape, cost=JOIN_COST)
    two_xy = [box_permute(after(a, *two_rows), 2) for a in two_y]

    def join_far_kernel(sc, own_ref, x_ref, *refs):
        join_kernel(sc, own_ref, x_ref, refs[-1])
        for h in range(2):
            refs[h][...] = refs[-1][:, :, h * 3 * half : (h + 1) * 3 * half]

    for own, other in zip(two_y, two_xy):
        two_rows += call(
            join_far_kernel, after(scalars, solved_one), [own, other], [sds((2, hr, 3 * half), BF16)] * 2,
            scratch=[pltpu.VMEM((2, hr, 3 * k), BF16)],
        )
    two_sib = [box_permute(a, 1) for a in two_rows[:1]]

    def layout_kernel(sc, own_ref, sib_ref, out_ref):
        for ref, take in zip((own_ref, sib_ref), halves(sc[0])):
            out_ref[:, take, :] = ref[...]

    (two_first,) = call(
        layout_kernel, scalars, [two_rows[0], two_sib[0]], [sds((2, fr, 3 * k), BF16)]
    )

    ends_far = [face_permute(after(a, two_own), i + 1) for i, a in enumerate(kept_out[:nf])]
    ends_fwd = [box_permute(after(a, solved_one), 1) for a in ends_far]
    two_sib += [box_permute(a, 1) for a in two_rows[1:]]

    def level_one_kernel(sc, end_ref, kept_ref, *refs):
        parts = [refs[i * nf : (i + 1) * nf] for i in range(4)]
        col_ref, one_ref, w_ref, hid_out, first_out, slots_out, zs = refs[4 * nf :]
        p, q, f = sc[0], sc[1], sc[2]

        @pl.when(p == q)
        def _():
            zs[...] = end_ref[...]

        @pl.when(p != q)
        def _():
            for h, take in enumerate(halves(p)):
                for part, cols, source in (
                    (parts[h], slice(2 * k, 3 * k), slice(k, 2 * k)), (parts[2 + h], slice(0, 2 * k), slice(0, 2 * k)),
                ):
                    total = kept_ref[:, take, cols]
                    for ref in part:
                        total = total + ref[:, :, source]
                    zs[:, take, cols] = total

        slots = col_ref[pl.ds(pl.multiple_of(f * fr, fr), fr), :]
        right = jnp.where(slots >= k, 1, 0)
        right = jnp.where(p == q, p, right) > 0
        lefts = [zs[t, :, :k] for t in range(2)]
        rights = [zs[t, :, k : 2 * k] for t in range(2)]
        left = stacked(*[jnp.where(right, a, b) for a, b in zip(lefts, rights)])
        nothing = jnp.zeros((fr, k), BF16)
        start = [
            jnp.concatenate([jnp.where(right, nothing, a) for a in lefts], axis=0),
            jnp.concatenate([jnp.where(right, a, nothing) for a in rights], axis=0),
            flat(zs[:, :, 2 * k :]),
        ]
        merged = [
            (start[c].astype(F32) - dot(left, flat(one_ref[:, :, c * k : (c + 1) * k]))).astype(BF16)
            for c in range(3)
        ]
        is_left = q == 0
        first_out[...] = jnp.where(is_left, merged[0], merged[1])
        slots_out[...] = merged[2]
        couple = jnp.where(is_left, merged[1], merged[0])
        second = dot(stacked(couple[:fr], couple[fr:]), flat(w_ref[...])).astype(BF16)
        for s in range(n_face):
            hid_out[s] = piece((second[:fr], second[fr:]), s * fr, fr)

    hid_two, first_two, slots_two = call(
        level_one_kernel, after(scalars, two_first),
        [end_kept, kept, *mixed_far, *mixed_fwd, *ends_far, *ends_fwd, skel_col, solved_one, weight_two],
        [sds((n_face, 2 * fr, 2 * fr), BF16), sds((2 * fr, k), BF16), sds((2 * fr, k), BF16)],
        scratch=[pltpu.VMEM((2, fr, 3 * k), BF16)], cost=KEEP_COST,
    )

    def level_two_kernel(sc, hid_ref, first_ref, slots_ref, near_ref, *refs):
        out_ref, rows, stage, sems = refs[4 * nf :]
        q = sc[1]
        far = jnp.concatenate([hid_ref[s] for s in range(1, n_face)], axis=1)
        for h, take in enumerate(halves(sc[0])):
            for i, ref in enumerate(refs[h * 2 * nf : (h + 1) * 2 * nf]):
                rows[i // 2, :, take, i % 2 * 3 * half : (i % 2 + 1) * 3 * half] = ref[...]
        copies = []
        for c in range(3):
            cols = slice(c * k, (c + 1) * k)
            first = slots_ref[...]
            if c < 2:
                first = jnp.where(q == c, first_ref[...], jnp.zeros((2 * fr, k), BF16))
            total = first.astype(F32) - dot(hid_ref[0], flat(near_ref[:, :, cols]))
            total = total - dot(far, rows[:, :, :, cols].reshape(nf * 2 * fr, k))
            stage[c] = total.astype(BF16).reshape(2, fr, k)
            for t in range(2):
                copies.append(pltpu.make_async_copy(
                    stage.at[c, t], out_ref.at[t, 0, :, pl.ds(c * k, k)], sems.at[c, t]
                ))
                copies[-1].start()
        for copy in copies:
            copy.wait()

    (out,) = call(
        level_two_kernel, scalars, [hid_two, first_two, slots_two, two_first, *two_rows[1:], *two_sib[1:]],
        [sds((2, 1, fr, 3 * k), BF16)], out_specs=[in_hbm],
        scratch=[pltpu.VMEM((nf, 2, fr, 3 * k), BF16), pltpu.VMEM((3, 2, fr, k), BF16),
                 pltpu.SemaphoreType.DMA((3, 2))],
    )
    return out


def solution(mesh):
    return jax.shard_map(
        on_device,
        mesh=mesh,
        in_specs=(
            P(None, None, "box", None, "face", None),
            P(None, None, "box", None),
            P(None, None, "box", None),
            P(),
            P(),
        ),
        out_specs=P(None, None, ("box", "face"), None),
        check_vma=False,
    )
```

```python
import functools

import jax
import jax.numpy as jnp
from jax import lax
from jax.experimental import pallas as pl
from jax.experimental.pallas import tpu as pltpu
from jax.sharding import PartitionSpec as P

BF16 = jnp.bfloat16
F32 = jnp.float32
VMEM_BYTES = 16 * 1024 * 1024
JOIN_COST = 300000000
SLOTS_COST = 0
OWN_COST = 700_000_000
SOLVED_COST = 800_000_000
KEEP_COST = 300_000_000


def dot(first, second):
    return jnp.dot(first, second, preferred_element_type=F32)


def stacked(real, imag):
    return jnp.concatenate(
        [jnp.concatenate([real, -imag], axis=1), jnp.concatenate([imag, real], axis=1)], axis=0
    )


def flat(array):
    return array.reshape(array.shape[0] * array.shape[1], array.shape[2])


def column_picker(index, offset, count):
    rows = lax.broadcasted_iota(jnp.int32, (count, index.shape[1]), 0) + offset
    return jnp.where(rows == index, 1.0, 0.0).astype(BF16)


def row_picker(index, offset, count):
    cols = lax.broadcasted_iota(jnp.int32, (index.shape[0], count), 1) + offset
    return jnp.where(cols == index, 1.0, 0.0).astype(BF16)


def call(kernel, scalars, inputs, out_shapes, specs=None, out_specs=None, scratch=(), cost=0):
    in_vmem = pl.BlockSpec(memory_space=pltpu.VMEM)
    specs = specs or [in_vmem] * len(inputs)
    out_specs = out_specs or [in_vmem] * len(out_shapes)
    return pl.pallas_call(
        kernel,
        in_specs=[pl.BlockSpec(memory_space=pltpu.SMEM)] + specs,
        out_specs=out_specs,
        out_shape=out_shapes,
        scratch_shapes=list(scratch),
        compiler_params=pltpu.CompilerParams(vmem_limit_bytes=VMEM_BYTES),
        cost_estimate=pl.CostEstimate(flops=cost, bytes_accessed=0, transcendentals=0),
    )(scalars, *inputs)


def after(array, *others):
    return lax.optimization_barrier((array, *others))[0]


def on_device(leaf_maps, w_first, w_second, skel_first, skel_second):
    box = lax.axis_index("box")
    face = lax.axis_index("face")
    n_box, n_face = lax.axis_size("box"), lax.axis_size("face")
    nf = n_face - 1
    fr = leaf_maps.shape[4]
    hr = fr // 2
    k = leaf_maps.shape[5] // 3
    half = k // 2
    leaf = leaf_maps[:, 0, 0]
    scalars = jnp.stack([box % 2, box // 2 % 2, face, box % 4, box // 2, box // 4]).astype(jnp.int32)
    sds = jax.ShapeDtypeStruct
    in_hbm = pl.BlockSpec(memory_space=pltpu.HBM)

    def box_permute(array, mask):
        return lax.ppermute(array, "box", [(b, b ^ mask) for b in range(n_box)])

    def face_permute(array, step):
        pairs = [
            (b * n_face + f, b * n_face + (f + n_face - step) % n_face)
            for b in range(n_box) for f in range(n_face)
        ]
        return lax.ppermute(array, ("box", "face"), pairs)

    def over_face(array):
        return [face_permute(array, s) for s in range(1, n_face)]

    def halves(p):
        mine = pl.ds(pl.multiple_of(p * hr, hr), hr)
        other = pl.ds(pl.multiple_of((1 - p) * hr, hr), hr)
        return mine, other

    def slots_kernel(sc, skel_ref, skel2_ref, comp_out, col_out):
        q = sc[1]
        rows = lax.broadcasted_iota(jnp.int32, (k, k), 0)
        cols = lax.broadcasted_iota(jnp.int32, (k, k), 1)
        skel = jnp.broadcast_to(skel_ref[pl.ds(sc[4], 1), :].astype(F32), (k, k))
        column = jnp.sum(jnp.where(rows == cols, skel, 0.0), axis=1, keepdims=True)
        col_out[...] = column.astype(jnp.int32)
        place = skel2_ref[pl.ds(sc[5], 1), :] - q * k
        taken = jnp.where(rows == place, jnp.broadcast_to(column, (k, k)), 0.0)
        found = jnp.sum(taken, axis=0, keepdims=True).astype(jnp.int32)
        comp_out[...] = jnp.where(jnp.logical_and(place >= 0, place < k), found, -1)

    comp, skel_col = call(
        slots_kernel, scalars, [skel_first[0], skel_second[0]], [sds((1, k), jnp.int32), sds((k, 1), jnp.int32)],
        cost=SLOTS_COST,
    )

    def parts_kernel(sc, leaf_ref, end_out, side_out, *rows_outs):
        p = sc[0]
        end_out[...] = leaf_ref[:, 1 - p, :, pl.ds(pl.multiple_of(p * k, k), k)]
        side_out[...] = leaf_ref[:, 1 - p, :, 2 * k :]
        for i, rows_out in enumerate(rows_outs):
            rows_out[...] = leaf_ref[:, 2, :, i * k : (i + 1) * k]

    end_own, sides_raw, *s_rows = call(
        parts_kernel, scalars, [leaf], [sds((2, fr, k), BF16)] * 5
    )
    sides_sib = box_permute(sides_raw, 1)
    end_sib = box_permute(end_own, 1)
    s_sib = [box_permute(a, 1) for a in s_rows]

    def side_kernel(sc, own_ref, sib_ref, comp_ref, end_ref, side_out, *send_outs):
        p, q = sc[0], sc[1]
        pick_own = column_picker(comp_ref[...], p * k, k)
        pick_sib = column_picker(comp_ref[...], (1 - p) * k, k)
        side = dot(flat(own_ref[...]), pick_own) + dot(flat(sib_ref[...]), pick_sib)
        side_out[...] = side.astype(BF16).reshape(2, fr, k)
        for h, send_out in enumerate(send_outs):
            take = slice(h * hr, (h + 1) * hr)
            send_out[...] = jnp.where(p == q, end_ref[:, take, :], side_out[:, take, :])

    side, *first_send = call(
        side_kernel, scalars, [sides_raw, sides_sib, comp, end_own],
        [sds((2, fr, k), BF16)] + [sds((2, hr, k), BF16)] * 2,
    )
    first_far = [face_permute(a, s) for s in range(1, n_face) for a in first_send]

    def ends_kernel(sc, leaf_ref, comp_ref, keep_out, couple_out, slots_out, end_out):
        p = sc[0]
        pick_own = column_picker(comp_ref[...], p * k, k)
        for t in range(2):
            end_out[t, :, : 2 * k] = leaf_ref[t, p, :, : 2 * k]
            end_out[t, :, 2 * k :] = dot(leaf_ref[t, p, :, 2 * k :], pick_own).astype(BF16)
        couple = pl.ds(pl.multiple_of((1 - p) * k, k), k)
        mine, other = halves(p)
        keep_out[:, :, :k] = end_out[:, mine, couple]
        keep_out[:, :, k:] = end_out[:, mine, 2 * k :]
        couple_out[...] = end_out[:, other, couple]
        slots_out[...] = end_out[:, other, 2 * k :]

    v_keep, *v_send, end_kept = call(
        ends_kernel, after(scalars, side), [leaf, comp],
        [sds((2, hr, 2 * k), BF16)] + [sds((2, hr, k), BF16)] * 2 + [sds((2, fr, 3 * k), BF16)],
    )
    v_recv = [box_permute(a, 1) for a in v_send]

    w_one, w_two = w_first[:, 0], w_second[:, 0]
    w_one_sib = box_permute(after(w_one, side), 1)
    w_two_x = box_permute(after(w_two, side), 2)
    w_two_sib = box_permute(after(w_two, side), 1)
    w_two_x_sib = box_permute(w_two_x, 1)

    def weight_kernel(place, sc, *refs):
        out_ref = refs[-1]
        count = refs[0].shape[1]
        for i, ref in enumerate(refs[:-1]):
            take = pl.ds(pl.multiple_of(place(sc, i) * count, count), count)
            for f in range(n_face):
                @pl.when(sc[2] == f)
                def _(ref=ref, take=take, f=f):
                    out_ref[:, take, : k - f * fr] = ref[:, :, f * fr :]
                    if f > 0:
                        out_ref[:, take, k - f * fr :] = ref[:, :, : f * fr]

    (weight_one,) = call(
        functools.partial(weight_kernel, lambda sc, i: sc[0] ^ i), scalars, [w_one, w_one_sib],
        [sds((2, k, k), BF16)],
    )
    (weight_two,) = call(
        functools.partial(weight_kernel, lambda sc, i: sc[3] ^ (0, 2, 1, 3)[i]), scalars,
        [w_two, w_two_x, w_two_sib, w_two_x_sib], [sds((2, k, k), BF16)],
    )

    def rows_kernel(sc, *refs):
        owns, sibs, refs = refs[:3], refs[3:6], refs[6:]
        comp_ref, col_ref, end_ref, endsib_ref, kept_out, *outs = refs
        p, q, f = sc[0], sc[1], sc[2]
        mine, _ = halves(p)
        rest = jnp.where(p == q, endsib_ref[:, mine, :], end_ref[:, mine, :])
        for s in range(nf):
            outs[nf + s][:, :, :k] = rest
        pick_own = column_picker(comp_ref[...], p * k, k)
        pick_sib = column_picker(comp_ref[...], (1 - p) * k, k)

        def pick(slots, write):
            take_own = row_picker(slots, p * k + f * fr, fr)
            take_sib = row_picker(slots, (1 - p) * k + f * fr, fr)
            for t in range(2):
                for c in range(3):
                    own, sib = owns[c][t], sibs[c][t]
                    if c == 2:
                        own, sib = [dot(a, b).astype(BF16) for a, b in ((own, pick_own), (sib, pick_sib))]
                    write(t, c, (dot(take_own, own) + dot(take_sib, sib)).astype(BF16))

        def write_far(s, t, c, picked):
            if c < 2:
                outs[s][t, :, c * k : (c + 1) * k] = picked
            else:
                outs[nf + s][t, :, k:] = picked

        def col_half(s):
            start = (f + n_face - s - 1) % n_face * fr + p * hr
            return col_ref[pl.ds(pl.multiple_of(start, hr), hr), :]

        far = jnp.concatenate([col_half(s) for s in range(nf)], axis=0)

        @pl.when(p == q)
        def _():
            def write(t, c, picked):
                for s in range(nf):
                    write_far(s, t, c, picked[s * hr : (s + 1) * hr])

            pick(far, write)

        @pl.when(p != q)
        def _():
            def write(t, c, picked):
                kept_out[t, :, c * k : (c + 1) * k] = picked[:fr]
                for s in range(nf):
                    write_far(s, t, c, picked[fr + s * hr : fr + (s + 1) * hr])

            pick(jnp.concatenate([col_ref[pl.ds(pl.multiple_of(f * fr, fr), fr), :], far], axis=0), write)

    kept, *kept_out = call(
        rows_kernel, scalars, [*s_rows, *s_sib, comp, skel_col, end_own, end_sib],
        [sds((2, fr, 3 * k), BF16)] + [sds((2, hr, 2 * k), BF16)] * (2 * nf),
    )
    mixed_far = [face_permute(a, i + 1) for i, a in enumerate(kept_out[nf:])]

    def piece(hidden, start, count):
        return stacked(hidden[0][:, start : start + count], hidden[1][:, start : start + count])

    def iface_kernel(sc, keep_ref, couple_ref, slots_ref, w_ref, end_ref, endsib_ref, side_ref,
                     acc_out, hid_out, rows):
        p, q = sc[0], sc[1]

        @pl.when(p == q)
        def _():
            rows[:, :, :k] = couple_ref[...]
            rows[:, :, k:] = slots_ref[...]

        @pl.when(p != q)
        def _():
            rows[...] = keep_ref[...]

        both = dot(stacked(rows[0, :, :k], rows[1, :, :k]), flat(w_ref[...])).astype(BF16)
        hidden = both[:hr], both[hr:]
        hid_out[0] = hidden[0]
        hid_out[1] = hidden[1]
        left = piece(hidden, 0, fr)
        is_end = p == q
        ends = jnp.where(is_end, end_ref[...], endsib_ref[...])
        acc_out[:, :, :k] = -dot(left, flat(ends)).reshape(2, hr, k)
        acc_out[:, :, k:] = rows[:, :, k:].astype(F32) - dot(left, flat(side_ref[...])).reshape(2, hr, k)

    v_acc, v_hid = call(
        iface_kernel, scalars, [v_keep, *v_recv, weight_one, end_own, end_sib, side],
        [sds((2, hr, 2 * k), F32), sds((2, hr, k), BF16)],
        scratch=[pltpu.VMEM((2, hr, 2 * k), BF16)], cost=OWN_COST,
    )
    first_fwd = [box_permute(after(a, kept, w_two_x), 1) for a in first_far]

    def iface_far_kernel(sc, acc_ref, hid_ref, *rest):
        far, fwd = rest[: 2 * nf], rest[2 * nf : 4 * nf]
        end_out, keep_out, send_out = rest[4 * nf :]
        q = sc[1]
        is_end = sc[0] == q
        hidden = [hid_ref[0], hid_ref[1]]
        total = acc_ref[...]
        for i in range(2 * nf):
            left = piece(hidden, fr + i * hr, hr)
            mine, other = dot(left, flat(far[i][...])), dot(left, flat(fwd[i][...]))
            both = [jnp.where(is_end, mine, other), jnp.where(is_end, other, mine)]
            total = total - jnp.concatenate(both, axis=1).reshape(2, hr, 2 * k)
        total = total.astype(BF16)
        end_out[...] = total[:, :, :k]
        low, high = total[:, :, k : k + half], total[:, :, k + half :]
        keep_out[...] = jnp.where(q == 0, low, high)
        send_out[...] = jnp.where(q == 0, high, low)

    two_end, side_keep, side_send = call(
        iface_far_kernel, scalars, [v_acc, v_hid, *first_far, *first_fwd],
        [sds((2, hr, k), BF16)] + [sds((2, hr, half), BF16)] * 2,
    )

    side_x = box_permute(side_send, 2)

    def pack_kernel(sc, end_ref, keep_ref, x_ref, out_ref):
        out_ref[:, :, :k] = end_ref[...]
        out_ref[:, :, k:] = keep_ref[...] + x_ref[...]

    (two_own,) = call(
        pack_kernel, scalars, [two_end, side_keep, side_x], [sds((2, hr, k + half), BF16)]
    )
    two_x = box_permute(two_own, 2)
    two_y = over_face(two_own)
    mixed_fwd = [box_permute(after(a, two_own), 1) for a in mixed_far]

    def weighted(w_ref, rows, out_ref):
        left = jnp.concatenate([piece((w_ref[0], w_ref[1]), s * fr, fr) for s in range(n_face)], axis=1)
        for c in range(3):
            cols = slice(c * k, (c + 1) * k)
            right = rows[:, :, :, cols].reshape(n_face * 2 * fr, k)
            out_ref[:, :, cols] = dot(left, right).astype(BF16).reshape(2, k, k)

    def weighted_one_kernel(sc, w_ref, own_ref, sib_ref, side_ref, *rest):
        refs = [rest[i * nf : (i + 1) * nf] for i in range(6)]
        far, fwd = rest[: 2 * nf], rest[2 * nf : 4 * nf]
        out_ref, rows = rest[6 * nf :]
        p, q = sc[0], sc[1]
        is_end = p == q
        first_cols = pl.ds(pl.multiple_of(q * k, k), k)
        rest_cols = pl.ds(pl.multiple_of((1 - q) * k, k), k)
        rows[0, :, :, pl.ds(pl.multiple_of(p * k, k), k)] = own_ref[...]
        rows[0, :, :, pl.ds(pl.multiple_of((1 - p) * k, k), k)] = sib_ref[...]
        rows[0, :, :, 2 * k :] = side_ref[...]
        for s in range(nf):
            for h in range(2):
                take = slice(h * hr, (h + 1) * hr)
                mine, other = far[2 * s + h][...], fwd[2 * s + h][...]
                rows[s + 1, :, take, first_cols] = jnp.where(is_end, mine, other)
                rows[s + 1, :, take, 2 * k :] = jnp.where(is_end, other, mine)
            for take, parts in zip(halves(p), refs[4:]):
                rows[s + 1, :, take, rest_cols] = parts[s][:, :, :k]
        weighted(w_ref, rows, out_ref)

    (solved_one,) = call(
        weighted_one_kernel, scalars,
        [weight_one, end_own, end_sib, side, *first_far, *first_fwd, *mixed_far, *mixed_fwd],
        [sds((2, k, 3 * k), BF16)], scratch=[pltpu.VMEM((n_face, 2, fr, 3 * k), BF16)], cost=SOLVED_COST,
    )

    def join_kernel(sc, own_ref, x_ref, out_ref):
        q = sc[1]
        for ref, which in ((own_ref, q), (x_ref, 1 - q)):
            out_ref[:, :, pl.ds(pl.multiple_of(which * k, k), k)] = ref[:, :, :k]
            out_ref[:, :, pl.ds(pl.multiple_of(2 * k + which * half, half), half)] = ref[:, :, k:]

    two_shape = [sds((2, hr, 3 * k), BF16)]
    two_rows = call(join_kernel, after(scalars, weight_two), [two_own, two_x], two_shape, cost=JOIN_COST)
    two_xy = [box_permute(after(a, *two_rows), 2) for a in two_y]

    def join_far_kernel(sc, own_ref, x_ref, *refs):
        join_kernel(sc, own_ref, x_ref, refs[-1])
        for h in range(2):
            refs[h][...] = refs[-1][:, :, h * 3 * half : (h + 1) * 3 * half]

    for own, other in zip(two_y, two_xy):
        two_rows += call(
            join_far_kernel, after(scalars, solved_one), [own, other], [sds((2, hr, 3 * half), BF16)] * 2,
            scratch=[pltpu.VMEM((2, hr, 3 * k), BF16)],
        )
    two_sib = [box_permute(a, 1) for a in two_rows[:1]]

    ends_far = [face_permute(after(a, two_own), i + 1) for i, a in enumerate(kept_out[:nf])]
    ends_fwd = [box_permute(after(a, solved_one), 1) for a in ends_far]
    two_sib += [box_permute(a, 1) for a in two_rows[1:]]

    def level_one_kernel(sc, end_ref, kept_ref, *refs):
        parts = [refs[i * nf : (i + 1) * nf] for i in range(4)]
        col_ref, one_ref, w_ref, hid_out, first_out, slots_out, zs = refs[4 * nf :]
        p, q, f = sc[0], sc[1], sc[2]

        @pl.when(p == q)
        def _():
            zs[...] = end_ref[...]

        @pl.when(p != q)
        def _():
            for h, take in enumerate(halves(p)):
                for part, cols, source in (
                    (parts[h], slice(2 * k, 3 * k), slice(k, 2 * k)), (parts[2 + h], slice(0, 2 * k), slice(0, 2 * k)),
                ):
                    total = kept_ref[:, take, cols]
                    for ref in part:
                        total = total + ref[:, :, source]
                    zs[:, take, cols] = total

        slots = col_ref[pl.ds(pl.multiple_of(f * fr, fr), fr), :]
        right = jnp.where(slots >= k, 1, 0)
        right = jnp.where(p == q, p, right) > 0
        lefts = [zs[t, :, :k] for t in range(2)]
        rights = [zs[t, :, k : 2 * k] for t in range(2)]
        left = stacked(*[jnp.where(right, a, b) for a, b in zip(lefts, rights)])
        nothing = jnp.zeros((fr, k), BF16)
        start = [
            jnp.concatenate([jnp.where(right, nothing, a) for a in lefts], axis=0),
            jnp.concatenate([jnp.where(right, a, nothing) for a in rights], axis=0),
            flat(zs[:, :, 2 * k :]),
        ]
        merged = [
            (start[c].astype(F32) - dot(left, flat(one_ref[:, :, c * k : (c + 1) * k]))).astype(BF16)
            for c in range(3)
        ]
        is_left = q == 0
        first_out[...] = jnp.where(is_left, merged[0], merged[1])
        slots_out[...] = merged[2]
        couple = jnp.where(is_left, merged[1], merged[0])
        second = dot(stacked(couple[:fr], couple[fr:]), flat(w_ref[...])).astype(BF16)
        for s in range(n_face):
            hid_out[s] = piece((second[:fr], second[fr:]), s * fr, fr)

    hid_two, first_two, slots_two = call(
        level_one_kernel, scalars,
        [end_kept, kept, *mixed_far, *mixed_fwd, *ends_far, *ends_fwd, skel_col, solved_one, weight_two],
        [sds((n_face, 2 * fr, 2 * fr), BF16), sds((2 * fr, k), BF16), sds((2 * fr, k), BF16)],
        scratch=[pltpu.VMEM((2, fr, 3 * k), BF16)], cost=KEEP_COST,
    )

    def level_two_kernel(sc, hid_ref, first_ref, slots_ref, *refs):
        mine, other = refs[: 1 + 2 * nf], refs[1 + 2 * nf : 2 + 4 * nf]
        out_ref, rows, stage, sems = refs[2 + 4 * nf :]
        q = sc[1]
        left = jnp.concatenate([hid_ref[s] for s in range(n_face)], axis=1)
        for take, parts in zip(halves(sc[0]), (mine, other)):
            rows[0, :, take, :] = parts[0][...]
            for i, ref in enumerate(parts[1:]):
                rows[1 + i // 2, :, take, i % 2 * 3 * half : (i % 2 + 1) * 3 * half] = ref[...]
        copies = []
        for c in range(3):
            first = slots_ref[...]
            if c < 2:
                first = jnp.where(q == c, first_ref[...], jnp.zeros((2 * fr, k), BF16))
            right = rows[:, :, :, c * k : (c + 1) * k].reshape(n_face * 2 * fr, k)
            stage[c] = (first.astype(F32) - dot(left, right)).astype(BF16).reshape(2, fr, k)
            for t in range(2):
                copies.append(pltpu.make_async_copy(
                    stage.at[c, t], out_ref.at[t, 0, :, pl.ds(c * k, k)], sems.at[c, t]
                ))
                copies[-1].start()
        for copy in copies:
            copy.wait()

    (out,) = call(
        level_two_kernel, scalars, [hid_two, first_two, slots_two, *two_rows, *two_sib],
        [sds((2, 1, fr, 3 * k), BF16)], out_specs=[in_hbm],
        scratch=[pltpu.VMEM((n_face, 2, fr, 3 * k), BF16), pltpu.VMEM((3, 2, fr, k), BF16),
                 pltpu.SemaphoreType.DMA((3, 2))],
    )
    return out


def solution(mesh):
    return jax.shard_map(
        on_device,
        mesh=mesh,
        in_specs=(
            P(None, None, "box", None, "face", None),
            P(None, None, "box", None),
            P(None, None, "box", None),
            P(),
            P(),
        ),
        out_specs=P(None, None, ("box", "face"), None),
        check_vma=False,
    )
```

```python
import functools

import jax
import jax.numpy as jnp
from jax import lax
from jax.experimental import pallas as pl
from jax.experimental.pallas import tpu as pltpu
from jax.sharding import PartitionSpec as P

BF16 = jnp.bfloat16
F32 = jnp.float32
VMEM_BYTES = 16 * 1024 * 1024
JOIN_COST = 300000000
SLOTS_COST = 0
OWN_COST = 700_000_000
SOLVED_COST = 500_000_000
KEEP_COST = 300_000_000


def dot(first, second):
    return jnp.dot(first, second, preferred_element_type=F32)


def stacked(real, imag):
    return jnp.concatenate(
        [jnp.concatenate([real, -imag], axis=1), jnp.concatenate([imag, real], axis=1)], axis=0
    )


def flat(array):
    return array.reshape(array.shape[0] * array.shape[1], array.shape[2])


def column_picker(index, offset, count):
    rows = lax.broadcasted_iota(jnp.int32, (count, index.shape[1]), 0) + offset
    return jnp.where(rows == index, 1.0, 0.0).astype(BF16)


def row_picker(index, offset, count):
    cols = lax.broadcasted_iota(jnp.int32, (index.shape[0], count), 1) + offset
    return jnp.where(cols == index, 1.0, 0.0).astype(BF16)


def call(kernel, scalars, inputs, out_shapes, specs=None, out_specs=None, scratch=(), cost=0):
    in_vmem = pl.BlockSpec(memory_space=pltpu.VMEM)
    specs = specs or [in_vmem] * len(inputs)
    out_specs = out_specs or [in_vmem] * len(out_shapes)
    return pl.pallas_call(
        kernel,
        in_specs=[pl.BlockSpec(memory_space=pltpu.SMEM)] + specs,
        out_specs=out_specs,
        out_shape=out_shapes,
        scratch_shapes=list(scratch),
        compiler_params=pltpu.CompilerParams(vmem_limit_bytes=VMEM_BYTES),
        cost_estimate=pl.CostEstimate(flops=cost, bytes_accessed=0, transcendentals=0),
    )(scalars, *inputs)


def after(array, *others):
    return lax.optimization_barrier((array, *others))[0]


def on_device(leaf_maps, w_first, w_second, skel_first, skel_second):
    box = lax.axis_index("box")
    face = lax.axis_index("face")
    n_box, n_face = lax.axis_size("box"), lax.axis_size("face")
    nf = n_face - 1
    fr = leaf_maps.shape[4]
    hr = fr // 2
    k = leaf_maps.shape[5] // 3
    half = k // 2
    leaf = leaf_maps[:, 0, 0]
    scalars = jnp.stack([box % 2, box // 2 % 2, face, box % 4, box // 2, box // 4]).astype(jnp.int32)
    sds = jax.ShapeDtypeStruct
    in_hbm = pl.BlockSpec(memory_space=pltpu.HBM)

    def box_permute(array, mask):
        return lax.ppermute(array, "box", [(b, b ^ mask) for b in range(n_box)])

    def face_permute(array, step):
        pairs = [
            (b * n_face + f, b * n_face + (f + n_face - step) % n_face)
            for b in range(n_box) for f in range(n_face)
        ]
        return lax.ppermute(array, ("box", "face"), pairs)

    def over_face(array):
        return [face_permute(array, s) for s in range(1, n_face)]

    def halves(p):
        mine = pl.ds(pl.multiple_of(p * hr, hr), hr)
        other = pl.ds(pl.multiple_of((1 - p) * hr, hr), hr)
        return mine, other

    def slots_kernel(sc, skel_ref, skel2_ref, comp_out, col_out):
        q = sc[1]
        rows = lax.broadcasted_iota(jnp.int32, (k, k), 0)
        cols = lax.broadcasted_iota(jnp.int32, (k, k), 1)
        skel = jnp.broadcast_to(skel_ref[pl.ds(sc[4], 1), :].astype(F32), (k, k))
        column = jnp.sum(jnp.where(rows == cols, skel, 0.0), axis=1, keepdims=True)
        col_out[...] = column.astype(jnp.int32)
        place = skel2_ref[pl.ds(sc[5], 1), :] - q * k
        taken = jnp.where(rows == place, jnp.broadcast_to(column, (k, k)), 0.0)
        found = jnp.sum(taken, axis=0, keepdims=True).astype(jnp.int32)
        comp_out[...] = jnp.where(jnp.logical_and(place >= 0, place < k), found, -1)

    comp, skel_col = call(
        slots_kernel, scalars, [skel_first[0], skel_second[0]], [sds((1, k), jnp.int32), sds((k, 1), jnp.int32)],
        cost=SLOTS_COST,
    )

    def parts_kernel(sc, leaf_ref, end_out, side_out, *rows_outs):
        p = sc[0]
        end_out[...] = leaf_ref[:, 1 - p, :, pl.ds(pl.multiple_of(p * k, k), k)]
        side_out[...] = leaf_ref[:, 1 - p, :, 2 * k :]
        for i, rows_out in enumerate(rows_outs):
            rows_out[...] = leaf_ref[:, 2, :, i * k : (i + 1) * k]

    end_own, sides_raw, *s_rows = call(
        parts_kernel, scalars, [leaf], [sds((2, fr, k), BF16)] * 5
    )
    sides_sib = box_permute(sides_raw, 1)
    end_sib = box_permute(end_own, 1)
    s_sib = [box_permute(a, 1) for a in s_rows]

    def side_kernel(sc, own_ref, sib_ref, comp_ref, end_ref, side_out, *send_outs):
        p, q = sc[0], sc[1]
        pick_own = column_picker(comp_ref[...], p * k, k)
        pick_sib = column_picker(comp_ref[...], (1 - p) * k, k)
        side = dot(flat(own_ref[...]), pick_own) + dot(flat(sib_ref[...]), pick_sib)
        side_out[...] = side.astype(BF16).reshape(2, fr, k)
        for h, send_out in enumerate(send_outs):
            take = slice(h * hr, (h + 1) * hr)
            send_out[...] = jnp.where(p == q, end_ref[:, take, :], side_out[:, take, :])

    side, *first_send = call(
        side_kernel, scalars, [sides_raw, sides_sib, comp, end_own],
        [sds((2, fr, k), BF16)] + [sds((2, hr, k), BF16)] * 2,
    )
    first_far = [face_permute(a, s) for s in range(1, n_face) for a in first_send]

    def ends_kernel(sc, leaf_ref, comp_ref, keep_out, couple_out, slots_out, end_out):
        p = sc[0]
        pick_own = column_picker(comp_ref[...], p * k, k)
        for t in range(2):
            end_out[t, :, : 2 * k] = leaf_ref[t, p, :, : 2 * k]
            end_out[t, :, 2 * k :] = dot(leaf_ref[t, p, :, 2 * k :], pick_own).astype(BF16)
        couple = pl.ds(pl.multiple_of((1 - p) * k, k), k)
        mine, other = halves(p)
        keep_out[:, :, :k] = end_out[:, mine, couple]
        keep_out[:, :, k:] = end_out[:, mine, 2 * k :]
        couple_out[...] = end_out[:, other, couple]
        slots_out[...] = end_out[:, other, 2 * k :]

    v_keep, *v_send, end_kept = call(
        ends_kernel, after(scalars, side), [leaf, comp],
        [sds((2, hr, 2 * k), BF16)] + [sds((2, hr, k), BF16)] * 2 + [sds((2, fr, 3 * k), BF16)],
    )
    v_recv = [box_permute(a, 1) for a in v_send]

    w_one, w_two = w_first[:, 0], w_second[:, 0]
    w_one_sib = box_permute(after(w_one, side), 1)
    w_two_x = box_permute(after(w_two, side), 2)
    w_two_sib = box_permute(after(w_two, side), 1)
    w_two_x_sib = box_permute(w_two_x, 1)

    def weight_kernel(place, sc, *refs):
        out_ref = refs[-1]
        count = refs[0].shape[1]
        for i, ref in enumerate(refs[:-1]):
            take = pl.ds(pl.multiple_of(place(sc, i) * count, count), count)
            for f in range(n_face):
                @pl.when(sc[2] == f)
                def _(ref=ref, take=take, f=f):
                    out_ref[:, take, : k - f * fr] = ref[:, :, f * fr :]
                    if f > 0:
                        out_ref[:, take, k - f * fr :] = ref[:, :, : f * fr]

    (weight_one,) = call(
        functools.partial(weight_kernel, lambda sc, i: sc[0] ^ i), scalars, [w_one, w_one_sib],
        [sds((2, k, k), BF16)],
    )
    (weight_two,) = call(
        functools.partial(weight_kernel, lambda sc, i: sc[3] ^ (0, 2, 1, 3)[i]), scalars,
        [w_two, w_two_x, w_two_sib, w_two_x_sib], [sds((2, k, k), BF16)],
    )

    def rows_kernel(sc, *refs):
        owns, sibs, refs = refs[:3], refs[3:6], refs[6:]
        comp_ref, col_ref, end_ref, endsib_ref, kept_out, *outs = refs
        p, q, f = sc[0], sc[1], sc[2]
        mine, _ = halves(p)
        rest = jnp.where(p == q, endsib_ref[:, mine, :], end_ref[:, mine, :])
        for s in range(nf):
            outs[nf + s][:, :, :k] = rest
        pick_own = column_picker(comp_ref[...], p * k, k)
        pick_sib = column_picker(comp_ref[...], (1 - p) * k, k)

        def pick(slots, write):
            take_own = row_picker(slots, p * k + f * fr, fr)
            take_sib = row_picker(slots, (1 - p) * k + f * fr, fr)
            for t in range(2):
                for c in range(3):
                    own, sib = owns[c][t], sibs[c][t]
                    if c == 2:
                        own, sib = [dot(a, b).astype(BF16) for a, b in ((own, pick_own), (sib, pick_sib))]
                    write(t, c, (dot(take_own, own) + dot(take_sib, sib)).astype(BF16))

        def write_far(s, t, c, picked):
            if c < 2:
                outs[s][t, :, c * k : (c + 1) * k] = picked
            else:
                outs[nf + s][t, :, k:] = picked

        def col_half(s):
            start = (f + n_face - s - 1) % n_face * fr + p * hr
            return col_ref[pl.ds(pl.multiple_of(start, hr), hr), :]

        far = jnp.concatenate([col_half(s) for s in range(nf)], axis=0)

        @pl.when(p == q)
        def _():
            def write(t, c, picked):
                for s in range(nf):
                    write_far(s, t, c, picked[s * hr : (s + 1) * hr])

            pick(far, write)

        @pl.when(p != q)
        def _():
            def write(t, c, picked):
                kept_out[t, :, c * k : (c + 1) * k] = picked[:fr]
                for s in range(nf):
                    write_far(s, t, c, picked[fr + s * hr : fr + (s + 1) * hr])

            pick(jnp.concatenate([col_ref[pl.ds(pl.multiple_of(f * fr, fr), fr), :], far], axis=0), write)

    kept, *kept_out = call(
        rows_kernel, scalars, [*s_rows, *s_sib, comp, skel_col, end_own, end_sib],
        [sds((2, fr, 3 * k), BF16)] + [sds((2, hr, 2 * k), BF16)] * (2 * nf),
    )
    mixed_far = [face_permute(a, i + 1) for i, a in enumerate(kept_out[nf:])]

    def piece(hidden, start, count):
        return stacked(hidden[0][:, start : start + count], hidden[1][:, start : start + count])

    def iface_kernel(sc, keep_ref, couple_ref, slots_ref, w_ref, end_ref, endsib_ref, side_ref,
                     acc_out, hid_out, rows):
        p, q = sc[0], sc[1]

        @pl.when(p == q)
        def _():
            rows[:, :, :k] = couple_ref[...]
            rows[:, :, k:] = slots_ref[...]

        @pl.when(p != q)
        def _():
            rows[...] = keep_ref[...]

        both = dot(stacked(rows[0, :, :k], rows[1, :, :k]), flat(w_ref[...])).astype(BF16)
        hidden = both[:hr], both[hr:]
        hid_out[0] = hidden[0]
        hid_out[1] = hidden[1]
        left = piece(hidden, 0, fr)
        is_end = p == q
        ends = jnp.where(is_end, end_ref[...], endsib_ref[...])
        acc_out[:, :, :k] = -dot(left, flat(ends)).reshape(2, hr, k)
        acc_out[:, :, k:] = rows[:, :, k:].astype(F32) - dot(left, flat(side_ref[...])).reshape(2, hr, k)

    v_acc, v_hid = call(
        iface_kernel, scalars, [v_keep, *v_recv, weight_one, end_own, end_sib, side],
        [sds((2, hr, 2 * k), F32), sds((2, hr, k), BF16)],
        scratch=[pltpu.VMEM((2, hr, 2 * k), BF16)], cost=OWN_COST,
    )
    first_fwd = [box_permute(after(a, kept, w_two_x), 1) for a in first_far]

    def iface_far_kernel(sc, acc_ref, hid_ref, *rest):
        far, fwd = rest[: 2 * nf], rest[2 * nf : 4 * nf]
        end_out, keep_out, send_out = rest[4 * nf :]
        q = sc[1]
        is_end = sc[0] == q
        hidden = [hid_ref[0], hid_ref[1]]
        total = acc_ref[...]
        for i in range(2 * nf):
            left = piece(hidden, fr + i * hr, hr)
            mine, other = dot(left, flat(far[i][...])), dot(left, flat(fwd[i][...]))
            both = [jnp.where(is_end, mine, other), jnp.where(is_end, other, mine)]
            total = total - jnp.concatenate(both, axis=1).reshape(2, hr, 2 * k)
        total = total.astype(BF16)
        end_out[...] = total[:, :, :k]
        low, high = total[:, :, k : k + half], total[:, :, k + half :]
        keep_out[...] = jnp.where(q == 0, low, high)
        send_out[...] = jnp.where(q == 0, high, low)

    two_end, side_keep, side_send = call(
        iface_far_kernel, scalars, [v_acc, v_hid, *first_far, *first_fwd],
        [sds((2, hr, k), BF16)] + [sds((2, hr, half), BF16)] * 2,
    )

    side_x = box_permute(side_send, 2)

    def pack_kernel(sc, end_ref, keep_ref, x_ref, out_ref):
        out_ref[:, :, :k] = end_ref[...]
        out_ref[:, :, k:] = keep_ref[...] + x_ref[...]

    (two_own,) = call(
        pack_kernel, scalars, [two_end, side_keep, side_x], [sds((2, hr, k + half), BF16)]
    )
    two_x = box_permute(two_own, 2)
    two_y = over_face(two_own)
    mixed_fwd = [box_permute(after(a, two_own), 1) for a in mixed_far]

    def weighted(w_ref, rows, out_ref):
        left = jnp.concatenate([piece((w_ref[0], w_ref[1]), s * fr, fr) for s in range(n_face)], axis=1)
        for c in range(3):
            cols = slice(c * k, (c + 1) * k)
            right = rows[:, :, :, cols].reshape(n_face * 2 * fr, k)
            out_ref[:, :, cols] = dot(left, right).astype(BF16).reshape(2, k, k)

    def weighted_one_kernel(sc, w_ref, own_ref, sib_ref, side_ref, *rest):
        refs = [rest[i * nf : (i + 1) * nf] for i in range(6)]
        far, fwd = rest[: 2 * nf], rest[2 * nf : 4 * nf]
        out_ref, rows = rest[6 * nf :]
        p, q = sc[0], sc[1]
        is_end = p == q
        first_cols = pl.ds(pl.multiple_of(q * k, k), k)
        rest_cols = pl.ds(pl.multiple_of((1 - q) * k, k), k)
        rows[0, :, :, pl.ds(pl.multiple_of(p * k, k), k)] = own_ref[...]
        rows[0, :, :, pl.ds(pl.multiple_of((1 - p) * k, k), k)] = sib_ref[...]
        rows[0, :, :, 2 * k :] = side_ref[...]
        for s in range(nf):
            for h in range(2):
                take = slice(h * hr, (h + 1) * hr)
                mine, other = far[2 * s + h][...], fwd[2 * s + h][...]
                rows[s + 1, :, take, first_cols] = jnp.where(is_end, mine, other)
                rows[s + 1, :, take, 2 * k :] = jnp.where(is_end, other, mine)
            for take, parts in zip(halves(p), refs[4:]):
                rows[s + 1, :, take, rest_cols] = parts[s][:, :, :k]
        weighted(w_ref, rows, out_ref)

    (solved_one,) = call(
        weighted_one_kernel, scalars,
        [weight_one, end_own, end_sib, side, *first_far, *first_fwd, *mixed_far, *mixed_fwd],
        [sds((2, k, 3 * k), BF16)], scratch=[pltpu.VMEM((n_face, 2, fr, 3 * k), BF16)], cost=SOLVED_COST,
    )

    def join_kernel(sc, own_ref, x_ref, out_ref):
        q = sc[1]
        for ref, which in ((own_ref, q), (x_ref, 1 - q)):
            out_ref[:, :, pl.ds(pl.multiple_of(which * k, k), k)] = ref[:, :, :k]
            out_ref[:, :, pl.ds(pl.multiple_of(2 * k + which * half, half), half)] = ref[:, :, k:]

    two_shape = [sds((2, hr, 3 * k), BF16)]
    two_rows = call(join_kernel, after(scalars, weight_two), [two_own, two_x], two_shape, cost=JOIN_COST)
    two_xy = [box_permute(after(a, *two_rows), 2) for a in two_y]

    def join_far_kernel(sc, own_ref, x_ref, *refs):
        join_kernel(sc, own_ref, x_ref, refs[-1])
        for h in range(2):
            refs[h][...] = refs[-1][:, :, h * 3 * half : (h + 1) * 3 * half]

    for own, other in zip(two_y, two_xy):
        two_rows += call(
            join_far_kernel, after(scalars, solved_one), [own, other], [sds((2, hr, 3 * half), BF16)] * 2,
            scratch=[pltpu.VMEM((2, hr, 3 * k), BF16)],
        )
    two_sib = [box_permute(a, 1) for a in two_rows[:1]]

    ends_far = [face_permute(after(a, two_own), i + 1) for i, a in enumerate(kept_out[:nf])]
    ends_fwd = [box_permute(after(a, solved_one), 1) for a in ends_far]
    two_sib += [box_permute(a, 1) for a in two_rows[1:]]

    def level_one_kernel(sc, end_ref, kept_ref, *refs):
        parts = [refs[i * nf : (i + 1) * nf] for i in range(4)]
        col_ref, one_ref, w_ref, hid_out, first_out, slots_out, zs = refs[4 * nf :]
        p, q, f = sc[0], sc[1], sc[2]

        @pl.when(p == q)
        def _():
            zs[...] = end_ref[...]

        @pl.when(p != q)
        def _():
            for h, take in enumerate(halves(p)):
                for part, cols, source in (
                    (parts[h], slice(2 * k, 3 * k), slice(k, 2 * k)), (parts[2 + h], slice(0, 2 * k), slice(0, 2 * k)),
                ):
                    total = kept_ref[:, take, cols]
                    for ref in part:
                        total = total + ref[:, :, source]
                    zs[:, take, cols] = total

        slots = col_ref[pl.ds(pl.multiple_of(f * fr, fr), fr), :]
        right = jnp.where(slots >= k, 1, 0)
        right = jnp.where(p == q, p, right) > 0
        lefts = [zs[t, :, :k] for t in range(2)]
        rights = [zs[t, :, k : 2 * k] for t in range(2)]
        left = stacked(*[jnp.where(right, a, b) for a, b in zip(lefts, rights)])
        nothing = jnp.zeros((fr, k), BF16)
        start = [
            jnp.concatenate([jnp.where(right, nothing, a) for a in lefts], axis=0),
            jnp.concatenate([jnp.where(right, a, nothing) for a in rights], axis=0),
            flat(zs[:, :, 2 * k :]),
        ]
        merged = [
            (start[c].astype(F32) - dot(left, flat(one_ref[:, :, c * k : (c + 1) * k]))).astype(BF16)
            for c in range(3)
        ]
        is_left = q == 0
        first_out[...] = jnp.where(is_left, merged[0], merged[1])
        slots_out[...] = merged[2]
        couple = jnp.where(is_left, merged[1], merged[0])
        second = dot(stacked(couple[:fr], couple[fr:]), flat(w_ref[...])).astype(BF16)
        for s in range(n_face):
            hid_out[s] = piece((second[:fr], second[fr:]), s * fr, fr)

    hid_two, first_two, slots_two = call(
        level_one_kernel, scalars,
        [end_kept, kept, *mixed_far, *mixed_fwd, *ends_far, *ends_fwd, skel_col, solved_one, weight_two],
        [sds((n_face, 2 * fr, 2 * fr), BF16), sds((2 * fr, k), BF16), sds((2 * fr, k), BF16)],
        scratch=[pltpu.VMEM((2, fr, 3 * k), BF16)], cost=KEEP_COST,
    )

    def level_two_kernel(sc, hid_ref, first_ref, slots_ref, *refs):
        mine, other = refs[: 1 + 2 * nf], refs[1 + 2 * nf : 2 + 4 * nf]
        out_ref, rows, stage, sems = refs[2 + 4 * nf :]
        q = sc[1]
        left = jnp.concatenate([hid_ref[s] for s in range(n_face)], axis=1)
        for take, parts in zip(halves(sc[0]), (mine, other)):
            rows[0, :, take, :] = parts[0][...]
            for i, ref in enumerate(parts[1:]):
                rows[1 + i // 2, :, take, i % 2 * 3 * half : (i % 2 + 1) * 3 * half] = ref[...]
        copies = []
        for c in range(3):
            first = slots_ref[...]
            if c < 2:
                first = jnp.where(q == c, first_ref[...], jnp.zeros((2 * fr, k), BF16))
            right = rows[:, :, :, c * k : (c + 1) * k].reshape(n_face * 2 * fr, k)
            stage[c] = (first.astype(F32) - dot(left, right)).astype(BF16).reshape(2, fr, k)
            for t in range(2):
                copies.append(pltpu.make_async_copy(
                    stage.at[c, t], out_ref.at[t, 0, :, pl.ds(c * k, k)], sems.at[c, t]
                ))
                copies[-1].start()
        for copy in copies:
            copy.wait()

    (out,) = call(
        level_two_kernel, scalars, [hid_two, first_two, slots_two, *two_rows, *two_sib],
        [sds((2, 1, fr, 3 * k), BF16)], out_specs=[in_hbm],
        scratch=[pltpu.VMEM((n_face, 2, fr, 3 * k), BF16), pltpu.VMEM((3, 2, fr, k), BF16),
                 pltpu.SemaphoreType.DMA((3, 2))],
    )
    return out


def solution(mesh):
    return jax.shard_map(
        on_device,
        mesh=mesh,
        in_specs=(
            P(None, None, "box", None, "face", None),
            P(None, None, "box", None),
            P(None, None, "box", None),
            P(),
            P(),
        ),
        out_specs=P(None, None, ("box", "face"), None),
        check_vma=False,
    )
```

```python
import functools

import jax
import jax.numpy as jnp
from jax import lax
from jax.experimental import pallas as pl
from jax.experimental.pallas import tpu as pltpu
from jax.sharding import PartitionSpec as P

BF16 = jnp.bfloat16
F32 = jnp.float32
VMEM_BYTES = 16 * 1024 * 1024
JOIN_COST = 300000000
SLOTS_COST = 0
OWN_COST = 700_000_000
SOLVED_COST = 500_000_000
KEEP_COST = 0
HALF_COST = 3_200_000_000


def dot(first, second):
    return jnp.dot(first, second, preferred_element_type=F32)


def stacked(real, imag):
    return jnp.concatenate(
        [jnp.concatenate([real, -imag], axis=1), jnp.concatenate([imag, real], axis=1)], axis=0
    )


def flat(array):
    return array.reshape(array.shape[0] * array.shape[1], array.shape[2])


def column_picker(index, offset, count):
    rows = lax.broadcasted_iota(jnp.int32, (count, index.shape[1]), 0) + offset
    return jnp.where(rows == index, 1.0, 0.0).astype(BF16)


def row_picker(index, offset, count):
    cols = lax.broadcasted_iota(jnp.int32, (index.shape[0], count), 1) + offset
    return jnp.where(cols == index, 1.0, 0.0).astype(BF16)


def call(kernel, scalars, inputs, out_shapes, specs=None, out_specs=None, scratch=(), cost=0):
    in_vmem = pl.BlockSpec(memory_space=pltpu.VMEM)
    specs = specs or [in_vmem] * len(inputs)
    out_specs = out_specs or [in_vmem] * len(out_shapes)
    return pl.pallas_call(
        kernel,
        in_specs=[pl.BlockSpec(memory_space=pltpu.SMEM)] + specs,
        out_specs=out_specs,
        out_shape=out_shapes,
        scratch_shapes=list(scratch),
        compiler_params=pltpu.CompilerParams(vmem_limit_bytes=VMEM_BYTES),
        cost_estimate=pl.CostEstimate(flops=cost, bytes_accessed=0, transcendentals=0),
    )(scalars, *inputs)


def after(array, *others):
    return lax.optimization_barrier((array, *others))[0]


def on_device(leaf_maps, w_first, w_second, skel_first, skel_second):
    box = lax.axis_index("box")
    face = lax.axis_index("face")
    n_box, n_face = lax.axis_size("box"), lax.axis_size("face")
    nf = n_face - 1
    fr = leaf_maps.shape[4]
    hr = fr // 2
    k = leaf_maps.shape[5] // 3
    half = k // 2
    leaf = leaf_maps[:, 0, 0]
    scalars = jnp.stack([box % 2, box // 2 % 2, face, box % 4, box // 2, box // 4]).astype(jnp.int32)
    sds = jax.ShapeDtypeStruct
    in_hbm = pl.BlockSpec(memory_space=pltpu.HBM)

    def box_permute(array, mask):
        return lax.ppermute(array, "box", [(b, b ^ mask) for b in range(n_box)])

    def face_permute(array, step):
        pairs = [
            (b * n_face + f, b * n_face + (f + n_face - step) % n_face)
            for b in range(n_box) for f in range(n_face)
        ]
        return lax.ppermute(array, ("box", "face"), pairs)

    def over_face(array):
        return [face_permute(array, s) for s in range(1, n_face)]

    def halves(p):
        mine = pl.ds(pl.multiple_of(p * hr, hr), hr)
        other = pl.ds(pl.multiple_of((1 - p) * hr, hr), hr)
        return mine, other

    def slots_kernel(sc, skel_ref, skel2_ref, comp_out, col_out):
        q = sc[1]
        rows = lax.broadcasted_iota(jnp.int32, (k, k), 0)
        cols = lax.broadcasted_iota(jnp.int32, (k, k), 1)
        skel = jnp.broadcast_to(skel_ref[pl.ds(sc[4], 1), :].astype(F32), (k, k))
        column = jnp.sum(jnp.where(rows == cols, skel, 0.0), axis=1, keepdims=True)
        col_out[...] = column.astype(jnp.int32)
        place = skel2_ref[pl.ds(sc[5], 1), :] - q * k
        taken = jnp.where(rows == place, jnp.broadcast_to(column, (k, k)), 0.0)
        found = jnp.sum(taken, axis=0, keepdims=True).astype(jnp.int32)
        comp_out[...] = jnp.where(jnp.logical_and(place >= 0, place < k), found, -1)

    comp, skel_col = call(
        slots_kernel, scalars, [skel_first[0], skel_second[0]], [sds((1, k), jnp.int32), sds((k, 1), jnp.int32)],
        cost=SLOTS_COST,
    )

    def parts_kernel(sc, leaf_ref, end_out, side_out, *rows_outs):
        p = sc[0]
        end_out[...] = leaf_ref[:, 1 - p, :, pl.ds(pl.multiple_of(p * k, k), k)]
        side_out[...] = leaf_ref[:, 1 - p, :, 2 * k :]
        for i, rows_out in enumerate(rows_outs):
            rows_out[...] = leaf_ref[:, 2, :, i * k : (i + 1) * k]

    end_own, sides_raw, *s_rows = call(
        parts_kernel, scalars, [leaf], [sds((2, fr, k), BF16)] * 5
    )
    sides_sib = box_permute(sides_raw, 1)
    end_sib = box_permute(end_own, 1)
    s_sib = [box_permute(a, 1) for a in s_rows]

    def side_kernel(sc, own_ref, sib_ref, comp_ref, end_ref, side_out, *send_outs):
        p, q = sc[0], sc[1]
        pick_own = column_picker(comp_ref[...], p * k, k)
        pick_sib = column_picker(comp_ref[...], (1 - p) * k, k)
        side = dot(flat(own_ref[...]), pick_own) + dot(flat(sib_ref[...]), pick_sib)
        side_out[...] = side.astype(BF16).reshape(2, fr, k)
        for h, send_out in enumerate(send_outs):
            take = slice(h * hr, (h + 1) * hr)
            send_out[...] = jnp.where(p == q, end_ref[:, take, :], side_out[:, take, :])

    side, *first_send = call(
        side_kernel, scalars, [sides_raw, sides_sib, comp, end_own],
        [sds((2, fr, k), BF16)] + [sds((2, hr, k), BF16)] * 2,
    )
    first_far = [face_permute(a, s) for s in range(1, n_face) for a in first_send]

    def ends_kernel(sc, leaf_ref, comp_ref, keep_out, couple_out, slots_out, end_out):
        p = sc[0]
        pick_own = column_picker(comp_ref[...], p * k, k)
        for t in range(2):
            end_out[t, :, : 2 * k] = leaf_ref[t, p, :, : 2 * k]
            end_out[t, :, 2 * k :] = dot(leaf_ref[t, p, :, 2 * k :], pick_own).astype(BF16)
        couple = pl.ds(pl.multiple_of((1 - p) * k, k), k)
        mine, other = halves(p)
        keep_out[:, :, :k] = end_out[:, mine, couple]
        keep_out[:, :, k:] = end_out[:, mine, 2 * k :]
        couple_out[...] = end_out[:, other, couple]
        slots_out[...] = end_out[:, other, 2 * k :]

    v_keep, *v_send, end_kept = call(
        ends_kernel, after(scalars, side), [leaf, comp],
        [sds((2, hr, 2 * k), BF16)] + [sds((2, hr, k), BF16)] * 2 + [sds((2, fr, 3 * k), BF16)],
    )
    v_recv = [box_permute(a, 1) for a in v_send]

    w_one, w_two = w_first[:, 0], w_second[:, 0]
    w_one_sib = box_permute(after(w_one, side), 1)
    w_two_x = box_permute(after(w_two, side), 2)
    w_two_sib = box_permute(after(w_two, side), 1)
    w_two_x_sib = box_permute(w_two_x, 1)

    def weight_kernel(place, sc, *refs):
        out_ref = refs[-1]
        count = refs[0].shape[1]
        for i, ref in enumerate(refs[:-1]):
            take = pl.ds(pl.multiple_of(place(sc, i) * count, count), count)
            for f in range(n_face):
                @pl.when(sc[2] == f)
                def _(ref=ref, take=take, f=f):
                    out_ref[:, take, : k - f * fr] = ref[:, :, f * fr :]
                    if f > 0:
                        out_ref[:, take, k - f * fr :] = ref[:, :, : f * fr]

    (weight_one,) = call(
        functools.partial(weight_kernel, lambda sc, i: sc[0] ^ i), scalars, [w_one, w_one_sib],
        [sds((2, k, k), BF16)],
    )
    (weight_two,) = call(
        functools.partial(weight_kernel, lambda sc, i: sc[3] ^ (0, 2, 1, 3)[i]), scalars,
        [w_two, w_two_x, w_two_sib, w_two_x_sib], [sds((2, k, k), BF16)],
    )

    def rows_kernel(sc, *refs):
        owns, sibs, refs = refs[:3], refs[3:6], refs[6:]
        comp_ref, col_ref, end_ref, endsib_ref, kept_out, *outs = refs
        p, q, f = sc[0], sc[1], sc[2]
        mine, _ = halves(p)
        rest = jnp.where(p == q, endsib_ref[:, mine, :], end_ref[:, mine, :])
        for s in range(nf):
            outs[nf + s][:, :, :k] = rest
        pick_own = column_picker(comp_ref[...], p * k, k)
        pick_sib = column_picker(comp_ref[...], (1 - p) * k, k)

        def pick(slots, write):
            take_own = row_picker(slots, p * k + f * fr, fr)
            take_sib = row_picker(slots, (1 - p) * k + f * fr, fr)
            for t in range(2):
                for c in range(3):
                    own, sib = owns[c][t], sibs[c][t]
                    if c == 2:
                        own, sib = [dot(a, b).astype(BF16) for a, b in ((own, pick_own), (sib, pick_sib))]
                    write(t, c, (dot(take_own, own) + dot(take_sib, sib)).astype(BF16))

        def write_far(s, t, c, picked):
            if c == 0:
                outs[nf + s][t, :, k:] = picked
            else:
                outs[(c - 1) * 2 * nf + s][t] = picked

        def col_half(s):
            start = (f + n_face - s - 1) % n_face * fr + p * hr
            return col_ref[pl.ds(pl.multiple_of(start, hr), hr), :]

        far = jnp.concatenate([col_half(s) for s in range(nf)], axis=0)

        @pl.when(p == q)
        def _():
            def write(t, c, picked):
                for s in range(nf):
                    write_far(s, t, c, picked[s * hr : (s + 1) * hr])

            pick(far, write)

        @pl.when(p != q)
        def _():
            def write(t, c, picked):
                kept_out[t, :, c * k : (c + 1) * k] = picked[:fr]
                for s in range(nf):
                    write_far(s, t, c, picked[fr + s * hr : fr + (s + 1) * hr])

            pick(jnp.concatenate([col_ref[pl.ds(pl.multiple_of(f * fr, fr), fr), :], far], axis=0), write)

    kept, *kept_out = call(
        rows_kernel, scalars, [*s_rows, *s_sib, comp, skel_col, end_own, end_sib],
        [sds((2, fr, 3 * k), BF16)]
        + [sds((2, hr, width), BF16) for width in (k, 2 * k, k) for _ in range(nf)],
    )
    mixed_far = [face_permute(a, i + 1) for i, a in enumerate(kept_out[nf : 2 * nf])]

    def piece(hidden, start, count):
        return stacked(hidden[0][:, start : start + count], hidden[1][:, start : start + count])

    def iface_kernel(sc, keep_ref, couple_ref, slots_ref, w_ref, end_ref, endsib_ref, side_ref,
                     acc_out, hid_out, rows):
        p, q = sc[0], sc[1]

        @pl.when(p == q)
        def _():
            rows[:, :, :k] = couple_ref[...]
            rows[:, :, k:] = slots_ref[...]

        @pl.when(p != q)
        def _():
            rows[...] = keep_ref[...]

        both = dot(stacked(rows[0, :, :k], rows[1, :, :k]), flat(w_ref[...])).astype(BF16)
        hidden = both[:hr], both[hr:]
        hid_out[0] = hidden[0]
        hid_out[1] = hidden[1]
        left = piece(hidden, 0, fr)
        is_end = p == q
        ends = jnp.where(is_end, end_ref[...], endsib_ref[...])
        acc_out[:, :, :k] = -dot(left, flat(ends)).reshape(2, hr, k)
        acc_out[:, :, k:] = rows[:, :, k:].astype(F32) - dot(left, flat(side_ref[...])).reshape(2, hr, k)

    v_acc, v_hid = call(
        iface_kernel, scalars, [v_keep, *v_recv, weight_one, end_own, end_sib, side],
        [sds((2, hr, 2 * k), F32), sds((2, hr, k), BF16)],
        scratch=[pltpu.VMEM((2, hr, 2 * k), BF16)], cost=OWN_COST,
    )
    first_fwd = [box_permute(after(a, kept, w_two_x), 1) for a in first_far]

    def iface_far_kernel(sc, acc_ref, hid_ref, *rest):
        far, fwd = rest[: 2 * nf], rest[2 * nf : 4 * nf]
        end_out, keep_out, send_out = rest[4 * nf :]
        q = sc[1]
        is_end = sc[0] == q
        hidden = [hid_ref[0], hid_ref[1]]
        total = acc_ref[...]
        for i in range(2 * nf):
            left = piece(hidden, fr + i * hr, hr)
            mine, other = dot(left, flat(far[i][...])), dot(left, flat(fwd[i][...]))
            both = [jnp.where(is_end, mine, other), jnp.where(is_end, other, mine)]
            total = total - jnp.concatenate(both, axis=1).reshape(2, hr, 2 * k)
        total = total.astype(BF16)
        end_out[...] = total[:, :, :k]
        low, high = total[:, :, k : k + half], total[:, :, k + half :]
        keep_out[...] = jnp.where(q == 0, low, high)
        send_out[...] = jnp.where(q == 0, high, low)

    two_end, side_keep, side_send = call(
        iface_far_kernel, scalars, [v_acc, v_hid, *first_far, *first_fwd],
        [sds((2, hr, k), BF16)] + [sds((2, hr, half), BF16)] * 2,
    )

    side_x = box_permute(side_send, 2)

    def pack_kernel(sc, end_ref, keep_ref, x_ref, out_ref):
        out_ref[:, :, :k] = end_ref[...]
        out_ref[:, :, k:] = keep_ref[...] + x_ref[...]

    (two_own,) = call(
        pack_kernel, scalars, [two_end, side_keep, side_x], [sds((2, hr, k + half), BF16)]
    )
    two_x = box_permute(two_own, 2)
    two_y = over_face(two_own)
    mixed_fwd = [box_permute(after(a, two_own), 1) for a in mixed_far]

    def weighted(w_ref, rows, out_ref):
        left = jnp.concatenate([piece((w_ref[0], w_ref[1]), s * fr, fr) for s in range(n_face)], axis=1)
        for c in range(3):
            cols = slice(c * k, (c + 1) * k)
            right = rows[:, :, :, cols].reshape(n_face * 2 * fr, k)
            out_ref[:, :, cols] = dot(left, right).astype(BF16).reshape(2, k, k)

    def weighted_one_kernel(sc, w_ref, own_ref, sib_ref, side_ref, *rest):
        refs = [rest[i * nf : (i + 1) * nf] for i in range(6)]
        far, fwd = rest[: 2 * nf], rest[2 * nf : 4 * nf]
        out_ref, rows = rest[6 * nf :]
        p, q = sc[0], sc[1]
        is_end = p == q
        first_cols = pl.ds(pl.multiple_of(q * k, k), k)
        rest_cols = pl.ds(pl.multiple_of((1 - q) * k, k), k)
        rows[0, :, :, pl.ds(pl.multiple_of(p * k, k), k)] = own_ref[...]
        rows[0, :, :, pl.ds(pl.multiple_of((1 - p) * k, k), k)] = sib_ref[...]
        rows[0, :, :, 2 * k :] = side_ref[...]
        for s in range(nf):
            for h in range(2):
                take = slice(h * hr, (h + 1) * hr)
                mine, other = far[2 * s + h][...], fwd[2 * s + h][...]
                rows[s + 1, :, take, first_cols] = jnp.where(is_end, mine, other)
                rows[s + 1, :, take, 2 * k :] = jnp.where(is_end, other, mine)
            for take, parts in zip(halves(p), refs[4:]):
                rows[s + 1, :, take, rest_cols] = parts[s][:, :, :k]
        weighted(w_ref, rows, out_ref)

    (solved_one,) = call(
        weighted_one_kernel, scalars,
        [weight_one, end_own, end_sib, side, *first_far, *first_fwd, *mixed_far, *mixed_fwd],
        [sds((2, k, 3 * k), BF16)], scratch=[pltpu.VMEM((n_face, 2, fr, 3 * k), BF16)], cost=SOLVED_COST,
    )

    def join_kernel(sc, own_ref, x_ref, out_ref):
        q = sc[1]
        for ref, which in ((own_ref, q), (x_ref, 1 - q)):
            out_ref[:, :, pl.ds(pl.multiple_of(which * k, k), k)] = ref[:, :, :k]
            out_ref[:, :, pl.ds(pl.multiple_of(2 * k + which * half, half), half)] = ref[:, :, k:]

    two_shape = [sds((2, hr, 3 * k), BF16)]
    two_rows = call(join_kernel, after(scalars, weight_two), [two_own, two_x], two_shape, cost=JOIN_COST)
    two_xy = [box_permute(after(a, *two_rows), 2) for a in two_y]

    def join_far_kernel(sc, own_ref, x_ref, *refs):
        join_kernel(sc, own_ref, x_ref, refs[-1])
        for h in range(2):
            refs[h][...] = refs[-1][:, :, h * 3 * half : (h + 1) * 3 * half]

    for own, other in zip(two_y, two_xy):
        two_rows += call(
            join_far_kernel, after(scalars, solved_one), [own, other], [sds((2, hr, 3 * half), BF16)] * 2,
            scratch=[pltpu.VMEM((2, hr, 3 * k), BF16)],
        )
    two_sib = [box_permute(a, 1) for a in two_rows[:1]]

    ends_far = [face_permute(after(a, two_own), i + 1) for i, a in enumerate(kept_out[:nf])]
    ends_fwd = [box_permute(after(a, solved_one), 1) for a in ends_far]
    slots_far = [face_permute(after(a, two_own), i + 1) for i, a in enumerate(kept_out[2 * nf :])]
    two_sib += [box_permute(a, 1) for a in two_rows[1:]]

    def whole_rows(sc, out_ref, base, end_ref, kept_ref, pieces):
        p, q = sc[0], sc[1]

        @pl.when(p == q)
        def _():
            for _, _, cols, _ in pieces:
                out_ref[:, :, cols] = end_ref[:, :, slice(cols.start + base, cols.stop + base)]

        @pl.when(p != q)
        def _():
            for far, fwd, cols, source in pieces:
                for take, parts in zip(halves(p), (far, fwd)):
                    total = kept_ref[:, take, cols.start + base : cols.stop + base]
                    for part in parts:
                        total = total + part[:, :, source]
                    out_ref[:, take, cols] = total

    def level_one_kernel(sc, end_ref, kept_ref, *refs):
        parts = [refs[i * nf : (i + 1) * nf] for i in range(4)]
        col_ref, one_ref, w_ref, hid_out, first_out, sub_out, zs = refs[4 * nf :]
        p, q, f = sc[0], sc[1], sc[2]
        whole_rows(sc, zs, 0, end_ref, kept_ref, [
            (parts[0], parts[1], slice(0, k), slice(k, 2 * k)), (parts[2], parts[3], slice(k, 2 * k), slice(0, k)),
        ])
        slots = col_ref[pl.ds(pl.multiple_of(f * fr, fr), fr), :]
        right = jnp.where(slots >= k, 1, 0)
        right = jnp.where(p == q, p, right) > 0
        lefts = [zs[t, :, :k] for t in range(2)]
        rights = [zs[t, :, k : 2 * k] for t in range(2)]
        left = stacked(*[jnp.where(right, a, b) for a, b in zip(lefts, rights)])
        nothing = jnp.zeros((fr, k), BF16)
        start = [
            jnp.concatenate([jnp.where(right, nothing, a) for a in lefts], axis=0),
            jnp.concatenate([jnp.where(right, a, nothing) for a in rights], axis=0),
        ]
        merged = [
            (start[c].astype(F32) - dot(left, flat(one_ref[:, :, c * k : (c + 1) * k]))).astype(BF16)
            for c in range(2)
        ]
        sub_out[...] = dot(left, flat(one_ref[:, :, 2 * k :]))
        is_left = q == 0
        first_out[...] = jnp.where(is_left, merged[0], merged[1])
        couple = jnp.where(is_left, merged[1], merged[0])
        second = dot(stacked(couple[:fr], couple[fr:]), flat(w_ref[...])).astype(BF16)
        for s in range(n_face):
            hid_out[s] = piece((second[:fr], second[fr:]), s * fr, fr)

    hid_two, first_two, sub_one = call(
        level_one_kernel, scalars,
        [end_kept, kept, *mixed_far, *mixed_fwd, *ends_far, *ends_fwd, skel_col, solved_one, weight_two],
        [sds((n_face, 2 * fr, 2 * fr), BF16), sds((2 * fr, k), BF16), sds((2 * fr, k), F32)],
        scratch=[pltpu.VMEM((2, fr, 2 * k), BF16)], cost=KEEP_COST,
    )
    slots_fwd = [box_permute(after(a, hid_two), 1) for a in slots_far]

    def slots_half_kernel(sc, kept_ref, *refs):
        mine, _ = halves(sc[0])
        total = kept_ref[:, mine, 2 * k :]
        for ref in refs[:nf]:
            total = total + ref[...]
        refs[nf][...] = total

    (slots_half,) = call(
        slots_half_kernel, after(scalars, hid_two), [kept, *slots_far], [sds((2, hr, k), BF16)], cost=HALF_COST
    )

    def level_two_kernel(sc, hid_ref, first_ref, sub_ref, end_ref, kept_ref, half_ref, *refs):
        fwd, refs = refs[:nf], refs[nf:]
        mine, other = refs[: 1 + 2 * nf], refs[1 + 2 * nf : 2 + 4 * nf]
        out_ref, rows, slots, stage, sems = refs[2 + 4 * nf :]
        p, q = sc[0], sc[1]

        @pl.when(p == q)
        def _():
            slots[...] = end_ref[:, :, 2 * k :]

        @pl.when(p != q)
        def _():
            own_rows, sib_rows = halves(p)
            slots[:, own_rows, :] = half_ref[...]
            total = kept_ref[:, sib_rows, 2 * k :]
            for ref in fwd:
                total = total + ref[...]
            slots[:, sib_rows, :] = total

        left = jnp.concatenate([hid_ref[s] for s in range(n_face)], axis=1)
        for take, parts in zip(halves(sc[0]), (mine, other)):
            rows[0, :, take, :] = parts[0][...]
            for i, ref in enumerate(parts[1:]):
                rows[1 + i // 2, :, take, i % 2 * 3 * half : (i % 2 + 1) * 3 * half] = ref[...]
        copies = []
        for c in range(3):
            if c == 2:
                first = (flat(slots[...]).astype(F32) - sub_ref[...]).astype(BF16)
            else:
                first = jnp.where(q == c, first_ref[...], jnp.zeros((2 * fr, k), BF16))
            right = rows[:, :, :, c * k : (c + 1) * k].reshape(n_face * 2 * fr, k)
            stage[c] = (first.astype(F32) - dot(left, right)).astype(BF16).reshape(2, fr, k)
            for t in range(2):
                copies.append(pltpu.make_async_copy(
                    stage.at[c, t], out_ref.at[t, 0, :, pl.ds(c * k, k)], sems.at[c, t]
                ))
                copies[-1].start()
        for copy in copies:
            copy.wait()

    (out,) = call(
        level_two_kernel, scalars,
        [hid_two, first_two, sub_one, end_kept, kept, slots_half, *slots_fwd, *two_rows, *two_sib],
        [sds((2, 1, fr, 3 * k), BF16)], out_specs=[in_hbm],
        scratch=[pltpu.VMEM((n_face, 2, fr, 3 * k), BF16), pltpu.VMEM((2, fr, k), BF16),
                 pltpu.VMEM((3, 2, fr, k), BF16),
                 pltpu.SemaphoreType.DMA((3, 2))],
    )
    return out


def solution(mesh):
    return jax.shard_map(
        on_device,
        mesh=mesh,
        in_specs=(
            P(None, None, "box", None, "face", None),
            P(None, None, "box", None),
            P(None, None, "box", None),
            P(),
            P(),
        ),
        out_specs=P(None, None, ("box", "face"), None),
        check_vma=False,
    )
```

```python
import functools

import jax
import jax.numpy as jnp
from jax import lax
from jax.experimental import pallas as pl
from jax.experimental.pallas import tpu as pltpu
from jax.sharding import PartitionSpec as P

BF16 = jnp.bfloat16
F32 = jnp.float32
VMEM_BYTES = 16 * 1024 * 1024
JOIN_COST = 300000000
SLOTS_COST = 0
OWN_COST = 700_000_000
SOLVED_COST = 400_000_000
KEEP_COST = 3_000_000_000


def dot(first, second):
    return jnp.dot(first, second, preferred_element_type=F32)


def stacked(real, imag):
    return jnp.concatenate(
        [jnp.concatenate([real, -imag], axis=1), jnp.concatenate([imag, real], axis=1)], axis=0
    )


def flat(array):
    return array.reshape(array.shape[0] * array.shape[1], array.shape[2])


def column_picker(index, offset, count):
    rows = lax.broadcasted_iota(jnp.int32, (count, index.shape[1]), 0) + offset
    return jnp.where(rows == index, 1.0, 0.0).astype(BF16)


def row_picker(index, offset, count):
    cols = lax.broadcasted_iota(jnp.int32, (index.shape[0], count), 1) + offset
    return jnp.where(cols == index, 1.0, 0.0).astype(BF16)


def call(kernel, scalars, inputs, out_shapes, specs=None, out_specs=None, scratch=(), cost=0):
    in_vmem = pl.BlockSpec(memory_space=pltpu.VMEM)
    specs = specs or [in_vmem] * len(inputs)
    out_specs = out_specs or [in_vmem] * len(out_shapes)
    return pl.pallas_call(
        kernel,
        in_specs=[pl.BlockSpec(memory_space=pltpu.SMEM)] + specs,
        out_specs=out_specs,
        out_shape=out_shapes,
        scratch_shapes=list(scratch),
        compiler_params=pltpu.CompilerParams(vmem_limit_bytes=VMEM_BYTES),
        cost_estimate=pl.CostEstimate(flops=cost, bytes_accessed=0, transcendentals=0),
    )(scalars, *inputs)


def after(array, *others):
    return lax.optimization_barrier((array, *others))[0]


def on_device(leaf_maps, w_first, w_second, skel_first, skel_second):
    box = lax.axis_index("box")
    face = lax.axis_index("face")
    n_box, n_face = lax.axis_size("box"), lax.axis_size("face")
    nf = n_face - 1
    fr = leaf_maps.shape[4]
    hr = fr // 2
    qr = hr // 2
    k = leaf_maps.shape[5] // 3
    half = k // 2
    leaf = leaf_maps[:, 0, 0]
    scalars = jnp.stack([box % 2, box // 2 % 2, face, box % 4, box // 2, box // 4]).astype(jnp.int32)
    sds = jax.ShapeDtypeStruct
    in_hbm = pl.BlockSpec(memory_space=pltpu.HBM)

    def box_permute(array, mask):
        return lax.ppermute(array, "box", [(b, b ^ mask) for b in range(n_box)])

    def face_permute(array, step):
        pairs = [
            (b * n_face + f, b * n_face + (f + n_face - step) % n_face)
            for b in range(n_box) for f in range(n_face)
        ]
        return lax.ppermute(array, ("box", "face"), pairs)

    def over_face(array):
        return [face_permute(array, s) for s in range(1, n_face)]

    def halves(p):
        mine = pl.ds(pl.multiple_of(p * hr, hr), hr)
        other = pl.ds(pl.multiple_of((1 - p) * hr, hr), hr)
        return mine, other

    def slots_kernel(sc, skel_ref, skel2_ref, comp_out, col_out):
        q = sc[1]
        rows = lax.broadcasted_iota(jnp.int32, (k, k), 0)
        cols = lax.broadcasted_iota(jnp.int32, (k, k), 1)
        skel = jnp.broadcast_to(skel_ref[pl.ds(sc[4], 1), :].astype(F32), (k, k))
        column = jnp.sum(jnp.where(rows == cols, skel, 0.0), axis=1, keepdims=True)
        col_out[...] = column.astype(jnp.int32)
        place = skel2_ref[pl.ds(sc[5], 1), :] - q * k
        taken = jnp.where(rows == place, jnp.broadcast_to(column, (k, k)), 0.0)
        found = jnp.sum(taken, axis=0, keepdims=True).astype(jnp.int32)
        comp_out[...] = jnp.where(jnp.logical_and(place >= 0, place < k), found, -1)

    comp, skel_col = call(
        slots_kernel, scalars, [skel_first[0], skel_second[0]], [sds((1, k), jnp.int32), sds((k, 1), jnp.int32)],
        cost=SLOTS_COST,
    )

    def parts_kernel(sc, leaf_ref, end_out, side_out, *rows_outs):
        p = sc[0]
        end_out[...] = leaf_ref[:, 1 - p, :, pl.ds(pl.multiple_of(p * k, k), k)]
        side_out[...] = leaf_ref[:, 1 - p, :, 2 * k :]
        for i, rows_out in enumerate(rows_outs):
            rows_out[...] = leaf_ref[:, 2, :, i * k : (i + 1) * k]

    end_own, sides_raw, *s_rows = call(
        parts_kernel, scalars, [leaf], [sds((2, fr, k), BF16)] * 5
    )
    sides_sib = box_permute(sides_raw, 1)
    end_sib = box_permute(end_own, 1)
    s_sib = [box_permute(a, 1) for a in s_rows]

    def side_kernel(sc, own_ref, sib_ref, comp_ref, end_ref, side_out, *send_outs):
        p, q = sc[0], sc[1]
        pick_own = column_picker(comp_ref[...], p * k, k)
        pick_sib = column_picker(comp_ref[...], (1 - p) * k, k)
        side = dot(flat(own_ref[...]), pick_own) + dot(flat(sib_ref[...]), pick_sib)
        side_out[...] = side.astype(BF16).reshape(2, fr, k)
        for h, send_out in enumerate(send_outs):
            take = slice(h * hr, (h + 1) * hr)
            send_out[...] = jnp.where(p == q, end_ref[:, take, :], side_out[:, take, :])

    side, *first_send = call(
        side_kernel, scalars, [sides_raw, sides_sib, comp, end_own],
        [sds((2, fr, k), BF16)] + [sds((2, hr, k), BF16)] * 2,
    )
    first_far = [face_permute(a, s) for s in range(1, n_face) for a in first_send]

    def ends_kernel(sc, leaf_ref, comp_ref, keep_out, couple_out, slots_out, end_out):
        p = sc[0]
        pick_own = column_picker(comp_ref[...], p * k, k)
        for t in range(2):
            end_out[t, :, : 2 * k] = leaf_ref[t, p, :, : 2 * k]
            end_out[t, :, 2 * k :] = dot(leaf_ref[t, p, :, 2 * k :], pick_own).astype(BF16)
        couple = pl.ds(pl.multiple_of((1 - p) * k, k), k)
        mine, other = halves(p)
        keep_out[:, :, :k] = end_out[:, mine, couple]
        keep_out[:, :, k:] = end_out[:, mine, 2 * k :]
        couple_out[...] = end_out[:, other, couple]
        slots_out[...] = end_out[:, other, 2 * k :]

    v_keep, *v_send, end_kept = call(
        ends_kernel, after(scalars, side), [leaf, comp],
        [sds((2, hr, 2 * k), BF16)] + [sds((2, hr, k), BF16)] * 2 + [sds((2, fr, 3 * k), BF16)],
    )
    v_recv = [box_permute(a, 1) for a in v_send]

    w_one, w_two = w_first[:, 0], w_second[:, 0]
    w_one_sib = box_permute(after(w_one, side), 1)
    w_two_x = box_permute(after(w_two, side), 2)
    w_two_sib = box_permute(after(w_two, side), 1)
    w_two_x_sib = box_permute(w_two_x, 1)

    def weight_kernel(place, sc, *refs):
        out_ref = refs[-1]
        count = refs[0].shape[1]
        for i, ref in enumerate(refs[:-1]):
            take = pl.ds(pl.multiple_of(place(sc, i) * count, count), count)
            for f in range(n_face):
                @pl.when(sc[2] == f)
                def _(ref=ref, take=take, f=f):
                    out_ref[:, take, : k - f * fr] = ref[:, :, f * fr :]
                    if f > 0:
                        out_ref[:, take, k - f * fr :] = ref[:, :, : f * fr]

    (weight_one,) = call(
        functools.partial(weight_kernel, lambda sc, i: sc[0] ^ i), scalars, [w_one, w_one_sib],
        [sds((2, k, k), BF16)],
    )
    (weight_two,) = call(
        functools.partial(weight_kernel, lambda sc, i: sc[3] ^ (0, 2, 1, 3)[i]), scalars,
        [w_two, w_two_x, w_two_sib, w_two_x_sib], [sds((2, k, k), BF16)],
    )

    def rows_kernel(sc, *refs):
        owns, sibs, refs = refs[:3], refs[3:6], refs[6:]
        comp_ref, col_ref, end_ref, endsib_ref, kept_out, *outs = refs
        p, q, f = sc[0], sc[1], sc[2]
        mine, _ = halves(p)
        rest = jnp.where(p == q, endsib_ref[:, mine, :], end_ref[:, mine, :])
        for s in range(nf):
            outs[2 * nf + s][:, :, :k] = rest
        pick_own = column_picker(comp_ref[...], p * k, k)
        pick_sib = column_picker(comp_ref[...], (1 - p) * k, k)

        def pick(slots, write):
            take_own = row_picker(slots, p * k + f * fr, fr)
            take_sib = row_picker(slots, (1 - p) * k + f * fr, fr)
            for t in range(2):
                for c in range(3):
                    own, sib = owns[c][t], sibs[c][t]
                    if c == 2:
                        own, sib = [dot(a, b).astype(BF16) for a, b in ((own, pick_own), (sib, pick_sib))]
                    write(t, c, (dot(take_own, own) + dot(take_sib, sib)).astype(BF16))

        def write_far(s, t, c, picked):
            if c < 2:
                for j in range(2):
                    outs[2 * s + j][t, :, c * k : (c + 1) * k] = picked[j * qr : (j + 1) * qr]
            else:
                outs[2 * nf + s][t, :, k:] = picked

        def col_half(s):
            start = (f + n_face - s - 1) % n_face * fr + p * hr
            return col_ref[pl.ds(pl.multiple_of(start, hr), hr), :]

        far = jnp.concatenate([col_half(s) for s in range(nf)], axis=0)

        @pl.when(p == q)
        def _():
            def write(t, c, picked):
                for s in range(nf):
                    write_far(s, t, c, picked[s * hr : (s + 1) * hr])

            pick(far, write)

        @pl.when(p != q)
        def _():
            def write(t, c, picked):
                kept_out[t, :, c * k : (c + 1) * k] = picked[:fr]
                for s in range(nf):
                    write_far(s, t, c, picked[fr + s * hr : fr + (s + 1) * hr])

            pick(jnp.concatenate([col_ref[pl.ds(pl.multiple_of(f * fr, fr), fr), :], far], axis=0), write)

    kept, *kept_out = call(
        rows_kernel, scalars, [*s_rows, *s_sib, comp, skel_col, end_own, end_sib],
        [sds((2, fr, 3 * k), BF16)] + [sds((2, qr, 2 * k), BF16)] * (2 * nf) + [sds((2, hr, 2 * k), BF16)] * nf,
    )
    mixed_far = [face_permute(a, i + 1) for i, a in enumerate(kept_out[2 * nf :])]

    def piece(hidden, start, count):
        return stacked(hidden[0][:, start : start + count], hidden[1][:, start : start + count])

    def iface_kernel(sc, keep_ref, couple_ref, slots_ref, w_ref, end_ref, endsib_ref, side_ref,
                     acc_out, hid_out, rows):
        p, q = sc[0], sc[1]

        @pl.when(p == q)
        def _():
            rows[:, :, :k] = couple_ref[...]
            rows[:, :, k:] = slots_ref[...]

        @pl.when(p != q)
        def _():
            rows[...] = keep_ref[...]

        both = dot(stacked(rows[0, :, :k], rows[1, :, :k]), flat(w_ref[...])).astype(BF16)
        hidden = both[:hr], both[hr:]
        hid_out[0] = hidden[0]
        hid_out[1] = hidden[1]
        left = piece(hidden, 0, fr)
        is_end = p == q
        ends = jnp.where(is_end, end_ref[...], endsib_ref[...])
        acc_out[:, :, :k] = -dot(left, flat(ends)).reshape(2, hr, k)
        acc_out[:, :, k:] = rows[:, :, k:].astype(F32) - dot(left, flat(side_ref[...])).reshape(2, hr, k)

    v_acc, v_hid = call(
        iface_kernel, scalars, [v_keep, *v_recv, weight_one, end_own, end_sib, side],
        [sds((2, hr, 2 * k), F32), sds((2, hr, k), BF16)],
        scratch=[pltpu.VMEM((2, hr, 2 * k), BF16)], cost=OWN_COST,
    )
    first_fwd = [box_permute(after(a, kept, w_two_x), 1) for a in first_far]

    def iface_far_kernel(sc, acc_ref, hid_ref, *rest):
        far, fwd = rest[: 2 * nf], rest[2 * nf : 4 * nf]
        end_out, keep_out, send_out = rest[4 * nf :]
        q = sc[1]
        is_end = sc[0] == q
        hidden = [hid_ref[0], hid_ref[1]]
        total = acc_ref[...]
        for i in range(2 * nf):
            left = piece(hidden, fr + i * hr, hr)
            mine, other = dot(left, flat(far[i][...])), dot(left, flat(fwd[i][...]))
            both = [jnp.where(is_end, mine, other), jnp.where(is_end, other, mine)]
            total = total - jnp.concatenate(both, axis=1).reshape(2, hr, 2 * k)
        total = total.astype(BF16)
        end_out[...] = total[:, :, :k]
        low, high = total[:, :, k : k + half], total[:, :, k + half :]
        keep_out[...] = jnp.where(q == 0, low, high)
        send_out[...] = jnp.where(q == 0, high, low)

    two_end, side_keep, side_send = call(
        iface_far_kernel, scalars, [v_acc, v_hid, *first_far, *first_fwd],
        [sds((2, hr, k), BF16)] + [sds((2, hr, half), BF16)] * 2,
    )

    side_x = box_permute(side_send, 2)

    def pack_kernel(sc, end_ref, keep_ref, x_ref, out_ref):
        out_ref[:, :, :k] = end_ref[...]
        out_ref[:, :, k:] = keep_ref[...] + x_ref[...]

    (two_own,) = call(
        pack_kernel, scalars, [two_end, side_keep, side_x], [sds((2, hr, k + half), BF16)]
    )
    two_x = box_permute(two_own, 2)
    two_y = over_face(two_own)
    mixed_fwd = [box_permute(after(a, two_own), 1) for a in mixed_far]

    def weighted(w_ref, rows, out_ref):
        left = jnp.concatenate([piece((w_ref[0], w_ref[1]), s * fr, fr) for s in range(n_face)], axis=1)
        for c in range(3):
            cols = slice(c * k, (c + 1) * k)
            right = rows[:, :, :, cols].reshape(n_face * 2 * fr, k)
            out_ref[:, :, cols] = dot(left, right).astype(BF16).reshape(2, k, k)

    def weighted_one_kernel(sc, w_ref, own_ref, sib_ref, side_ref, *rest):
        refs = [rest[i * nf : (i + 1) * nf] for i in range(6)]
        far, fwd = rest[: 2 * nf], rest[2 * nf : 4 * nf]
        out_ref, rows = rest[6 * nf :]
        p, q = sc[0], sc[1]
        is_end = p == q
        first_cols = pl.ds(pl.multiple_of(q * k, k), k)
        rest_cols = pl.ds(pl.multiple_of((1 - q) * k, k), k)
        rows[0, :, :, pl.ds(pl.multiple_of(p * k, k), k)] = own_ref[...]
        rows[0, :, :, pl.ds(pl.multiple_of((1 - p) * k, k), k)] = sib_ref[...]
        rows[0, :, :, 2 * k :] = side_ref[...]
        for s in range(nf):
            for h in range(2):
                take = slice(h * hr, (h + 1) * hr)
                mine, other = far[2 * s + h][...], fwd[2 * s + h][...]
                rows[s + 1, :, take, first_cols] = jnp.where(is_end, mine, other)
                rows[s + 1, :, take, 2 * k :] = jnp.where(is_end, other, mine)
            for take, parts in zip(halves(p), refs[4:]):
                rows[s + 1, :, take, rest_cols] = parts[s][:, :, :k]
        weighted(w_ref, rows, out_ref)

    (solved_one,) = call(
        weighted_one_kernel, scalars,
        [weight_one, end_own, end_sib, side, *first_far, *first_fwd, *mixed_far, *mixed_fwd],
        [sds((2, k, 3 * k), BF16)], scratch=[pltpu.VMEM((n_face, 2, fr, 3 * k), BF16)], cost=SOLVED_COST,
    )

    def join_kernel(sc, own_ref, x_ref, out_ref):
        q = sc[1]
        for ref, which in ((own_ref, q), (x_ref, 1 - q)):
            out_ref[:, :, pl.ds(pl.multiple_of(which * k, k), k)] = ref[:, :, :k]
            out_ref[:, :, pl.ds(pl.multiple_of(2 * k + which * half, half), half)] = ref[:, :, k:]

    two_shape = [sds((2, hr, 3 * k), BF16)]
    two_rows = call(join_kernel, after(scalars, weight_two), [two_own, two_x], two_shape, cost=JOIN_COST)
    two_xy = [box_permute(after(a, *two_rows), 2) for a in two_y]

    def join_far_kernel(sc, own_ref, x_ref, *refs):
        join_kernel(sc, own_ref, x_ref, refs[-1])
        for h in range(2):
            refs[h][...] = refs[-1][:, :, h * 3 * half : (h + 1) * 3 * half]

    for own, other in zip(two_y, two_xy):
        two_rows += call(
            join_far_kernel, after(scalars, solved_one), [own, other], [sds((2, hr, 3 * half), BF16)] * 2,
            scratch=[pltpu.VMEM((2, hr, 3 * k), BF16)],
        )
    two_sib = [box_permute(a, 1) for a in two_rows[:1]]

    ends_far = [face_permute(after(a, two_own), i // 2 + 1) for i, a in enumerate(kept_out[: 2 * nf])]
    ends_fwd = [box_permute(after(a, solved_one), 1) for a in ends_far]
    two_sib += [box_permute(a, 1) for a in two_rows[1:]]

    def level_one_kernel(sc, end_ref, kept_ref, *refs):
        mixed = refs[:nf], refs[nf : 2 * nf]
        ends = refs[2 * nf : 4 * nf], refs[4 * nf : 6 * nf]
        col_ref, one_ref, w_ref, hid_out, first_out, slots_out, zs = refs[6 * nf :]
        p, q, f = sc[0], sc[1], sc[2]

        @pl.when(p == q)
        def _():
            zs[...] = end_ref[...]

        @pl.when(p != q)
        def _():
            for h, take in enumerate(halves(p)):
                total = kept_ref[:, take, 2 * k :]
                for ref in mixed[h]:
                    total = total + ref[:, :, k:]
                zs[:, take, 2 * k :] = total
                for j in range(2):
                    take = pl.ds(pl.multiple_of((p ^ h) * hr + j * qr, qr), qr)
                    total = kept_ref[:, take, : 2 * k]
                    for ref in ends[h][j::2]:
                        total = total + ref[...]
                    zs[:, take, : 2 * k] = total

        slots = col_ref[pl.ds(pl.multiple_of(f * fr, fr), fr), :]
        right = jnp.where(slots >= k, 1, 0)
        right = jnp.where(p == q, p, right) > 0
        lefts = [zs[t, :, :k] for t in range(2)]
        rights = [zs[t, :, k : 2 * k] for t in range(2)]
        left = stacked(*[jnp.where(right, a, b) for a, b in zip(lefts, rights)])
        nothing = jnp.zeros((fr, k), BF16)
        start = [
            jnp.concatenate([jnp.where(right, nothing, a) for a in lefts], axis=0),
            jnp.concatenate([jnp.where(right, a, nothing) for a in rights], axis=0),
            flat(zs[:, :, 2 * k :]),
        ]
        merged = [
            (start[c].astype(F32) - dot(left, flat(one_ref[:, :, c * k : (c + 1) * k]))).astype(BF16)
            for c in range(3)
        ]
        is_left = q == 0
        first_out[...] = jnp.where(is_left, merged[0], merged[1])
        slots_out[...] = merged[2]
        couple = jnp.where(is_left, merged[1], merged[0])
        second = dot(stacked(couple[:fr], couple[fr:]), flat(w_ref[...])).astype(BF16)
        for s in range(n_face):
            hid_out[s] = piece((second[:fr], second[fr:]), s * fr, fr)

    hid_two, first_two, slots_two = call(
        level_one_kernel, scalars,
        [end_kept, kept, *mixed_far, *mixed_fwd, *ends_far, *ends_fwd, skel_col, solved_one, weight_two],
        [sds((n_face, 2 * fr, 2 * fr), BF16), sds((2 * fr, k), BF16), sds((2 * fr, k), BF16)],
        scratch=[pltpu.VMEM((2, fr, 3 * k), BF16)], cost=KEEP_COST,
    )

    def level_two_kernel(sc, hid_ref, first_ref, slots_ref, *refs):
        mine, other = refs[: 1 + 2 * nf], refs[1 + 2 * nf : 2 + 4 * nf]
        out_ref, rows, stage, sems = refs[2 + 4 * nf :]
        q = sc[1]
        left = jnp.concatenate([hid_ref[s] for s in range(n_face)], axis=1)
        for take, parts in zip(halves(sc[0]), (mine, other)):
            rows[0, :, take, :] = parts[0][...]
            for i, ref in enumerate(parts[1:]):
                rows[1 + i // 2, :, take, i % 2 * 3 * half : (i % 2 + 1) * 3 * half] = ref[...]
        copies = []
        for c in range(3):
            first = slots_ref[...]
            if c < 2:
                first = jnp.where(q == c, first_ref[...], jnp.zeros((2 * fr, k), BF16))
            right = rows[:, :, :, c * k : (c + 1) * k].reshape(n_face * 2 * fr, k)
            stage[c] = (first.astype(F32) - dot(left, right)).astype(BF16).reshape(2, fr, k)
            for t in range(2):
                copies.append(pltpu.make_async_copy(
                    stage.at[c, t], out_ref.at[t, 0, :, pl.ds(c * k, k)], sems.at[c, t]
                ))
                copies[-1].start()
        for copy in copies:
            copy.wait()

    (out,) = call(
        level_two_kernel, scalars, [hid_two, first_two, slots_two, *two_rows, *two_sib],
        [sds((2, 1, fr, 3 * k), BF16)], out_specs=[in_hbm],
        scratch=[pltpu.VMEM((n_face, 2, fr, 3 * k), BF16), pltpu.VMEM((3, 2, fr, k), BF16),
                 pltpu.SemaphoreType.DMA((3, 2))],
    )
    return out


def solution(mesh):
    return jax.shard_map(
        on_device,
        mesh=mesh,
        in_specs=(
            P(None, None, "box", None, "face", None),
            P(None, None, "box", None),
            P(None, None, "box", None),
            P(),
            P(),
        ),
        out_specs=P(None, None, ("box", "face"), None),
        check_vma=False,
    )
```

```python
import functools

import jax
import jax.numpy as jnp
from jax import lax
from jax.experimental import pallas as pl
from jax.experimental.pallas import tpu as pltpu
from jax.sharding import PartitionSpec as P

BF16 = jnp.bfloat16
F32 = jnp.float32
VMEM_BYTES = 16 * 1024 * 1024
JOIN_COST = 300000000
SLOTS_COST = 0
OWN_COST = 700_000_000
SOLVED_COST = 400_000_000
KEEP_COST = 3_000_000_000


def dot(first, second):
    return jnp.dot(first, second, preferred_element_type=F32)


def stacked(real, imag):
    return jnp.concatenate(
        [jnp.concatenate([real, -imag], axis=1), jnp.concatenate([imag, real], axis=1)], axis=0
    )


def flat(array):
    return array.reshape(array.shape[0] * array.shape[1], array.shape[2])


def column_picker(index, offset, count):
    rows = lax.broadcasted_iota(jnp.int32, (count, index.shape[1]), 0) + offset
    return jnp.where(rows == index, 1.0, 0.0).astype(BF16)


def row_picker(index, offset, count):
    cols = lax.broadcasted_iota(jnp.int32, (index.shape[0], count), 1) + offset
    return jnp.where(cols == index, 1.0, 0.0).astype(BF16)


def call(kernel, scalars, inputs, out_shapes, specs=None, out_specs=None, scratch=(), cost=0):
    in_vmem = pl.BlockSpec(memory_space=pltpu.VMEM)
    specs = specs or [in_vmem] * len(inputs)
    out_specs = out_specs or [in_vmem] * len(out_shapes)
    return pl.pallas_call(
        kernel,
        in_specs=[pl.BlockSpec(memory_space=pltpu.SMEM)] + specs,
        out_specs=out_specs,
        out_shape=out_shapes,
        scratch_shapes=list(scratch),
        compiler_params=pltpu.CompilerParams(vmem_limit_bytes=VMEM_BYTES),
        cost_estimate=pl.CostEstimate(flops=cost, bytes_accessed=0, transcendentals=0),
    )(scalars, *inputs)


def after(array, *others):
    return lax.optimization_barrier((array, *others))[0]


def on_device(leaf_maps, w_first, w_second, skel_first, skel_second):
    box = lax.axis_index("box")
    face = lax.axis_index("face")
    n_box, n_face = lax.axis_size("box"), lax.axis_size("face")
    nf = n_face - 1
    fr = leaf_maps.shape[4]
    hr = fr // 2
    qr = hr // 2
    k = leaf_maps.shape[5] // 3
    half = k // 2
    leaf = leaf_maps[:, 0, 0]
    scalars = jnp.stack([box % 2, box // 2 % 2, face, box % 4, box // 2, box // 4]).astype(jnp.int32)
    sds = jax.ShapeDtypeStruct
    in_hbm = pl.BlockSpec(memory_space=pltpu.HBM)

    def box_permute(array, mask):
        return lax.ppermute(array, "box", [(b, b ^ mask) for b in range(n_box)])

    def face_permute(array, step):
        pairs = [
            (b * n_face + f, b * n_face + (f + n_face - step) % n_face)
            for b in range(n_box) for f in range(n_face)
        ]
        return lax.ppermute(array, ("box", "face"), pairs)

    def over_face(array):
        return [face_permute(array, s) for s in range(1, n_face)]

    def halves(p):
        mine = pl.ds(pl.multiple_of(p * hr, hr), hr)
        other = pl.ds(pl.multiple_of((1 - p) * hr, hr), hr)
        return mine, other

    def slots_kernel(sc, skel_ref, skel2_ref, comp_out, col_out):
        q = sc[1]
        rows = lax.broadcasted_iota(jnp.int32, (k, k), 0)
        cols = lax.broadcasted_iota(jnp.int32, (k, k), 1)
        skel = jnp.broadcast_to(skel_ref[pl.ds(sc[4], 1), :].astype(F32), (k, k))
        column = jnp.sum(jnp.where(rows == cols, skel, 0.0), axis=1, keepdims=True)
        col_out[...] = column.astype(jnp.int32)
        place = skel2_ref[pl.ds(sc[5], 1), :] - q * k
        taken = jnp.where(rows == place, jnp.broadcast_to(column, (k, k)), 0.0)
        found = jnp.sum(taken, axis=0, keepdims=True).astype(jnp.int32)
        comp_out[...] = jnp.where(jnp.logical_and(place >= 0, place < k), found, -1)

    comp, skel_col = call(
        slots_kernel, scalars, [skel_first[0], skel_second[0]], [sds((1, k), jnp.int32), sds((k, 1), jnp.int32)],
        cost=SLOTS_COST,
    )

    def parts_kernel(sc, leaf_ref, end_out, side_out, *rows_outs):
        p = sc[0]
        end_out[...] = leaf_ref[:, 1 - p, :, pl.ds(pl.multiple_of(p * k, k), k)]
        side_out[...] = leaf_ref[:, 1 - p, :, 2 * k :]
        for i, rows_out in enumerate(rows_outs):
            rows_out[...] = leaf_ref[:, 2, :, i * k : (i + 1) * k]

    end_own, sides_raw, *s_rows = call(
        parts_kernel, scalars, [leaf], [sds((2, fr, k), BF16)] * 5
    )
    sides_sib = box_permute(sides_raw, 1)
    end_sib = box_permute(end_own, 1)
    s_sib = [box_permute(a, 1) for a in s_rows]

    def side_kernel(sc, own_ref, sib_ref, comp_ref, end_ref, side_out, *send_outs):
        p, q = sc[0], sc[1]
        pick_own = column_picker(comp_ref[...], p * k, k)
        pick_sib = column_picker(comp_ref[...], (1 - p) * k, k)
        side = dot(flat(own_ref[...]), pick_own) + dot(flat(sib_ref[...]), pick_sib)
        side_out[...] = side.astype(BF16).reshape(2, fr, k)
        for h, send_out in enumerate(send_outs):
            take = slice(h * hr, (h + 1) * hr)
            send_out[...] = jnp.where(p == q, end_ref[:, take, :], side_out[:, take, :])

    side, *first_send = call(
        side_kernel, scalars, [sides_raw, sides_sib, comp, end_own],
        [sds((2, fr, k), BF16)] + [sds((2, hr, k), BF16)] * 2,
    )
    first_far = [face_permute(a, s) for s in range(1, n_face) for a in first_send]

    def ends_kernel(sc, leaf_ref, comp_ref, keep_out, couple_out, slots_out, end_out):
        p = sc[0]
        pick_own = column_picker(comp_ref[...], p * k, k)
        for t in range(2):
            end_out[t, :, : 2 * k] = leaf_ref[t, p, :, : 2 * k]
            end_out[t, :, 2 * k :] = dot(leaf_ref[t, p, :, 2 * k :], pick_own).astype(BF16)
        couple = pl.ds(pl.multiple_of((1 - p) * k, k), k)
        mine, other = halves(p)
        keep_out[:, :, :k] = end_out[:, mine, couple]
        keep_out[:, :, k:] = end_out[:, mine, 2 * k :]
        couple_out[...] = end_out[:, other, couple]
        slots_out[...] = end_out[:, other, 2 * k :]

    v_keep, *v_send, end_kept = call(
        ends_kernel, after(scalars, side), [leaf, comp],
        [sds((2, hr, 2 * k), BF16)] + [sds((2, hr, k), BF16)] * 2 + [sds((2, fr, 3 * k), BF16)],
    )
    v_recv = [box_permute(a, 1) for a in v_send]

    w_one, w_two = w_first[:, 0], w_second[:, 0]
    w_one_sib = box_permute(after(w_one, side), 1)
    w_two_x = box_permute(after(w_two, side), 2)
    w_two_sib = box_permute(after(w_two, side), 1)
    w_two_x_sib = box_permute(w_two_x, 1)

    def weight_kernel(place, sc, *refs):
        out_ref = refs[-1]
        count = refs[0].shape[1]
        for i, ref in enumerate(refs[:-1]):
            take = pl.ds(pl.multiple_of(place(sc, i) * count, count), count)
            for f in range(n_face):
                @pl.when(sc[2] == f)
                def _(ref=ref, take=take, f=f):
                    out_ref[:, take, : k - f * fr] = ref[:, :, f * fr :]
                    if f > 0:
                        out_ref[:, take, k - f * fr :] = ref[:, :, : f * fr]

    (weight_one,) = call(
        functools.partial(weight_kernel, lambda sc, i: sc[0] ^ i), scalars, [w_one, w_one_sib],
        [sds((2, k, k), BF16)],
    )
    (weight_two,) = call(
        functools.partial(weight_kernel, lambda sc, i: sc[3] ^ (0, 2, 1, 3)[i]), scalars,
        [w_two, w_two_x, w_two_sib, w_two_x_sib], [sds((2, k, k), BF16)],
    )

    def rows_kernel(sc, *refs):
        owns, sibs, refs = refs[:3], refs[3:6], refs[6:]
        comp_ref, col_ref, end_ref, endsib_ref, kept_out, *outs = refs
        p, q, f = sc[0], sc[1], sc[2]
        mine, _ = halves(p)
        rest = jnp.where(p == q, endsib_ref[:, mine, :], end_ref[:, mine, :])
        for s in range(nf):
            outs[2 * nf + s][:, :, :k] = rest
        pick_own = column_picker(comp_ref[...], p * k, k)
        pick_sib = column_picker(comp_ref[...], (1 - p) * k, k)

        def pick(slots, write):
            take_own = row_picker(slots, p * k + f * fr, fr)
            take_sib = row_picker(slots, (1 - p) * k + f * fr, fr)
            for t in range(2):
                for c in range(3):
                    own, sib = owns[c][t], sibs[c][t]
                    if c == 2:
                        own, sib = [dot(a, b).astype(BF16) for a, b in ((own, pick_own), (sib, pick_sib))]
                    write(t, c, (dot(take_own, own) + dot(take_sib, sib)).astype(BF16))

        def write_far(s, t, c, picked):
            if c < 2:
                for j in range(2):
                    outs[2 * s + j][t, :, c * k : (c + 1) * k] = picked[j * qr : (j + 1) * qr]
            else:
                outs[2 * nf + s][t, :, k:] = picked

        def col_half(s):
            start = (f + n_face - s - 1) % n_face * fr + p * hr
            return col_ref[pl.ds(pl.multiple_of(start, hr), hr), :]

        far = jnp.concatenate([col_half(s) for s in range(nf)], axis=0)

        @pl.when(p == q)
        def _():
            def write(t, c, picked):
                for s in range(nf):
                    write_far(s, t, c, picked[s * hr : (s + 1) * hr])

            pick(far, write)

        @pl.when(p != q)
        def _():
            def write(t, c, picked):
                kept_out[t, :, c * k : (c + 1) * k] = picked[:fr]
                for s in range(nf):
                    write_far(s, t, c, picked[fr + s * hr : fr + (s + 1) * hr])

            pick(jnp.concatenate([col_ref[pl.ds(pl.multiple_of(f * fr, fr), fr), :], far], axis=0), write)

    kept, *kept_out = call(
        rows_kernel, scalars, [*s_rows, *s_sib, comp, skel_col, end_own, end_sib],
        [sds((2, fr, 3 * k), BF16)] + [sds((2, qr, 2 * k), BF16)] * (2 * nf) + [sds((2, hr, 2 * k), BF16)] * nf,
    )
    mixed_far = [face_permute(a, i + 1) for i, a in enumerate(kept_out[2 * nf :])]

    def piece(hidden, start, count):
        return stacked(hidden[0][:, start : start + count], hidden[1][:, start : start + count])

    def iface_kernel(sc, keep_ref, couple_ref, slots_ref, w_ref, end_ref, endsib_ref, side_ref,
                     acc_out, hid_out, rows):
        p, q = sc[0], sc[1]

        @pl.when(p == q)
        def _():
            rows[:, :, :k] = couple_ref[...]
            rows[:, :, k:] = slots_ref[...]

        @pl.when(p != q)
        def _():
            rows[...] = keep_ref[...]

        both = dot(stacked(rows[0, :, :k], rows[1, :, :k]), flat(w_ref[...])).astype(BF16)
        hidden = both[:hr], both[hr:]
        hid_out[0] = hidden[0]
        hid_out[1] = hidden[1]
        left = piece(hidden, 0, fr)
        is_end = p == q
        ends = jnp.where(is_end, end_ref[...], endsib_ref[...])
        acc_out[:, :, :k] = -dot(left, flat(ends)).reshape(2, hr, k)
        acc_out[:, :, k:] = rows[:, :, k:].astype(F32) - dot(left, flat(side_ref[...])).reshape(2, hr, k)

    v_acc, v_hid = call(
        iface_kernel, scalars, [v_keep, *v_recv, weight_one, end_own, end_sib, side],
        [sds((2, hr, 2 * k), F32), sds((2, hr, k), BF16)],
        scratch=[pltpu.VMEM((2, hr, 2 * k), BF16)], cost=OWN_COST,
    )
    first_fwd = [box_permute(after(a, kept, w_two_x), 1) for a in first_far]

    def iface_far_kernel(sc, acc_ref, hid_ref, *rest):
        far, fwd = rest[: 2 * nf], rest[2 * nf : 4 * nf]
        end_out, keep_out, send_out = rest[4 * nf :]
        q = sc[1]
        is_end = sc[0] == q
        hidden = [hid_ref[0], hid_ref[1]]
        total = acc_ref[...]
        for i in range(2 * nf):
            left = piece(hidden, fr + i * hr, hr)
            mine, other = dot(left, flat(far[i][...])), dot(left, flat(fwd[i][...]))
            both = [jnp.where(is_end, mine, other), jnp.where(is_end, other, mine)]
            total = total - jnp.concatenate(both, axis=1).reshape(2, hr, 2 * k)
        total = total.astype(BF16)
        end_out[...] = total[:, :, :k]
        low, high = total[:, :, k : k + half], total[:, :, k + half :]
        keep_out[...] = jnp.where(q == 0, low, high)
        send_out[...] = jnp.where(q == 0, high, low)

    two_end, side_keep, side_send = call(
        iface_far_kernel, scalars, [v_acc, v_hid, *first_far, *first_fwd],
        [sds((2, hr, k), BF16)] + [sds((2, hr, half), BF16)] * 2,
    )

    side_x = box_permute(side_send, 2)

    def pack_kernel(sc, end_ref, keep_ref, x_ref, out_ref):
        out_ref[:, :, :k] = end_ref[...]
        out_ref[:, :, k:] = keep_ref[...] + x_ref[...]

    (two_own,) = call(
        pack_kernel, scalars, [two_end, side_keep, side_x], [sds((2, hr, k + half), BF16)]
    )
    two_x = box_permute(two_own, 2)
    two_y = over_face(two_own)
    mixed_fwd = [box_permute(after(a, two_own), 1) for a in mixed_far]

    def weighted(w_ref, rows, out_ref):
        left = jnp.concatenate([piece((w_ref[0], w_ref[1]), s * fr, fr) for s in range(n_face)], axis=1)
        for c in range(3):
            cols = slice(c * k, (c + 1) * k)
            right = rows[:, :, :, cols].reshape(n_face * 2 * fr, k)
            out_ref[:, :, cols] = dot(left, right).astype(BF16).reshape(2, k, k)

    def weighted_one_kernel(sc, w_ref, own_ref, sib_ref, side_ref, *rest):
        refs = [rest[i * nf : (i + 1) * nf] for i in range(6)]
        far, fwd = rest[: 2 * nf], rest[2 * nf : 4 * nf]
        out_ref, rows = rest[6 * nf :]
        p, q = sc[0], sc[1]
        is_end = p == q
        first_cols = pl.ds(pl.multiple_of(q * k, k), k)
        rest_cols = pl.ds(pl.multiple_of((1 - q) * k, k), k)
        rows[0, :, :, pl.ds(pl.multiple_of(p * k, k), k)] = own_ref[...]
        rows[0, :, :, pl.ds(pl.multiple_of((1 - p) * k, k), k)] = sib_ref[...]
        rows[0, :, :, 2 * k :] = side_ref[...]
        for s in range(nf):
            for h in range(2):
                take = slice(h * hr, (h + 1) * hr)
                mine, other = far[2 * s + h][...], fwd[2 * s + h][...]
                rows[s + 1, :, take, first_cols] = jnp.where(is_end, mine, other)
                rows[s + 1, :, take, 2 * k :] = jnp.where(is_end, other, mine)
            for take, parts in zip(halves(p), refs[4:]):
                rows[s + 1, :, take, rest_cols] = parts[s][:, :, :k]
        weighted(w_ref, rows, out_ref)

    (solved_one,) = call(
        weighted_one_kernel, scalars,
        [weight_one, end_own, end_sib, side, *first_far, *first_fwd, *mixed_far, *mixed_fwd],
        [sds((2, k, 3 * k), BF16)], scratch=[pltpu.VMEM((n_face, 2, fr, 3 * k), BF16)], cost=SOLVED_COST,
    )

    def join_kernel(sc, own_ref, x_ref, out_ref):
        q = sc[1]
        for ref, which in ((own_ref, q), (x_ref, 1 - q)):
            out_ref[:, :, pl.ds(pl.multiple_of(which * k, k), k)] = ref[:, :, :k]
            out_ref[:, :, pl.ds(pl.multiple_of(2 * k + which * half, half), half)] = ref[:, :, k:]

    two_shape = [sds((2, hr, 3 * k), BF16)]
    two_rows = call(join_kernel, after(scalars, weight_two), [two_own, two_x], two_shape, cost=JOIN_COST)
    two_xy = [box_permute(after(a, *two_rows), 2) for a in two_y]
    two_rows = [*two_rows, *(a for pair in zip(two_y, two_xy) for a in pair)]
    two_sib = [box_permute(a, 1) for a in two_rows]

    ends_far = [face_permute(after(a, two_own), i // 2 + 1) for i, a in enumerate(kept_out[: 2 * nf])]
    ends_fwd = [box_permute(after(a, solved_one), 1) for a in ends_far]

    def level_one_kernel(sc, end_ref, kept_ref, *refs):
        mixed = refs[:nf], refs[nf : 2 * nf]
        ends = refs[2 * nf : 4 * nf], refs[4 * nf : 6 * nf]
        col_ref, one_ref, w_ref, hid_out, first_out, slots_out, zs = refs[6 * nf :]
        p, q, f = sc[0], sc[1], sc[2]

        @pl.when(p == q)
        def _():
            zs[...] = end_ref[...]

        @pl.when(p != q)
        def _():
            for h, take in enumerate(halves(p)):
                total = kept_ref[:, take, 2 * k :]
                for ref in mixed[h]:
                    total = total + ref[:, :, k:]
                zs[:, take, 2 * k :] = total
                for j in range(2):
                    take = pl.ds(pl.multiple_of((p ^ h) * hr + j * qr, qr), qr)
                    total = kept_ref[:, take, : 2 * k]
                    for ref in ends[h][j::2]:
                        total = total + ref[...]
                    zs[:, take, : 2 * k] = total

        slots = col_ref[pl.ds(pl.multiple_of(f * fr, fr), fr), :]
        right = jnp.where(slots >= k, 1, 0)
        right = jnp.where(p == q, p, right) > 0
        lefts = [zs[t, :, :k] for t in range(2)]
        rights = [zs[t, :, k : 2 * k] for t in range(2)]
        left = stacked(*[jnp.where(right, a, b) for a, b in zip(lefts, rights)])
        nothing = jnp.zeros((fr, k), BF16)
        start = [
            jnp.concatenate([jnp.where(right, nothing, a) for a in lefts], axis=0),
            jnp.concatenate([jnp.where(right, a, nothing) for a in rights], axis=0),
            flat(zs[:, :, 2 * k :]),
        ]
        merged = [
            (start[c].astype(F32) - dot(left, flat(one_ref[:, :, c * k : (c + 1) * k]))).astype(BF16)
            for c in range(3)
        ]
        is_left = q == 0
        first_out[...] = jnp.where(is_left, merged[0], merged[1])
        slots_out[...] = merged[2]
        couple = jnp.where(is_left, merged[1], merged[0])
        second = dot(stacked(couple[:fr], couple[fr:]), flat(w_ref[...])).astype(BF16)
        for s in range(n_face):
            hid_out[s] = piece((second[:fr], second[fr:]), s * fr, fr)

    hid_two, first_two, slots_two = call(
        level_one_kernel, scalars,
        [end_kept, kept, *mixed_far, *mixed_fwd, *ends_far, *ends_fwd, skel_col, solved_one, weight_two],
        [sds((n_face, 2 * fr, 2 * fr), BF16), sds((2 * fr, k), BF16), sds((2 * fr, k), BF16)],
        scratch=[pltpu.VMEM((2, fr, 3 * k), BF16)], cost=KEEP_COST,
    )

    def level_two_kernel(sc, hid_ref, first_ref, slots_ref, *refs):
        mine, other = refs[: 1 + 2 * nf], refs[1 + 2 * nf : 2 + 4 * nf]
        out_ref, rows, stage, sems = refs[2 + 4 * nf :]
        q = sc[1]
        left = jnp.concatenate([hid_ref[s] for s in range(n_face)], axis=1)
        for take, parts in zip(halves(sc[0]), (mine, other)):
            rows[0, :, take, :] = parts[0][...]
            for i, ref in enumerate(parts[1:]):
                which = q ^ (i % 2)
                rows[1 + i // 2, :, take, pl.ds(pl.multiple_of(which * k, k), k)] = ref[:, :, :k]
                rows[1 + i // 2, :, take, pl.ds(pl.multiple_of(2 * k + which * half, half), half)] = ref[:, :, k:]
        copies = []
        for c in range(3):
            first = slots_ref[...]
            if c < 2:
                first = jnp.where(q == c, first_ref[...], jnp.zeros((2 * fr, k), BF16))
            right = rows[:, :, :, c * k : (c + 1) * k].reshape(n_face * 2 * fr, k)
            stage[c] = (first.astype(F32) - dot(left, right)).astype(BF16).reshape(2, fr, k)
            for t in range(2):
                copies.append(pltpu.make_async_copy(
                    stage.at[c, t], out_ref.at[t, 0, :, pl.ds(c * k, k)], sems.at[c, t]
                ))
                copies[-1].start()
        for copy in copies:
            copy.wait()

    (out,) = call(
        level_two_kernel, scalars, [hid_two, first_two, slots_two, *two_rows, *two_sib],
        [sds((2, 1, fr, 3 * k), BF16)], out_specs=[in_hbm],
        scratch=[pltpu.VMEM((n_face, 2, fr, 3 * k), BF16), pltpu.VMEM((3, 2, fr, k), BF16),
                 pltpu.SemaphoreType.DMA((3, 2))],
    )
    return out


def solution(mesh):
    return jax.shard_map(
        on_device,
        mesh=mesh,
        in_specs=(
            P(None, None, "box", None, "face", None),
            P(None, None, "box", None),
            P(None, None, "box", None),
            P(),
            P(),
        ),
        out_specs=P(None, None, ("box", "face"), None),
        check_vma=False,
    )
```

```python
import functools

import jax
import jax.numpy as jnp
from jax import lax
from jax.experimental import pallas as pl
from jax.experimental.pallas import tpu as pltpu
from jax.sharding import PartitionSpec as P

BF16 = jnp.bfloat16
F32 = jnp.float32
VMEM_BYTES = 16 * 1024 * 1024
JOIN_COST = 300000000
SLOTS_COST = 0
OWN_COST = 700_000_000
SOLVED_COST = 400_000_000
KEEP_COST = 3_000_000_000


def dot(first, second):
    return jnp.dot(first, second, preferred_element_type=F32)


def stacked(real, imag):
    return jnp.concatenate(
        [jnp.concatenate([real, -imag], axis=1), jnp.concatenate([imag, real], axis=1)], axis=0
    )


def flat(array):
    return array.reshape(array.shape[0] * array.shape[1], array.shape[2])


def column_picker(index, offset, count):
    rows = lax.broadcasted_iota(jnp.int32, (count, index.shape[1]), 0) + offset
    return jnp.where(rows == index, 1.0, 0.0).astype(BF16)


def row_picker(index, offset, count):
    cols = lax.broadcasted_iota(jnp.int32, (index.shape[0], count), 1) + offset
    return jnp.where(cols == index, 1.0, 0.0).astype(BF16)


def call(kernel, scalars, inputs, out_shapes, specs=None, out_specs=None, scratch=(), cost=0):
    in_vmem = pl.BlockSpec(memory_space=pltpu.VMEM)
    specs = specs or [in_vmem] * len(inputs)
    out_specs = out_specs or [in_vmem] * len(out_shapes)
    return pl.pallas_call(
        kernel,
        in_specs=[pl.BlockSpec(memory_space=pltpu.SMEM)] + specs,
        out_specs=out_specs,
        out_shape=out_shapes,
        scratch_shapes=list(scratch),
        compiler_params=pltpu.CompilerParams(vmem_limit_bytes=VMEM_BYTES),
        cost_estimate=pl.CostEstimate(flops=cost, bytes_accessed=0, transcendentals=0),
    )(scalars, *inputs)


def after(array, *others):
    return lax.optimization_barrier((array, *others))[0]


def on_device(leaf_maps, w_first, w_second, skel_first, skel_second):
    box = lax.axis_index("box")
    face = lax.axis_index("face")
    n_box, n_face = lax.axis_size("box"), lax.axis_size("face")
    nf = n_face - 1
    fr = leaf_maps.shape[4]
    hr = fr // 2
    qr = hr // 2
    k = leaf_maps.shape[5] // 3
    half = k // 2
    leaf = leaf_maps[:, 0, 0]
    scalars = jnp.stack([box % 2, box // 2 % 2, face, box % 4, box // 2, box // 4]).astype(jnp.int32)
    sds = jax.ShapeDtypeStruct
    in_hbm = pl.BlockSpec(memory_space=pltpu.HBM)

    def box_permute(array, mask):
        return lax.ppermute(array, "box", [(b, b ^ mask) for b in range(n_box)])

    def face_permute(array, step):
        pairs = [
            (b * n_face + f, b * n_face + (f + n_face - step) % n_face)
            for b in range(n_box) for f in range(n_face)
        ]
        return lax.ppermute(array, ("box", "face"), pairs)

    def over_face(array):
        return [face_permute(array, s) for s in range(1, n_face)]

    def halves(p):
        mine = pl.ds(pl.multiple_of(p * hr, hr), hr)
        other = pl.ds(pl.multiple_of((1 - p) * hr, hr), hr)
        return mine, other

    def slots_kernel(sc, skel_ref, skel2_ref, comp_out, col_out):
        q = sc[1]
        rows = lax.broadcasted_iota(jnp.int32, (k, k), 0)
        cols = lax.broadcasted_iota(jnp.int32, (k, k), 1)
        skel = jnp.broadcast_to(skel_ref[pl.ds(sc[4], 1), :].astype(F32), (k, k))
        column = jnp.sum(jnp.where(rows == cols, skel, 0.0), axis=1, keepdims=True)
        col_out[...] = column.astype(jnp.int32)
        place = skel2_ref[pl.ds(sc[5], 1), :] - q * k
        taken = jnp.where(rows == place, jnp.broadcast_to(column, (k, k)), 0.0)
        found = jnp.sum(taken, axis=0, keepdims=True).astype(jnp.int32)
        comp_out[...] = jnp.where(jnp.logical_and(place >= 0, place < k), found, -1)

    comp, skel_col = call(
        slots_kernel, scalars, [skel_first[0], skel_second[0]], [sds((1, k), jnp.int32), sds((k, 1), jnp.int32)],
        cost=SLOTS_COST,
    )

    def parts_kernel(sc, leaf_ref, end_out, side_out, *rows_outs):
        p = sc[0]
        end_out[...] = leaf_ref[:, 1 - p, :, pl.ds(pl.multiple_of(p * k, k), k)]
        side_out[...] = leaf_ref[:, 1 - p, :, 2 * k :]
        for i, rows_out in enumerate(rows_outs):
            rows_out[...] = leaf_ref[:, 2, :, i * k : (i + 1) * k]

    end_own, sides_raw, *s_rows = call(
        parts_kernel, scalars, [leaf], [sds((2, fr, k), BF16)] * 5
    )
    sides_sib = box_permute(sides_raw, 1)
    end_sib = box_permute(end_own, 1)
    s_sib = [box_permute(a, 1) for a in s_rows]

    def side_kernel(sc, own_ref, sib_ref, comp_ref, end_ref, side_out, *send_outs):
        p, q = sc[0], sc[1]
        pick_own = column_picker(comp_ref[...], p * k, k)
        pick_sib = column_picker(comp_ref[...], (1 - p) * k, k)
        side = dot(flat(own_ref[...]), pick_own) + dot(flat(sib_ref[...]), pick_sib)
        side_out[...] = side.astype(BF16).reshape(2, fr, k)
        for h, send_out in enumerate(send_outs):
            take = slice(h * hr, (h + 1) * hr)
            send_out[...] = jnp.where(p == q, end_ref[:, take, :], side_out[:, take, :])

    side, *first_send = call(
        side_kernel, scalars, [sides_raw, sides_sib, comp, end_own],
        [sds((2, fr, k), BF16)] + [sds((2, hr, k), BF16)] * 2,
    )
    first_far = [face_permute(a, s) for s in range(1, n_face) for a in first_send]

    def ends_kernel(sc, leaf_ref, comp_ref, keep_out, couple_out, slots_out, end_out):
        p = sc[0]
        pick_own = column_picker(comp_ref[...], p * k, k)
        for t in range(2):
            end_out[t, :, : 2 * k] = leaf_ref[t, p, :, : 2 * k]
            end_out[t, :, 2 * k :] = dot(leaf_ref[t, p, :, 2 * k :], pick_own).astype(BF16)
        couple = pl.ds(pl.multiple_of((1 - p) * k, k), k)
        mine, other = halves(p)
        keep_out[:, :, :k] = end_out[:, mine, couple]
        keep_out[:, :, k:] = end_out[:, mine, 2 * k :]
        couple_out[...] = end_out[:, other, couple]
        slots_out[...] = end_out[:, other, 2 * k :]

    v_keep, *v_send, end_kept = call(
        ends_kernel, after(scalars, side), [leaf, comp],
        [sds((2, hr, 2 * k), BF16)] + [sds((2, hr, k), BF16)] * 2 + [sds((2, fr, 3 * k), BF16)],
    )
    v_recv = [box_permute(a, 1) for a in v_send]

    w_one, w_two = w_first[:, 0], w_second[:, 0]
    w_one_sib = box_permute(after(w_one, side), 1)
    w_two_x = box_permute(after(w_two, side), 2)
    w_two_sib = box_permute(after(w_two, side), 1)
    w_two_x_sib = box_permute(w_two_x, 1)

    def weight_kernel(place, sc, *refs):
        out_ref = refs[-1]
        count = refs[0].shape[1]
        for i, ref in enumerate(refs[:-1]):
            take = pl.ds(pl.multiple_of(place(sc, i) * count, count), count)
            for f in range(n_face):
                @pl.when(sc[2] == f)
                def _(ref=ref, take=take, f=f):
                    out_ref[:, take, : k - f * fr] = ref[:, :, f * fr :]
                    if f > 0:
                        out_ref[:, take, k - f * fr :] = ref[:, :, : f * fr]

    (weight_one,) = call(
        functools.partial(weight_kernel, lambda sc, i: sc[0] ^ i), scalars, [w_one, w_one_sib],
        [sds((2, k, k), BF16)],
    )
    (weight_two,) = call(
        functools.partial(weight_kernel, lambda sc, i: sc[3] ^ (0, 2, 1, 3)[i]), scalars,
        [w_two, w_two_x, w_two_sib, w_two_x_sib], [sds((2, k, k), BF16)],
    )

    def rows_kernel(sc, *refs):
        owns, sibs, refs = refs[:3], refs[3:6], refs[6:]
        comp_ref, col_ref, end_ref, endsib_ref, kept_out, *outs = refs
        p, q, f = sc[0], sc[1], sc[2]
        mine, _ = halves(p)
        rest = jnp.where(p == q, endsib_ref[:, mine, :], end_ref[:, mine, :])
        for s in range(nf):
            outs[2 * nf + s][:, :, :k] = rest
        pick_own = column_picker(comp_ref[...], p * k, k)
        pick_sib = column_picker(comp_ref[...], (1 - p) * k, k)

        def pick(slots, write):
            take_own = row_picker(slots, p * k + f * fr, fr)
            take_sib = row_picker(slots, (1 - p) * k + f * fr, fr)
            for t in range(2):
                for c in range(3):
                    own, sib = owns[c][t], sibs[c][t]
                    if c == 2:
                        own, sib = [dot(a, b).astype(BF16) for a, b in ((own, pick_own), (sib, pick_sib))]
                    write(t, c, (dot(take_own, own) + dot(take_sib, sib)).astype(BF16))

        def write_far(s, t, c, picked):
            if c < 2:
                for j in range(2):
                    outs[2 * s + j][t, :, c * k : (c + 1) * k] = picked[j * qr : (j + 1) * qr]
            else:
                outs[2 * nf + s][t, :, k:] = picked

        def col_half(s):
            start = (f + n_face - s - 1) % n_face * fr + p * hr
            return col_ref[pl.ds(pl.multiple_of(start, hr), hr), :]

        far = jnp.concatenate([col_half(s) for s in range(nf)], axis=0)

        @pl.when(p == q)
        def _():
            def write(t, c, picked):
                for s in range(nf):
                    write_far(s, t, c, picked[s * hr : (s + 1) * hr])

            pick(far, write)

        @pl.when(p != q)
        def _():
            def write(t, c, picked):
                kept_out[t, :, c * k : (c + 1) * k] = picked[:fr]
                for s in range(nf):
                    write_far(s, t, c, picked[fr + s * hr : fr + (s + 1) * hr])

            pick(jnp.concatenate([col_ref[pl.ds(pl.multiple_of(f * fr, fr), fr), :], far], axis=0), write)

    kept, *kept_out = call(
        rows_kernel, scalars, [*s_rows, *s_sib, comp, skel_col, end_own, end_sib],
        [sds((2, fr, 3 * k), BF16)] + [sds((2, qr, 2 * k), BF16)] * (2 * nf) + [sds((2, hr, 2 * k), BF16)] * nf,
    )
    mixed_far = [face_permute(a, i + 1) for i, a in enumerate(kept_out[2 * nf :])]

    def piece(hidden, start, count):
        return stacked(hidden[0][:, start : start + count], hidden[1][:, start : start + count])

    def iface_kernel(sc, keep_ref, couple_ref, slots_ref, w_ref, end_ref, endsib_ref, side_ref,
                     acc_out, hid_out, rows):
        p, q = sc[0], sc[1]

        @pl.when(p == q)
        def _():
            rows[:, :, :k] = couple_ref[...]
            rows[:, :, k:] = slots_ref[...]

        @pl.when(p != q)
        def _():
            rows[...] = keep_ref[...]

        both = dot(stacked(rows[0, :, :k], rows[1, :, :k]), flat(w_ref[...])).astype(BF16)
        hidden = both[:hr], both[hr:]
        hid_out[0] = hidden[0]
        hid_out[1] = hidden[1]
        left = piece(hidden, 0, fr)
        is_end = p == q
        ends = jnp.where(is_end, end_ref[...], endsib_ref[...])
        acc_out[:, :, :k] = -dot(left, flat(ends)).reshape(2, hr, k)
        acc_out[:, :, k:] = rows[:, :, k:].astype(F32) - dot(left, flat(side_ref[...])).reshape(2, hr, k)

    v_acc, v_hid = call(
        iface_kernel, scalars, [v_keep, *v_recv, weight_one, end_own, end_sib, side],
        [sds((2, hr, 2 * k), F32), sds((2, hr, k), BF16)],
        scratch=[pltpu.VMEM((2, hr, 2 * k), BF16)], cost=OWN_COST,
    )
    first_fwd = [box_permute(after(a, kept, w_two_x), 1) for a in first_far]

    def iface_far_kernel(sc, acc_ref, hid_ref, *rest):
        far, fwd = rest[: 2 * nf], rest[2 * nf : 4 * nf]
        end_out, keep_out, send_out = rest[4 * nf :]
        q = sc[1]
        is_end = sc[0] == q
        hidden = [hid_ref[0], hid_ref[1]]
        total = acc_ref[...]
        for i in range(2 * nf):
            left = piece(hidden, fr + i * hr, hr)
            mine, other = dot(left, flat(far[i][...])), dot(left, flat(fwd[i][...]))
            both = [jnp.where(is_end, mine, other), jnp.where(is_end, other, mine)]
            total = total - jnp.concatenate(both, axis=1).reshape(2, hr, 2 * k)
        total = total.astype(BF16)
        end_out[...] = total[:, :, :k]
        low, high = total[:, :, k : k + half], total[:, :, k + half :]
        keep_out[...] = jnp.where(q == 0, low, high)
        send_out[...] = jnp.where(q == 0, high, low)

    two_end, side_keep, side_send = call(
        iface_far_kernel, scalars, [v_acc, v_hid, *first_far, *first_fwd],
        [sds((2, hr, k), BF16)] + [sds((2, hr, half), BF16)] * 2,
    )

    side_x = box_permute(side_send, 2)

    def pack_kernel(sc, end_ref, keep_ref, x_ref, out_ref):
        out_ref[:, :, :k] = end_ref[...]
        out_ref[:, :, k:] = keep_ref[...] + x_ref[...]

    (two_own,) = call(
        pack_kernel, scalars, [two_end, side_keep, side_x], [sds((2, hr, k + half), BF16)]
    )
    two_x = box_permute(two_own, 2)
    two_y = over_face(two_own)
    mixed_fwd = [box_permute(after(a, two_own), 1) for a in mixed_far]

    def weighted(w_ref, rows, out_ref):
        left = jnp.concatenate([piece((w_ref[0], w_ref[1]), s * fr, fr) for s in range(n_face)], axis=1)
        for c in range(3):
            cols = slice(c * k, (c + 1) * k)
            right = rows[:, :, :, cols].reshape(n_face * 2 * fr, k)
            out_ref[:, :, cols] = dot(left, right).astype(BF16).reshape(2, k, k)

    def weighted_one_kernel(sc, w_ref, own_ref, sib_ref, side_ref, end_ref, kept_ref, *rest):
        refs = [rest[i * nf : (i + 1) * nf] for i in range(6)]
        far, fwd = rest[: 2 * nf], rest[2 * nf : 4 * nf]
        out_ref, slots_out, rows = rest[6 * nf :]
        p, q = sc[0], sc[1]
        is_end = p == q

        @pl.when(is_end)
        def _():
            slots_out[...] = end_ref[:, :, 2 * k :]

        @pl.when(p != q)
        def _():
            for take, parts in zip(halves(p), refs[4:]):
                total = kept_ref[:, take, 2 * k :]
                for ref in parts:
                    total = total + ref[:, :, k:]
                slots_out[:, take, :] = total

        first_cols = pl.ds(pl.multiple_of(q * k, k), k)
        rest_cols = pl.ds(pl.multiple_of((1 - q) * k, k), k)
        rows[0, :, :, pl.ds(pl.multiple_of(p * k, k), k)] = own_ref[...]
        rows[0, :, :, pl.ds(pl.multiple_of((1 - p) * k, k), k)] = sib_ref[...]
        rows[0, :, :, 2 * k :] = side_ref[...]
        for s in range(nf):
            for h in range(2):
                take = slice(h * hr, (h + 1) * hr)
                mine, other = far[2 * s + h][...], fwd[2 * s + h][...]
                rows[s + 1, :, take, first_cols] = jnp.where(is_end, mine, other)
                rows[s + 1, :, take, 2 * k :] = jnp.where(is_end, other, mine)
            for take, parts in zip(halves(p), refs[4:]):
                rows[s + 1, :, take, rest_cols] = parts[s][:, :, :k]
        weighted(w_ref, rows, out_ref)

    solved_one, slot_rows = call(
        weighted_one_kernel, scalars,
        [weight_one, end_own, end_sib, side, end_kept, kept, *first_far, *first_fwd, *mixed_far, *mixed_fwd],
        [sds((2, k, 3 * k), BF16), sds((2, fr, k), BF16)],
        scratch=[pltpu.VMEM((n_face, 2, fr, 3 * k), BF16)], cost=SOLVED_COST,
    )

    def join_kernel(sc, own_ref, x_ref, out_ref):
        q = sc[1]
        for ref, which in ((own_ref, q), (x_ref, 1 - q)):
            out_ref[:, :, pl.ds(pl.multiple_of(which * k, k), k)] = ref[:, :, :k]
            out_ref[:, :, pl.ds(pl.multiple_of(2 * k + which * half, half), half)] = ref[:, :, k:]

    two_shape = [sds((2, hr, 3 * k), BF16)]
    two_rows = call(join_kernel, after(scalars, weight_two), [two_own, two_x], two_shape, cost=JOIN_COST)
    two_xy = [box_permute(after(a, *two_rows), 2) for a in two_y]
    two_rows = [*two_rows, *(a for pair in zip(two_y, two_xy) for a in pair)]
    two_sib = [box_permute(a, 1) for a in two_rows]

    ends_far = [face_permute(after(a, two_own), i // 2 + 1) for i, a in enumerate(kept_out[: 2 * nf])]
    ends_fwd = [box_permute(after(a, solved_one), 1) for a in ends_far]

    def level_one_kernel(sc, end_ref, kept_ref, *refs):
        slot_ref, refs = refs[0], refs[1:]
        ends = refs[: 2 * nf], refs[2 * nf : 4 * nf]
        col_ref, one_ref, w_ref, hid_out, first_out, slots_out, zs = refs[4 * nf :]
        p, q, f = sc[0], sc[1], sc[2]

        @pl.when(p == q)
        def _():
            zs[...] = end_ref[:, :, : 2 * k]

        @pl.when(p != q)
        def _():
            for h in range(2):
                for j in range(2):
                    take = pl.ds(pl.multiple_of((p ^ h) * hr + j * qr, qr), qr)
                    total = kept_ref[:, take, : 2 * k]
                    for ref in ends[h][j::2]:
                        total = total + ref[...]
                    zs[:, take, :] = total

        slots = col_ref[pl.ds(pl.multiple_of(f * fr, fr), fr), :]
        right = jnp.where(slots >= k, 1, 0)
        right = jnp.where(p == q, p, right) > 0
        lefts = [zs[t, :, :k] for t in range(2)]
        rights = [zs[t, :, k : 2 * k] for t in range(2)]
        left = stacked(*[jnp.where(right, a, b) for a, b in zip(lefts, rights)])
        nothing = jnp.zeros((fr, k), BF16)
        start = [
            jnp.concatenate([jnp.where(right, nothing, a) for a in lefts], axis=0),
            jnp.concatenate([jnp.where(right, a, nothing) for a in rights], axis=0),
            flat(slot_ref[...]),
        ]
        merged = [
            (start[c].astype(F32) - dot(left, flat(one_ref[:, :, c * k : (c + 1) * k]))).astype(BF16)
            for c in range(3)
        ]
        is_left = q == 0
        first_out[...] = jnp.where(is_left, merged[0], merged[1])
        slots_out[...] = merged[2]
        couple = jnp.where(is_left, merged[1], merged[0])
        second = dot(stacked(couple[:fr], couple[fr:]), flat(w_ref[...])).astype(BF16)
        for s in range(n_face):
            hid_out[s] = piece((second[:fr], second[fr:]), s * fr, fr)

    hid_two, first_two, slots_two = call(
        level_one_kernel, scalars,
        [end_kept, kept, slot_rows, *ends_far, *ends_fwd, skel_col, solved_one, weight_two],
        [sds((n_face, 2 * fr, 2 * fr), BF16), sds((2 * fr, k), BF16), sds((2 * fr, k), BF16)],
        scratch=[pltpu.VMEM((2, fr, 2 * k), BF16)], cost=KEEP_COST,
    )

    def level_two_kernel(sc, hid_ref, first_ref, slots_ref, *refs):
        mine, other = refs[: 1 + 2 * nf], refs[1 + 2 * nf : 2 + 4 * nf]
        out_ref, rows, stage, sems = refs[2 + 4 * nf :]
        q = sc[1]
        left = jnp.concatenate([hid_ref[s] for s in range(n_face)], axis=1)
        for take, parts in zip(halves(sc[0]), (mine, other)):
            rows[0, :, take, :] = parts[0][...]
            for i, ref in enumerate(parts[1:]):
                which = q ^ (i % 2)
                rows[1 + i // 2, :, take, pl.ds(pl.multiple_of(which * k, k), k)] = ref[:, :, :k]
                rows[1 + i // 2, :, take, pl.ds(pl.multiple_of(2 * k + which * half, half), half)] = ref[:, :, k:]
        copies = []
        for c in range(3):
            first = slots_ref[...]
            if c < 2:
                first = jnp.where(q == c, first_ref[...], jnp.zeros((2 * fr, k), BF16))
            right = rows[:, :, :, c * k : (c + 1) * k].reshape(n_face * 2 * fr, k)
            stage[c] = (first.astype(F32) - dot(left, right)).astype(BF16).reshape(2, fr, k)
            for t in range(2):
                copies.append(pltpu.make_async_copy(
                    stage.at[c, t], out_ref.at[t, 0, :, pl.ds(c * k, k)], sems.at[c, t]
                ))
                copies[-1].start()
        for copy in copies:
            copy.wait()

    (out,) = call(
        level_two_kernel, scalars, [hid_two, first_two, slots_two, *two_rows, *two_sib],
        [sds((2, 1, fr, 3 * k), BF16)], out_specs=[in_hbm],
        scratch=[pltpu.VMEM((n_face, 2, fr, 3 * k), BF16), pltpu.VMEM((3, 2, fr, k), BF16),
                 pltpu.SemaphoreType.DMA((3, 2))],
    )
    return out


def solution(mesh):
    return jax.shard_map(
        on_device,
        mesh=mesh,
        in_specs=(
            P(None, None, "box", None, "face", None),
            P(None, None, "box", None),
            P(None, None, "box", None),
            P(),
            P(),
        ),
        out_specs=P(None, None, ("box", "face"), None),
        check_vma=False,
    )
```

```python
import functools

import jax
import jax.numpy as jnp
from jax import lax
from jax.experimental import pallas as pl
from jax.experimental.pallas import tpu as pltpu
from jax.sharding import PartitionSpec as P

BF16 = jnp.bfloat16
F32 = jnp.float32
VMEM_BYTES = 16 * 1024 * 1024
JOIN_COST = 300000000
SLOTS_COST = 0
OWN_COST = 700_000_000
SOLVED_COST = 400_000_000
KEEP_COST = 3_000_000_000


def dot(first, second):
    return jnp.dot(first, second, preferred_element_type=F32)


def stacked(real, imag):
    return jnp.concatenate(
        [jnp.concatenate([real, -imag], axis=1), jnp.concatenate([imag, real], axis=1)], axis=0
    )


def flat(array):
    return array.reshape(array.shape[0] * array.shape[1], array.shape[2])


def column_picker(index, offset, count):
    rows = lax.broadcasted_iota(jnp.int32, (count, index.shape[1]), 0) + offset
    return jnp.where(rows == index, 1.0, 0.0).astype(BF16)


def row_picker(index, offset, count):
    cols = lax.broadcasted_iota(jnp.int32, (index.shape[0], count), 1) + offset
    return jnp.where(cols == index, 1.0, 0.0).astype(BF16)


def call(kernel, scalars, inputs, out_shapes, specs=None, out_specs=None, scratch=(), cost=0):
    in_vmem = pl.BlockSpec(memory_space=pltpu.VMEM)
    specs = specs or [in_vmem] * len(inputs)
    out_specs = out_specs or [in_vmem] * len(out_shapes)
    return pl.pallas_call(
        kernel,
        in_specs=[pl.BlockSpec(memory_space=pltpu.SMEM)] + specs,
        out_specs=out_specs,
        out_shape=out_shapes,
        scratch_shapes=list(scratch),
        compiler_params=pltpu.CompilerParams(vmem_limit_bytes=VMEM_BYTES),
        cost_estimate=pl.CostEstimate(flops=cost, bytes_accessed=0, transcendentals=0),
    )(scalars, *inputs)


def after(array, *others):
    return lax.optimization_barrier((array, *others))[0]


def on_device(leaf_maps, w_first, w_second, skel_first, skel_second):
    box = lax.axis_index("box")
    face = lax.axis_index("face")
    n_box, n_face = lax.axis_size("box"), lax.axis_size("face")
    nf = n_face - 1
    fr = leaf_maps.shape[4]
    hr = fr // 2
    qr = hr // 2
    k = leaf_maps.shape[5] // 3
    half = k // 2
    leaf = leaf_maps[:, 0, 0]
    scalars = jnp.stack([box % 2, box // 2 % 2, face, box % 4, box // 2, box // 4]).astype(jnp.int32)
    sds = jax.ShapeDtypeStruct
    in_hbm = pl.BlockSpec(memory_space=pltpu.HBM)

    def box_permute(array, mask):
        return lax.ppermute(array, "box", [(b, b ^ mask) for b in range(n_box)])

    def face_permute(array, step):
        pairs = [
            (b * n_face + f, b * n_face + (f + n_face - step) % n_face)
            for b in range(n_box) for f in range(n_face)
        ]
        return lax.ppermute(array, ("box", "face"), pairs)

    def over_face(array):
        return [face_permute(array, s) for s in range(1, n_face)]

    def halves(p):
        mine = pl.ds(pl.multiple_of(p * hr, hr), hr)
        other = pl.ds(pl.multiple_of((1 - p) * hr, hr), hr)
        return mine, other

    def slots_kernel(sc, skel_ref, skel2_ref, comp_out, col_out):
        q = sc[1]
        rows = lax.broadcasted_iota(jnp.int32, (k, k), 0)
        cols = lax.broadcasted_iota(jnp.int32, (k, k), 1)
        skel = jnp.broadcast_to(skel_ref[pl.ds(sc[4], 1), :].astype(F32), (k, k))
        column = jnp.sum(jnp.where(rows == cols, skel, 0.0), axis=1, keepdims=True)
        col_out[...] = column.astype(jnp.int32)
        place = skel2_ref[pl.ds(sc[5], 1), :] - q * k
        taken = jnp.where(rows == place, jnp.broadcast_to(column, (k, k)), 0.0)
        found = jnp.sum(taken, axis=0, keepdims=True).astype(jnp.int32)
        comp_out[...] = jnp.where(jnp.logical_and(place >= 0, place < k), found, -1)

    comp, skel_col = call(
        slots_kernel, scalars, [skel_first[0], skel_second[0]], [sds((1, k), jnp.int32), sds((k, 1), jnp.int32)],
        cost=SLOTS_COST,
    )

    def parts_kernel(sc, leaf_ref, end_out, side_out, *rows_outs):
        p = sc[0]
        end_out[...] = leaf_ref[:, 1 - p, :, pl.ds(pl.multiple_of(p * k, k), k)]
        side_out[...] = leaf_ref[:, 1 - p, :, 2 * k :]
        for i, rows_out in enumerate(rows_outs):
            rows_out[...] = leaf_ref[:, 2, :, i * k : (i + 1) * k]

    end_own, sides_raw, *s_rows = call(
        parts_kernel, scalars, [leaf], [sds((2, fr, k), BF16)] * 5
    )
    sides_sib = box_permute(sides_raw, 1)
    end_sib = box_permute(end_own, 1)
    s_sib = [box_permute(a, 1) for a in s_rows]

    def side_kernel(sc, own_ref, sib_ref, comp_ref, end_ref, side_out, *send_outs):
        p, q = sc[0], sc[1]
        pick_own = column_picker(comp_ref[...], p * k, k)
        pick_sib = column_picker(comp_ref[...], (1 - p) * k, k)
        side = dot(flat(own_ref[...]), pick_own) + dot(flat(sib_ref[...]), pick_sib)
        side_out[...] = side.astype(BF16).reshape(2, fr, k)
        for h, send_out in enumerate(send_outs):
            take = slice(h * hr, (h + 1) * hr)
            send_out[...] = jnp.where(p == q, end_ref[:, take, :], side_out[:, take, :])

    side, *first_send = call(
        side_kernel, scalars, [sides_raw, sides_sib, comp, end_own],
        [sds((2, fr, k), BF16)] + [sds((2, hr, k), BF16)] * 2,
    )
    first_far = [face_permute(a, s) for s in range(1, n_face) for a in first_send]

    def ends_kernel(sc, leaf_ref, comp_ref, keep_out, couple_out, slots_out, end_out):
        p = sc[0]
        pick_own = column_picker(comp_ref[...], p * k, k)
        for t in range(2):
            end_out[t, :, : 2 * k] = leaf_ref[t, p, :, : 2 * k]
            end_out[t, :, 2 * k :] = dot(leaf_ref[t, p, :, 2 * k :], pick_own).astype(BF16)
        couple = pl.ds(pl.multiple_of((1 - p) * k, k), k)
        mine, other = halves(p)
        keep_out[:, :, :k] = end_out[:, mine, couple]
        keep_out[:, :, k:] = end_out[:, mine, 2 * k :]
        couple_out[...] = end_out[:, other, couple]
        slots_out[...] = end_out[:, other, 2 * k :]

    v_keep, *v_send, end_kept = call(
        ends_kernel, after(scalars, side), [leaf, comp],
        [sds((2, hr, 2 * k), BF16)] + [sds((2, hr, k), BF16)] * 2 + [sds((2, fr, 3 * k), BF16)],
    )
    v_recv = [box_permute(a, 1) for a in v_send]

    w_one, w_two = w_first[:, 0], w_second[:, 0]
    w_one_sib = box_permute(after(w_one, side), 1)
    w_two_x = box_permute(after(w_two, side), 2)
    w_two_sib = box_permute(after(w_two, side), 1)
    w_two_x_sib = box_permute(w_two_x, 1)

    def weight_kernel(place, sc, *refs):
        out_ref = refs[-1]
        count = refs[0].shape[1]
        for i, ref in enumerate(refs[:-1]):
            take = pl.ds(pl.multiple_of(place(sc, i) * count, count), count)
            for f in range(n_face):
                @pl.when(sc[2] == f)
                def _(ref=ref, take=take, f=f):
                    out_ref[:, take, : k - f * fr] = ref[:, :, f * fr :]
                    if f > 0:
                        out_ref[:, take, k - f * fr :] = ref[:, :, : f * fr]

    (weight_one,) = call(
        functools.partial(weight_kernel, lambda sc, i: sc[0] ^ i), scalars, [w_one, w_one_sib],
        [sds((2, k, k), BF16)],
    )
    (weight_two,) = call(
        functools.partial(weight_kernel, lambda sc, i: sc[3] ^ (0, 2, 1, 3)[i]), scalars,
        [w_two, w_two_x, w_two_sib, w_two_x_sib], [sds((2, k, k), BF16)],
    )

    def rows_kernel(sc, *refs):
        owns, sibs, refs = refs[:3], refs[3:6], refs[6:]
        comp_ref, col_ref, end_ref, endsib_ref, kept_out, *outs = refs
        p, q, f = sc[0], sc[1], sc[2]
        mine, _ = halves(p)
        rest = jnp.where(p == q, endsib_ref[:, mine, :], end_ref[:, mine, :])
        for s in range(nf):
            outs[2 * nf + s][:, :, :k] = rest
        pick_own = column_picker(comp_ref[...], p * k, k)
        pick_sib = column_picker(comp_ref[...], (1 - p) * k, k)

        def pick(slots, write):
            take_own = row_picker(slots, p * k + f * fr, fr)
            take_sib = row_picker(slots, (1 - p) * k + f * fr, fr)
            for t in range(2):
                for c in range(3):
                    own, sib = owns[c][t], sibs[c][t]
                    if c == 2:
                        own, sib = [dot(a, b).astype(BF16) for a, b in ((own, pick_own), (sib, pick_sib))]
                    write(t, c, (dot(take_own, own) + dot(take_sib, sib)).astype(BF16))

        def write_far(s, t, c, picked):
            if c < 2:
                for j in range(2):
                    outs[2 * s + j][t, :, c * k : (c + 1) * k] = picked[j * qr : (j + 1) * qr]
            else:
                outs[2 * nf + s][t, :, k:] = picked

        def col_half(s):
            start = (f + n_face - s - 1) % n_face * fr + p * hr
            return col_ref[pl.ds(pl.multiple_of(start, hr), hr), :]

        far = jnp.concatenate([col_half(s) for s in range(nf)], axis=0)

        @pl.when(p == q)
        def _():
            def write(t, c, picked):
                for s in range(nf):
                    write_far(s, t, c, picked[s * hr : (s + 1) * hr])

            pick(far, write)

        @pl.when(p != q)
        def _():
            def write(t, c, picked):
                kept_out[t, :, c * k : (c + 1) * k] = picked[:fr]
                for s in range(nf):
                    write_far(s, t, c, picked[fr + s * hr : fr + (s + 1) * hr])

            pick(jnp.concatenate([col_ref[pl.ds(pl.multiple_of(f * fr, fr), fr), :], far], axis=0), write)

    kept, *kept_out = call(
        rows_kernel, scalars, [*s_rows, *s_sib, comp, skel_col, end_own, end_sib],
        [sds((2, fr, 3 * k), BF16)] + [sds((2, qr, 2 * k), BF16)] * (2 * nf) + [sds((2, hr, 2 * k), BF16)] * nf,
    )
    mixed_far = [face_permute(a, i + 1) for i, a in enumerate(kept_out[2 * nf :])]

    def piece(hidden, start, count):
        return stacked(hidden[0][:, start : start + count], hidden[1][:, start : start + count])

    def iface_kernel(sc, keep_ref, couple_ref, slots_ref, w_ref, end_ref, endsib_ref, side_ref,
                     acc_out, hid_out, rows):
        p, q = sc[0], sc[1]

        @pl.when(p == q)
        def _():
            rows[:, :, :k] = couple_ref[...]
            rows[:, :, k:] = slots_ref[...]

        @pl.when(p != q)
        def _():
            rows[...] = keep_ref[...]

        both = dot(stacked(rows[0, :, :k], rows[1, :, :k]), flat(w_ref[...])).astype(BF16)
        hidden = both[:hr], both[hr:]
        hid_out[0] = hidden[0]
        hid_out[1] = hidden[1]
        left = piece(hidden, 0, fr)
        is_end = p == q
        ends = jnp.where(is_end, end_ref[...], endsib_ref[...])
        acc_out[:, :, :k] = -dot(left, flat(ends)).reshape(2, hr, k)
        acc_out[:, :, k:] = rows[:, :, k:].astype(F32) - dot(left, flat(side_ref[...])).reshape(2, hr, k)

    v_acc, v_hid = call(
        iface_kernel, scalars, [v_keep, *v_recv, weight_one, end_own, end_sib, side],
        [sds((2, hr, 2 * k), F32), sds((2, hr, k), BF16)],
        scratch=[pltpu.VMEM((2, hr, 2 * k), BF16)], cost=OWN_COST,
    )
    first_fwd = [box_permute(after(a, kept, w_two_x), 1) for a in first_far]

    def iface_far_kernel(sc, acc_ref, hid_ref, *rest):
        far, fwd = rest[: 2 * nf], rest[2 * nf : 4 * nf]
        end_out, keep_out, send_out = rest[4 * nf :]
        q = sc[1]
        is_end = sc[0] == q
        hidden = [hid_ref[0], hid_ref[1]]
        total = acc_ref[...]
        for i in range(2 * nf):
            left = piece(hidden, fr + i * hr, hr)
            mine, other = dot(left, flat(far[i][...])), dot(left, flat(fwd[i][...]))
            both = [jnp.where(is_end, mine, other), jnp.where(is_end, other, mine)]
            total = total - jnp.concatenate(both, axis=1).reshape(2, hr, 2 * k)
        total = total.astype(BF16)
        end_out[...] = total[:, :, :k]
        low, high = total[:, :, k : k + half], total[:, :, k + half :]
        keep_out[...] = jnp.where(q == 0, low, high)
        send_out[...] = jnp.where(q == 0, high, low)

    two_end, side_keep, side_send = call(
        iface_far_kernel, scalars, [v_acc, v_hid, *first_far, *first_fwd],
        [sds((2, hr, k), BF16)] + [sds((2, hr, half), BF16)] * 2,
    )

    side_x = box_permute(side_send, 2)

    def pack_kernel(sc, end_ref, keep_ref, x_ref, out_ref):
        out_ref[:, :, :k] = end_ref[...]
        out_ref[:, :, k:] = keep_ref[...] + x_ref[...]

    (two_own,) = call(
        pack_kernel, scalars, [two_end, side_keep, side_x], [sds((2, hr, k + half), BF16)]
    )
    two_x = box_permute(two_own, 2)
    two_y = over_face(two_own)
    mixed_fwd = [box_permute(after(a, two_own), 1) for a in mixed_far]

    def weighted(w_ref, rows, out_ref):
        left = jnp.concatenate([piece((w_ref[0], w_ref[1]), s * fr, fr) for s in range(n_face)], axis=1)
        for c in range(3):
            cols = slice(c * k, (c + 1) * k)
            right = rows[:, :, :, cols].reshape(n_face * 2 * fr, k)
            out_ref[:, :, cols] = dot(left, right).astype(BF16).reshape(2, k, k)

    def weighted_one_kernel(sc, w_ref, own_ref, sib_ref, side_ref, *rest):
        refs = [rest[i * nf : (i + 1) * nf] for i in range(6)]
        far, fwd = rest[: 2 * nf], rest[2 * nf : 4 * nf]
        out_ref, rows = rest[6 * nf :]
        p, q = sc[0], sc[1]
        is_end = p == q
        first_cols = pl.ds(pl.multiple_of(q * k, k), k)
        rest_cols = pl.ds(pl.multiple_of((1 - q) * k, k), k)
        rows[0, :, :, pl.ds(pl.multiple_of(p * k, k), k)] = own_ref[...]
        rows[0, :, :, pl.ds(pl.multiple_of((1 - p) * k, k), k)] = sib_ref[...]
        rows[0, :, :, 2 * k :] = side_ref[...]
        for s in range(nf):
            for h in range(2):
                take = slice(h * hr, (h + 1) * hr)
                mine, other = far[2 * s + h][...], fwd[2 * s + h][...]
                rows[s + 1, :, take, first_cols] = jnp.where(is_end, mine, other)
                rows[s + 1, :, take, 2 * k :] = jnp.where(is_end, other, mine)
            for take, parts in zip(halves(p), refs[4:]):
                rows[s + 1, :, take, rest_cols] = parts[s][:, :, :k]
        weighted(w_ref, rows, out_ref)

    (solved_one,) = call(
        weighted_one_kernel, scalars,
        [weight_one, end_own, end_sib, side, *first_far, *first_fwd, *mixed_far, *mixed_fwd],
        [sds((2, k, 3 * k), BF16)], scratch=[pltpu.VMEM((n_face, 2, fr, 3 * k), BF16)], cost=SOLVED_COST,
    )

    def join_kernel(sc, own_ref, x_ref, out_ref):
        q = sc[1]
        for ref, which in ((own_ref, q), (x_ref, 1 - q)):
            out_ref[:, :, pl.ds(pl.multiple_of(which * k, k), k)] = ref[:, :, :k]
            out_ref[:, :, pl.ds(pl.multiple_of(2 * k + which * half, half), half)] = ref[:, :, k:]

    two_shape = [sds((2, hr, 3 * k), BF16)]
    two_rows = call(join_kernel, after(scalars, weight_two), [two_own, two_x], two_shape, cost=JOIN_COST)
    two_xy = [box_permute(after(a, *two_rows), 2) for a in two_y]
    two_rows = [*two_rows, *(a for pair in zip(two_y, two_xy) for a in pair)]
    two_sib = [box_permute(two_rows[0], 1)]

    ends_far = [face_permute(after(a, two_own), i // 2 + 1) for i, a in enumerate(kept_out[: 2 * nf])]
    ends_fwd = [box_permute(after(a, solved_one), 1) for a in ends_far]
    two_sib += [box_permute(after(a, *ends_fwd), 1) for a in two_rows[1:]]

    def level_one_kernel(sc, end_ref, kept_ref, *refs):
        mixed = refs[:nf], refs[nf : 2 * nf]
        ends = refs[2 * nf : 4 * nf], refs[4 * nf : 6 * nf]
        col_ref, one_ref, w_ref, hid_out, first_out, slots_out, zs = refs[6 * nf :]
        p, q, f = sc[0], sc[1], sc[2]

        @pl.when(p == q)
        def _():
            zs[...] = end_ref[...]

        @pl.when(p != q)
        def _():
            for h, take in enumerate(halves(p)):
                total = kept_ref[:, take, 2 * k :]
                for ref in mixed[h]:
                    total = total + ref[:, :, k:]
                zs[:, take, 2 * k :] = total
                for j in range(2):
                    take = pl.ds(pl.multiple_of((p ^ h) * hr + j * qr, qr), qr)
                    total = kept_ref[:, take, : 2 * k]
                    for ref in ends[h][j::2]:
                        total = total + ref[...]
                    zs[:, take, : 2 * k] = total

        slots = col_ref[pl.ds(pl.multiple_of(f * fr, fr), fr), :]
        right = jnp.where(slots >= k, 1, 0)
        right = jnp.where(p == q, p, right) > 0
        lefts = [zs[t, :, :k] for t in range(2)]
        rights = [zs[t, :, k : 2 * k] for t in range(2)]
        left = stacked(*[jnp.where(right, a, b) for a, b in zip(lefts, rights)])
        nothing = jnp.zeros((fr, k), BF16)
        start = [
            jnp.concatenate([jnp.where(right, nothing, a) for a in lefts], axis=0),
            jnp.concatenate([jnp.where(right, a, nothing) for a in rights], axis=0),
            flat(zs[:, :, 2 * k :]),
        ]
        merged = [
            (start[c].astype(F32) - dot(left, flat(one_ref[:, :, c * k : (c + 1) * k]))).astype(BF16)
            for c in range(3)
        ]
        is_left = q == 0
        first_out[...] = jnp.where(is_left, merged[0], merged[1])
        slots_out[...] = merged[2]
        couple = jnp.where(is_left, merged[1], merged[0])
        second = dot(stacked(couple[:fr], couple[fr:]), flat(w_ref[...])).astype(BF16)
        for s in range(n_face):
            hid_out[s] = piece((second[:fr], second[fr:]), s * fr, fr)

    hid_two, first_two, slots_two = call(
        level_one_kernel, scalars,
        [end_kept, kept, *mixed_far, *mixed_fwd, *ends_far, *ends_fwd, skel_col, solved_one, weight_two],
        [sds((n_face, 2 * fr, 2 * fr), BF16), sds((2 * fr, k), BF16), sds((2 * fr, k), BF16)],
        scratch=[pltpu.VMEM((2, fr, 3 * k), BF16)], cost=KEEP_COST,
    )

    def level_two_kernel(sc, hid_ref, first_ref, slots_ref, *refs):
        mine, other = refs[: 1 + 2 * nf], refs[1 + 2 * nf : 2 + 4 * nf]
        out_ref, rows, stage, sems = refs[2 + 4 * nf :]
        q = sc[1]
        left = jnp.concatenate([hid_ref[s] for s in range(n_face)], axis=1)
        for take, parts in zip(halves(sc[0]), (mine, other)):
            rows[0, :, take, :] = parts[0][...]
            for i, ref in enumerate(parts[1:]):
                which = q ^ (i % 2)
                rows[1 + i // 2, :, take, pl.ds(pl.multiple_of(which * k, k), k)] = ref[:, :, :k]
                rows[1 + i // 2, :, take, pl.ds(pl.multiple_of(2 * k + which * half, half), half)] = ref[:, :, k:]
        copies = []
        for c in range(3):
            first = slots_ref[...]
            if c < 2:
                first = jnp.where(q == c, first_ref[...], jnp.zeros((2 * fr, k), BF16))
            right = rows[:, :, :, c * k : (c + 1) * k].reshape(n_face * 2 * fr, k)
            stage[c] = (first.astype(F32) - dot(left, right)).astype(BF16).reshape(2, fr, k)
            for t in range(2):
                copies.append(pltpu.make_async_copy(
                    stage.at[c, t], out_ref.at[t, 0, :, pl.ds(c * k, k)], sems.at[c, t]
                ))
                copies[-1].start()
        for copy in copies:
            copy.wait()

    (out,) = call(
        level_two_kernel, scalars, [hid_two, first_two, slots_two, *two_rows, *two_sib],
        [sds((2, 1, fr, 3 * k), BF16)], out_specs=[in_hbm],
        scratch=[pltpu.VMEM((n_face, 2, fr, 3 * k), BF16), pltpu.VMEM((3, 2, fr, k), BF16),
                 pltpu.SemaphoreType.DMA((3, 2))],
    )
    return out


def solution(mesh):
    return jax.shard_map(
        on_device,
        mesh=mesh,
        in_specs=(
            P(None, None, "box", None, "face", None),
            P(None, None, "box", None),
            P(None, None, "box", None),
            P(),
            P(),
        ),
        out_specs=P(None, None, ("box", "face"), None),
        check_vma=False,
    )
```
